32 devices in a mesh: ctx: 8 (over z, y), wt: 4 (over x, core).
Axes of the slice: x: 2, y: 2, z: 4, core: 2. Of those that a mesh axis runs over, the one named last changes fastest.
Arguments:
- tokens: bfloat16 [5, 1024, 1024], P(None, 'ctx'), may hold values from -6 to 6
- segments: int32 [5, 1024], P(None, 'ctx'), may hold values from 0 to 1023, as said below
- attn_gain: bfloat16 [1024], replicated, may hold values from 0.099609375 to 1.8984375
- w_query: bfloat16 [1024, 1024], P(None, 'wt'), may hold values from -0.1875 to 0.1875
- key_matrix: bfloat16 [1024, 512], P(None, 'wt'), may hold values from -0.1875 to 0.1875
- value_matrix: bfloat16 [1024, 512], P(None, 'wt'), may hold values from -0.1875 to 0.1875
- q_gain: bfloat16 [64], replicated, may hold values from 0.099609375 to 1.8984375
- k_gain: bfloat16 [64], replicated, may hold values from 0.099609375 to 1.8984375
- w_out: bfloat16 [1024, 1024], P(None, 'wt'), may hold values from -0.75 to 0.75
- ffn_gain: bfloat16 [1024], replicated, may hold values from 0.099609375 to 1.8984375
- w_gate: bfloat16 [1024, 4608], P(None, 'wt'), may hold values from -0.1875 to 0.1875
- w_up: bfloat16 [1024, 4608], P(None, 'wt'), may hold values from -0.1875 to 0.1875
- w_down: bfloat16 [1024, 4608], P(None, 'wt'), may hold values from -0.09375 to 0.09375
- cotangent: bfloat16 [5, 1024, 1024], P(None, 'ctx'), may hold values from -6 to 6
Outputs:
- output: bfloat16 [5, 1024, 1024], P(None, 'ctx')
- tokens_grad: bfloat16 [5, 1024, 1024], P(None, 'ctx')
- attn_gain_grad: float32 [1024], replicated
- w_query_grad: float32 [1024, 1024], P('ctx', 'wt')
- w_key_grad: float32 [1024, 512], P('ctx', 'wt')
- w_value_grad: float32 [1024, 512], P('ctx', 'wt')
- q_gain_grad: float32 [64], replicated
- k_gain_grad: float32 [64], replicated
- w_out_grad: float32 [1024, 1024], P('ctx', 'wt')
- ffn_gain_grad: float32 [1024], replicated
- w_gate_grad: float32 [1024, 4608], P('ctx', 'wt')
- w_up_grad: float32 [1024, 4608], P('ctx', 'wt')
- w_down_grad: float32 [1024, 4608], P('ctx', 'wt')
The draws below stay inside these ranges and needn't reach their ends.
Inputs may be any that keep to these rules, and one draw needn't show every extreme that they name: `segments`: segment numbers are 0 or more and never fall along a sequence; the last document of each sequence is numbered 1024 - 1.
All inputs are finite; a program needn't handle non-finite values.
Results may differ from the reference program's by a relative error of at most 0.03.
Values may be sent and summed in bfloat16 or wider, within the bound.
A program may use at most 192 MiB of HBM per device.

```python
import math
import jax
import jax.numpy as jnp
from jax import lax

MODEL_DIMENSION = 1024
HQ = 16
KEY_VALUE_HEADS = 8
HEAD_SIZE = 64
FF = 4608
SEQS = 5
TSD = 128
LENGTH = 1024


def draw_segments(key, part):
    key = jax.random.fold_in(key, 11)
    subkeys = jax.random.split(key, 7)
    exponent = jax.random.randint(subkeys[0], (SEQS, 1), 2, 7)
    period = jnp.maximum(LENGTH // jnp.left_shift(jnp.ones_like(exponent), exponent), 2)
    rolled = jax.random.randint(subkeys[1], (SEQS, LENGTH), 0, 1 << 20)
    boundary = rolled % period == 0
    places = jnp.arange(LENGTH, dtype=jnp.int32)
    rows = jnp.arange(SEQS, dtype=jnp.int32)[:, None]
    chosen = jax.random.randint(subkeys[2], (), 0, SEQS)
    other = (chosen + 1) % SEQS
    left_end = jax.random.randint(subkeys[3], (), 1, TSD)
    right_end = LENGTH - TSD + jax.random.randint(subkeys[4], (), 0, TSD - 1)
    half = LENGTH // 2
    first_mid = half - TSD + jax.random.randint(subkeys[5], (), 0, TSD)
    second_mid = half + jax.random.randint(subkeys[6], (), 1, TSD)
    quiet_one = (rows == chosen) & (places[None, :] >= left_end) & (places[None, :] <= right_end + 1)
    quiet_two = (rows == other) & (places[None, :] >= first_mid) & (places[None, :] < half + 2 * TSD)
    forced_one = (rows == chosen) & ((places[None, :] == left_end) | (places[None, :] == right_end + 1))
    forced_two = (rows == other) & ((places[None, :] == first_mid) | (places[None, :] == second_mid))
    boundary = boundary & jnp.logical_not(quiet_one | quiet_two) | forced_one | forced_two
    boundary = boundary & (places[None, :] > 0)
    counted = jnp.cumsum(boundary.astype(jnp.int32), axis=1).astype(jnp.int32)
    return (LENGTH - 1 - counted[:, -1:] + counted).astype(jnp.int32)


def strengthened(array, rng, source, target, shards_of, factor):
    def block_of(dim):
        return (jnp.arange(array.shape[dim]) // (array.shape[dim] // shards_of)).reshape((-1,) + (1,) * (array.ndim - 1 - dim))

    one_side = jax.random.permutation(rng, shards_of)[block_of(target)]
    other_side = (block_of(target) + shards_of // 2) % shards_of
    return jnp.where((block_of(source) == one_side) | (block_of(source) == other_side), factor * array, array)


def shard_levels(stream_key, extent, cuts, smallest, largest):
    loudness, own = 1.0, jax.random.fold_in(stream_key, 6)
    for position, parts in cuts:
        steps = jnp.exp(jax.random.uniform(jax.random.fold_in(own, position), (parts,), jnp.float32, smallest / len(cuts), largest / len(cuts)))
        loudness = loudness * jnp.repeat(steps, extent[position] // parts).reshape([-1 if axis == position else 1 for axis in range(len(extent))])
    return loudness


def scatter_about(own_key, extent, deviation, reach, pieces=(), kind=jnp.bfloat16):
    entries = deviation * jax.random.normal(own_key, extent, jnp.float32)
    if pieces:
        entries = entries * shard_levels(own_key, extent, pieces, -0.22, 0.18)
    return jnp.clip(entries, -reach, reach).astype(kind)


def gaussian_with(own_key, dims, spread, most, pieces, heavy, kind=jnp.bfloat16):
    array = spread * jax.random.normal(own_key, dims, jnp.float32)
    if pieces:
        array = array * shard_levels(own_key, dims, pieces, -0.22, 0.18)
    return jnp.clip(strengthened(array, jax.random.fold_in(own_key, 3), *heavy), -most, most).astype(kind)


def setup_inputs(seed: int = 0) -> dict:
    keys = jax.random.split(jax.random.key(seed), 15)
    tokens = gaussian_with(keys[0], (SEQS, LENGTH, MODEL_DIMENSION), 1.0, 6.0, ((1, 8),), (1, 2, 8, 2.0))
    segments = draw_segments(jax.random.fold_in(keys[14], 71), 0)
    attn_gain = jnp.clip(1.0 + 0.18 * jax.random.normal(keys[2], (MODEL_DIMENSION,), jnp.float32), 0.099609375, 1.8984375).astype(jnp.bfloat16)
    w_query = scatter_about(keys[3], (MODEL_DIMENSION, HQ * HEAD_SIZE), MODEL_DIMENSION ** -0.5, 0.1875, ((1, 4),))
    key_matrix = scatter_about(keys[4], (MODEL_DIMENSION, KEY_VALUE_HEADS * HEAD_SIZE), MODEL_DIMENSION ** -0.5, 0.1875, ((1, 4),))
    value_matrix = scatter_about(keys[5], (MODEL_DIMENSION, KEY_VALUE_HEADS * HEAD_SIZE), MODEL_DIMENSION ** -0.5, 0.1875, ((1, 4),))
    q_gain = jnp.clip(1.0 + 0.18 * jax.random.normal(keys[6], (HEAD_SIZE,), jnp.float32), 0.099609375, 1.8984375).astype(jnp.bfloat16)
    k_gain = jnp.clip(1.0 + 0.18 * jax.random.normal(keys[7], (HEAD_SIZE,), jnp.float32), 0.099609375, 1.8984375).astype(jnp.bfloat16)
    w_out = scatter_about(keys[8], (MODEL_DIMENSION, HQ * HEAD_SIZE), (HQ * HEAD_SIZE // 16) ** -0.5, 0.75, ((1, 4),))
    ffn_gain = jnp.clip(1.0 + 0.18 * jax.random.normal(keys[9], (MODEL_DIMENSION,), jnp.float32), 0.099609375, 1.8984375).astype(jnp.bfloat16)
    w_gate = scatter_about(keys[10], (MODEL_DIMENSION, FF), MODEL_DIMENSION ** -0.5, 0.1875, ((1, 4),))
    w_up = scatter_about(keys[11], (MODEL_DIMENSION, FF), MODEL_DIMENSION ** -0.5, 0.1875, ((1, 4),))
    w_down = scatter_about(keys[12], (MODEL_DIMENSION, FF), FF ** -0.5, 0.09375, ((1, 4),))
    cotangent = gaussian_with(keys[13], (SEQS, LENGTH, MODEL_DIMENSION), 1.0, 6.0, ((1, 8),), (1, 2, 8, 2.0))
    return {"tokens": tokens, "segments": segments, "attn_gain": attn_gain, "w_query": w_query, "key_matrix": key_matrix, "value_matrix": value_matrix, "q_gain": q_gain, "k_gain": k_gain, "w_out": w_out, "ffn_gain": ffn_gain, "w_gate": w_gate, "w_up": w_up, "w_down": w_down, "cotangent": cotangent}


EPS = 1e-05
THETA = 1000000.0
NEG = -1e+30
HIGHEST = lax.Precision.HIGHEST

@jax.custom_vjp
def low(v):
    return lax.optimization_barrier(v.astype(jnp.bfloat16)).astype(jnp.float32)

@jax.custom_vjp
def low_back(v):
    return v

def low_keep(v):
    return (low(v), None)

def low_pass(kept, grad):
    return (grad,)

def back_keep(v):
    return (v, None)

def back_low(kept, grad):
    return (low(grad),)
low.defvjp(low_keep, low_pass)
low_back.defvjp(back_keep, back_low)

def matmul(left, right):
    return jnp.dot(left, right, precision=HIGHEST, preferred_element_type=jnp.float32)

def matmul_t(left, right):
    return lax.dot_general(left, right, (((1,), (1,)), ((), ())), precision=HIGHEST, preferred_element_type=jnp.float32)

def norm_rows(values, gain):
    return values * lax.rsqrt(lax.optimization_barrier(jnp.mean(values * values, axis=-1, keepdims=True)) + EPS) * gain

def rotate(values, cosine_table, sine_table):
    half_dim = values.shape[-1] // 2
    first_half = values[..., :half_dim]
    second_half = values[..., half_dim:]
    return jnp.concatenate([first_half * cosine_table - second_half * sine_table, second_half * cosine_table + first_half * sine_table], axis=-1)

def doc_positions(segments):
    places = jnp.arange(segments.shape[1], dtype=jnp.int32)
    preceding = jnp.concatenate([segments[:, :1] - 1, segments[:, :-1]], axis=1)
    marks = jnp.where(segments != preceding, places[None, :], 0).astype(jnp.int32)
    return places[None, :] - lax.cummax(marks, axis=1)

def layer(inputs, segment_ids, positions, attn_gain, w_query, key_matrix, value_matrix, q_gain, k_gain, w_out, ffn_gain, w_gate, w_up, w_down):
    seq_len = inputs.shape[0]
    head_dim = q_gain.shape[0]
    q_heads = w_query.shape[1] // head_dim
    kv_heads = key_matrix.shape[1] // head_dim
    score_scale = 1.0 / math.sqrt(head_dim)
    normed = low(norm_rows(inputs, attn_gain))
    queries = low_back(matmul(normed, w_query)).reshape(seq_len, q_heads, head_dim)
    keys_all = low_back(matmul(normed, key_matrix)).reshape(seq_len, kv_heads, head_dim)
    values_all = low(low_back(matmul(normed, value_matrix))).reshape(seq_len, kv_heads, head_dim)
    frequency = THETA ** (-jnp.arange(0, head_dim, 2, dtype=jnp.float32) / head_dim)
    angles = positions.astype(jnp.float32)[:, None] * frequency[None, :]
    cosine_table = jnp.cos(angles)[:, None, :]
    sine_table = jnp.sin(angles)[:, None, :]
    queries = low(rotate(norm_rows(queries, q_gain), cosine_table, sine_table))
    keys_all = low(rotate(norm_rows(keys_all, k_gain), cosine_table, sine_table))
    keys_all = jnp.repeat(keys_all, q_heads // kv_heads, axis=1)
    values_all = jnp.repeat(values_all, q_heads // kv_heads, axis=1)
    block_len = math.gcd(seq_len, 512)
    places = jnp.arange(seq_len, dtype=jnp.int32)

    def attend(first_row):
        rows_here = lax.dynamic_slice_in_dim(queries, first_row, block_len, 0)
        row_places = first_row + jnp.arange(block_len, dtype=jnp.int32)
        row_segs = lax.dynamic_slice_in_dim(segment_ids, first_row, block_len, 0)
        allowed = (places[None, :] <= row_places[:, None]) & (segment_ids[None, :] == row_segs[:, None])
        scores = low_back(score_scale * jnp.einsum('qhd,khd->hqk', rows_here, keys_all, precision=HIGHEST))
        scores = jnp.where(allowed[None], scores, NEG)
        weights = jnp.exp(scores - lax.optimization_barrier(jnp.max(scores, axis=-1, keepdims=True)))
        probs = weights / lax.optimization_barrier(jnp.sum(weights, axis=-1, keepdims=True))
        return jnp.einsum('hqk,khd->qhd', low(probs), values_all, precision=HIGHEST)
    starts = jnp.arange(0, seq_len, block_len, dtype=jnp.int32)
    heads = lax.map(jax.checkpoint(attend), starts).reshape(seq_len, q_heads * head_dim)
    heads = low(low_back(heads))
    residual = inputs + low_back(matmul_t(heads, w_out))
    normed_ffn = low(norm_rows(residual, ffn_gain))
    gate_proj = low_back(matmul(normed_ffn, w_gate))
    up_proj = low_back(matmul(normed_ffn, w_up))
    hidden = low(jax.nn.silu(gate_proj) * up_proj)
    return residual + low_back(matmul_t(hidden, w_down))

def reference(tokens, segments, attn_gain, w_query, key_matrix, value_matrix, q_gain, k_gain, w_out, ffn_gain, w_gate, w_up, w_down, cotangent):
    positions = doc_positions(segments)
    step_layer = jax.checkpoint(layer)

    def forward(inputs, *weights):

        def per_sequence(unused, sequence_item):
            seq_in, seq_ids, seq_pos = sequence_item
            return (unused, step_layer(seq_in, seq_ids, seq_pos, *weights))
        return lax.scan(per_sequence, jnp.zeros((), jnp.float32), (inputs, segments, positions))[1]
    weights = (attn_gain, w_query, key_matrix, value_matrix, q_gain, k_gain, w_out, ffn_gain, w_gate, w_up, w_down)
    weights = tuple((weight.astype(jnp.float32) for weight in weights))
    output, pullback = jax.vjp(forward, tokens.astype(jnp.float32), *weights)
    gradients = pullback(cotangent.astype(jnp.float32))
    return (output.astype(jnp.bfloat16), gradients[0].astype(jnp.bfloat16), gradients[1], gradients[2], gradients[3], gradients[4], gradients[5], gradients[6], gradients[7], gradients[8], gradients[9], gradients[10], gradients[11])
```

```python
from functools import partial
import math

import jax
import jax.numpy as jnp
from jax import lax
from jax.sharding import PartitionSpec as P

EPS = 1e-05
THETA = 1000000.0
NEG = -1e30


def product(left, right):
    return jnp.dot(left, right, preferred_element_type=jnp.float32)


def by_transpose(left, right):
    return lax.dot_general(
        left, right, (((1,), (1,)), ((), ())), preferred_element_type=jnp.float32
    )


def transpose_by(left, right):
    return lax.dot_general(
        left, right, (((0,), (0,)), ((), ())), preferred_element_type=jnp.float32
    )


def norm_rows(values, gain):
    inverse = lax.rsqrt(jnp.mean(values * values, axis=-1, keepdims=True) + EPS)
    unit_rows = values * inverse
    return (unit_rows * gain, unit_rows, inverse)


def norm_back(grads, unit_rows, inverse, gain):
    scaled = grads * gain
    return inverse * (scaled - unit_rows * jnp.mean(scaled * unit_rows, axis=-1, keepdims=True))


def rotate(values, cosine_table, sine_table, direction):
    half_dim = values.shape[-1] // 2
    first_half = values[..., :half_dim]
    second_half = values[..., half_dim:]
    return jnp.concatenate(
        [
            first_half * cosine_table - direction * second_half * sine_table,
            second_half * cosine_table + direction * first_half * sine_table,
        ],
        axis=-1,
    )


def split_blocks(array, block_len):
    shaped = array.reshape(
        (array.shape[0], array.shape[1] // block_len, block_len) + array.shape[2:]
    )
    return jnp.moveaxis(shaped, 1, 0)


def attend_piece(folded, pieces, first_row, queries, query_places, query_segs, score_scale):
    key_piece, value_piece, seg_piece = pieces
    sequences, piece_rows = seg_piece.shape
    kv_local = queries.shape[2]
    head_dim = queries.shape[4]
    block_len = math.gcd(piece_rows, 512)
    key_blocks = split_blocks(
        key_piece.reshape(sequences, piece_rows, kv_local, head_dim), block_len
    )
    value_tiles = split_blocks(
        value_piece.reshape(sequences, piece_rows, kv_local, head_dim), block_len
    )
    seg_blocks = split_blocks(seg_piece, block_len)
    offsets = block_len * jnp.arange(piece_rows // block_len, dtype=jnp.int32)

    def attend_block_step(running, block_item):
        row_max, row_sum, weighted = running
        key_block, value_block, seg_block, offset = block_item
        key_places = offset + jnp.arange(block_len, dtype=jnp.int32)
        allowed = (key_places[None, None, :] <= query_places[None, :, None]) & (
            query_segs[:, :, None] == seg_block[:, None, :]
        )
        allowed = allowed[:, None, None]
        scores = (
            jnp.einsum("sqgrd,skgd->sgrqk", queries, key_block, preferred_element_type=jnp.float32)
            * score_scale
        )
        scores = jnp.where(allowed, scores, NEG)
        new_max = jnp.maximum(row_max, jnp.max(scores, axis=-1))
        weights = jnp.where(allowed, jnp.exp(scores - new_max[..., None]), 0.0)
        fading = jnp.exp(row_max - new_max)
        row_sum = row_sum * fading + jnp.sum(weights, axis=-1)
        fade_rows = jnp.transpose(fading, (0, 3, 1, 2))[..., None]
        weighted = weighted * fade_rows + jnp.einsum(
            "sgrqk,skgd->sqgrd",
            weights.astype(jnp.bfloat16),
            value_block,
            preferred_element_type=jnp.float32,
        )
        return ((new_max, row_sum, weighted), None)

    folded, unused = lax.scan(
        attend_block_step, folded, (key_blocks, value_tiles, seg_blocks, offsets)
    )
    return folded


def grad_piece(
    folded,
    pieces,
    first_row,
    queries,
    grad_heads,
    log_total,
    row_delta,
    query_places,
    query_segs,
    score_scale,
):
    key_piece, value_piece, seg_piece = pieces
    sequences, piece_rows = seg_piece.shape
    kv_local = queries.shape[2]
    head_dim = queries.shape[4]
    block_len = math.gcd(piece_rows, 512)
    key_blocks = split_blocks(
        key_piece.reshape(sequences, piece_rows, kv_local, head_dim), block_len
    )
    value_tiles = split_blocks(
        value_piece.reshape(sequences, piece_rows, kv_local, head_dim), block_len
    )
    seg_blocks = split_blocks(seg_piece, block_len)
    offsets = block_len * jnp.arange(piece_rows // block_len, dtype=jnp.int32)

    def grad_block_step(running, block_item):
        key_block, value_block, seg_block, offset = block_item
        key_places = offset + jnp.arange(block_len, dtype=jnp.int32)
        allowed = (key_places[None, None, :] <= query_places[None, :, None]) & (
            query_segs[:, :, None] == seg_block[:, None, :]
        )
        allowed = allowed[:, None, None]
        scores = (
            jnp.einsum("sqgrd,skgd->sgrqk", queries, key_block, preferred_element_type=jnp.float32)
            * score_scale
        )
        probs = jnp.where(allowed, jnp.exp(scores - log_total[..., None]), 0.0)
        grad_probs = jnp.einsum(
            "sqgrd,skgd->sgrqk", grad_heads, value_block, preferred_element_type=jnp.float32
        )
        grad_scores = (probs * (grad_probs - row_delta[..., None])).astype(jnp.bfloat16)
        running = running + jnp.einsum(
            "sgrqk,skgd->sqgrd", grad_scores, key_block, preferred_element_type=jnp.float32
        )
        grad_keys = jnp.einsum(
            "sgrqk,sqgrd->skgd", grad_scores, queries, preferred_element_type=jnp.float32
        )
        grad_values = jnp.einsum(
            "sgrqk,sqgrd->skgd",
            probs.astype(jnp.bfloat16),
            grad_heads,
            preferred_element_type=jnp.float32,
        )
        grads = jnp.stack([grad_keys, grad_values], axis=2).astype(jnp.bfloat16)
        return (running, grads)

    folded, grads = lax.scan(
        grad_block_step, folded, (key_blocks, value_tiles, seg_blocks, offsets)
    )
    return folded, jnp.moveaxis(grads, 0, 1).reshape((sequences, piece_rows) + grads.shape[3:])


def on_device(
    tokens,
    segments,
    attn_gain,
    w_query,
    key_matrix,
    value_matrix,
    q_gain,
    k_gain,
    w_out,
    ffn_gain,
    w_gate,
    w_up,
    w_down,
    cotangent,
):
    sequences, seq_rows, model_width = tokens.shape
    head_dim = q_gain.shape[0]
    q_local = w_query.shape[1] // head_dim
    kv_local = key_matrix.shape[1] // head_dim
    per_group = q_local // kv_local
    score_scale = 1.0 / math.sqrt(head_dim)
    all_rows = sequences * seq_rows
    places = lax.axis_index("ctx") * seq_rows + jnp.arange(seq_rows, dtype=jnp.int32)
    frequency = THETA ** (-jnp.arange(0, head_dim, 2, dtype=jnp.float32) / head_dim)
    angles = places.astype(jnp.float32)[None, :, None] * frequency
    cosine_table = jnp.cos(angles)[:, :, None, :]
    sine_table = jnp.sin(angles)[:, :, None, :]
    inputs = tokens.astype(jnp.float32).reshape(all_rows, model_width)
    normed, attn_unit, attn_inverse = norm_rows(inputs, attn_gain)
    normed_low = normed.astype(jnp.bfloat16)
    query_raw = product(normed_low, w_query).reshape(sequences, seq_rows, q_local, head_dim)
    key_raw = product(normed_low, key_matrix).reshape(sequences, seq_rows, kv_local, head_dim)
    value_low = (
        product(normed_low, value_matrix)
        .astype(jnp.bfloat16)
        .reshape(sequences, seq_rows, kv_local * head_dim)
    )
    query_normed, query_unit, query_inverse = norm_rows(query_raw, q_gain)
    key_normed, key_unit, key_inverse = norm_rows(key_raw, k_gain)
    query_low = rotate(query_normed, cosine_table, sine_table, 1.0).astype(jnp.bfloat16)
    key_low = rotate(key_normed, cosine_table, sine_table, 1.0).astype(jnp.bfloat16)
    key_flat = key_low.reshape(sequences, seq_rows, kv_local * head_dim)
    query_groups = query_low.reshape(sequences, seq_rows, kv_local, per_group, head_dim)
    attend = partial(
        attend_piece,
        queries=query_groups,
        query_places=places,
        query_segs=segments,
        score_scale=score_scale,
    )
    start_state = (
        jnp.full((sequences, kv_local, per_group, seq_rows), NEG, jnp.float32),
        jnp.zeros((sequences, kv_local, per_group, seq_rows), jnp.float32),
        jnp.zeros((sequences, seq_rows, kv_local, per_group, head_dim), jnp.float32),
    )
    keys_values = lax.all_gather(
        jnp.concatenate([key_flat, value_low], axis=-1), "ctx", axis=1, tiled=True
    )
    kv_width = kv_local * head_dim
    gathered = (
        keys_values[..., :kv_width],
        keys_values[..., kv_width:],
        lax.all_gather(segments, "ctx", axis=1, tiled=True),
    )
    row_max, row_sum, weighted = attend(
        start_state,
        gathered,
        jnp.int32(0),
    )
    mixed_heads = weighted / jnp.transpose(row_sum, (0, 3, 1, 2))[..., None]
    mixed_low = mixed_heads.astype(jnp.bfloat16).reshape(all_rows, q_local * head_dim)
    attn_term = by_transpose(mixed_low, w_out)
    residual = inputs + lax.psum(attn_term.astype(jnp.bfloat16), "wt").astype(jnp.float32)
    normed_ffn, ffn_unit, ffn_inverse = norm_rows(residual, ffn_gain)
    normed_ffn_low = normed_ffn.astype(jnp.bfloat16)
    gate_proj = product(normed_ffn_low, w_gate)
    up_proj = product(normed_ffn_low, w_up)
    gate_sigmoid = jax.nn.sigmoid(gate_proj)
    gate_silu = gate_proj * gate_sigmoid
    hidden_low = (gate_silu * up_proj).astype(jnp.bfloat16)
    mlp_term = by_transpose(hidden_low, w_down)
    output_rows = (
        residual + lax.psum(mlp_term.astype(jnp.bfloat16), "wt").astype(jnp.float32)
    ).astype(jnp.bfloat16)
    log_total = row_max + jnp.log(row_sum)
    grad_rows = cotangent.reshape(all_rows, model_width)
    w_down_grad = transpose_by(grad_rows, hidden_low)
    grad_hidden = product(grad_rows, w_down)
    grad_gate = (
        grad_hidden * up_proj * gate_sigmoid * (1.0 + gate_proj * (1.0 - gate_sigmoid))
    ).astype(jnp.bfloat16)
    grad_up = (grad_hidden * gate_silu).astype(jnp.bfloat16)
    w_gate_grad = transpose_by(normed_ffn_low, grad_gate)
    w_up_grad = transpose_by(normed_ffn_low, grad_up)
    grad_normed_ffn = by_transpose(grad_gate, w_gate) + by_transpose(grad_up, w_up)
    ffn_gain_part = jnp.sum(grad_normed_ffn * ffn_unit, axis=0)
    grad_normed_ffn = lax.psum(grad_normed_ffn.astype(jnp.bfloat16), "wt").astype(jnp.float32)
    grad_residual = grad_rows.astype(jnp.float32) + norm_back(
        grad_normed_ffn, ffn_unit, ffn_inverse, ffn_gain
    )
    grad_residual_low = grad_residual.astype(jnp.bfloat16)
    w_out_grad = transpose_by(grad_residual_low, mixed_low)
    grad_heads_low = product(grad_residual_low, w_out).astype(jnp.bfloat16)
    grad_groups = grad_heads_low.reshape(sequences, seq_rows, kv_local, per_group, head_dim)
    delta_rows = jnp.sum(grad_groups.astype(jnp.float32) * mixed_heads, axis=-1)
    delta_cols = jnp.transpose(delta_rows, (0, 2, 3, 1))
    query_grad_fn = partial(
        grad_piece,
        queries=query_groups,
        grad_heads=grad_groups,
        log_total=log_total,
        row_delta=delta_cols,
        query_places=places,
        query_segs=segments,
        score_scale=score_scale,
    )
    grad_query, grad_pairs = query_grad_fn(
        jnp.zeros((sequences, seq_rows, kv_local, per_group, head_dim), jnp.float32),
        gathered,
        jnp.int32(0),
    )
    grad_pairs = lax.psum_scatter(grad_pairs, "ctx", scatter_dimension=1, tiled=True).astype(
        jnp.float32
    )
    grad_key = grad_pairs[:, :, 0]
    grad_value = grad_pairs[:, :, 1]
    grad_query = rotate(
        grad_query.reshape(sequences, seq_rows, q_local, head_dim) * score_scale,
        cosine_table,
        sine_table,
        -1.0,
    )
    grad_key = rotate(grad_key * score_scale, cosine_table, sine_table, -1.0)
    q_gain_part = jnp.sum(grad_query * query_unit, axis=(0, 1, 2))
    k_gain_part = jnp.sum(grad_key * key_unit, axis=(0, 1, 2))
    grad_query_low = (
        norm_back(grad_query, query_unit, query_inverse, q_gain)
        .astype(jnp.bfloat16)
        .reshape(all_rows, q_local * head_dim)
    )
    grad_key_low = (
        norm_back(grad_key, key_unit, key_inverse, k_gain)
        .astype(jnp.bfloat16)
        .reshape(all_rows, kv_local * head_dim)
    )
    grad_value_low = grad_value.astype(jnp.bfloat16).reshape(all_rows, kv_local * head_dim)
    w_query_grad = transpose_by(normed_low, grad_query_low)
    w_key_grad = transpose_by(normed_low, grad_key_low)
    w_value_grad = transpose_by(normed_low, grad_value_low)
    grad_normed = (
        by_transpose(grad_query_low, w_query)
        + by_transpose(grad_key_low, key_matrix)
        + by_transpose(grad_value_low, value_matrix)
    )
    attn_gain_part = jnp.sum(grad_normed * attn_unit, axis=0)
    grad_normed = lax.psum(grad_normed.astype(jnp.bfloat16), "wt").astype(jnp.float32)
    tokens_rows = (
        grad_residual + norm_back(grad_normed, attn_unit, attn_inverse, attn_gain)
    ).astype(jnp.bfloat16)
    output = output_rows.reshape(sequences, seq_rows, model_width)
    tokens_grad = tokens_rows.reshape(sequences, seq_rows, model_width)
    partial_sums = (
        w_down_grad,
        w_gate_grad,
        w_up_grad,
        w_out_grad,
        w_query_grad,
        w_key_grad,
        w_value_grad,
    )
    summed = [
        lax.psum_scatter(part.astype(jnp.bfloat16), "ctx", scatter_dimension=0, tiled=True).astype(
            jnp.float32
        )
        for part in partial_sums
    ]
    w_down_grad, w_gate_grad, w_up_grad, w_out_grad, w_query_grad, w_key_grad, w_value_grad = summed
    attn_gain_grad, q_gain_grad, k_gain_grad, ffn_gain_grad = lax.psum(
        (attn_gain_part, q_gain_part, k_gain_part, ffn_gain_part), ("ctx", "wt")
    )
    return (
        output,
        tokens_grad,
        attn_gain_grad,
        w_query_grad,
        w_key_grad,
        w_value_grad,
        q_gain_grad,
        k_gain_grad,
        w_out_grad,
        ffn_gain_grad,
        w_gate_grad,
        w_up_grad,
        w_down_grad,
    )


def solution(mesh):
    in_specs = (
        P(None, "ctx", None),
        P(None, "ctx"),
        P(),
        P(None, "wt"),
        P(None, "wt"),
        P(None, "wt"),
        P(),
        P(),
        P(None, "wt"),
        P(),
        P(None, "wt"),
        P(None, "wt"),
        P(None, "wt"),
        P(None, "ctx", None),
    )
    out_specs = (
        P(None, "ctx", None),
        P(None, "ctx", None),
        P(),
        P("ctx", "wt"),
        P("ctx", "wt"),
        P("ctx", "wt"),
        P(),
        P(),
        P("ctx", "wt"),
        P(),
        P("ctx", "wt"),
        P("ctx", "wt"),
        P("ctx", "wt"),
    )
    return jax.shard_map(
        on_device, mesh=mesh, in_specs=in_specs, out_specs=out_specs, check_vma=False
    )
```

```python
from functools import partial
import math

import jax
import jax.numpy as jnp
from jax import lax
from jax.experimental import pallas as pl
from jax.experimental.pallas import tpu as pltpu
from jax.sharding import PartitionSpec as P

EPS = 1e-05
THETA = 1000000.0
NEG = -1e30


def product(left, right):
    return jnp.dot(left, right, preferred_element_type=jnp.float32)


def by_transpose(left, right):
    return lax.dot_general(
        left, right, (((1,), (1,)), ((), ())), preferred_element_type=jnp.float32
    )


def transpose_by(left, right):
    return lax.dot_general(
        left, right, (((0,), (0,)), ((), ())), preferred_element_type=jnp.float32
    )


def norm_rows(values, gain):
    inverse = lax.rsqrt(jnp.mean(values * values, axis=-1, keepdims=True) + EPS)
    unit_rows = values * inverse
    return (unit_rows * gain, unit_rows, inverse)


def norm_back(grads, unit_rows, inverse, gain):
    scaled = grads * gain
    return inverse * (scaled - unit_rows * jnp.mean(scaled * unit_rows, axis=-1, keepdims=True))


def rotate(values, cosine_table, sine_table, direction):
    half_dim = values.shape[-1] // 2
    first_half = values[..., :half_dim]
    second_half = values[..., half_dim:]
    return jnp.concatenate(
        [
            first_half * cosine_table - direction * second_half * sine_table,
            second_half * cosine_table + direction * first_half * sine_table,
        ],
        axis=-1,
    )


def split_blocks(array, block_len):
    shaped = array.reshape(
        (array.shape[0], array.shape[1] // block_len, block_len) + array.shape[2:]
    )
    return jnp.moveaxis(shaped, 1, 0)


def attend_piece(folded, pieces, first_row, queries, query_places, query_segs, score_scale):
    key_piece, value_piece, seg_piece = pieces
    sequences, piece_rows = seg_piece.shape
    kv_local = queries.shape[2]
    head_dim = queries.shape[4]
    block_len = math.gcd(piece_rows, 512)
    key_blocks = split_blocks(
        key_piece.reshape(sequences, piece_rows, kv_local, head_dim), block_len
    )
    value_tiles = split_blocks(
        value_piece.reshape(sequences, piece_rows, kv_local, head_dim), block_len
    )
    seg_blocks = split_blocks(seg_piece, block_len)
    offsets = block_len * jnp.arange(piece_rows // block_len, dtype=jnp.int32)

    def attend_block_step(running, block_item):
        row_max, row_sum, weighted = running
        key_block, value_block, seg_block, offset = block_item
        key_places = offset + jnp.arange(block_len, dtype=jnp.int32)
        allowed = (key_places[None, None, :] <= query_places[None, :, None]) & (
            query_segs[:, :, None] == seg_block[:, None, :]
        )
        allowed = allowed[:, None, None]
        scores = (
            jnp.einsum("sqgrd,skgd->sgrqk", queries, key_block, preferred_element_type=jnp.float32)
            * score_scale
        )
        scores = jnp.where(allowed, scores, NEG)
        new_max = jnp.maximum(row_max, jnp.max(scores, axis=-1))
        weights = jnp.where(allowed, jnp.exp(scores - new_max[..., None]), 0.0)
        fading = jnp.exp(row_max - new_max)
        row_sum = row_sum * fading + jnp.sum(weights, axis=-1)
        fade_rows = jnp.transpose(fading, (0, 3, 1, 2))[..., None]
        weighted = weighted * fade_rows + jnp.einsum(
            "sgrqk,skgd->sqgrd",
            weights.astype(jnp.bfloat16),
            value_block,
            preferred_element_type=jnp.float32,
        )
        return ((new_max, row_sum, weighted), None)

    folded, unused = lax.scan(
        attend_block_step, folded, (key_blocks, value_tiles, seg_blocks, offsets)
    )
    return folded


def grad_piece(
    folded,
    pieces,
    first_row,
    queries,
    grad_heads,
    log_total,
    row_delta,
    query_places,
    query_segs,
    score_scale,
):
    key_piece, value_piece, seg_piece = pieces
    sequences, piece_rows = seg_piece.shape
    kv_local = queries.shape[2]
    head_dim = queries.shape[4]
    block_len = math.gcd(piece_rows, 512)
    key_blocks = split_blocks(
        key_piece.reshape(sequences, piece_rows, kv_local, head_dim), block_len
    )
    value_tiles = split_blocks(
        value_piece.reshape(sequences, piece_rows, kv_local, head_dim), block_len
    )
    seg_blocks = split_blocks(seg_piece, block_len)
    offsets = block_len * jnp.arange(piece_rows // block_len, dtype=jnp.int32)

    def grad_block_step(running, block_item):
        key_block, value_block, seg_block, offset = block_item
        key_places = offset + jnp.arange(block_len, dtype=jnp.int32)
        allowed = (key_places[None, None, :] <= query_places[None, :, None]) & (
            query_segs[:, :, None] == seg_block[:, None, :]
        )
        allowed = allowed[:, None, None]
        scores = (
            jnp.einsum("sqgrd,skgd->sgrqk", queries, key_block, preferred_element_type=jnp.float32)
            * score_scale
        )
        probs = jnp.where(allowed, jnp.exp(scores - log_total[..., None]), 0.0)
        grad_probs = jnp.einsum(
            "sqgrd,skgd->sgrqk", grad_heads, value_block, preferred_element_type=jnp.float32
        )
        grad_scores = (probs * (grad_probs - row_delta[..., None])).astype(jnp.bfloat16)
        running = running + jnp.einsum(
            "sgrqk,skgd->sqgrd", grad_scores, key_block, preferred_element_type=jnp.float32
        )
        grad_keys = jnp.einsum(
            "sgrqk,sqgrd->skgd", grad_scores, queries, preferred_element_type=jnp.float32
        )
        grad_values = jnp.einsum(
            "sgrqk,sqgrd->skgd",
            probs.astype(jnp.bfloat16),
            grad_heads,
            preferred_element_type=jnp.float32,
        )
        grads = jnp.stack([grad_keys, grad_values], axis=2).astype(jnp.bfloat16)
        return (running, grads)

    folded, grads = lax.scan(
        grad_block_step, folded, (key_blocks, value_tiles, seg_blocks, offsets)
    )
    return folded, jnp.moveaxis(grads, 0, 1).reshape((sequences, piece_rows) + grads.shape[3:])


MESH = pl.DeviceIdType.MESH
MIB = 1 << 20


def ring_place(index, count):
    return lax.select(
        lax.rem(index, 2) == 0, lax.div(index, 2), count - 1 - lax.div(index, 2)
    )


def ring_index(place, count):
    place = lax.rem(place + 2 * count, count)
    return lax.select(
        place < lax.div(count, 2), 2 * place, 2 * (count - 1 - place) + 1
    )


class Ring:
    def __init__(self, count, slots, send_sems, recv_sems):
        self.count, self.slots = count, slots
        self.send_sems, self.recv_sems = send_sems, recv_sems
        self.other = lax.axis_index("wt")
        self.place = ring_place(lax.axis_index("ctx"), count)
        self.right = ring_index(self.place + 1, count)
        self.left = ring_index(self.place + count - 1, count)
        self.half = slots.shape[2] // 2

    def copy(self, which, step, way):
        rows = pl.ds(way * self.half, self.half)
        later = step + 1 if isinstance(step, int) else lax.add(step, 1)
        return pltpu.make_async_remote_copy(
            src_ref=self.slots.at[which, step, rows],
            dst_ref=self.slots.at[which, later, rows],
            send_sem=self.send_sems.at[which, step, way],
            recv_sem=self.recv_sems.at[which, step, way],
            device_id=((self.right, self.left)[way], self.other),
            device_id_type=MESH,
        )

    def tick(self, which, step, left_ref, right_ref, first=False, result=None):
        half = self.half
        rows = [
            ring_index(target, self.count) * (2 * half) + way * half
            for way, target in enumerate(
                (self.place + self.count - 1 - step, self.place + 1 + step)
            )
        ]
        left = jnp.concatenate(
            [left_ref[pl.ds(pl.multiple_of(row, half), half), :] for row in rows], axis=0
        )
        total = jnp.dot(left, right_ref[...], preferred_element_type=jnp.float32)
        if not first:
            for way in range(2):
                self.copy(which, step - 1, way).wait_recv()
            total = total + self.slots[which, step].astype(jnp.float32)
        if result is None:
            self.slots[which, step] = total.astype(jnp.bfloat16)
            for way in range(2):
                self.copy(which, step, way).start()
        else:
            result[...] = total

    def finish(self, which):
        for way in range(2):

            def wait(step, carry):
                self.copy(which, step, way).wait_send()
                return carry

            lax.fori_loop(0, self.count - 1, wait, 0)


def greet(peers):
    barrier = pltpu.get_barrier_semaphore()
    for peer in peers:
        pl.semaphore_signal(barrier, inc=1, device_id=peer, device_id_type=MESH)
    pl.semaphore_wait(barrier, len(peers))


def ring_kernel(count, *refs):
    (cot_t, normed_ffn_t, grad_res_t, normed_t, ffn_grads, heads, grad_qkv) = refs[:7]
    (ffn_sums, out_sums, qkv_sums) = refs[7:10]
    scratch = refs[10:]
    rings = [Ring(count, *scratch[3 * i : 3 * i + 3]) for i in range(3)]
    greet([(rings[0].right, rings[0].other), (rings[0].left, rings[0].other)])
    ffn, out, qkv = rings
    lefts = (cot_t, normed_ffn_t, normed_ffn_t)
    for i in range(3):
        ffn.tick(i, 0, lefts[i], ffn_grads.at[i], first=True)
    out.tick(0, 0, grad_res_t, heads, first=True)
    qkv.tick(0, 0, normed_t, grad_qkv, first=True)

    def middle(step, carry):
        for i in range(3):
            ffn.tick(i, step, lefts[i], ffn_grads.at[i])
        out.tick(0, step, grad_res_t, heads)
        qkv.tick(0, step, normed_t, grad_qkv)
        return carry

    lax.fori_loop(1, count - 1, middle, 0)
    for i in range(3):
        ffn.tick(i, count - 1, lefts[i], ffn_grads.at[i], result=ffn_sums.at[i])
    out.tick(0, count - 1, grad_res_t, heads, result=out_sums)
    qkv.tick(0, count - 1, normed_t, grad_qkv, result=qkv_sums)
    for i in range(3):
        ffn.finish(i)
    out.finish(0)
    qkv.finish(0)


def ring_sums(cot_t, normed_ffn_t, grad_res_t, normed_t, ffn_grads, heads, grad_qkv):
    count = lax.axis_size("ctx")
    rows = cot_t.shape[0] // count
    widths = [(3, ffn_grads.shape[2]), (1, heads.shape[1]), (1, grad_qkv.shape[1])]
    scratch = []
    for arrays, width in widths:
        scratch += [
            pltpu.VMEM((arrays, count, rows, width), jnp.bfloat16),
            pltpu.SemaphoreType.DMA((arrays, count - 1, 2)),
            pltpu.SemaphoreType.DMA((arrays, count - 1, 2)),
        ]
    vmem = pl.BlockSpec(memory_space=pltpu.VMEM)
    return pl.pallas_call(
        partial(ring_kernel, count),
        out_shape=[
            jax.ShapeDtypeStruct((3, rows, widths[0][1]), jnp.float32),
            jax.ShapeDtypeStruct((rows, widths[1][1]), jnp.float32),
            jax.ShapeDtypeStruct((rows, widths[2][1]), jnp.float32),
        ],
        in_specs=[vmem] * 7,
        out_specs=[vmem] * 3,
        scratch_shapes=scratch,
        compiler_params=pltpu.CompilerParams(
            collective_id=1, has_side_effects=True, vmem_limit_bytes=60 * MIB
        ),
    )(cot_t, normed_ffn_t, grad_res_t, normed_t, ffn_grads, heads, grad_qkv)


def ring_fits(model_width, all_rows):
    count = lax.axis_size("ctx")
    return count % 2 == 0 and model_width % (32 * count) == 0 and all_rows <= 640


def on_device(
    tokens,
    segments,
    attn_gain,
    w_query,
    key_matrix,
    value_matrix,
    q_gain,
    k_gain,
    w_out,
    ffn_gain,
    w_gate,
    w_up,
    w_down,
    cotangent,
):
    sequences, seq_rows, model_width = tokens.shape
    head_dim = q_gain.shape[0]
    q_local = w_query.shape[1] // head_dim
    kv_local = key_matrix.shape[1] // head_dim
    per_group = q_local // kv_local
    score_scale = 1.0 / math.sqrt(head_dim)
    all_rows = sequences * seq_rows
    places = lax.axis_index("ctx") * seq_rows + jnp.arange(seq_rows, dtype=jnp.int32)
    frequency = THETA ** (-jnp.arange(0, head_dim, 2, dtype=jnp.float32) / head_dim)
    angles = places.astype(jnp.float32)[None, :, None] * frequency
    cosine_table = jnp.cos(angles)[:, :, None, :]
    sine_table = jnp.sin(angles)[:, :, None, :]
    inputs = tokens.astype(jnp.float32).reshape(all_rows, model_width)
    normed, attn_unit, attn_inverse = norm_rows(inputs, attn_gain)
    normed_low = normed.astype(jnp.bfloat16)
    query_raw = product(normed_low, w_query).reshape(sequences, seq_rows, q_local, head_dim)
    key_raw = product(normed_low, key_matrix).reshape(sequences, seq_rows, kv_local, head_dim)
    value_low = (
        product(normed_low, value_matrix)
        .astype(jnp.bfloat16)
        .reshape(sequences, seq_rows, kv_local * head_dim)
    )
    query_normed, query_unit, query_inverse = norm_rows(query_raw, q_gain)
    key_normed, key_unit, key_inverse = norm_rows(key_raw, k_gain)
    query_low = rotate(query_normed, cosine_table, sine_table, 1.0).astype(jnp.bfloat16)
    key_low = rotate(key_normed, cosine_table, sine_table, 1.0).astype(jnp.bfloat16)
    key_flat = key_low.reshape(sequences, seq_rows, kv_local * head_dim)
    query_groups = query_low.reshape(sequences, seq_rows, kv_local, per_group, head_dim)
    attend = partial(
        attend_piece,
        queries=query_groups,
        query_places=places,
        query_segs=segments,
        score_scale=score_scale,
    )
    start_state = (
        jnp.full((sequences, kv_local, per_group, seq_rows), NEG, jnp.float32),
        jnp.zeros((sequences, kv_local, per_group, seq_rows), jnp.float32),
        jnp.zeros((sequences, seq_rows, kv_local, per_group, head_dim), jnp.float32),
    )
    keys_values = lax.all_gather(
        jnp.concatenate([key_flat, value_low], axis=-1), "ctx", axis=1, tiled=True
    )
    kv_width = kv_local * head_dim
    gathered = (
        keys_values[..., :kv_width],
        keys_values[..., kv_width:],
        lax.all_gather(segments, "ctx", axis=1, tiled=True),
    )
    row_max, row_sum, weighted = attend(
        start_state,
        gathered,
        jnp.int32(0),
    )
    mixed_heads = weighted / jnp.transpose(row_sum, (0, 3, 1, 2))[..., None]
    mixed_low = mixed_heads.astype(jnp.bfloat16).reshape(all_rows, q_local * head_dim)
    attn_term = by_transpose(mixed_low, w_out)
    residual = inputs + lax.psum(attn_term.astype(jnp.bfloat16), "wt").astype(jnp.float32)
    normed_ffn, ffn_unit, ffn_inverse = norm_rows(residual, ffn_gain)
    normed_ffn_low = normed_ffn.astype(jnp.bfloat16)
    gate_proj = product(normed_ffn_low, w_gate)
    up_proj = product(normed_ffn_low, w_up)
    gate_sigmoid = jax.nn.sigmoid(gate_proj)
    gate_silu = gate_proj * gate_sigmoid
    hidden_low = (gate_silu * up_proj).astype(jnp.bfloat16)
    mlp_term = by_transpose(hidden_low, w_down)
    output_rows = (
        residual + lax.psum(mlp_term.astype(jnp.bfloat16), "wt").astype(jnp.float32)
    ).astype(jnp.bfloat16)
    log_total = row_max + jnp.log(row_sum)
    grad_rows = cotangent.reshape(all_rows, model_width)
    grad_hidden = product(grad_rows, w_down)
    grad_gate = (
        grad_hidden * up_proj * gate_sigmoid * (1.0 + gate_proj * (1.0 - gate_sigmoid))
    ).astype(jnp.bfloat16)
    grad_up = (grad_hidden * gate_silu).astype(jnp.bfloat16)
    grad_normed_ffn = by_transpose(grad_gate, w_gate) + by_transpose(grad_up, w_up)
    ffn_gain_part = jnp.sum(grad_normed_ffn * ffn_unit, axis=0)
    grad_normed_ffn = lax.psum(grad_normed_ffn.astype(jnp.bfloat16), "wt").astype(jnp.float32)
    grad_residual = grad_rows.astype(jnp.float32) + norm_back(
        grad_normed_ffn, ffn_unit, ffn_inverse, ffn_gain
    )
    grad_residual_low = grad_residual.astype(jnp.bfloat16)
    grad_heads_low = product(grad_residual_low, w_out).astype(jnp.bfloat16)
    grad_groups = grad_heads_low.reshape(sequences, seq_rows, kv_local, per_group, head_dim)
    delta_rows = jnp.sum(grad_groups.astype(jnp.float32) * mixed_heads, axis=-1)
    delta_cols = jnp.transpose(delta_rows, (0, 2, 3, 1))
    query_grad_fn = partial(
        grad_piece,
        queries=query_groups,
        grad_heads=grad_groups,
        log_total=log_total,
        row_delta=delta_cols,
        query_places=places,
        query_segs=segments,
        score_scale=score_scale,
    )
    grad_query, grad_pairs = query_grad_fn(
        jnp.zeros((sequences, seq_rows, kv_local, per_group, head_dim), jnp.float32),
        gathered,
        jnp.int32(0),
    )
    grad_pairs = lax.psum_scatter(grad_pairs, "ctx", scatter_dimension=1, tiled=True).astype(
        jnp.float32
    )
    grad_key = grad_pairs[:, :, 0]
    grad_value = grad_pairs[:, :, 1]
    grad_query = rotate(
        grad_query.reshape(sequences, seq_rows, q_local, head_dim) * score_scale,
        cosine_table,
        sine_table,
        -1.0,
    )
    grad_key = rotate(grad_key * score_scale, cosine_table, sine_table, -1.0)
    q_gain_part = jnp.sum(grad_query * query_unit, axis=(0, 1, 2))
    k_gain_part = jnp.sum(grad_key * key_unit, axis=(0, 1, 2))
    grad_query_low = (
        norm_back(grad_query, query_unit, query_inverse, q_gain)
        .astype(jnp.bfloat16)
        .reshape(all_rows, q_local * head_dim)
    )
    grad_key_low = (
        norm_back(grad_key, key_unit, key_inverse, k_gain)
        .astype(jnp.bfloat16)
        .reshape(all_rows, kv_local * head_dim)
    )
    grad_value_low = grad_value.astype(jnp.bfloat16).reshape(all_rows, kv_local * head_dim)
    grad_normed = (
        by_transpose(grad_query_low, w_query)
        + by_transpose(grad_key_low, key_matrix)
        + by_transpose(grad_value_low, value_matrix)
    )
    attn_gain_part = jnp.sum(grad_normed * attn_unit, axis=0)
    grad_normed = lax.psum(grad_normed.astype(jnp.bfloat16), "wt").astype(jnp.float32)
    tokens_rows = (
        grad_residual + norm_back(grad_normed, attn_unit, attn_inverse, attn_gain)
    ).astype(jnp.bfloat16)
    output = output_rows.reshape(sequences, seq_rows, model_width)
    tokens_grad = tokens_rows.reshape(sequences, seq_rows, model_width)
    if not ring_fits(model_width, all_rows):
        partial_sums = (
            transpose_by(grad_rows, hidden_low),
            transpose_by(normed_ffn_low, grad_gate),
            transpose_by(normed_ffn_low, grad_up),
            transpose_by(grad_residual_low, mixed_low),
            transpose_by(normed_low, grad_query_low),
            transpose_by(normed_low, grad_key_low),
            transpose_by(normed_low, grad_value_low),
        )
        summed = [
            lax.psum_scatter(
                part.astype(jnp.bfloat16), "ctx", scatter_dimension=0, tiled=True
            ).astype(jnp.float32)
            for part in partial_sums
        ]
        w_down_grad, w_gate_grad, w_up_grad, w_out_grad = summed[:4]
        w_query_grad, w_key_grad, w_value_grad = summed[4:]
    else:
        ffn_sums, w_out_grad, qkv_sums = ring_sums(
            grad_rows.T,
            normed_ffn_low.T,
            grad_residual_low.T,
            normed_low.T,
            jnp.stack([hidden_low, grad_gate, grad_up]),
            mixed_low,
            jnp.concatenate([grad_query_low, grad_key_low, grad_value_low], axis=1),
        )
        w_down_grad, w_gate_grad, w_up_grad = ffn_sums[0], ffn_sums[1], ffn_sums[2]
        query_width, key_width = q_local * head_dim, kv_local * head_dim
        w_query_grad = qkv_sums[:, :query_width]
        w_key_grad = qkv_sums[:, query_width : query_width + key_width]
        w_value_grad = qkv_sums[:, query_width + key_width :]
    attn_gain_grad, q_gain_grad, k_gain_grad, ffn_gain_grad = lax.psum(
        (attn_gain_part, q_gain_part, k_gain_part, ffn_gain_part), ("ctx", "wt")
    )
    return (
        output,
        tokens_grad,
        attn_gain_grad,
        w_query_grad,
        w_key_grad,
        w_value_grad,
        q_gain_grad,
        k_gain_grad,
        w_out_grad,
        ffn_gain_grad,
        w_gate_grad,
        w_up_grad,
        w_down_grad,
    )


def solution(mesh):
    in_specs = (
        P(None, "ctx", None),
        P(None, "ctx"),
        P(),
        P(None, "wt"),
        P(None, "wt"),
        P(None, "wt"),
        P(),
        P(),
        P(None, "wt"),
        P(),
        P(None, "wt"),
        P(None, "wt"),
        P(None, "wt"),
        P(None, "ctx", None),
    )
    out_specs = (
        P(None, "ctx", None),
        P(None, "ctx", None),
        P(),
        P("ctx", "wt"),
        P("ctx", "wt"),
        P("ctx", "wt"),
        P(),
        P(),
        P("ctx", "wt"),
        P(),
        P("ctx", "wt"),
        P("ctx", "wt"),
        P("ctx", "wt"),
    )
    return jax.shard_map(
        on_device, mesh=mesh, in_specs=in_specs, out_specs=out_specs, check_vma=False
    )
```

```python
from functools import partial
import math

import jax
import jax.numpy as jnp
import numpy as np
from jax import lax
from jax.experimental import pallas as pl
from jax.experimental.pallas import tpu as pltpu
from jax.sharding import PartitionSpec as P

EPS = 1e-05
THETA = 1000000.0
NEG = -1e30


def product(left, right):
    return jnp.dot(left, right, preferred_element_type=jnp.float32)


def by_transpose(left, right):
    return lax.dot_general(
        left, right, (((1,), (1,)), ((), ())), preferred_element_type=jnp.float32
    )


def transpose_by(left, right):
    return lax.dot_general(
        left, right, (((0,), (0,)), ((), ())), preferred_element_type=jnp.float32
    )


def norm_rows(values, gain):
    inverse = lax.rsqrt(jnp.mean(values * values, axis=-1, keepdims=True) + EPS)
    unit_rows = values * inverse
    return (unit_rows * gain, unit_rows, inverse)


def norm_back(grads, unit_rows, inverse, gain):
    scaled = grads * gain
    return inverse * (scaled - unit_rows * jnp.mean(scaled * unit_rows, axis=-1, keepdims=True))


def rotate(values, cosine_table, sine_table, direction):
    half_dim = values.shape[-1] // 2
    first_half = values[..., :half_dim]
    second_half = values[..., half_dim:]
    return jnp.concatenate(
        [
            first_half * cosine_table - direction * second_half * sine_table,
            second_half * cosine_table + direction * first_half * sine_table,
        ],
        axis=-1,
    )


def split_blocks(array, block_len):
    shaped = array.reshape(
        (array.shape[0], array.shape[1] // block_len, block_len) + array.shape[2:]
    )
    return jnp.moveaxis(shaped, 1, 0)


def attend_piece(folded, pieces, first_row, queries, query_places, query_segs, score_scale):
    key_piece, value_piece, seg_piece = pieces
    sequences, piece_rows = seg_piece.shape
    kv_local = queries.shape[2]
    head_dim = queries.shape[4]
    block_len = math.gcd(piece_rows, 512)
    key_blocks = split_blocks(
        key_piece.reshape(sequences, piece_rows, kv_local, head_dim), block_len
    )
    value_tiles = split_blocks(
        value_piece.reshape(sequences, piece_rows, kv_local, head_dim), block_len
    )
    seg_blocks = split_blocks(seg_piece, block_len)
    offsets = block_len * jnp.arange(piece_rows // block_len, dtype=jnp.int32)

    def attend_block_step(running, block_item):
        row_max, row_sum, weighted = running
        key_block, value_block, seg_block, offset = block_item
        key_places = offset + jnp.arange(block_len, dtype=jnp.int32)
        allowed = (key_places[None, None, :] <= query_places[None, :, None]) & (
            query_segs[:, :, None] == seg_block[:, None, :]
        )
        allowed = allowed[:, None, None]
        scores = (
            jnp.einsum("sqgrd,skgd->sgrqk", queries, key_block, preferred_element_type=jnp.float32)
            * score_scale
        )
        scores = jnp.where(allowed, scores, NEG)
        new_max = jnp.maximum(row_max, jnp.max(scores, axis=-1))
        weights = jnp.where(allowed, jnp.exp(scores - new_max[..., None]), 0.0)
        fading = jnp.exp(row_max - new_max)
        row_sum = row_sum * fading + jnp.sum(weights, axis=-1)
        fade_rows = jnp.transpose(fading, (0, 3, 1, 2))[..., None]
        weighted = weighted * fade_rows + jnp.einsum(
            "sgrqk,skgd->sqgrd",
            weights.astype(jnp.bfloat16),
            value_block,
            preferred_element_type=jnp.float32,
        )
        return ((new_max, row_sum, weighted), None)

    folded, unused = lax.scan(
        attend_block_step, folded, (key_blocks, value_tiles, seg_blocks, offsets)
    )
    return folded


def grad_piece(
    folded,
    pieces,
    first_row,
    queries,
    grad_heads,
    log_total,
    row_delta,
    query_places,
    query_segs,
    score_scale,
):
    key_piece, value_piece, seg_piece = pieces
    sequences, piece_rows = seg_piece.shape
    kv_local = queries.shape[2]
    head_dim = queries.shape[4]
    block_len = math.gcd(piece_rows, 512)
    key_blocks = split_blocks(
        key_piece.reshape(sequences, piece_rows, kv_local, head_dim), block_len
    )
    value_tiles = split_blocks(
        value_piece.reshape(sequences, piece_rows, kv_local, head_dim), block_len
    )
    seg_blocks = split_blocks(seg_piece, block_len)
    offsets = block_len * jnp.arange(piece_rows // block_len, dtype=jnp.int32)

    def grad_block_step(running, block_item):
        key_block, value_block, seg_block, offset = block_item
        key_places = offset + jnp.arange(block_len, dtype=jnp.int32)
        allowed = (key_places[None, None, :] <= query_places[None, :, None]) & (
            query_segs[:, :, None] == seg_block[:, None, :]
        )
        allowed = allowed[:, None, None]
        scores = (
            jnp.einsum("sqgrd,skgd->sgrqk", queries, key_block, preferred_element_type=jnp.float32)
            * score_scale
        )
        probs = jnp.where(allowed, jnp.exp(scores - log_total[..., None]), 0.0)
        grad_probs = jnp.einsum(
            "sqgrd,skgd->sgrqk", grad_heads, value_block, preferred_element_type=jnp.float32
        )
        grad_scores = (probs * (grad_probs - row_delta[..., None])).astype(jnp.bfloat16)
        running = running + jnp.einsum(
            "sgrqk,skgd->sqgrd", grad_scores, key_block, preferred_element_type=jnp.float32
        )
        grad_keys = jnp.einsum(
            "sgrqk,sqgrd->skgd", grad_scores, queries, preferred_element_type=jnp.float32
        )
        grad_values = jnp.einsum(
            "sgrqk,sqgrd->skgd",
            probs.astype(jnp.bfloat16),
            grad_heads,
            preferred_element_type=jnp.float32,
        )
        grads = jnp.stack([grad_keys, grad_values], axis=2).astype(jnp.bfloat16)
        return (running, grads)

    folded, grads = lax.scan(
        grad_block_step, folded, (key_blocks, value_tiles, seg_blocks, offsets)
    )
    return folded, jnp.moveaxis(grads, 0, 1).reshape((sequences, piece_rows) + grads.shape[3:])


MESH = pl.DeviceIdType.MESH
MIB = 1 << 20


def ring_place(index, count):
    return lax.select(
        lax.rem(index, 2) == 0, lax.div(index, 2), count - 1 - lax.div(index, 2)
    )


def ring_index(place, count):
    place = lax.rem(place + 2 * count, count)
    return lax.select(
        place < lax.div(count, 2), 2 * place, 2 * (count - 1 - place) + 1
    )


class Ring:
    def __init__(self, count, slots, send_sems, recv_sems):
        self.count, self.slots = count, slots
        self.send_sems, self.recv_sems = send_sems, recv_sems
        self.other = lax.axis_index("wt")
        self.place = ring_place(lax.axis_index("ctx"), count)
        self.right = ring_index(self.place + 1, count)
        self.left = ring_index(self.place + count - 1, count)
        self.half = slots.shape[2] // 2

    def copy(self, which, step, way):
        rows = pl.ds(way * self.half, self.half)
        later = step + 1 if isinstance(step, int) else lax.add(step, 1)
        return pltpu.make_async_remote_copy(
            src_ref=self.slots.at[which, step, rows],
            dst_ref=self.slots.at[which, later, rows],
            send_sem=self.send_sems.at[which, step, way],
            recv_sem=self.recv_sems.at[which, step, way],
            device_id=((self.right, self.left)[way], self.other),
            device_id_type=MESH,
        )

    def tick(self, which, step, left_ref, right_ref, first=False, result=None):
        half = self.half
        rows = [
            ring_index(target, self.count) * (2 * half) + way * half
            for way, target in enumerate(
                (self.place + self.count - 1 - step, self.place + 1 + step)
            )
        ]
        left = jnp.concatenate(
            [left_ref[pl.ds(pl.multiple_of(row, half), half), :] for row in rows], axis=0
        )
        total = jnp.dot(left, right_ref[...], preferred_element_type=jnp.float32)
        if not first:
            for way in range(2):
                self.copy(which, step - 1, way).wait_recv()
            total = total + self.slots[which, step].astype(jnp.float32)
        if result is None:
            self.slots[which, step] = total.astype(jnp.bfloat16)
            for way in range(2):
                self.copy(which, step, way).start()
        else:
            result[...] = total

    def finish(self, which):
        for way in range(2):

            def wait(step, carry):
                self.copy(which, step, way).wait_send()
                return carry

            lax.fori_loop(0, self.count - 1, wait, 0)


def pair_lanes(shape):
    return lax.broadcasted_iota(jnp.int32, shape, 1)


def swap_halves(values, head_dim):
    lanes = pair_lanes(values.shape)
    width = values.shape[1]
    quarter = head_dim // 2
    return jnp.where(
        lax.rem(lanes, head_dim) < quarter,
        pltpu.roll(values, width - quarter, 1),
        pltpu.roll(values, quarter, 1),
    )


def pair_mean(values, head_dim):
    low = pair_lanes(values.shape) < head_dim
    first = jnp.sum(jnp.where(low, values, 0.0), axis=-1, keepdims=True)
    second = jnp.sum(jnp.where(low, 0.0, values), axis=-1, keepdims=True)
    return jnp.where(low, first, second) * (1.0 / head_dim)


def pair_norm(values, head_dim):
    inverse = lax.rsqrt(pair_mean(values * values, head_dim) + EPS)
    return values * inverse, inverse


def double(row):
    return jnp.concatenate([row, row], axis=-1)


def dot_nn(left, right):
    return jnp.dot(left, right, preferred_element_type=jnp.float32)


def dot_nt(left, right):
    return lax.dot_general(
        left, right, (((1,), (1,)), ((), ())), preferred_element_type=jnp.float32
    )


def as_column(row):
    size = row.shape[1]
    rows = lax.broadcasted_iota(jnp.int32, (size, size), 0)
    lanes = lax.broadcasted_iota(jnp.int32, (size, size), 1)
    return jnp.sum(jnp.where(rows == lanes, row, 0.0), axis=1, keepdims=True)


class Place:
    def __init__(self, count):
        self.count = count
        self.ctx, self.wt = lax.axis_index("ctx"), lax.axis_index("wt")
        self.odd = lax.rem(self.ctx, 2)
        self.level = lax.div(self.ctx, 2)
        self.core_bit = lax.rem(self.wt, 2)
        self.beside_ctx = self.ctx + 1 - 2 * self.odd
        self.beside = (self.beside_ctx, self.wt)
        self.above = (lax.rem(self.ctx + 2, count), self.wt)
        self.below = (lax.rem(self.ctx + count - 2, count), self.wt)
        self.has_above = self.ctx + 2 < count
        self.has_below = self.ctx >= 2
        self.core_wt = self.wt + 1 - 2 * self.core_bit
        self.chip_wt = lax.rem(self.wt + 2, 4)
        self.far_wt = lax.rem(self.core_wt + 2, 4)
        self.core = (self.ctx, self.core_wt)
        self.chip = (self.ctx, self.chip_wt)

    def greet(self, more=()):
        barrier = pltpu.get_barrier_semaphore()
        peers = [self.beside, self.core, self.chip, *more]
        for peer in peers:
            pl.semaphore_signal(barrier, inc=1, device_id=peer, device_id_type=MESH)
        for there, peer in ((self.has_above, self.above), (self.has_below, self.below)):

            @pl.when(there)
            def _():
                pl.semaphore_signal(barrier, inc=1, device_id=peer, device_id_type=MESH)

        edges = self.has_above.astype(jnp.int32) + self.has_below.astype(jnp.int32)
        pl.semaphore_wait(barrier, len(peers) + edges)


    def greet_all(self):
        barrier = pltpu.get_barrier_semaphore()

        def signal(peer):
            pl.semaphore_signal(barrier, inc=1, device_id=peer, device_id_type=MESH)

        for shift in range(1, self.count):
            signal((lax.rem(self.ctx + shift, self.count), self.wt))
        signal(self.core)
        signal(self.chip)
        pl.semaphore_wait(barrier, self.count + 1)


def send_to(source, target, send_sem, recv_sem, device):
    return pltpu.make_async_remote_copy(
        src_ref=source,
        dst_ref=target,
        send_sem=send_sem,
        recv_sem=recv_sem,
        device_id=device,
        device_id_type=MESH,
    )


def forward_kernel(
    count,
    tokens,
    segments,
    table,
    attn_gain,
    q_gain,
    k_gain,
    w_query,
    w_key,
    w_value,
    w_out,
    residual,
    heads_out,
    mixed_t,
    query_t,
    logs,
    starts,
    keys_values,
    keys_t,
    query_raw,
    key_raw,
    normed_t,
    all_segs,
    all_out,
    all_heads,
    acc,
    row_sum,
    up_send,
    up_recv,
    side_send,
    side_recv,
    seg_send,
    seg_recv,
    out_send,
    out_recv,
    head_send,
    head_recv,
):
    sequences, tile = segments.shape
    head_dim = q_gain.shape[1]
    levels = count // 2
    here = Place(count)
    me = here.ctx
    all_segs[me] = jnp.zeros_like(all_segs[me])
    all_segs[me, pl.ds(0, sequences)] = segments[...]
    all_out[here.wt] = w_out[...]
    here.greet()

    def out_copy(hop, arriving=False):
        sent = (here.wt, here.wt, here.chip_wt)
        landed = (here.chip_wt, here.core_wt, here.far_wt)
        ref = all_out.at[(landed if arriving else sent)[hop]]
        device = here.chip if hop == 0 else here.core
        return send_to(ref, ref, out_send.at[hop], out_recv.at[hop], device)

    out_copy(0).start()
    out_copy(1).start()

    def rows_of(seq):
        return pl.ds(pl.multiple_of(seq * tile, tile), tile)

    def block_of(index, step):
        return lax.rem(index - 2 * step + 2 * count, count)

    def up_copy(step, seq):
        rows = keys_values.at[block_of(me, step), rows_of(seq)]
        return send_to(rows, rows, up_send.at[step, seq], up_recv.at[step, seq], here.above)

    def up_wait(step, seq):
        rows = keys_values.at[block_of(me, step), rows_of(seq)]
        earlier = step - 1
        send_to(
            rows, rows, up_send.at[earlier, seq], up_recv.at[earlier, seq], here.above
        ).wait_recv()

    def side_copy(step, seq, index=me):
        rows = keys_values.at[block_of(index, step), rows_of(seq)]
        return send_to(
            rows, rows, side_send.at[step, seq], side_recv.at[step, seq], here.beside
        )

    def side_wait(step, seq):
        side_copy(step, seq, here.beside_ctx).wait_recv()

    def seg_copy(step, way, index=me):
        ref = all_segs.at[block_of(index, step)]
        device = here.beside if way else here.above
        return send_to(ref, ref, seg_send.at[step, way], seg_recv.at[step, way], device)

    def seg_wait(step, way):
        if way:
            seg_copy(step, 1, here.beside_ctx).wait_recv()
        else:
            ref = all_segs.at[block_of(me, step)]
            earlier = step - 1
            send_to(
                ref, ref, seg_send.at[earlier, 0], seg_recv.at[earlier, 0], here.above
            ).wait_recv()

    def goes_up(step):
        return here.has_above & (me >= 2 * step)

    def goes_aside(step):
        block = me - 2 * step
        return (block >= 0) & (block < here.beside_ctx)

    def pass_segs(step):
        @pl.when(goes_up(step))
        def _():
            seg_copy(step, 0).start()

        @pl.when(goes_aside(step))
        def _():
            seg_copy(step, 1).start()

    def pass_rows(step, seq):
        @pl.when(goes_up(step))
        def _():
            up_copy(step, seq).start()

        @pl.when(goes_aside(step))
        def _():
            side_copy(step, seq).start()

    pass_segs(0)
    cosine = table[:, pl.ds(0, 2 * head_dim)]
    sine = table[:, pl.ds(2 * head_dim, 2 * head_dim)]
    q_gain_pair = double(q_gain[...].astype(jnp.float32))
    k_gain_pair = double(k_gain[...].astype(jnp.float32))
    gain = attn_gain[...].astype(jnp.float32)

    def turn(values):
        return values * cosine + swap_halves(values, head_dim) * sine

    def project(seq, carry):
        rows = rows_of(seq)
        inputs = tokens[rows, :].astype(jnp.float32)
        inverse = lax.rsqrt(jnp.mean(inputs * inputs, axis=-1, keepdims=True) + EPS)
        normed = (inputs * inverse * gain).astype(jnp.bfloat16)
        raw_k = dot_nn(normed, w_key[...])
        key_raw[rows, :] = raw_k
        unit, unused = pair_norm(raw_k, head_dim)
        keys_values[me, rows, pl.ds(0, 2 * head_dim)] = turn(unit * k_gain_pair).astype(
            jnp.bfloat16
        )
        keys_values[me, rows, pl.ds(2 * head_dim, 2 * head_dim)] = dot_nn(
            normed, w_value[...]
        ).astype(jnp.bfloat16)
        pass_rows(0, seq)
        raw_q = dot_nn(normed, w_query[...])
        query_raw[rows, :] = raw_q
        query_t[seq] = jnp.zeros_like(query_t[seq])
        for group in range(2):
            unit, unused = pair_norm(
                raw_q[:, group * 2 * head_dim : (group + 1) * 2 * head_dim], head_dim
            )
            turned = turn(unit * q_gain_pair) * (head_dim**-0.5)
            flipped = turned.T.astype(jnp.bfloat16)
            for member in range(2):
                query_t[
                    seq,
                    pl.ds(group * head_dim, head_dim),
                    pl.ds((2 * group + member) * tile, tile),
                ] = flipped[member * head_dim : (member + 1) * head_dim]
        normed_t[:, rows] = normed.T
        acc[seq] = jnp.zeros_like(acc[seq])
        row_sum[seq] = jnp.zeros_like(row_sum[seq])
        starts[seq] = jnp.zeros_like(starts[seq])
        return carry

    lax.fori_loop(0, sequences, project, 0)
    key_rows = lax.broadcasted_iota(jnp.int32, (tile, 4 * tile), 0)
    query_cols = lax.rem(lax.broadcasted_iota(jnp.int32, (tile, 4 * tile), 1), tile)

    def attend(block, seq, own):
        rows = rows_of(seq)
        keys = keys_values[block, rows, pl.ds(0, 2 * head_dim)]
        values = keys_values[block, rows, pl.ds(2 * head_dim, 2 * head_dim)]
        seg_query = all_segs[me, pl.ds(seq, 1)].astype(jnp.float32)
        seg_key = as_column(all_segs[block, pl.ds(seq, 1)].astype(jnp.float32))
        earlier = jnp.where(seg_key < seg_query, 1.0, 0.0)
        starts[seq] += jnp.sum(earlier, axis=0, keepdims=True)
        seg_wide = jnp.concatenate([seg_query] * 4, axis=1)
        if own:
            allowed = (seg_key == seg_wide) & (key_rows <= query_cols)
        else:
            allowed = seg_key >= seg_wide
        scores = dot_nn(keys, query_t[seq])
        weights = jnp.where(allowed, jnp.exp(scores), 0.0)
        row_sum[seq] += jnp.sum(weights, axis=0, keepdims=True)
        low = weights.astype(jnp.bfloat16)
        values_t = values.T
        for group in range(2):
            acc[seq, group] += dot_nn(
                values_t[group * head_dim : (group + 1) * head_dim],
                low[:, group * 2 * tile : (group + 1) * 2 * tile],
            )
        keys_t[block, seq] = keys.T

    def own_block(seq, carry):
        attend(me, seq, True)
        return carry

    lax.fori_loop(0, sequences, own_block, 0)

    @pl.when(goes_back_aside(here, 0))
    def _():
        seg_wait(0, 1)

        def side_block(seq, carry):
            side_wait(0, seq)
            attend(here.beside_ctx, seq, False)
            return carry

        lax.fori_loop(0, sequences, side_block, 0)

    out_copy(0, True).wait_recv()
    out_copy(2).start()

    def level(step, carry):
        @pl.when(me >= 2 * step)
        def _():
            seg_wait(step, 0)
            pass_segs(step)
            seg_wait(step, 1)

            def line_block(seq, carry):
                up_wait(step, seq)
                pass_rows(step, seq)
                attend(me - 2 * step, seq, False)
                return carry

            lax.fori_loop(0, sequences, line_block, 0)

            def side_block(seq, carry):
                side_wait(step, seq)
                attend(here.beside_ctx - 2 * step, seq, False)
                return carry

            lax.fori_loop(0, sequences, side_block, 0)

        return carry

    lax.fori_loop(1, levels, level, 0)

    def head_copy(hop, seq, arriving=False):
        sent = (here.wt, here.wt, here.chip_wt)
        landed = (here.chip_wt, here.core_wt, here.far_wt)
        ref = all_heads.at[(landed if arriving else sent)[hop], rows_of(seq)]
        device = here.chip if hop == 0 else here.core
        return send_to(ref, ref, head_send.at[hop, seq], head_recv.at[hop, seq], device)

    def mix(seq, carry):
        rows = rows_of(seq)
        total = row_sum[seq]
        logs[seq] = jnp.log(total)
        for group in range(2):
            cols = slice(group * 2 * tile, (group + 1) * 2 * tile)
            part = acc[seq, group] / total[:, cols]
            mixed = jnp.concatenate([part[:, :tile], part[:, tile:]], axis=0)
            mixed_t[seq, group] = mixed
            all_heads[here.wt, rows, pl.ds(group * 2 * head_dim, 2 * head_dim)] = mixed.T.astype(
                jnp.bfloat16
            )
        head_copy(0, seq).start()
        head_copy(1, seq).start()
        return carry

    lax.fori_loop(0, sequences, mix, 0)
    heads_out[...] = all_heads[here.wt]
    out_copy(1, True).wait_recv()
    out_copy(2, True).wait_recv()

    def finish(turn_, carry):
        @pl.when(turn_ < sequences)
        def _():
            head_copy(0, turn_, True).wait_recv()
            head_copy(2, turn_).start()

        @pl.when(turn_ > 0)
        def _():
            seq = turn_ - 1
            rows = rows_of(seq)
            head_copy(1, seq, True).wait_recv()
            head_copy(2, seq, True).wait_recv()
            total = tokens[rows, :].astype(jnp.float32)
            for slot in range(4):
                total = total + dot_nt(all_heads[slot, rows], all_out[slot])
            residual[rows, :] = total

        return carry

    lax.fori_loop(0, sequences + 1, finish, 0)
    for hop in range(3):
        out_copy(hop).wait_send()

        def sent(seq, carry):
            head_copy(hop, seq).wait_send()
            return carry

        lax.fori_loop(0, sequences, sent, 0)

    def drain(step, carry):
        @pl.when(goes_up(step))
        def _():
            seg_copy(step, 0).wait_send()

            def sent(seq, carry):
                up_copy(step, seq).wait_send()
                return carry

            lax.fori_loop(0, sequences, sent, 0)

        @pl.when(goes_aside(step))
        def _():
            seg_copy(step, 1).wait_send()

            def sent(seq, carry):
                side_copy(step, seq).wait_send()
                return carry

            lax.fori_loop(0, sequences, sent, 0)

        return carry

    lax.fori_loop(0, levels, drain, 0)


def goes_back_aside(here, step):
    block = here.beside_ctx - 2 * step
    return (block >= 0) & (block < here.ctx)


def forward(tokens, segments, table, attn_gain, q_gain, k_gain, w_query, w_key, w_value, w_out):
    count = lax.axis_size("ctx")
    sequences, tile = segments.shape
    rows, width = tokens.shape
    head_dim = q_gain.shape[1]
    pair = 2 * head_dim
    levels = count // 2
    vmem = pl.BlockSpec(memory_space=pltpu.VMEM)
    f32, bf16 = jnp.float32, jnp.bfloat16
    outs = [
        ((rows, width), f32),
        ((rows, 2 * pair), bf16),
        ((sequences, 2, pair, tile), f32),
        ((sequences, pair, 4 * tile), bf16),
        ((sequences, 1, 4 * tile), f32),
        ((sequences, 1, tile), f32),
        ((count, rows, 2 * pair), bf16),
        ((count, sequences, pair, tile), bf16),
        ((rows, 2 * pair), f32),
        ((rows, pair), f32),
        ((width, rows), bf16),
    ]
    dma = pltpu.SemaphoreType.DMA
    return pl.pallas_call(
        partial(forward_kernel, count),
        out_shape=[jax.ShapeDtypeStruct(shape, kind) for shape, kind in outs],
        in_specs=[vmem] * 10,
        out_specs=[vmem] * len(outs),
        scratch_shapes=[
            pltpu.VMEM((count, 8, tile), jnp.int32),
            pltpu.VMEM((4, width, 2 * pair), bf16),
            pltpu.VMEM((4, rows, 2 * pair), bf16),
            pltpu.VMEM((sequences, 2, head_dim, 2 * tile), f32),
            pltpu.VMEM((sequences, 1, 4 * tile), f32),
            dma((levels, sequences)),
            dma((levels, sequences)),
            dma((levels, sequences)),
            dma((levels, sequences)),
            dma((levels, 2)),
            dma((levels, 2)),
            dma((3,)),
            dma((3,)),
            dma((3, sequences)),
            dma((3, sequences)),
        ],
        compiler_params=pltpu.CompilerParams(
            collective_id=2, has_side_effects=True, vmem_limit_bytes=60 * MIB
        ),
    )(tokens, segments, table, attn_gain, q_gain, k_gain, w_query, w_key, w_value, w_out)


class WtSum:
    def __init__(self, here, tile, part, got, far, full, send_sems, recv_sems):
        self.here, self.tile = here, tile
        self.part, self.got, self.far, self.full = part, got, far, full
        self.send_sems, self.recv_sems = send_sems, recv_sems
        self.mine, self.theirs = here.core_bit, 1 - here.core_bit

    def rows(self, seq):
        return pl.ds(pl.multiple_of(seq * self.tile, self.tile), self.tile)

    def copy(self, hop, seq, arriving=False):
        rows = self.rows(seq)
        half = self.theirs if arriving else self.mine
        source = (
            self.part.at[self.theirs, rows],
            self.got.at[rows],
            self.full.at[half, rows],
        )[hop]
        target = (self.got.at[rows], self.far.at[rows], self.full.at[half, rows])[hop]
        device = self.here.chip if hop == 1 else self.here.core
        return send_to(
            source, target, self.send_sems.at[hop, seq], self.recv_sems.at[hop, seq], device
        )

    def offer(self, seq, value):
        rows = self.rows(seq)
        half = value.shape[1] // 2
        self.part[0, rows] = value[:, :half].astype(jnp.bfloat16)
        self.part[1, rows] = value[:, half:].astype(jnp.bfloat16)
        self.copy(0, seq).start()

    def cross(self, seq):
        rows = self.rows(seq)
        self.copy(0, seq).wait_recv()
        total = self.part[self.mine, rows].astype(jnp.float32) + self.got[rows].astype(
            jnp.float32
        )
        self.got[rows] = total.astype(jnp.bfloat16)
        self.copy(1, seq).start()

    def close(self, seq):
        rows = self.rows(seq)
        self.copy(1, seq).wait_recv()
        total = self.got[rows].astype(jnp.float32) + self.far[rows].astype(jnp.float32)
        self.full[self.mine, rows] = total.astype(jnp.bfloat16)
        self.copy(2, seq).start()

    def result(self, seq):
        rows = self.rows(seq)
        self.copy(2, seq, True).wait_recv()
        return jnp.concatenate([self.full[0, rows], self.full[1, rows]], axis=1).astype(
            jnp.float32
        )

    def finish(self, sequences):
        def sent(seq, carry):
            for hop in range(3):
                self.copy(hop, seq).wait_send()
            return carry

        lax.fori_loop(0, sequences, sent, 0)


def wt_sum_scratch(sequences, rows, width):
    half = width // 2
    return [
        pltpu.VMEM((2, rows, half), jnp.bfloat16),
        pltpu.VMEM((rows, half), jnp.bfloat16),
        pltpu.VMEM((rows, half), jnp.bfloat16),
        pltpu.VMEM((2, rows, half), jnp.bfloat16),
        pltpu.SemaphoreType.DMA((3, sequences)),
        pltpu.SemaphoreType.DMA((3, sequences)),
    ]


def ring_scratch(count, arrays, rows, width):
    return [
        pltpu.VMEM((arrays, count, rows, width), jnp.bfloat16),
        pltpu.SemaphoreType.DMA((arrays, count - 1, 2)),
        pltpu.SemaphoreType.DMA((arrays, count - 1, 2)),
    ]


class GainSum:
    def __init__(self, here, slots, beside, sends, recvs, pair_sends, pair_recvs):
        self.here, self.slots, self.beside = here, slots, beside
        self.sends, self.recvs = sends, recvs
        self.pair_sends, self.pair_recvs = pair_sends, pair_recvs

    def copy(self, shift, arriving=False):
        here = self.here
        target = lax.rem(here.ctx + shift, here.count)
        origin = lax.rem(here.ctx + here.count - shift, here.count)
        ref = self.slots.at[origin if arriving else here.ctx]
        return send_to(
            ref, ref, self.sends.at[shift - 1], self.recvs.at[shift - 1], (target, here.wt)
        )

    def pair_copy(self, hop):
        device = (self.here.core, self.here.chip)[hop]
        return send_to(
            self.beside.at[hop, 0],
            self.beside.at[hop, 1],
            self.pair_sends.at[hop],
            self.pair_recvs.at[hop],
            device,
        )

    def start(self):
        for shift in range(1, self.here.count):
            self.copy(shift).start()

    def total(self):
        for shift in range(1, self.here.count):
            self.copy(shift, True).wait_recv()
        total = self.slots[0]
        for index in range(1, self.here.count):
            total = total + self.slots[index]
        for hop in range(2):
            self.beside[hop, 0] = total
            self.pair_copy(hop).start()
            self.pair_copy(hop).wait_recv()
            total = total + self.beside[hop, 1]
        for shift in range(1, self.here.count):
            self.copy(shift).wait_send()
        for hop in range(2):
            self.pair_copy(hop).wait_send()
        return total


def backward_kernel(count, *refs):
    (
        grad_res,
        tokens,
        table,
        attn_gain,
        q_gain,
        k_gain,
        w_query,
        w_key,
        w_value,
        w_out,
        heads,
        mixed_t,
        query_t,
        logs,
        starts,
        keys_values,
        keys_t,
        query_raw,
        key_raw,
        normed_t,
        cot_t,
        normed_ffn_t,
        ffn_grads,
        ffn_gain_part,
    ) = refs[:24]
    (
        tokens_grad,
        down_sum,
        gate_sum,
        up_sum,
        out_sum,
        query_sum,
        key_sum,
        value_sum,
        attn_gain_sum,
        ffn_gain_sum,
        q_gain_sum,
        k_gain_sum,
    ) = refs[24:36]
    (
        grad_res_t,
        grad_heads_t,
        deltas,
        grad_query_t,
        own_grads,
        grad_qkv,
        side_in,
        side_out,
        line_in,
        line_out,
        qkv_total,
        side_send,
        side_recv,
        line_send,
        line_recv,
    ) = refs[36:51]
    rest = refs[51:]
    sequences, tile = mixed_t.shape[0], mixed_t.shape[3]
    head_dim = q_gain.shape[1]
    pair = 2 * head_dim
    levels = count // 2
    here = Place(count)
    me = here.ctx
    wt_sum = WtSum(here, tile, *rest[:6])
    gains = GainSum(here, *rest[6:12])
    gain_slots = rest[6]
    ffn = Ring(count, *rest[12:15])
    out = Ring(count, *rest[15:18])
    qkv = Ring(count, *rest[18:21])
    last = count - 1
    here.greet_all()
    lefts = (cot_t, normed_ffn_t, normed_ffn_t)
    ffn_sums = (down_sum, gate_sum, up_sum)

    def ffn_ticks(step, first=False, final=False):
        for i in range(3):
            ffn.tick(
                i,
                step,
                lefts[i],
                ffn_grads.at[i],
                first=first,
                result=ffn_sums[i] if final else None,
            )

    def rows_of(seq):
        return pl.ds(pl.multiple_of(seq * tile, tile), tile)

    ffn_ticks(0, first=True)

    def prepare(seq, carry):
        rows = rows_of(seq)
        grads = grad_res[rows, :]
        grad_res_t[:, rows] = grads.T
        grad_heads_t[seq] = jnp.zeros_like(grad_heads_t[seq])
        low = dot_nn(grads, w_out[...]).astype(jnp.bfloat16)
        for group in range(2):
            flipped = low[:, group * pair : (group + 1) * pair].T
            product_t = flipped.astype(jnp.float32) * mixed_t[seq, group]
            for member in range(2):
                part = slice(member * head_dim, (member + 1) * head_dim)
                cols = pl.ds((2 * group + member) * tile, tile)
                grad_heads_t[seq, pl.ds(group * head_dim, head_dim), cols] = flipped[part]
                deltas[seq, :, cols] = jnp.sum(product_t[part], axis=0, keepdims=True)
        grad_query_t[seq] = jnp.zeros_like(grad_query_t[seq])
        return carry

    lax.fori_loop(0, sequences, prepare, 0)
    out.tick(0, 0, grad_res_t, heads, first=True)
    key_rows = lax.broadcasted_iota(jnp.int32, (tile, 4 * tile), 0)
    query_cols = lax.rem(lax.broadcasted_iota(jnp.int32, (tile, 4 * tile), 1), tile)

    def grads_of(block, seq, own):
        rows = rows_of(seq)
        keys = keys_values[block, rows, pl.ds(0, pair)]
        values = keys_values[block, rows, pl.ds(pair, pair)]
        places = (key_rows + block * tile).astype(jnp.float32)
        start = starts[seq]
        allowed = places >= jnp.concatenate([start] * 4, axis=1)
        if own:
            allowed = allowed & (key_rows <= query_cols)
        queries = query_t[seq]
        grad_heads = grad_heads_t[seq]
        scores = dot_nn(keys, queries)
        probs = jnp.where(allowed, jnp.exp(scores - logs[seq]), 0.0)
        grad_probs = dot_nn(values, grad_heads)
        grad_scores = (probs * (grad_probs - deltas[seq])).astype(jnp.bfloat16)
        flipped = keys_t[block, seq]
        for group in range(2):
            cols = slice(group * 2 * tile, (group + 1) * 2 * tile)
            grad_query_t[seq, group] += dot_nn(
                flipped[group * head_dim : (group + 1) * head_dim], grad_scores[:, cols]
            )
        grad_keys = dot_nt(grad_scores, queries)
        grad_values = dot_nt(probs.astype(jnp.bfloat16), grad_heads)
        return jnp.concatenate([grad_keys, grad_values], axis=1)

    def side_copy(step, seq):
        return send_to(
            side_out.at[step, rows_of(seq)],
            side_in.at[step, rows_of(seq)],
            side_send.at[step, seq],
            side_recv.at[step, seq],
            here.beside,
        )

    def line_copy(step, seq):
        earlier = step - 1
        return send_to(
            line_out.at[earlier, rows_of(seq)],
            line_in.at[earlier, rows_of(seq)],
            line_send.at[earlier, seq],
            line_recv.at[earlier, seq],
            here.below,
        )

    def from_above(step, seq):
        later = step + 1
        return line_copy(later, seq)

    def block_there(step):
        block = here.beside_ctx - 2 * step
        return (block >= 0) & (block < me)

    def block_comes(step):
        return (me >= 2 * step) & (me - 2 * step < here.beside_ctx)

    def send_aside(step):
        @pl.when(block_there(step))
        def _():
            def one(seq, carry):
                side_out[step, rows_of(seq)] = grads_of(
                    here.beside_ctx - 2 * step, seq, False
                ).astype(jnp.bfloat16)
                side_copy(step, seq).start()
                return carry

            lax.fori_loop(0, sequences, one, 0)

    def level(turn_, carry):
        step = levels - 1 - turn_
        send_aside(step)

        @pl.when(me >= 2 * step)
        def _():
            def one(seq, carry):
                rows = rows_of(seq)
                own_grads[rows, :] = grads_of(me - 2 * step, seq, False)
                side_copy(step, seq).wait_recv()
                total = own_grads[rows, :] + side_in[step, rows].astype(jnp.float32)
                own_grads[rows, :] = total

                @pl.when(here.has_above)
                def _():
                    from_above(step, seq).wait_recv()
                    own_grads[rows, :] += line_in[step, rows].astype(jnp.float32)

                line_out[step - 1, rows] = own_grads[rows, :].astype(jnp.bfloat16)
                line_copy(step, seq).start()
                return carry

            lax.fori_loop(0, sequences, one, 0)

        ffn_ticks(1 + turn_)
        return carry

    lax.fori_loop(0, levels - 1, level, 0)
    send_aside(0)

    def own_block(seq, carry):
        own_grads[rows_of(seq), :] = grads_of(me, seq, True)
        return carry

    lax.fori_loop(0, sequences, own_block, 0)
    ffn_ticks(levels)
    out.tick(0, 1, grad_res_t, heads)
    cosine = table[:, pl.ds(0, pair)]
    sine = table[:, pl.ds(pair, pair)]
    q_gain_pair = double(q_gain[...].astype(jnp.float32))
    k_gain_pair = double(k_gain[...].astype(jnp.float32))
    gain = attn_gain[...].astype(jnp.float32)
    gain_slots[me] = jnp.zeros_like(gain_slots[me])
    gain_slots[me, pl.ds(1, 1)] = ffn_gain_part[...]

    def back_through(grads, raw, gain_pair, row):
        turned = grads * cosine - swap_halves(grads, head_dim) * sine
        unit, inverse = pair_norm(raw, head_dim)
        gain_slots[me, pl.ds(row, 1), pl.ds(0, pair)] += jnp.sum(
            turned * unit, axis=0, keepdims=True
        )
        scaled = turned * gain_pair
        return (inverse * (scaled - unit * pair_mean(scaled * unit, head_dim))).astype(
            jnp.bfloat16
        )

    def token_unit(rows):
        inputs = tokens[rows, :].astype(jnp.float32)
        inverse = lax.rsqrt(jnp.mean(inputs * inputs, axis=-1, keepdims=True) + EPS)
        return inputs * inverse, inverse

    def project_back(seq, carry):
        rows = rows_of(seq)
        for group in range(2):
            grads = grad_query_t[seq, group] * (head_dim**-0.5)
            grads = jnp.concatenate([grads[:, :tile], grads[:, tile:]], axis=0).T
            cols = pl.ds(group * pair, pair)
            grad_qkv[rows, cols] = back_through(grads, query_raw[rows, cols], q_gain_pair, 2)

        @pl.when(block_comes(0))
        def _():
            side_copy(0, seq).wait_recv()
            own_grads[rows, :] += side_in[0, rows].astype(jnp.float32)

        @pl.when(here.has_above)
        def _():
            from_above(0, seq).wait_recv()
            own_grads[rows, :] += line_in[0, rows].astype(jnp.float32)

        grad_qkv[rows, pl.ds(2 * pair, pair)] = back_through(
            own_grads[rows, pl.ds(0, pair)], key_raw[rows, :], k_gain_pair, 3
        )
        grad_qkv[rows, pl.ds(3 * pair, pair)] = own_grads[rows, pl.ds(pair, pair)].astype(
            jnp.bfloat16
        )
        grads = (
            dot_nt(grad_qkv[rows, pl.ds(0, 2 * pair)], w_query[...])
            + dot_nt(grad_qkv[rows, pl.ds(2 * pair, pair)], w_key[...])
            + dot_nt(grad_qkv[rows, pl.ds(3 * pair, pair)], w_value[...])
        )
        unit, inverse = token_unit(rows)
        gain_slots[me, pl.ds(0, 1)] += jnp.sum(grads * unit, axis=0, keepdims=True)
        wt_sum.offer(seq, grads)
        return carry

    lax.fori_loop(0, sequences, project_back, 0)
    gains.start()
    qkv.tick(0, 0, normed_t, grad_qkv, first=True)

    def crossing(seq, carry):
        wt_sum.cross(seq)
        return carry

    lax.fori_loop(0, sequences, crossing, 0)

    def tail(step, carry):
        qkv.tick(0, step, normed_t, grad_qkv)
        out.tick(0, step + 1, grad_res_t, heads)

        @pl.when(step + levels < last)
        def _():
            ffn_ticks(step + levels)

        return carry

    lax.fori_loop(1, last - 1, tail, 0)
    ffn_ticks(last, final=True)
    out.tick(0, last, grad_res_t, heads, result=out_sum)

    def closing(seq, carry):
        wt_sum.close(seq)
        return carry

    lax.fori_loop(0, sequences, closing, 0)
    qkv.tick(0, last - 1, normed_t, grad_qkv)

    def token_rows(seq, carry):
        rows = rows_of(seq)
        unit, inverse = token_unit(rows)
        scaled = wt_sum.result(seq) * gain
        grads = inverse * (scaled - unit * jnp.mean(scaled * unit, axis=-1, keepdims=True))
        tokens_grad[rows, :] = (grad_res[rows, :].astype(jnp.float32) + grads).astype(
            jnp.bfloat16
        )
        return carry

    lax.fori_loop(0, sequences, token_rows, 0)
    total = gains.total()
    attn_gain_sum[...] = total[0:1]
    ffn_gain_sum[...] = total[1:2]
    folded = total[:, :pair]
    folded = folded + pltpu.roll(folded, head_dim, 1)
    q_gain_sum[...] = folded[2:3, :head_dim]
    k_gain_sum[...] = folded[3:4, :head_dim]
    qkv.tick(0, last, normed_t, grad_qkv, result=qkv_total)
    query_sum[...] = qkv_total[:, pl.ds(0, 2 * pair)]
    key_sum[...] = qkv_total[:, pl.ds(2 * pair, pair)]
    value_sum[...] = qkv_total[:, pl.ds(3 * pair, pair)]
    wt_sum.finish(sequences)
    for i in range(3):
        ffn.finish(i)
    out.finish(0)
    qkv.finish(0)

    def drain(step, carry):
        @pl.when(block_there(step))
        def _():
            def sent(seq, carry):
                side_copy(step, seq).wait_send()
                return carry

            lax.fori_loop(0, sequences, sent, 0)

        @pl.when((step > 0) & (me >= 2 * step))
        def _():
            def sent(seq, carry):
                line_copy(step, seq).wait_send()
                return carry

            lax.fori_loop(0, sequences, sent, 0)

        return carry

    lax.fori_loop(0, levels, drain, 0)


def backward(*arrays):
    (grad_res, tokens, table, attn_gain, q_gain) = arrays[:5]
    mixed_t, cot_t, ffn_grads = arrays[11], arrays[20], arrays[22]
    count = lax.axis_size("ctx")
    sequences, tile = mixed_t.shape[0], mixed_t.shape[3]
    rows, width = tokens.shape
    head_dim = q_gain.shape[1]
    pair = 2 * head_dim
    levels = count // 2
    block = width // count
    hidden = ffn_grads.shape[2]
    vmem = pl.BlockSpec(memory_space=pltpu.VMEM)
    f32, bf16 = jnp.float32, jnp.bfloat16
    outs = [
        ((rows, width), bf16),
        ((block, hidden), f32),
        ((block, hidden), f32),
        ((block, hidden), f32),
        ((block, 2 * pair), f32),
        ((block, 2 * pair), f32),
        ((block, pair), f32),
        ((block, pair), f32),
        ((1, width), f32),
        ((1, width), f32),
        ((1, head_dim), f32),
        ((1, head_dim), f32),
    ]
    dma = pltpu.SemaphoreType.DMA
    return pl.pallas_call(
        partial(backward_kernel, count),
        out_shape=[jax.ShapeDtypeStruct(shape, kind) for shape, kind in outs],
        in_specs=[vmem] * len(arrays),
        out_specs=[vmem] * len(outs),
        scratch_shapes=[
            pltpu.VMEM((width, rows), bf16),
            pltpu.VMEM((sequences, pair, 4 * tile), bf16),
            pltpu.VMEM((sequences, 1, 4 * tile), f32),
            pltpu.VMEM((sequences, 2, head_dim, 2 * tile), f32),
            pltpu.VMEM((rows, 2 * pair), f32),
            pltpu.VMEM((rows, 4 * pair), bf16),
            pltpu.VMEM((levels, rows, 2 * pair), bf16),
            pltpu.VMEM((levels, rows, 2 * pair), bf16),
            pltpu.VMEM((levels - 1, rows, 2 * pair), bf16),
            pltpu.VMEM((levels - 1, rows, 2 * pair), bf16),
            pltpu.VMEM((block, 4 * pair), f32),
            dma((levels, sequences)),
            dma((levels, sequences)),
            dma((levels - 1, sequences)),
            dma((levels - 1, sequences)),
            *wt_sum_scratch(sequences, rows, width),
            pltpu.VMEM((count, 8, width), f32),
            pltpu.VMEM((2, 2, 8, width), f32),
            dma((count - 1,)),
            dma((count - 1,)),
            dma((2,)),
            dma((2,)),
            *ring_scratch(count, 3, block, hidden),
            *ring_scratch(count, 1, block, 2 * pair),
            *ring_scratch(count, 1, block, 4 * pair),
        ],
        compiler_params=pltpu.CompilerParams(
            collective_id=3, has_side_effects=True, vmem_limit_bytes=62 * MIB
        ),
    )(*arrays)


def rotary_table(length, head_dim):
    half = head_dim // 2
    frequency = THETA ** (-2.0 * np.arange(half) / head_dim)
    angles = np.arange(length)[:, None] * frequency[None, :]
    cosine, sine = np.cos(angles), np.sin(angles)
    return np.concatenate([cosine] * 4 + [-sine, sine] * 2, axis=1).astype(np.float32)


def kernels_fit(tokens, w_query, key_matrix, q_gain):
    sequences, tile, width = tokens.shape
    count, head_dim = lax.axis_size("ctx"), q_gain.shape[0]
    return (
        lax.axis_size("wt") == 4
        and count % 2 == 0
        and count >= 4
        and tile == 128
        and sequences <= 8
        and sequences * count <= 40
        and head_dim == 64
        and w_query.shape[1] == 4 * head_dim
        and key_matrix.shape[1] == 2 * head_dim
        and width % (128 * count) == 0
    )


def on_device_plain(
    tokens,
    segments,
    attn_gain,
    w_query,
    key_matrix,
    value_matrix,
    q_gain,
    k_gain,
    w_out,
    ffn_gain,
    w_gate,
    w_up,
    w_down,
    cotangent,
):
    sequences, seq_rows, model_width = tokens.shape
    head_dim = q_gain.shape[0]
    q_local = w_query.shape[1] // head_dim
    kv_local = key_matrix.shape[1] // head_dim
    per_group = q_local // kv_local
    score_scale = 1.0 / math.sqrt(head_dim)
    all_rows = sequences * seq_rows
    places = lax.axis_index("ctx") * seq_rows + jnp.arange(seq_rows, dtype=jnp.int32)
    frequency = THETA ** (-jnp.arange(0, head_dim, 2, dtype=jnp.float32) / head_dim)
    angles = places.astype(jnp.float32)[None, :, None] * frequency
    cosine_table = jnp.cos(angles)[:, :, None, :]
    sine_table = jnp.sin(angles)[:, :, None, :]
    inputs = tokens.astype(jnp.float32).reshape(all_rows, model_width)
    normed, attn_unit, attn_inverse = norm_rows(inputs, attn_gain)
    normed_low = normed.astype(jnp.bfloat16)
    query_raw = product(normed_low, w_query).reshape(sequences, seq_rows, q_local, head_dim)
    key_raw = product(normed_low, key_matrix).reshape(sequences, seq_rows, kv_local, head_dim)
    value_low = (
        product(normed_low, value_matrix)
        .astype(jnp.bfloat16)
        .reshape(sequences, seq_rows, kv_local * head_dim)
    )
    query_normed, query_unit, query_inverse = norm_rows(query_raw, q_gain)
    key_normed, key_unit, key_inverse = norm_rows(key_raw, k_gain)
    query_low = rotate(query_normed, cosine_table, sine_table, 1.0).astype(jnp.bfloat16)
    key_low = rotate(key_normed, cosine_table, sine_table, 1.0).astype(jnp.bfloat16)
    key_flat = key_low.reshape(sequences, seq_rows, kv_local * head_dim)
    query_groups = query_low.reshape(sequences, seq_rows, kv_local, per_group, head_dim)
    attend = partial(
        attend_piece,
        queries=query_groups,
        query_places=places,
        query_segs=segments,
        score_scale=score_scale,
    )
    start_state = (
        jnp.full((sequences, kv_local, per_group, seq_rows), NEG, jnp.float32),
        jnp.zeros((sequences, kv_local, per_group, seq_rows), jnp.float32),
        jnp.zeros((sequences, seq_rows, kv_local, per_group, head_dim), jnp.float32),
    )
    keys_values = lax.all_gather(
        jnp.concatenate([key_flat, value_low], axis=-1), "ctx", axis=1, tiled=True
    )
    kv_width = kv_local * head_dim
    gathered = (
        keys_values[..., :kv_width],
        keys_values[..., kv_width:],
        lax.all_gather(segments, "ctx", axis=1, tiled=True),
    )
    row_max, row_sum, weighted = attend(
        start_state,
        gathered,
        jnp.int32(0),
    )
    mixed_heads = weighted / jnp.transpose(row_sum, (0, 3, 1, 2))[..., None]
    mixed_low = mixed_heads.astype(jnp.bfloat16).reshape(all_rows, q_local * head_dim)
    attn_term = by_transpose(mixed_low, w_out)
    residual = inputs + lax.psum(attn_term.astype(jnp.bfloat16), "wt").astype(jnp.float32)
    normed_ffn, ffn_unit, ffn_inverse = norm_rows(residual, ffn_gain)
    normed_ffn_low = normed_ffn.astype(jnp.bfloat16)
    gate_proj = product(normed_ffn_low, w_gate)
    up_proj = product(normed_ffn_low, w_up)
    gate_sigmoid = jax.nn.sigmoid(gate_proj)
    gate_silu = gate_proj * gate_sigmoid
    hidden_low = (gate_silu * up_proj).astype(jnp.bfloat16)
    mlp_term = by_transpose(hidden_low, w_down)
    output_rows = (
        residual + lax.psum(mlp_term.astype(jnp.bfloat16), "wt").astype(jnp.float32)
    ).astype(jnp.bfloat16)
    log_total = row_max + jnp.log(row_sum)
    grad_rows = cotangent.reshape(all_rows, model_width)
    grad_hidden = product(grad_rows, w_down)
    grad_gate = (
        grad_hidden * up_proj * gate_sigmoid * (1.0 + gate_proj * (1.0 - gate_sigmoid))
    ).astype(jnp.bfloat16)
    grad_up = (grad_hidden * gate_silu).astype(jnp.bfloat16)
    grad_normed_ffn = by_transpose(grad_gate, w_gate) + by_transpose(grad_up, w_up)
    ffn_gain_part = jnp.sum(grad_normed_ffn * ffn_unit, axis=0)
    grad_normed_ffn = lax.psum(grad_normed_ffn.astype(jnp.bfloat16), "wt").astype(jnp.float32)
    grad_residual = grad_rows.astype(jnp.float32) + norm_back(
        grad_normed_ffn, ffn_unit, ffn_inverse, ffn_gain
    )
    grad_residual_low = grad_residual.astype(jnp.bfloat16)
    grad_heads_low = product(grad_residual_low, w_out).astype(jnp.bfloat16)
    grad_groups = grad_heads_low.reshape(sequences, seq_rows, kv_local, per_group, head_dim)
    delta_rows = jnp.sum(grad_groups.astype(jnp.float32) * mixed_heads, axis=-1)
    delta_cols = jnp.transpose(delta_rows, (0, 2, 3, 1))
    query_grad_fn = partial(
        grad_piece,
        queries=query_groups,
        grad_heads=grad_groups,
        log_total=log_total,
        row_delta=delta_cols,
        query_places=places,
        query_segs=segments,
        score_scale=score_scale,
    )
    grad_query, grad_pairs = query_grad_fn(
        jnp.zeros((sequences, seq_rows, kv_local, per_group, head_dim), jnp.float32),
        gathered,
        jnp.int32(0),
    )
    grad_pairs = lax.psum_scatter(grad_pairs, "ctx", scatter_dimension=1, tiled=True).astype(
        jnp.float32
    )
    grad_key = grad_pairs[:, :, 0]
    grad_value = grad_pairs[:, :, 1]
    grad_query = rotate(
        grad_query.reshape(sequences, seq_rows, q_local, head_dim) * score_scale,
        cosine_table,
        sine_table,
        -1.0,
    )
    grad_key = rotate(grad_key * score_scale, cosine_table, sine_table, -1.0)
    q_gain_part = jnp.sum(grad_query * query_unit, axis=(0, 1, 2))
    k_gain_part = jnp.sum(grad_key * key_unit, axis=(0, 1, 2))
    grad_query_low = (
        norm_back(grad_query, query_unit, query_inverse, q_gain)
        .astype(jnp.bfloat16)
        .reshape(all_rows, q_local * head_dim)
    )
    grad_key_low = (
        norm_back(grad_key, key_unit, key_inverse, k_gain)
        .astype(jnp.bfloat16)
        .reshape(all_rows, kv_local * head_dim)
    )
    grad_value_low = grad_value.astype(jnp.bfloat16).reshape(all_rows, kv_local * head_dim)
    grad_normed = (
        by_transpose(grad_query_low, w_query)
        + by_transpose(grad_key_low, key_matrix)
        + by_transpose(grad_value_low, value_matrix)
    )
    attn_gain_part = jnp.sum(grad_normed * attn_unit, axis=0)
    grad_normed = lax.psum(grad_normed.astype(jnp.bfloat16), "wt").astype(jnp.float32)
    tokens_rows = (
        grad_residual + norm_back(grad_normed, attn_unit, attn_inverse, attn_gain)
    ).astype(jnp.bfloat16)
    output = output_rows.reshape(sequences, seq_rows, model_width)
    tokens_grad = tokens_rows.reshape(sequences, seq_rows, model_width)
    partial_sums = (
        transpose_by(grad_rows, hidden_low),
        transpose_by(normed_ffn_low, grad_gate),
        transpose_by(normed_ffn_low, grad_up),
        transpose_by(grad_residual_low, mixed_low),
        transpose_by(normed_low, grad_query_low),
        transpose_by(normed_low, grad_key_low),
        transpose_by(normed_low, grad_value_low),
    )
    summed = [
        lax.psum_scatter(part.astype(jnp.bfloat16), "ctx", scatter_dimension=0, tiled=True).astype(
            jnp.float32
        )
        for part in partial_sums
    ]
    w_down_grad, w_gate_grad, w_up_grad, w_out_grad = summed[:4]
    w_query_grad, w_key_grad, w_value_grad = summed[4:]
    attn_gain_grad, q_gain_grad, k_gain_grad, ffn_gain_grad = lax.psum(
        (attn_gain_part, q_gain_part, k_gain_part, ffn_gain_part), ("ctx", "wt")
    )
    return (
        output,
        tokens_grad,
        attn_gain_grad,
        w_query_grad,
        w_key_grad,
        w_value_grad,
        q_gain_grad,
        k_gain_grad,
        w_out_grad,
        ffn_gain_grad,
        w_gate_grad,
        w_up_grad,
        w_down_grad,
    )


def on_device(
    tokens,
    segments,
    attn_gain,
    w_query,
    key_matrix,
    value_matrix,
    q_gain,
    k_gain,
    w_out,
    ffn_gain,
    w_gate,
    w_up,
    w_down,
    cotangent,
):
    if not kernels_fit(tokens, w_query, key_matrix, q_gain):
        return on_device_plain(
            tokens,
            segments,
            attn_gain,
            w_query,
            key_matrix,
            value_matrix,
            q_gain,
            k_gain,
            w_out,
            ffn_gain,
            w_gate,
            w_up,
            w_down,
            cotangent,
        )
    sequences, seq_rows, model_width = tokens.shape
    count, head_dim = lax.axis_size("ctx"), q_gain.shape[0]
    token_rows = tokens.reshape(sequences * seq_rows, model_width)
    table = lax.dynamic_slice_in_dim(
        jnp.asarray(rotary_table(count * seq_rows, head_dim)),
        lax.axis_index("ctx") * seq_rows,
        seq_rows,
        0,
    )
    gains = (attn_gain[None], q_gain[None], k_gain[None])
    (
        residual,
        heads,
        mixed_t,
        query_t,
        logs,
        starts,
        keys_values,
        keys_t,
        query_raw,
        key_raw,
        normed_t,
    ) = forward(
        token_rows, segments, table, *gains, w_query, key_matrix, value_matrix, w_out
    )
    normed_ffn, ffn_unit, ffn_inverse = norm_rows(residual, ffn_gain)
    normed_ffn_low = normed_ffn.astype(jnp.bfloat16)
    gate_proj = product(normed_ffn_low, w_gate)
    up_proj = product(normed_ffn_low, w_up)
    gate_sigmoid = jax.nn.sigmoid(gate_proj)
    gate_silu = gate_proj * gate_sigmoid
    hidden_low = (gate_silu * up_proj).astype(jnp.bfloat16)
    mlp_term = by_transpose(hidden_low, w_down)
    output_rows = (
        residual + lax.psum(mlp_term.astype(jnp.bfloat16), "wt").astype(jnp.float32)
    ).astype(jnp.bfloat16)
    grad_rows = cotangent.reshape(token_rows.shape)
    grad_hidden = product(grad_rows, w_down)
    grad_gate = (
        grad_hidden * up_proj * gate_sigmoid * (1.0 + gate_proj * (1.0 - gate_sigmoid))
    ).astype(jnp.bfloat16)
    grad_up = (grad_hidden * gate_silu).astype(jnp.bfloat16)
    grad_normed_ffn = by_transpose(grad_gate, w_gate) + by_transpose(grad_up, w_up)
    ffn_gain_part = jnp.sum(grad_normed_ffn * ffn_unit, axis=0, keepdims=True)
    grad_normed_ffn = lax.psum(grad_normed_ffn.astype(jnp.bfloat16), "wt").astype(jnp.float32)
    grad_residual = (
        grad_rows.astype(jnp.float32)
        + norm_back(grad_normed_ffn, ffn_unit, ffn_inverse, ffn_gain)
    ).astype(jnp.bfloat16)
    (
        tokens_grad,
        w_down_grad,
        w_gate_grad,
        w_up_grad,
        w_out_grad,
        w_query_grad,
        w_key_grad,
        w_value_grad,
        attn_gain_grad,
        ffn_gain_grad,
        q_gain_grad,
        k_gain_grad,
    ) = backward(
        grad_residual,
        token_rows,
        table,
        *gains,
        w_query,
        key_matrix,
        value_matrix,
        w_out,
        heads,
        mixed_t,
        query_t,
        logs,
        starts,
        keys_values,
        keys_t,
        query_raw,
        key_raw,
        normed_t,
        grad_rows.T,
        normed_ffn_low.T,
        jnp.stack([hidden_low, grad_gate, grad_up]),
        ffn_gain_part,
    )
    return (
        output_rows.reshape(tokens.shape),
        tokens_grad.reshape(tokens.shape),
        attn_gain_grad[0],
        w_query_grad,
        w_key_grad,
        w_value_grad,
        q_gain_grad[0],
        k_gain_grad[0],
        w_out_grad,
        ffn_gain_grad[0],
        w_gate_grad,
        w_up_grad,
        w_down_grad,
    )


def solution(mesh):
    in_specs = (
        P(None, "ctx", None),
        P(None, "ctx"),
        P(),
        P(None, "wt"),
        P(None, "wt"),
        P(None, "wt"),
        P(),
        P(),
        P(None, "wt"),
        P(),
        P(None, "wt"),
        P(None, "wt"),
        P(None, "wt"),
        P(None, "ctx", None),
    )
    out_specs = (
        P(None, "ctx", None),
        P(None, "ctx", None),
        P(),
        P("ctx", "wt"),
        P("ctx", "wt"),
        P("ctx", "wt"),
        P(),
        P(),
        P("ctx", "wt"),
        P(),
        P("ctx", "wt"),
        P("ctx", "wt"),
        P("ctx", "wt"),
    )
    return jax.shard_map(
        on_device, mesh=mesh, in_specs=in_specs, out_specs=out_specs, check_vma=False
    )
```

```python
from functools import partial
import math

import jax
import jax.numpy as jnp
import numpy as np
from jax import lax
from jax.experimental import pallas as pl
from jax.experimental.pallas import tpu as pltpu
from jax.sharding import PartitionSpec as P

EPS = 1e-05
THETA = 1000000.0
NEG = -1e30


def product(left, right):
    return jnp.dot(left, right, preferred_element_type=jnp.float32)


def by_transpose(left, right):
    return lax.dot_general(
        left, right, (((1,), (1,)), ((), ())), preferred_element_type=jnp.float32
    )


def transpose_by(left, right):
    return lax.dot_general(
        left, right, (((0,), (0,)), ((), ())), preferred_element_type=jnp.float32
    )


def norm_rows(values, gain):
    inverse = lax.rsqrt(jnp.mean(values * values, axis=-1, keepdims=True) + EPS)
    unit_rows = values * inverse
    return (unit_rows * gain, unit_rows, inverse)


def norm_back(grads, unit_rows, inverse, gain):
    scaled = grads * gain
    return inverse * (scaled - unit_rows * jnp.mean(scaled * unit_rows, axis=-1, keepdims=True))


def rotate(values, cosine_table, sine_table, direction):
    half_dim = values.shape[-1] // 2
    first_half = values[..., :half_dim]
    second_half = values[..., half_dim:]
    return jnp.concatenate(
        [
            first_half * cosine_table - direction * second_half * sine_table,
            second_half * cosine_table + direction * first_half * sine_table,
        ],
        axis=-1,
    )


def split_blocks(array, block_len):
    shaped = array.reshape(
        (array.shape[0], array.shape[1] // block_len, block_len) + array.shape[2:]
    )
    return jnp.moveaxis(shaped, 1, 0)


def attend_piece(folded, pieces, first_row, queries, query_places, query_segs, score_scale):
    key_piece, value_piece, seg_piece = pieces
    sequences, piece_rows = seg_piece.shape
    kv_local = queries.shape[2]
    head_dim = queries.shape[4]
    block_len = math.gcd(piece_rows, 512)
    key_blocks = split_blocks(
        key_piece.reshape(sequences, piece_rows, kv_local, head_dim), block_len
    )
    value_tiles = split_blocks(
        value_piece.reshape(sequences, piece_rows, kv_local, head_dim), block_len
    )
    seg_blocks = split_blocks(seg_piece, block_len)
    offsets = block_len * jnp.arange(piece_rows // block_len, dtype=jnp.int32)

    def attend_block_step(running, block_item):
        row_max, row_sum, weighted = running
        key_block, value_block, seg_block, offset = block_item
        key_places = offset + jnp.arange(block_len, dtype=jnp.int32)
        allowed = (key_places[None, None, :] <= query_places[None, :, None]) & (
            query_segs[:, :, None] == seg_block[:, None, :]
        )
        allowed = allowed[:, None, None]
        scores = (
            jnp.einsum("sqgrd,skgd->sgrqk", queries, key_block, preferred_element_type=jnp.float32)
            * score_scale
        )
        scores = jnp.where(allowed, scores, NEG)
        new_max = jnp.maximum(row_max, jnp.max(scores, axis=-1))
        weights = jnp.where(allowed, jnp.exp(scores - new_max[..., None]), 0.0)
        fading = jnp.exp(row_max - new_max)
        row_sum = row_sum * fading + jnp.sum(weights, axis=-1)
        fade_rows = jnp.transpose(fading, (0, 3, 1, 2))[..., None]
        weighted = weighted * fade_rows + jnp.einsum(
            "sgrqk,skgd->sqgrd",
            weights.astype(jnp.bfloat16),
            value_block,
            preferred_element_type=jnp.float32,
        )
        return ((new_max, row_sum, weighted), None)

    folded, unused = lax.scan(
        attend_block_step, folded, (key_blocks, value_tiles, seg_blocks, offsets)
    )
    return folded


def grad_piece(
    folded,
    pieces,
    first_row,
    queries,
    grad_heads,
    log_total,
    row_delta,
    query_places,
    query_segs,
    score_scale,
):
    key_piece, value_piece, seg_piece = pieces
    sequences, piece_rows = seg_piece.shape
    kv_local = queries.shape[2]
    head_dim = queries.shape[4]
    block_len = math.gcd(piece_rows, 512)
    key_blocks = split_blocks(
        key_piece.reshape(sequences, piece_rows, kv_local, head_dim), block_len
    )
    value_tiles = split_blocks(
        value_piece.reshape(sequences, piece_rows, kv_local, head_dim), block_len
    )
    seg_blocks = split_blocks(seg_piece, block_len)
    offsets = block_len * jnp.arange(piece_rows // block_len, dtype=jnp.int32)

    def grad_block_step(running, block_item):
        key_block, value_block, seg_block, offset = block_item
        key_places = offset + jnp.arange(block_len, dtype=jnp.int32)
        allowed = (key_places[None, None, :] <= query_places[None, :, None]) & (
            query_segs[:, :, None] == seg_block[:, None, :]
        )
        allowed = allowed[:, None, None]
        scores = (
            jnp.einsum("sqgrd,skgd->sgrqk", queries, key_block, preferred_element_type=jnp.float32)
            * score_scale
        )
        probs = jnp.where(allowed, jnp.exp(scores - log_total[..., None]), 0.0)
        grad_probs = jnp.einsum(
            "sqgrd,skgd->sgrqk", grad_heads, value_block, preferred_element_type=jnp.float32
        )
        grad_scores = (probs * (grad_probs - row_delta[..., None])).astype(jnp.bfloat16)
        running = running + jnp.einsum(
            "sgrqk,skgd->sqgrd", grad_scores, key_block, preferred_element_type=jnp.float32
        )
        grad_keys = jnp.einsum(
            "sgrqk,sqgrd->skgd", grad_scores, queries, preferred_element_type=jnp.float32
        )
        grad_values = jnp.einsum(
            "sgrqk,sqgrd->skgd",
            probs.astype(jnp.bfloat16),
            grad_heads,
            preferred_element_type=jnp.float32,
        )
        grads = jnp.stack([grad_keys, grad_values], axis=2).astype(jnp.bfloat16)
        return (running, grads)

    folded, grads = lax.scan(
        grad_block_step, folded, (key_blocks, value_tiles, seg_blocks, offsets)
    )
    return folded, jnp.moveaxis(grads, 0, 1).reshape((sequences, piece_rows) + grads.shape[3:])


MESH = pl.DeviceIdType.MESH
MIB = 1 << 20


def ring_place(index, count):
    return lax.select(
        lax.rem(index, 2) == 0, lax.div(index, 2), count - 1 - lax.div(index, 2)
    )


def ring_index(place, count):
    place = lax.rem(place + 2 * count, count)
    return lax.select(
        place < lax.div(count, 2), 2 * place, 2 * (count - 1 - place) + 1
    )


class Ring:
    def __init__(self, count, slots, send_sems, recv_sems, base=0):
        self.count, self.slots, self.base = count, slots, base
        self.send_sems, self.recv_sems = send_sems, recv_sems
        self.other = lax.axis_index("wt")
        self.place = ring_place(lax.axis_index("ctx"), count)
        self.right = ring_index(self.place + 1, count)
        self.left = ring_index(self.place + count - 1, count)
        self.half = slots.shape[2] // 2

    def copy(self, which, step, way):
        rows = pl.ds(way * self.half, self.half)
        slot = step - self.base
        return pltpu.make_async_remote_copy(
            src_ref=self.slots.at[which, slot, rows],
            dst_ref=self.slots.at[which, slot + 1, rows],
            send_sem=self.send_sems.at[which, slot, way],
            recv_sem=self.recv_sems.at[which, slot, way],
            device_id=((self.right, self.left)[way], self.other),
            device_id_type=MESH,
        )

    def arrived(self, which, step):
        for way in range(2):
            self.copy(which, step - 1, way).wait_recv()

    def tick(self, which, step, left_ref, right_ref, first=False, given=None, result=None):
        half = self.half
        rows = [
            ring_index(target, self.count) * (2 * half) + way * half
            for way, target in enumerate(
                (self.place + self.count - 1 - step, self.place + 1 + step)
            )
        ]
        left = jnp.concatenate(
            [left_ref[pl.ds(pl.multiple_of(row, half), half), :] for row in rows], axis=0
        )
        total = jnp.dot(left, right_ref[...], preferred_element_type=jnp.float32)
        if given is not None:
            total = total + given[...].astype(jnp.float32)
        elif not first:
            self.arrived(which, step)
            total = total + self.slots[which, step - self.base].astype(jnp.float32)
        if result is None:
            self.slots[which, step - self.base] = total.astype(jnp.bfloat16)
            for way in range(2):
                self.copy(which, step, way).start()
        else:
            result[...] = total

    def finish(self, which, end):
        for way in range(2):

            def wait(step, carry):
                self.copy(which, step, way).wait_send()
                return carry

            lax.fori_loop(self.base, end, wait, 0)


def pair_lanes(shape):
    return lax.broadcasted_iota(jnp.int32, shape, 1)


def swap_halves(values, head_dim):
    lanes = pair_lanes(values.shape)
    width = values.shape[1]
    quarter = head_dim // 2
    return jnp.where(
        lax.rem(lanes, head_dim) < quarter,
        pltpu.roll(values, width - quarter, 1),
        pltpu.roll(values, quarter, 1),
    )


def pair_mean(values, head_dim):
    low = pair_lanes(values.shape) < head_dim
    first = jnp.sum(jnp.where(low, values, 0.0), axis=-1, keepdims=True)
    second = jnp.sum(jnp.where(low, 0.0, values), axis=-1, keepdims=True)
    return jnp.where(low, first, second) * (1.0 / head_dim)


def pair_norm(values, head_dim):
    inverse = lax.rsqrt(pair_mean(values * values, head_dim) + EPS)
    return values * inverse, inverse


def double(row):
    return jnp.concatenate([row, row], axis=-1)


def dot_nn(left, right):
    return jnp.dot(left, right, preferred_element_type=jnp.float32)


def dot_nt(left, right):
    return lax.dot_general(
        left, right, (((1,), (1,)), ((), ())), preferred_element_type=jnp.float32
    )


def as_column(row):
    size = row.shape[1]
    rows = lax.broadcasted_iota(jnp.int32, (size, size), 0)
    lanes = lax.broadcasted_iota(jnp.int32, (size, size), 1)
    return jnp.sum(jnp.where(rows == lanes, row, 0.0), axis=1, keepdims=True)


class Place:
    def __init__(self, count):
        self.count = count
        self.ctx, self.wt = lax.axis_index("ctx"), lax.axis_index("wt")
        self.odd = lax.rem(self.ctx, 2)
        self.level = lax.div(self.ctx, 2)
        self.core_bit = lax.rem(self.wt, 2)
        self.beside_ctx = self.ctx + 1 - 2 * self.odd
        self.beside = (self.beside_ctx, self.wt)
        self.above = (lax.rem(self.ctx + 2, count), self.wt)
        self.below = (lax.rem(self.ctx + count - 2, count), self.wt)
        self.has_above = self.ctx + 2 < count
        self.has_below = self.ctx >= 2
        self.core_wt = self.wt + 1 - 2 * self.core_bit
        self.chip_wt = lax.rem(self.wt + 2, 4)
        self.far_wt = lax.rem(self.core_wt + 2, 4)
        self.core = (self.ctx, self.core_wt)
        self.chip = (self.ctx, self.chip_wt)

    def greet(self, more=()):
        barrier = pltpu.get_barrier_semaphore()
        peers = [self.beside, self.core, self.chip, *more]
        for peer in peers:
            pl.semaphore_signal(barrier, inc=1, device_id=peer, device_id_type=MESH)
        for there, peer in ((self.has_above, self.above), (self.has_below, self.below)):

            @pl.when(there)
            def _():
                pl.semaphore_signal(barrier, inc=1, device_id=peer, device_id_type=MESH)

        edges = self.has_above.astype(jnp.int32) + self.has_below.astype(jnp.int32)
        pl.semaphore_wait(barrier, len(peers) + edges)


    def greet_all(self):
        barrier = pltpu.get_barrier_semaphore()

        def signal(peer):
            pl.semaphore_signal(barrier, inc=1, device_id=peer, device_id_type=MESH)

        for shift in range(1, self.count):
            signal((lax.rem(self.ctx + shift, self.count), self.wt))
        signal(self.core)
        signal(self.chip)
        pl.semaphore_wait(barrier, self.count + 1)


def send_to(source, target, send_sem, recv_sem, device):
    return pltpu.make_async_remote_copy(
        src_ref=source,
        dst_ref=target,
        send_sem=send_sem,
        recv_sem=recv_sem,
        device_id=device,
        device_id_type=MESH,
    )


class WtSum:
    def __init__(self, here, tile, part, got, far, full, send_sems, recv_sems):
        self.here, self.tile = here, tile
        self.part, self.got, self.far, self.full = part, got, far, full
        self.send_sems, self.recv_sems = send_sems, recv_sems
        self.mine, self.theirs = here.core_bit, 1 - here.core_bit

    def rows(self, seq):
        return pl.ds(pl.multiple_of(seq * self.tile, self.tile), self.tile)

    def copy(self, hop, seq, arriving=False):
        rows = self.rows(seq)
        half = self.theirs if arriving else self.mine
        source = (
            self.part.at[self.theirs, rows],
            self.got.at[rows],
            self.full.at[half, rows],
        )[hop]
        target = (self.got.at[rows], self.far.at[rows], self.full.at[half, rows])[hop]
        device = self.here.chip if hop == 1 else self.here.core
        return send_to(
            source, target, self.send_sems.at[hop, seq], self.recv_sems.at[hop, seq], device
        )

    def offer(self, seq, value):
        rows = self.rows(seq)
        half = value.shape[1] // 2
        self.part[0, rows] = value[:, :half].astype(jnp.bfloat16)
        self.part[1, rows] = value[:, half:].astype(jnp.bfloat16)
        self.copy(0, seq).start()

    def cross(self, seq):
        rows = self.rows(seq)
        self.copy(0, seq).wait_recv()
        total = self.part[self.mine, rows].astype(jnp.float32) + self.got[rows].astype(
            jnp.float32
        )
        self.got[rows] = total.astype(jnp.bfloat16)
        self.copy(1, seq).start()

    def close(self, seq):
        rows = self.rows(seq)
        self.copy(1, seq).wait_recv()
        total = self.got[rows].astype(jnp.float32) + self.far[rows].astype(jnp.float32)
        self.full[self.mine, rows] = total.astype(jnp.bfloat16)
        self.copy(2, seq).start()

    def result(self, seq):
        rows = self.rows(seq)
        self.copy(2, seq, True).wait_recv()
        return jnp.concatenate([self.full[0, rows], self.full[1, rows]], axis=1).astype(
            jnp.float32
        )

    def finish(self, sequences):
        def sent(seq, carry):
            for hop in range(3):
                self.copy(hop, seq).wait_send()
            return carry

        lax.fori_loop(0, sequences, sent, 0)


def wt_sum_scratch(sequences, rows, width):
    half = width // 2
    return [
        pltpu.VMEM((2, rows, half), jnp.bfloat16),
        pltpu.VMEM((rows, half), jnp.bfloat16),
        pltpu.VMEM((rows, half), jnp.bfloat16),
        pltpu.VMEM((2, rows, half), jnp.bfloat16),
        pltpu.SemaphoreType.DMA((3, sequences)),
        pltpu.SemaphoreType.DMA((3, sequences)),
    ]


def ring_scratch(count, arrays, rows, width):
    return [
        pltpu.VMEM((arrays, count, rows, width), jnp.bfloat16),
        pltpu.SemaphoreType.DMA((arrays, count - 1, 2)),
        pltpu.SemaphoreType.DMA((arrays, count - 1, 2)),
    ]


class GainSum:
    def __init__(self, here, slots, beside, sends, recvs, pair_sends, pair_recvs):
        self.here, self.slots, self.beside = here, slots, beside
        self.sends, self.recvs = sends, recvs
        self.pair_sends, self.pair_recvs = pair_sends, pair_recvs

    def copy(self, shift, arriving=False):
        here = self.here
        target = lax.rem(here.ctx + shift, here.count)
        origin = lax.rem(here.ctx + here.count - shift, here.count)
        ref = self.slots.at[origin if arriving else here.ctx]
        return send_to(
            ref, ref, self.sends.at[shift - 1], self.recvs.at[shift - 1], (target, here.wt)
        )

    def pair_copy(self, hop):
        device = (self.here.core, self.here.chip)[hop]
        return send_to(
            self.beside.at[hop, 0],
            self.beside.at[hop, 1],
            self.pair_sends.at[hop],
            self.pair_recvs.at[hop],
            device,
        )

    def start(self):
        for shift in range(1, self.here.count):
            self.copy(shift).start()

    def total(self):
        for shift in range(1, self.here.count):
            self.copy(shift, True).wait_recv()
        total = self.slots[0]
        for index in range(1, self.here.count):
            total = total + self.slots[index]
        for hop in range(2):
            self.beside[hop, 0] = total
            self.pair_copy(hop).start()
            self.pair_copy(hop).wait_recv()
            total = total + self.beside[hop, 1]
        for shift in range(1, self.here.count):
            self.copy(shift).wait_send()
        for hop in range(2):
            self.pair_copy(hop).wait_send()
        return total


def forward_kernel(
    count,
    tokens,
    segments,
    table,
    attn_gain,
    q_gain,
    k_gain,
    w_query,
    w_key,
    w_value,
    w_out,
    cotangent,
    ffn_gain,
    w_gate_in,
    w_up_in,
    w_down_in,
    residual,
    heads_out,
    mixed_t,
    query_t,
    logs,
    starts,
    keys_values,
    keys_t,
    query_raw,
    key_raw,
    normed_t,
    grad_res,
    cot_t,
    normed_ffn_t,
    ffn_grads,
    ffn_gain_part,
    mlp_part,
    ring_state,
    all_segs,
    all_out,
    all_heads,
    acc,
    row_sum,
    up_send,
    up_recv,
    side_send,
    side_recv,
    seg_send,
    seg_recv,
    out_send,
    out_recv,
    head_send,
    head_recv,
    w_gate,
    w_up,
    w_down,
    grad_hidden,
    load_sems,
    *rest,
):
    sequences, tile = segments.shape
    head_dim = q_gain.shape[1]
    levels = count // 2
    here = Place(count)
    me = here.ctx
    loads = [
        pltpu.make_async_copy(source, target, load_sems.at[i])
        for i, (source, target) in enumerate(
            ((w_down_in, w_down), (w_gate_in, w_gate), (w_up_in, w_up))
        )
    ]
    for load in loads:
        load.start()
    wt_sum = WtSum(here, tile, *rest[:6])
    ffn = Ring(count, *rest[6:9])
    all_segs[me] = jnp.zeros_like(all_segs[me])
    all_segs[me, pl.ds(0, sequences)] = segments[...]
    all_out[here.wt] = w_out[...]
    here.greet()

    def out_copy(hop, arriving=False):
        sent = (here.wt, here.wt, here.chip_wt)
        landed = (here.chip_wt, here.core_wt, here.far_wt)
        ref = all_out.at[(landed if arriving else sent)[hop]]
        device = here.chip if hop == 0 else here.core
        return send_to(ref, ref, out_send.at[hop], out_recv.at[hop], device)

    out_copy(0).start()
    out_copy(1).start()

    def rows_of(seq):
        return pl.ds(pl.multiple_of(seq * tile, tile), tile)

    def block_of(index, step):
        return lax.rem(index - 2 * step + 2 * count, count)

    def up_copy(step, seq):
        rows = keys_values.at[block_of(me, step), rows_of(seq)]
        return send_to(rows, rows, up_send.at[step, seq], up_recv.at[step, seq], here.above)

    def up_wait(step, seq):
        rows = keys_values.at[block_of(me, step), rows_of(seq)]
        earlier = step - 1
        send_to(
            rows, rows, up_send.at[earlier, seq], up_recv.at[earlier, seq], here.above
        ).wait_recv()

    def side_copy(step, seq, index=me):
        rows = keys_values.at[block_of(index, step), rows_of(seq)]
        return send_to(
            rows, rows, side_send.at[step, seq], side_recv.at[step, seq], here.beside
        )

    def side_wait(step, seq):
        side_copy(step, seq, here.beside_ctx).wait_recv()

    def seg_copy(step, way, index=me):
        ref = all_segs.at[block_of(index, step)]
        device = here.beside if way else here.above
        return send_to(ref, ref, seg_send.at[step, way], seg_recv.at[step, way], device)

    def seg_wait(step, way):
        if way:
            seg_copy(step, 1, here.beside_ctx).wait_recv()
        else:
            ref = all_segs.at[block_of(me, step)]
            earlier = step - 1
            send_to(
                ref, ref, seg_send.at[earlier, 0], seg_recv.at[earlier, 0], here.above
            ).wait_recv()

    def goes_up(step):
        return here.has_above & (me >= 2 * step)

    def goes_aside(step):
        block = me - 2 * step
        return (block >= 0) & (block < here.beside_ctx)

    def pass_segs(step):
        @pl.when(goes_up(step))
        def _():
            seg_copy(step, 0).start()

        @pl.when(goes_aside(step))
        def _():
            seg_copy(step, 1).start()

    def pass_rows(step, seq):
        @pl.when(goes_up(step))
        def _():
            up_copy(step, seq).start()

        @pl.when(goes_aside(step))
        def _():
            side_copy(step, seq).start()

    pass_segs(0)
    cosine = table[:, pl.ds(0, 2 * head_dim)]
    sine = table[:, pl.ds(2 * head_dim, 2 * head_dim)]
    q_gain_pair = double(q_gain[...].astype(jnp.float32))
    k_gain_pair = double(k_gain[...].astype(jnp.float32))
    gain = attn_gain[...].astype(jnp.float32)

    def turn(values):
        return values * cosine + swap_halves(values, head_dim) * sine

    def project(seq, carry):
        rows = rows_of(seq)
        inputs = tokens[rows, :].astype(jnp.float32)
        inverse = lax.rsqrt(jnp.mean(inputs * inputs, axis=-1, keepdims=True) + EPS)
        normed = (inputs * inverse * gain).astype(jnp.bfloat16)
        raw_k = dot_nn(normed, w_key[...])
        key_raw[rows, :] = raw_k
        unit, unused = pair_norm(raw_k, head_dim)
        keys_values[me, rows, pl.ds(0, 2 * head_dim)] = turn(unit * k_gain_pair).astype(
            jnp.bfloat16
        )
        keys_values[me, rows, pl.ds(2 * head_dim, 2 * head_dim)] = dot_nn(
            normed, w_value[...]
        ).astype(jnp.bfloat16)
        pass_rows(0, seq)
        raw_q = dot_nn(normed, w_query[...])
        query_raw[rows, :] = raw_q
        query_t[seq] = jnp.zeros_like(query_t[seq])
        for group in range(2):
            unit, unused = pair_norm(
                raw_q[:, group * 2 * head_dim : (group + 1) * 2 * head_dim], head_dim
            )
            turned = turn(unit * q_gain_pair) * (head_dim**-0.5)
            flipped = turned.T.astype(jnp.bfloat16)
            for member in range(2):
                query_t[
                    seq,
                    pl.ds(group * head_dim, head_dim),
                    pl.ds((2 * group + member) * tile, tile),
                ] = flipped[member * head_dim : (member + 1) * head_dim]
        normed_t[:, rows] = normed.T
        acc[seq] = jnp.zeros_like(acc[seq])
        row_sum[seq] = jnp.zeros_like(row_sum[seq])
        starts[seq] = jnp.zeros_like(starts[seq])
        return carry

    lax.fori_loop(0, sequences, project, 0)
    key_rows = lax.broadcasted_iota(jnp.int32, (tile, 4 * tile), 0)
    query_cols = lax.rem(lax.broadcasted_iota(jnp.int32, (tile, 4 * tile), 1), tile)

    def attend(block, seq, own):
        rows = rows_of(seq)
        keys = keys_values[block, rows, pl.ds(0, 2 * head_dim)]
        values = keys_values[block, rows, pl.ds(2 * head_dim, 2 * head_dim)]
        seg_query = all_segs[me, pl.ds(seq, 1)].astype(jnp.float32)
        seg_key = as_column(all_segs[block, pl.ds(seq, 1)].astype(jnp.float32))
        earlier = jnp.where(seg_key < seg_query, 1.0, 0.0)
        starts[seq] += jnp.sum(earlier, axis=0, keepdims=True)
        seg_wide = jnp.concatenate([seg_query] * 4, axis=1)
        if own:
            allowed = (seg_key == seg_wide) & (key_rows <= query_cols)
        else:
            allowed = seg_key >= seg_wide
        scores = dot_nn(keys, query_t[seq])
        weights = jnp.where(allowed, jnp.exp(scores), 0.0)
        row_sum[seq] += jnp.sum(weights, axis=0, keepdims=True)
        low = weights.astype(jnp.bfloat16)
        values_t = values.T
        for group in range(2):
            acc[seq, group] += dot_nn(
                values_t[group * head_dim : (group + 1) * head_dim],
                low[:, group * 2 * tile : (group + 1) * 2 * tile],
            )
        keys_t[block, seq] = keys.T

    def own_block(seq, carry):
        attend(me, seq, True)
        return carry

    lax.fori_loop(0, sequences, own_block, 0)
    loads[0].wait()

    def back_down(seq, carry):
        rows = rows_of(seq)
        grads = cotangent[rows, :]
        cot_t[:, rows] = grads.T
        grad_hidden[rows, :] = dot_nn(grads, w_down[...]).astype(jnp.bfloat16)
        return carry

    lax.fori_loop(0, sequences, back_down, 0)

    @pl.when(goes_back_aside(here, 0))
    def _():
        seg_wait(0, 1)

        def side_block(seq, carry):
            side_wait(0, seq)
            attend(here.beside_ctx, seq, False)
            return carry

        lax.fori_loop(0, sequences, side_block, 0)

    out_copy(0, True).wait_recv()
    out_copy(2).start()

    def level(step, carry):
        @pl.when(me >= 2 * step)
        def _():
            seg_wait(step, 0)
            pass_segs(step)
            seg_wait(step, 1)

            def line_block(seq, carry):
                up_wait(step, seq)
                pass_rows(step, seq)
                attend(me - 2 * step, seq, False)
                return carry

            lax.fori_loop(0, sequences, line_block, 0)

            def side_block(seq, carry):
                side_wait(step, seq)
                attend(here.beside_ctx - 2 * step, seq, False)
                return carry

            lax.fori_loop(0, sequences, side_block, 0)

        return carry

    lax.fori_loop(1, levels, level, 0)

    def head_copy(hop, seq, arriving=False):
        sent = (here.wt, here.wt, here.chip_wt)
        landed = (here.chip_wt, here.core_wt, here.far_wt)
        ref = all_heads.at[(landed if arriving else sent)[hop], rows_of(seq)]
        device = here.chip if hop == 0 else here.core
        return send_to(ref, ref, head_send.at[hop, seq], head_recv.at[hop, seq], device)

    def mix(seq, carry):
        rows = rows_of(seq)
        total = row_sum[seq]
        logs[seq] = jnp.log(total)
        for group in range(2):
            cols = slice(group * 2 * tile, (group + 1) * 2 * tile)
            part = acc[seq, group] / total[:, cols]
            mixed = jnp.concatenate([part[:, :tile], part[:, tile:]], axis=0)
            mixed_t[seq, group] = mixed
            all_heads[here.wt, rows, pl.ds(group * 2 * head_dim, 2 * head_dim)] = mixed.T.astype(
                jnp.bfloat16
            )
        head_copy(0, seq).start()
        head_copy(1, seq).start()
        return carry

    lax.fori_loop(0, sequences, mix, 0)
    heads_out[...] = all_heads[here.wt]
    out_copy(1, True).wait_recv()
    out_copy(2, True).wait_recv()

    loads[1].wait()
    loads[2].wait()
    ffn_gain_row = ffn_gain[...].astype(jnp.float32)
    ffn_gain_part[...] = jnp.zeros_like(ffn_gain_part)

    def ffn_unit(rows):
        values = residual[rows, :]
        inverse = lax.rsqrt(jnp.mean(values * values, axis=-1, keepdims=True) + EPS)
        return values * inverse, inverse

    def feed(seq):
        rows = rows_of(seq)
        total = tokens[rows, :].astype(jnp.float32)
        for slot in range(4):
            total = total + dot_nt(all_heads[slot, rows], all_out[slot])
        residual[rows, :] = total
        unit, unused = ffn_unit(rows)
        normed = (unit * ffn_gain_row).astype(jnp.bfloat16)
        normed_ffn_t[:, rows] = normed.T
        gate = dot_nn(normed, w_gate[...])
        up = dot_nn(normed, w_up[...])
        sigmoid = jax.nn.sigmoid(gate)
        silu = gate * sigmoid
        ffn_grads[0, rows] = (silu * up).astype(jnp.bfloat16)
        grads = grad_hidden[rows, :].astype(jnp.float32)
        grad_gate = (grads * up * sigmoid * (1.0 + gate * (1.0 - sigmoid))).astype(jnp.bfloat16)
        grad_up = (grads * silu).astype(jnp.bfloat16)
        ffn_grads[1, rows] = grad_gate
        ffn_grads[2, rows] = grad_up
        grad_normed = dot_nt(grad_gate, w_gate[...]) + dot_nt(grad_up, w_up[...])
        ffn_gain_part[...] += jnp.sum(grad_normed * unit, axis=0, keepdims=True)
        wt_sum.offer(seq, grad_normed)

    def feed_turn(turn_, carry):
        @pl.when(turn_ < sequences)
        def _():
            head_copy(0, turn_, True).wait_recv()
            head_copy(2, turn_).start()

        @pl.when(turn_ > 0)
        def _():
            seq = turn_ - 1
            head_copy(1, seq, True).wait_recv()
            head_copy(2, seq, True).wait_recv()
            feed(seq)

        @pl.when(turn_ > 1)
        def _():
            wt_sum.cross(turn_ - 2)

        return carry

    lax.fori_loop(0, sequences + 1, feed_turn, 0)
    wt_sum.cross(sequences - 1)
    lefts = (cot_t, normed_ffn_t, normed_ffn_t)
    for i in range(3):
        ffn.tick(i, 0, lefts[i], ffn_grads.at[i], first=True)
    half = tokens.shape[1] // 2

    def down(seq, carry):
        rows = rows_of(seq)
        term = dot_nt(ffn_grads[0, rows], w_down[...])
        mlp_part[0, rows] = term[:, :half].astype(jnp.bfloat16)
        mlp_part[1, rows] = term[:, half:].astype(jnp.bfloat16)
        wt_sum.close(seq)
        return carry

    lax.fori_loop(0, sequences, down, 0)
    for i in range(3):
        ffn.tick(i, 1, lefts[i], ffn_grads.at[i])

    def back_norm(seq, carry):
        rows = rows_of(seq)
        unit, inverse = ffn_unit(rows)
        scaled = wt_sum.result(seq) * ffn_gain_row
        grads = inverse * (scaled - unit * jnp.mean(scaled * unit, axis=-1, keepdims=True))
        grad_res[rows, :] = (cotangent[rows, :].astype(jnp.float32) + grads).astype(jnp.bfloat16)
        return carry

    lax.fori_loop(0, sequences, back_norm, 0)
    for i in range(3):
        ffn.arrived(i, 2)
        ring_state[i] = ffn.slots[i, 2]
        ffn.finish(i, 2)
    wt_sum.finish(sequences)
    for hop in range(3):
        out_copy(hop).wait_send()

        def sent(seq, carry):
            head_copy(hop, seq).wait_send()
            return carry

        lax.fori_loop(0, sequences, sent, 0)

    def drain(step, carry):
        @pl.when(goes_up(step))
        def _():
            seg_copy(step, 0).wait_send()

            def sent(seq, carry):
                up_copy(step, seq).wait_send()
                return carry

            lax.fori_loop(0, sequences, sent, 0)

        @pl.when(goes_aside(step))
        def _():
            seg_copy(step, 1).wait_send()

            def sent(seq, carry):
                side_copy(step, seq).wait_send()
                return carry

            lax.fori_loop(0, sequences, sent, 0)

        return carry

    lax.fori_loop(0, levels, drain, 0)


def goes_back_aside(here, step):
    block = here.beside_ctx - 2 * step
    return (block >= 0) & (block < here.ctx)


def forward(*arrays):
    tokens, segments, q_gain, w_gate = arrays[0], arrays[1], arrays[4], arrays[12]
    count = lax.axis_size("ctx")
    sequences, tile = segments.shape
    rows, width = tokens.shape
    head_dim = q_gain.shape[1]
    pair = 2 * head_dim
    levels = count // 2
    hidden = w_gate.shape[1]
    vmem = pl.BlockSpec(memory_space=pltpu.VMEM)
    f32, bf16 = jnp.float32, jnp.bfloat16
    outs = [
        ((rows, width), f32),
        ((rows, 2 * pair), bf16),
        ((sequences, 2, pair, tile), f32),
        ((sequences, pair, 4 * tile), bf16),
        ((sequences, 1, 4 * tile), f32),
        ((sequences, 1, tile), f32),
        ((count, rows, 2 * pair), bf16),
        ((count, sequences, pair, tile), bf16),
        ((rows, 2 * pair), f32),
        ((rows, pair), f32),
        ((width, rows), bf16),
        ((rows, width), bf16),
        ((width, rows), bf16),
        ((width, rows), bf16),
        ((3, rows, hidden), bf16),
        ((1, width), f32),
        ((2, rows, width // 2), bf16),
        ((3, width // count, hidden), bf16),
    ]
    dma = pltpu.SemaphoreType.DMA
    return pl.pallas_call(
        partial(forward_kernel, count),
        out_shape=[jax.ShapeDtypeStruct(shape, kind) for shape, kind in outs],
        in_specs=[vmem] * 12 + [pl.BlockSpec(memory_space=pl.ANY)] * 3,
        out_specs=[vmem] * len(outs),
        scratch_shapes=[
            pltpu.VMEM((count, 8, tile), jnp.int32),
            pltpu.VMEM((4, width, 2 * pair), bf16),
            pltpu.VMEM((4, rows, 2 * pair), bf16),
            pltpu.VMEM((sequences, 2, head_dim, 2 * tile), f32),
            pltpu.VMEM((sequences, 1, 4 * tile), f32),
            dma((levels, sequences)),
            dma((levels, sequences)),
            dma((levels, sequences)),
            dma((levels, sequences)),
            dma((levels, 2)),
            dma((levels, 2)),
            dma((3,)),
            dma((3,)),
            dma((3, sequences)),
            dma((3, sequences)),
            pltpu.VMEM((width, hidden), bf16),
            pltpu.VMEM((width, hidden), bf16),
            pltpu.VMEM((width, hidden), bf16),
            pltpu.VMEM((rows, hidden), bf16),
            dma((3,)),
            *wt_sum_scratch(sequences, rows, width),
            *ring_scratch(3, 3, width // count, hidden),
        ],
        compiler_params=pltpu.CompilerParams(
            collective_id=2, has_side_effects=True, vmem_limit_bytes=60 * MIB
        ),
    )(*arrays)


def backward_kernel(count, *refs):
    (
        grad_res,
        tokens,
        table,
        attn_gain,
        q_gain,
        k_gain,
        w_query,
        w_key,
        w_value,
        w_out,
        heads,
        mixed_t,
        query_t,
        logs,
        starts,
        keys_values,
        keys_t,
        query_raw,
        key_raw,
        normed_t,
        cot_t,
        normed_ffn_t,
        ffn_grads,
        ffn_gain_part,
        residual,
        mlp_part,
        ring_state,
    ) = refs[:27]
    (
        output,
        tokens_grad,
        down_sum,
        gate_sum,
        up_sum,
        out_sum,
        query_sum,
        key_sum,
        value_sum,
        attn_gain_sum,
        ffn_gain_sum,
        q_gain_sum,
        k_gain_sum,
    ) = refs[27:40]
    (
        grad_res_t,
        grad_heads_t,
        deltas,
        grad_query_t,
        own_grads,
        grad_qkv,
        side_in,
        side_out,
        line_in,
        line_out,
        qkv_total,
        side_send,
        side_recv,
        line_send,
        line_recv,
    ) = refs[40:55]
    rest = refs[55:]
    sequences, tile = mixed_t.shape[0], mixed_t.shape[3]
    head_dim = q_gain.shape[1]
    pair = 2 * head_dim
    levels = count // 2
    here = Place(count)
    me = here.ctx
    wt_sum = WtSum(here, tile, *rest[:6])
    gains = GainSum(here, *rest[6:12])
    gain_slots = rest[6]
    ffn = Ring(count, *rest[12:15], base=2)
    out = Ring(count, *rest[15:18])
    qkv = Ring(count, *rest[18:21])
    mlp_sum = WtSum(here, tile, mlp_part, *rest[21:26])
    last = count - 1
    here.greet_all()
    lefts = (cot_t, normed_ffn_t, normed_ffn_t)
    ffn_sums = (down_sum, gate_sum, up_sum)

    def ffn_ticks(step, given=False, final=False):
        for i in range(3):
            ffn.tick(
                i,
                step,
                lefts[i],
                ffn_grads.at[i],
                given=ring_state.at[i] if given else None,
                result=ffn_sums[i] if final else None,
            )

    def rows_of(seq):
        return pl.ds(pl.multiple_of(seq * tile, tile), tile)

    ffn_ticks(2, given=True)

    def each(step):
        def one(seq, carry):
            step(seq)
            return carry

        lax.fori_loop(0, sequences, one, 0)

    each(lambda seq: mlp_sum.copy(0, seq).start())

    def prepare(seq, carry):
        rows = rows_of(seq)
        grads = grad_res[rows, :]
        grad_res_t[:, rows] = grads.T
        grad_heads_t[seq] = jnp.zeros_like(grad_heads_t[seq])
        low = dot_nn(grads, w_out[...]).astype(jnp.bfloat16)
        for group in range(2):
            flipped = low[:, group * pair : (group + 1) * pair].T
            product_t = flipped.astype(jnp.float32) * mixed_t[seq, group]
            for member in range(2):
                part = slice(member * head_dim, (member + 1) * head_dim)
                cols = pl.ds((2 * group + member) * tile, tile)
                grad_heads_t[seq, pl.ds(group * head_dim, head_dim), cols] = flipped[part]
                deltas[seq, :, cols] = jnp.sum(product_t[part], axis=0, keepdims=True)
        grad_query_t[seq] = jnp.zeros_like(grad_query_t[seq])
        return carry

    lax.fori_loop(0, sequences, prepare, 0)
    out.tick(0, 0, grad_res_t, heads, first=True)
    each(mlp_sum.cross)
    key_rows = lax.broadcasted_iota(jnp.int32, (tile, 4 * tile), 0)
    query_cols = lax.rem(lax.broadcasted_iota(jnp.int32, (tile, 4 * tile), 1), tile)

    def grads_of(block, seq, own):
        rows = rows_of(seq)
        keys = keys_values[block, rows, pl.ds(0, pair)]
        values = keys_values[block, rows, pl.ds(pair, pair)]
        places = (key_rows + block * tile).astype(jnp.float32)
        start = starts[seq]
        allowed = places >= jnp.concatenate([start] * 4, axis=1)
        if own:
            allowed = allowed & (key_rows <= query_cols)
        queries = query_t[seq]
        grad_heads = grad_heads_t[seq]
        scores = dot_nn(keys, queries)
        probs = jnp.where(allowed, jnp.exp(scores - logs[seq]), 0.0)
        grad_probs = dot_nn(values, grad_heads)
        grad_scores = (probs * (grad_probs - deltas[seq])).astype(jnp.bfloat16)
        flipped = keys_t[block, seq]
        for group in range(2):
            cols = slice(group * 2 * tile, (group + 1) * 2 * tile)
            grad_query_t[seq, group] += dot_nn(
                flipped[group * head_dim : (group + 1) * head_dim], grad_scores[:, cols]
            )
        grad_keys = dot_nt(grad_scores, queries)
        grad_values = dot_nt(probs.astype(jnp.bfloat16), grad_heads)
        return jnp.concatenate([grad_keys, grad_values], axis=1)

    def side_copy(step, seq):
        return send_to(
            side_out.at[step, rows_of(seq)],
            side_in.at[step, rows_of(seq)],
            side_send.at[step, seq],
            side_recv.at[step, seq],
            here.beside,
        )

    def line_copy(step, seq):
        earlier = step - 1
        return send_to(
            line_out.at[earlier, rows_of(seq)],
            line_in.at[earlier, rows_of(seq)],
            line_send.at[earlier, seq],
            line_recv.at[earlier, seq],
            here.below,
        )

    def from_above(step, seq):
        later = step + 1
        return line_copy(later, seq)

    def block_there(step):
        block = here.beside_ctx - 2 * step
        return (block >= 0) & (block < me)

    def block_comes(step):
        return (me >= 2 * step) & (me - 2 * step < here.beside_ctx)

    def send_aside(step):
        @pl.when(block_there(step))
        def _():
            def one(seq, carry):
                side_out[step, rows_of(seq)] = grads_of(
                    here.beside_ctx - 2 * step, seq, False
                ).astype(jnp.bfloat16)
                side_copy(step, seq).start()
                return carry

            lax.fori_loop(0, sequences, one, 0)

    def level(turn_, carry):
        step = levels - 1 - turn_
        send_aside(step)

        @pl.when(me >= 2 * step)
        def _():
            def one(seq, carry):
                rows = rows_of(seq)
                own_grads[rows, :] = grads_of(me - 2 * step, seq, False)
                side_copy(step, seq).wait_recv()
                total = own_grads[rows, :] + side_in[step, rows].astype(jnp.float32)
                own_grads[rows, :] = total

                @pl.when(here.has_above)
                def _():
                    from_above(step, seq).wait_recv()
                    own_grads[rows, :] += line_in[step, rows].astype(jnp.float32)

                line_out[step - 1, rows] = own_grads[rows, :].astype(jnp.bfloat16)
                line_copy(step, seq).start()
                return carry

            lax.fori_loop(0, sequences, one, 0)

        ffn_ticks(3 + turn_)
        out.tick(0, 1 + turn_, grad_res_t, heads)
        return carry

    lax.fori_loop(0, levels - 1, level, 0)
    send_aside(0)
    each(mlp_sum.close)

    def own_block(seq, carry):
        own_grads[rows_of(seq), :] = grads_of(me, seq, True)
        return carry

    lax.fori_loop(0, sequences, own_block, 0)
    ffn_ticks(levels + 2)
    out.tick(0, levels, grad_res_t, heads)

    def output_rows(seq):
        rows = rows_of(seq)
        output[rows, :] = (residual[rows, :] + mlp_sum.result(seq)).astype(jnp.bfloat16)

    each(output_rows)
    cosine = table[:, pl.ds(0, pair)]
    sine = table[:, pl.ds(pair, pair)]
    q_gain_pair = double(q_gain[...].astype(jnp.float32))
    k_gain_pair = double(k_gain[...].astype(jnp.float32))
    gain = attn_gain[...].astype(jnp.float32)
    gain_slots[me] = jnp.zeros_like(gain_slots[me])
    gain_slots[me, pl.ds(1, 1)] = ffn_gain_part[...]

    def back_through(grads, raw, gain_pair, row):
        turned = grads * cosine - swap_halves(grads, head_dim) * sine
        unit, inverse = pair_norm(raw, head_dim)
        gain_slots[me, pl.ds(row, 1), pl.ds(0, pair)] += jnp.sum(
            turned * unit, axis=0, keepdims=True
        )
        scaled = turned * gain_pair
        return (inverse * (scaled - unit * pair_mean(scaled * unit, head_dim))).astype(
            jnp.bfloat16
        )

    def token_unit(rows):
        inputs = tokens[rows, :].astype(jnp.float32)
        inverse = lax.rsqrt(jnp.mean(inputs * inputs, axis=-1, keepdims=True) + EPS)
        return inputs * inverse, inverse

    def project_back(seq, carry):
        rows = rows_of(seq)
        for group in range(2):
            grads = grad_query_t[seq, group] * (head_dim**-0.5)
            grads = jnp.concatenate([grads[:, :tile], grads[:, tile:]], axis=0).T
            cols = pl.ds(group * pair, pair)
            grad_qkv[rows, cols] = back_through(grads, query_raw[rows, cols], q_gain_pair, 2)

        @pl.when(block_comes(0))
        def _():
            side_copy(0, seq).wait_recv()
            own_grads[rows, :] += side_in[0, rows].astype(jnp.float32)

        @pl.when(here.has_above)
        def _():
            from_above(0, seq).wait_recv()
            own_grads[rows, :] += line_in[0, rows].astype(jnp.float32)

        grad_qkv[rows, pl.ds(2 * pair, pair)] = back_through(
            own_grads[rows, pl.ds(0, pair)], key_raw[rows, :], k_gain_pair, 3
        )
        grad_qkv[rows, pl.ds(3 * pair, pair)] = own_grads[rows, pl.ds(pair, pair)].astype(
            jnp.bfloat16
        )
        grads = (
            dot_nt(grad_qkv[rows, pl.ds(0, 2 * pair)], w_query[...])
            + dot_nt(grad_qkv[rows, pl.ds(2 * pair, pair)], w_key[...])
            + dot_nt(grad_qkv[rows, pl.ds(3 * pair, pair)], w_value[...])
        )
        unit, inverse = token_unit(rows)
        gain_slots[me, pl.ds(0, 1)] += jnp.sum(grads * unit, axis=0, keepdims=True)
        wt_sum.offer(seq, grads)
        return carry

    lax.fori_loop(0, sequences, project_back, 0)
    gains.start()
    qkv.tick(0, 0, normed_t, grad_qkv, first=True)

    def crossing(seq, carry):
        wt_sum.cross(seq)
        return carry

    lax.fori_loop(0, sequences, crossing, 0)

    def tail(step, carry):
        qkv.tick(0, step, normed_t, grad_qkv)

        @pl.when(step + levels < last)
        def _():
            out.tick(0, step + levels, grad_res_t, heads)

        return carry

    ffn_ticks(last, final=True)
    lax.fori_loop(1, last - 1, tail, 0)
    out.tick(0, last, grad_res_t, heads, result=out_sum)

    def closing(seq, carry):
        wt_sum.close(seq)
        return carry

    lax.fori_loop(0, sequences, closing, 0)
    qkv.tick(0, last - 1, normed_t, grad_qkv)

    def token_rows(seq, carry):
        rows = rows_of(seq)
        unit, inverse = token_unit(rows)
        scaled = wt_sum.result(seq) * gain
        grads = inverse * (scaled - unit * jnp.mean(scaled * unit, axis=-1, keepdims=True))
        tokens_grad[rows, :] = (grad_res[rows, :].astype(jnp.float32) + grads).astype(
            jnp.bfloat16
        )
        return carry

    lax.fori_loop(0, sequences, token_rows, 0)
    total = gains.total()
    attn_gain_sum[...] = total[0:1]
    ffn_gain_sum[...] = total[1:2]
    folded = total[:, :pair]
    folded = folded + pltpu.roll(folded, head_dim, 1)
    q_gain_sum[...] = folded[2:3, :head_dim]
    k_gain_sum[...] = folded[3:4, :head_dim]
    qkv.tick(0, last, normed_t, grad_qkv, result=qkv_total)
    query_sum[...] = qkv_total[:, pl.ds(0, 2 * pair)]
    key_sum[...] = qkv_total[:, pl.ds(2 * pair, pair)]
    value_sum[...] = qkv_total[:, pl.ds(3 * pair, pair)]
    wt_sum.finish(sequences)
    for i in range(3):
        ffn.finish(i, last)
    out.finish(0, last)
    qkv.finish(0, last)
    mlp_sum.finish(sequences)

    def drain(step, carry):
        @pl.when(block_there(step))
        def _():
            def sent(seq, carry):
                side_copy(step, seq).wait_send()
                return carry

            lax.fori_loop(0, sequences, sent, 0)

        @pl.when((step > 0) & (me >= 2 * step))
        def _():
            def sent(seq, carry):
                line_copy(step, seq).wait_send()
                return carry

            lax.fori_loop(0, sequences, sent, 0)

        return carry

    lax.fori_loop(0, levels, drain, 0)


def backward(*arrays):
    (grad_res, tokens, table, attn_gain, q_gain) = arrays[:5]
    mixed_t, cot_t, ffn_grads = arrays[11], arrays[20], arrays[22]
    count = lax.axis_size("ctx")
    sequences, tile = mixed_t.shape[0], mixed_t.shape[3]
    rows, width = tokens.shape
    head_dim = q_gain.shape[1]
    pair = 2 * head_dim
    levels = count // 2
    block = width // count
    hidden = ffn_grads.shape[2]
    vmem = pl.BlockSpec(memory_space=pltpu.VMEM)
    f32, bf16 = jnp.float32, jnp.bfloat16
    outs = [
        ((rows, width), bf16),
        ((rows, width), bf16),
        ((block, hidden), f32),
        ((block, hidden), f32),
        ((block, hidden), f32),
        ((block, 2 * pair), f32),
        ((block, 2 * pair), f32),
        ((block, pair), f32),
        ((block, pair), f32),
        ((1, width), f32),
        ((1, width), f32),
        ((1, head_dim), f32),
        ((1, head_dim), f32),
    ]
    dma = pltpu.SemaphoreType.DMA
    return pl.pallas_call(
        partial(backward_kernel, count),
        out_shape=[jax.ShapeDtypeStruct(shape, kind) for shape, kind in outs],
        in_specs=[vmem] * len(arrays),
        out_specs=[vmem] * len(outs),
        scratch_shapes=[
            pltpu.VMEM((width, rows), bf16),
            pltpu.VMEM((sequences, pair, 4 * tile), bf16),
            pltpu.VMEM((sequences, 1, 4 * tile), f32),
            pltpu.VMEM((sequences, 2, head_dim, 2 * tile), f32),
            pltpu.VMEM((rows, 2 * pair), f32),
            pltpu.VMEM((rows, 4 * pair), bf16),
            pltpu.VMEM((levels, rows, 2 * pair), bf16),
            pltpu.VMEM((levels, rows, 2 * pair), bf16),
            pltpu.VMEM((levels - 1, rows, 2 * pair), bf16),
            pltpu.VMEM((levels - 1, rows, 2 * pair), bf16),
            pltpu.VMEM((block, 4 * pair), f32),
            dma((levels, sequences)),
            dma((levels, sequences)),
            dma((levels - 1, sequences)),
            dma((levels - 1, sequences)),
            *wt_sum_scratch(sequences, rows, width),
            pltpu.VMEM((count, 8, width), f32),
            pltpu.VMEM((2, 2, 8, width), f32),
            dma((count - 1,)),
            dma((count - 1,)),
            dma((2,)),
            dma((2,)),
            *ring_scratch(count - 2, 3, block, hidden),
            *ring_scratch(count, 1, block, 2 * pair),
            *ring_scratch(count, 1, block, 4 * pair),
            *wt_sum_scratch(sequences, rows, width)[1:],
        ],
        compiler_params=pltpu.CompilerParams(
            collective_id=3, has_side_effects=True, vmem_limit_bytes=62 * MIB
        ),
    )(*arrays)


def rotary_table(length, head_dim):
    half = head_dim // 2
    frequency = THETA ** (-2.0 * np.arange(half) / head_dim)
    angles = np.arange(length)[:, None] * frequency[None, :]
    cosine, sine = np.cos(angles), np.sin(angles)
    return np.concatenate([cosine] * 4 + [-sine, sine] * 2, axis=1).astype(np.float32)


def kernels_fit(tokens, w_query, key_matrix, q_gain):
    sequences, tile, width = tokens.shape
    count, head_dim = lax.axis_size("ctx"), q_gain.shape[0]
    return (
        lax.axis_size("wt") == 4
        and count % 2 == 0
        and count >= 4
        and tile == 128
        and sequences <= 8
        and sequences * count <= 40
        and head_dim == 64
        and w_query.shape[1] == 4 * head_dim
        and key_matrix.shape[1] == 2 * head_dim
        and width % (128 * count) == 0
    )


def on_device_plain(
    tokens,
    segments,
    attn_gain,
    w_query,
    key_matrix,
    value_matrix,
    q_gain,
    k_gain,
    w_out,
    ffn_gain,
    w_gate,
    w_up,
    w_down,
    cotangent,
):
    sequences, seq_rows, model_width = tokens.shape
    head_dim = q_gain.shape[0]
    q_local = w_query.shape[1] // head_dim
    kv_local = key_matrix.shape[1] // head_dim
    per_group = q_local // kv_local
    score_scale = 1.0 / math.sqrt(head_dim)
    all_rows = sequences * seq_rows
    places = lax.axis_index("ctx") * seq_rows + jnp.arange(seq_rows, dtype=jnp.int32)
    frequency = THETA ** (-jnp.arange(0, head_dim, 2, dtype=jnp.float32) / head_dim)
    angles = places.astype(jnp.float32)[None, :, None] * frequency
    cosine_table = jnp.cos(angles)[:, :, None, :]
    sine_table = jnp.sin(angles)[:, :, None, :]
    inputs = tokens.astype(jnp.float32).reshape(all_rows, model_width)
    normed, attn_unit, attn_inverse = norm_rows(inputs, attn_gain)
    normed_low = normed.astype(jnp.bfloat16)
    query_raw = product(normed_low, w_query).reshape(sequences, seq_rows, q_local, head_dim)
    key_raw = product(normed_low, key_matrix).reshape(sequences, seq_rows, kv_local, head_dim)
    value_low = (
        product(normed_low, value_matrix)
        .astype(jnp.bfloat16)
        .reshape(sequences, seq_rows, kv_local * head_dim)
    )
    query_normed, query_unit, query_inverse = norm_rows(query_raw, q_gain)
    key_normed, key_unit, key_inverse = norm_rows(key_raw, k_gain)
    query_low = rotate(query_normed, cosine_table, sine_table, 1.0).astype(jnp.bfloat16)
    key_low = rotate(key_normed, cosine_table, sine_table, 1.0).astype(jnp.bfloat16)
    key_flat = key_low.reshape(sequences, seq_rows, kv_local * head_dim)
    query_groups = query_low.reshape(sequences, seq_rows, kv_local, per_group, head_dim)
    attend = partial(
        attend_piece,
        queries=query_groups,
        query_places=places,
        query_segs=segments,
        score_scale=score_scale,
    )
    start_state = (
        jnp.full((sequences, kv_local, per_group, seq_rows), NEG, jnp.float32),
        jnp.zeros((sequences, kv_local, per_group, seq_rows), jnp.float32),
        jnp.zeros((sequences, seq_rows, kv_local, per_group, head_dim), jnp.float32),
    )
    keys_values = lax.all_gather(
        jnp.concatenate([key_flat, value_low], axis=-1), "ctx", axis=1, tiled=True
    )
    kv_width = kv_local * head_dim
    gathered = (
        keys_values[..., :kv_width],
        keys_values[..., kv_width:],
        lax.all_gather(segments, "ctx", axis=1, tiled=True),
    )
    row_max, row_sum, weighted = attend(
        start_state,
        gathered,
        jnp.int32(0),
    )
    mixed_heads = weighted / jnp.transpose(row_sum, (0, 3, 1, 2))[..., None]
    mixed_low = mixed_heads.astype(jnp.bfloat16).reshape(all_rows, q_local * head_dim)
    attn_term = by_transpose(mixed_low, w_out)
    residual = inputs + lax.psum(attn_term.astype(jnp.bfloat16), "wt").astype(jnp.float32)
    normed_ffn, ffn_unit, ffn_inverse = norm_rows(residual, ffn_gain)
    normed_ffn_low = normed_ffn.astype(jnp.bfloat16)
    gate_proj = product(normed_ffn_low, w_gate)
    up_proj = product(normed_ffn_low, w_up)
    gate_sigmoid = jax.nn.sigmoid(gate_proj)
    gate_silu = gate_proj * gate_sigmoid
    hidden_low = (gate_silu * up_proj).astype(jnp.bfloat16)
    mlp_term = by_transpose(hidden_low, w_down)
    output_rows = (
        residual + lax.psum(mlp_term.astype(jnp.bfloat16), "wt").astype(jnp.float32)
    ).astype(jnp.bfloat16)
    log_total = row_max + jnp.log(row_sum)
    grad_rows = cotangent.reshape(all_rows, model_width)
    grad_hidden = product(grad_rows, w_down)
    grad_gate = (
        grad_hidden * up_proj * gate_sigmoid * (1.0 + gate_proj * (1.0 - gate_sigmoid))
    ).astype(jnp.bfloat16)
    grad_up = (grad_hidden * gate_silu).astype(jnp.bfloat16)
    grad_normed_ffn = by_transpose(grad_gate, w_gate) + by_transpose(grad_up, w_up)
    ffn_gain_part = jnp.sum(grad_normed_ffn * ffn_unit, axis=0)
    grad_normed_ffn = lax.psum(grad_normed_ffn.astype(jnp.bfloat16), "wt").astype(jnp.float32)
    grad_residual = grad_rows.astype(jnp.float32) + norm_back(
        grad_normed_ffn, ffn_unit, ffn_inverse, ffn_gain
    )
    grad_residual_low = grad_residual.astype(jnp.bfloat16)
    grad_heads_low = product(grad_residual_low, w_out).astype(jnp.bfloat16)
    grad_groups = grad_heads_low.reshape(sequences, seq_rows, kv_local, per_group, head_dim)
    delta_rows = jnp.sum(grad_groups.astype(jnp.float32) * mixed_heads, axis=-1)
    delta_cols = jnp.transpose(delta_rows, (0, 2, 3, 1))
    query_grad_fn = partial(
        grad_piece,
        queries=query_groups,
        grad_heads=grad_groups,
        log_total=log_total,
        row_delta=delta_cols,
        query_places=places,
        query_segs=segments,
        score_scale=score_scale,
    )
    grad_query, grad_pairs = query_grad_fn(
        jnp.zeros((sequences, seq_rows, kv_local, per_group, head_dim), jnp.float32),
        gathered,
        jnp.int32(0),
    )
    grad_pairs = lax.psum_scatter(grad_pairs, "ctx", scatter_dimension=1, tiled=True).astype(
        jnp.float32
    )
    grad_key = grad_pairs[:, :, 0]
    grad_value = grad_pairs[:, :, 1]
    grad_query = rotate(
        grad_query.reshape(sequences, seq_rows, q_local, head_dim) * score_scale,
        cosine_table,
        sine_table,
        -1.0,
    )
    grad_key = rotate(grad_key * score_scale, cosine_table, sine_table, -1.0)
    q_gain_part = jnp.sum(grad_query * query_unit, axis=(0, 1, 2))
    k_gain_part = jnp.sum(grad_key * key_unit, axis=(0, 1, 2))
    grad_query_low = (
        norm_back(grad_query, query_unit, query_inverse, q_gain)
        .astype(jnp.bfloat16)
        .reshape(all_rows, q_local * head_dim)
    )
    grad_key_low = (
        norm_back(grad_key, key_unit, key_inverse, k_gain)
        .astype(jnp.bfloat16)
        .reshape(all_rows, kv_local * head_dim)
    )
    grad_value_low = grad_value.astype(jnp.bfloat16).reshape(all_rows, kv_local * head_dim)
    grad_normed = (
        by_transpose(grad_query_low, w_query)
        + by_transpose(grad_key_low, key_matrix)
        + by_transpose(grad_value_low, value_matrix)
    )
    attn_gain_part = jnp.sum(grad_normed * attn_unit, axis=0)
    grad_normed = lax.psum(grad_normed.astype(jnp.bfloat16), "wt").astype(jnp.float32)
    tokens_rows = (
        grad_residual + norm_back(grad_normed, attn_unit, attn_inverse, attn_gain)
    ).astype(jnp.bfloat16)
    output = output_rows.reshape(sequences, seq_rows, model_width)
    tokens_grad = tokens_rows.reshape(sequences, seq_rows, model_width)
    partial_sums = (
        transpose_by(grad_rows, hidden_low),
        transpose_by(normed_ffn_low, grad_gate),
        transpose_by(normed_ffn_low, grad_up),
        transpose_by(grad_residual_low, mixed_low),
        transpose_by(normed_low, grad_query_low),
        transpose_by(normed_low, grad_key_low),
        transpose_by(normed_low, grad_value_low),
    )
    summed = [
        lax.psum_scatter(part.astype(jnp.bfloat16), "ctx", scatter_dimension=0, tiled=True).astype(
            jnp.float32
        )
        for part in partial_sums
    ]
    w_down_grad, w_gate_grad, w_up_grad, w_out_grad = summed[:4]
    w_query_grad, w_key_grad, w_value_grad = summed[4:]
    attn_gain_grad, q_gain_grad, k_gain_grad, ffn_gain_grad = lax.psum(
        (attn_gain_part, q_gain_part, k_gain_part, ffn_gain_part), ("ctx", "wt")
    )
    return (
        output,
        tokens_grad,
        attn_gain_grad,
        w_query_grad,
        w_key_grad,
        w_value_grad,
        q_gain_grad,
        k_gain_grad,
        w_out_grad,
        ffn_gain_grad,
        w_gate_grad,
        w_up_grad,
        w_down_grad,
    )


def on_device(
    tokens,
    segments,
    attn_gain,
    w_query,
    key_matrix,
    value_matrix,
    q_gain,
    k_gain,
    w_out,
    ffn_gain,
    w_gate,
    w_up,
    w_down,
    cotangent,
):
    if not kernels_fit(tokens, w_query, key_matrix, q_gain):
        return on_device_plain(
            tokens,
            segments,
            attn_gain,
            w_query,
            key_matrix,
            value_matrix,
            q_gain,
            k_gain,
            w_out,
            ffn_gain,
            w_gate,
            w_up,
            w_down,
            cotangent,
        )
    sequences, seq_rows, model_width = tokens.shape
    count, head_dim = lax.axis_size("ctx"), q_gain.shape[0]
    token_rows = tokens.reshape(sequences * seq_rows, model_width)
    table = lax.dynamic_slice_in_dim(
        jnp.asarray(rotary_table(count * seq_rows, head_dim)),
        lax.axis_index("ctx") * seq_rows,
        seq_rows,
        0,
    )
    gains = (attn_gain[None], q_gain[None], k_gain[None])
    (
        residual,
        heads,
        mixed_t,
        query_t,
        logs,
        starts,
        keys_values,
        keys_t,
        query_raw,
        key_raw,
        normed_t,
        grad_residual,
        cot_t,
        normed_ffn_t,
        ffn_grads,
        ffn_gain_part,
        mlp_part,
        ring_state,
    ) = forward(
        token_rows,
        segments,
        table,
        *gains,
        w_query,
        key_matrix,
        value_matrix,
        w_out,
        cotangent.reshape(token_rows.shape),
        ffn_gain[None],
        w_gate,
        w_up,
        w_down,
    )
    (
        output_rows,
        tokens_grad,
        w_down_grad,
        w_gate_grad,
        w_up_grad,
        w_out_grad,
        w_query_grad,
        w_key_grad,
        w_value_grad,
        attn_gain_grad,
        ffn_gain_grad,
        q_gain_grad,
        k_gain_grad,
    ) = backward(
        grad_residual,
        token_rows,
        table,
        *gains,
        w_query,
        key_matrix,
        value_matrix,
        w_out,
        heads,
        mixed_t,
        query_t,
        logs,
        starts,
        keys_values,
        keys_t,
        query_raw,
        key_raw,
        normed_t,
        cot_t,
        normed_ffn_t,
        ffn_grads,
        ffn_gain_part,
        residual,
        mlp_part,
        ring_state,
    )
    return (
        output_rows.reshape(tokens.shape),
        tokens_grad.reshape(tokens.shape),
        attn_gain_grad[0],
        w_query_grad,
        w_key_grad,
        w_value_grad,
        q_gain_grad[0],
        k_gain_grad[0],
        w_out_grad,
        ffn_gain_grad[0],
        w_gate_grad,
        w_up_grad,
        w_down_grad,
    )


def solution(mesh):
    in_specs = (
        P(None, "ctx", None),
        P(None, "ctx"),
        P(),
        P(None, "wt"),
        P(None, "wt"),
        P(None, "wt"),
        P(),
        P(),
        P(None, "wt"),
        P(),
        P(None, "wt"),
        P(None, "wt"),
        P(None, "wt"),
        P(None, "ctx", None),
    )
    out_specs = (
        P(None, "ctx", None),
        P(None, "ctx", None),
        P(),
        P("ctx", "wt"),
        P("ctx", "wt"),
        P("ctx", "wt"),
        P(),
        P(),
        P("ctx", "wt"),
        P(),
        P("ctx", "wt"),
        P("ctx", "wt"),
        P("ctx", "wt"),
    )
    return jax.shard_map(
        on_device, mesh=mesh, in_specs=in_specs, out_specs=out_specs, check_vma=False
    )
```

```python
from functools import partial
import math

import jax
import jax.numpy as jnp
import numpy as np
from jax import lax
from jax.experimental import pallas as pl
from jax.experimental.pallas import tpu as pltpu
from jax.sharding import PartitionSpec as P

EPS = 1e-05
THETA = 1000000.0
NEG = -1e30


def product(left, right):
    return jnp.dot(left, right, preferred_element_type=jnp.float32)


def by_transpose(left, right):
    return lax.dot_general(
        left, right, (((1,), (1,)), ((), ())), preferred_element_type=jnp.float32
    )


def transpose_by(left, right):
    return lax.dot_general(
        left, right, (((0,), (0,)), ((), ())), preferred_element_type=jnp.float32
    )


def norm_rows(values, gain):
    inverse = lax.rsqrt(jnp.mean(values * values, axis=-1, keepdims=True) + EPS)
    unit_rows = values * inverse
    return (unit_rows * gain, unit_rows, inverse)


def norm_back(grads, unit_rows, inverse, gain):
    scaled = grads * gain
    return inverse * (scaled - unit_rows * jnp.mean(scaled * unit_rows, axis=-1, keepdims=True))


def rotate(values, cosine_table, sine_table, direction):
    half_dim = values.shape[-1] // 2
    first_half = values[..., :half_dim]
    second_half = values[..., half_dim:]
    return jnp.concatenate(
        [
            first_half * cosine_table - direction * second_half * sine_table,
            second_half * cosine_table + direction * first_half * sine_table,
        ],
        axis=-1,
    )


def split_blocks(array, block_len):
    shaped = array.reshape(
        (array.shape[0], array.shape[1] // block_len, block_len) + array.shape[2:]
    )
    return jnp.moveaxis(shaped, 1, 0)


def attend_piece(folded, pieces, first_row, queries, query_places, query_segs, score_scale):
    key_piece, value_piece, seg_piece = pieces
    sequences, piece_rows = seg_piece.shape
    kv_local = queries.shape[2]
    head_dim = queries.shape[4]
    block_len = math.gcd(piece_rows, 512)
    key_blocks = split_blocks(
        key_piece.reshape(sequences, piece_rows, kv_local, head_dim), block_len
    )
    value_tiles = split_blocks(
        value_piece.reshape(sequences, piece_rows, kv_local, head_dim), block_len
    )
    seg_blocks = split_blocks(seg_piece, block_len)
    offsets = block_len * jnp.arange(piece_rows // block_len, dtype=jnp.int32)

    def attend_block_step(running, block_item):
        row_max, row_sum, weighted = running
        key_block, value_block, seg_block, offset = block_item
        key_places = offset + jnp.arange(block_len, dtype=jnp.int32)
        allowed = (key_places[None, None, :] <= query_places[None, :, None]) & (
            query_segs[:, :, None] == seg_block[:, None, :]
        )
        allowed = allowed[:, None, None]
        scores = (
            jnp.einsum("sqgrd,skgd->sgrqk", queries, key_block, preferred_element_type=jnp.float32)
            * score_scale
        )
        scores = jnp.where(allowed, scores, NEG)
        new_max = jnp.maximum(row_max, jnp.max(scores, axis=-1))
        weights = jnp.where(allowed, jnp.exp(scores - new_max[..., None]), 0.0)
        fading = jnp.exp(row_max - new_max)
        row_sum = row_sum * fading + jnp.sum(weights, axis=-1)
        fade_rows = jnp.transpose(fading, (0, 3, 1, 2))[..., None]
        weighted = weighted * fade_rows + jnp.einsum(
            "sgrqk,skgd->sqgrd",
            weights.astype(jnp.bfloat16),
            value_block,
            preferred_element_type=jnp.float32,
        )
        return ((new_max, row_sum, weighted), None)

    folded, unused = lax.scan(
        attend_block_step, folded, (key_blocks, value_tiles, seg_blocks, offsets)
    )
    return folded


def grad_piece(
    folded,
    pieces,
    first_row,
    queries,
    grad_heads,
    log_total,
    row_delta,
    query_places,
    query_segs,
    score_scale,
):
    key_piece, value_piece, seg_piece = pieces
    sequences, piece_rows = seg_piece.shape
    kv_local = queries.shape[2]
    head_dim = queries.shape[4]
    block_len = math.gcd(piece_rows, 512)
    key_blocks = split_blocks(
        key_piece.reshape(sequences, piece_rows, kv_local, head_dim), block_len
    )
    value_tiles = split_blocks(
        value_piece.reshape(sequences, piece_rows, kv_local, head_dim), block_len
    )
    seg_blocks = split_blocks(seg_piece, block_len)
    offsets = block_len * jnp.arange(piece_rows // block_len, dtype=jnp.int32)

    def grad_block_step(running, block_item):
        key_block, value_block, seg_block, offset = block_item
        key_places = offset + jnp.arange(block_len, dtype=jnp.int32)
        allowed = (key_places[None, None, :] <= query_places[None, :, None]) & (
            query_segs[:, :, None] == seg_block[:, None, :]
        )
        allowed = allowed[:, None, None]
        scores = (
            jnp.einsum("sqgrd,skgd->sgrqk", queries, key_block, preferred_element_type=jnp.float32)
            * score_scale
        )
        probs = jnp.where(allowed, jnp.exp(scores - log_total[..., None]), 0.0)
        grad_probs = jnp.einsum(
            "sqgrd,skgd->sgrqk", grad_heads, value_block, preferred_element_type=jnp.float32
        )
        grad_scores = (probs * (grad_probs - row_delta[..., None])).astype(jnp.bfloat16)
        running = running + jnp.einsum(
            "sgrqk,skgd->sqgrd", grad_scores, key_block, preferred_element_type=jnp.float32
        )
        grad_keys = jnp.einsum(
            "sgrqk,sqgrd->skgd", grad_scores, queries, preferred_element_type=jnp.float32
        )
        grad_values = jnp.einsum(
            "sgrqk,sqgrd->skgd",
            probs.astype(jnp.bfloat16),
            grad_heads,
            preferred_element_type=jnp.float32,
        )
        grads = jnp.stack([grad_keys, grad_values], axis=2).astype(jnp.bfloat16)
        return (running, grads)

    folded, grads = lax.scan(
        grad_block_step, folded, (key_blocks, value_tiles, seg_blocks, offsets)
    )
    return folded, jnp.moveaxis(grads, 0, 1).reshape((sequences, piece_rows) + grads.shape[3:])


MESH = pl.DeviceIdType.MESH
MIB = 1 << 20


def ring_place(index, count):
    return lax.select(
        lax.rem(index, 2) == 0, lax.div(index, 2), count - 1 - lax.div(index, 2)
    )


def ring_index(place, count):
    place = lax.rem(place + 2 * count, count)
    return lax.select(
        place < lax.div(count, 2), 2 * place, 2 * (count - 1 - place) + 1
    )


class Ring:
    def __init__(self, count, slots, send_sems, recv_sems, base=0):
        self.count, self.slots, self.base = count, slots, base
        self.send_sems, self.recv_sems = send_sems, recv_sems
        self.other = lax.axis_index("wt")
        self.place = ring_place(lax.axis_index("ctx"), count)
        self.right = ring_index(self.place + 1, count)
        self.left = ring_index(self.place + count - 1, count)
        self.half = slots.shape[2] // 2

    def copy(self, which, step, way):
        rows = pl.ds(way * self.half, self.half)
        slot = step - self.base
        return pltpu.make_async_remote_copy(
            src_ref=self.slots.at[which, slot, rows],
            dst_ref=self.slots.at[which, slot + 1, rows],
            send_sem=self.send_sems.at[which, slot, way],
            recv_sem=self.recv_sems.at[which, slot, way],
            device_id=((self.right, self.left)[way], self.other),
            device_id_type=MESH,
        )

    def arrived(self, which, step):
        for way in range(2):
            self.copy(which, step - 1, way).wait_recv()

    def tick(
        self,
        which,
        step,
        left_ref,
        right_ref,
        first=False,
        given=None,
        result=None,
        final=True,
    ):
        half = self.half
        rows = [
            ring_index(target, self.count) * (2 * half) + way * half
            for way, target in enumerate(
                (self.place + self.count - 1 - step, self.place + 1 + step)
            )
        ]
        left = jnp.concatenate(
            [left_ref[pl.ds(pl.multiple_of(row, half), half), :] for row in rows], axis=0
        )
        total = jnp.dot(left, right_ref[...], preferred_element_type=jnp.float32)
        if given is not None:
            total = total + given[...].astype(jnp.float32)
        elif not first:
            self.arrived(which, step)
            total = total + self.slots[which, step - self.base].astype(jnp.float32)
        def pass_on():
            self.slots[which, step - self.base] = total.astype(jnp.bfloat16)
            for way in range(2):
                self.copy(which, step, way).start()

        def keep():
            result[...] = total

        if result is None:
            pass_on()
        elif final is True:
            keep()
        else:
            pl.when(final)(keep)
            pl.when(jnp.logical_not(final))(pass_on)

    def finish(self, which, end):
        for way in range(2):

            def wait(step, carry):
                self.copy(which, step, way).wait_send()
                return carry

            lax.fori_loop(self.base, end, wait, 0)


def pair_lanes(shape):
    return lax.broadcasted_iota(jnp.int32, shape, 1)


def swap_halves(values, head_dim):
    lanes = pair_lanes(values.shape)
    width = values.shape[1]
    quarter = head_dim // 2
    return jnp.where(
        lax.rem(lanes, head_dim) < quarter,
        pltpu.roll(values, width - quarter, 1),
        pltpu.roll(values, quarter, 1),
    )


def pair_mean(values, head_dim):
    low = pair_lanes(values.shape) < head_dim
    first = jnp.sum(jnp.where(low, values, 0.0), axis=-1, keepdims=True)
    second = jnp.sum(jnp.where(low, 0.0, values), axis=-1, keepdims=True)
    return jnp.where(low, first, second) * (1.0 / head_dim)


def pair_norm(values, head_dim):
    inverse = lax.rsqrt(pair_mean(values * values, head_dim) + EPS)
    return values * inverse, inverse


def as_row(ref):
    return ref[...].astype(jnp.float32).reshape(1, -1)


def double(row):
    return jnp.concatenate([row, row], axis=-1)


def dot_nn(left, right):
    return jnp.dot(left, right, preferred_element_type=jnp.float32)


def dot_nt(left, right):
    return lax.dot_general(
        left, right, (((1,), (1,)), ((), ())), preferred_element_type=jnp.float32
    )


def as_column(row):
    size = row.shape[1]
    rows = lax.broadcasted_iota(jnp.int32, (size, size), 0)
    lanes = lax.broadcasted_iota(jnp.int32, (size, size), 1)
    return jnp.sum(jnp.where(rows == lanes, row, 0.0), axis=1, keepdims=True)


class Place:
    def __init__(self, count):
        self.count = count
        self.ctx, self.wt = lax.axis_index("ctx"), lax.axis_index("wt")
        self.odd = lax.rem(self.ctx, 2)
        self.level = lax.div(self.ctx, 2)
        self.core_bit = lax.rem(self.wt, 2)
        self.beside_ctx = self.ctx + 1 - 2 * self.odd
        self.beside = (self.beside_ctx, self.wt)
        self.above = (lax.rem(self.ctx + 2, count), self.wt)
        self.below = (lax.rem(self.ctx + count - 2, count), self.wt)
        self.has_above = self.ctx + 2 < count
        self.has_below = self.ctx >= 2
        self.core_wt = self.wt + 1 - 2 * self.core_bit
        self.chip_wt = lax.rem(self.wt + 2, 4)
        self.far_wt = lax.rem(self.core_wt + 2, 4)
        self.core = (self.ctx, self.core_wt)
        self.chip = (self.ctx, self.chip_wt)

    def signal(self, peer):
        pl.semaphore_signal(
            pltpu.get_barrier_semaphore(), inc=1, device_id=peer, device_id_type=MESH
        )

    def signal_near(self):
        for peer in (self.beside, self.core, self.chip):
            self.signal(peer)
        for there, peer in ((self.has_above, self.above), (self.has_below, self.below)):

            @pl.when(there)
            def _():
                self.signal(peer)

    def await_near(self):
        edges = self.has_above.astype(jnp.int32) + self.has_below.astype(jnp.int32)
        pl.semaphore_wait(pltpu.get_barrier_semaphore(), 3 + edges)

    def signal_all(self):
        for shift in range(1, self.count):
            self.signal((lax.rem(self.ctx + shift, self.count), self.wt))
        self.signal(self.core)
        self.signal(self.chip)

    def await_all(self):
        pl.semaphore_wait(pltpu.get_barrier_semaphore(), self.count + 1)


def send_to(source, target, send_sem, recv_sem, device):
    return pltpu.make_async_remote_copy(
        src_ref=source,
        dst_ref=target,
        send_sem=send_sem,
        recv_sem=recv_sem,
        device_id=device,
        device_id_type=MESH,
    )


class WtSum:
    def __init__(self, here, tile, part, got, far, full, send_sems, recv_sems):
        self.here, self.tile = here, tile
        self.part, self.got, self.far, self.full = part, got, far, full
        self.send_sems, self.recv_sems = send_sems, recv_sems
        self.mine, self.theirs = here.core_bit, 1 - here.core_bit

    def rows(self, seq):
        return pl.ds(pl.multiple_of(seq * self.tile, self.tile), self.tile)

    def copy(self, hop, seq, arriving=False):
        rows = self.rows(seq)
        half = self.theirs if arriving else self.mine
        source = (
            self.part.at[self.theirs, rows],
            self.got.at[rows],
            self.full.at[half, rows],
        )[hop]
        target = (self.got.at[rows], self.far.at[rows], self.full.at[half, rows])[hop]
        device = self.here.chip if hop == 1 else self.here.core
        return send_to(
            source, target, self.send_sems.at[hop, seq], self.recv_sems.at[hop, seq], device
        )

    def offer(self, seq, value):
        rows = self.rows(seq)
        half = value.shape[1] // 2
        self.part[0, rows] = value[:, :half].astype(jnp.bfloat16)
        self.part[1, rows] = value[:, half:].astype(jnp.bfloat16)
        self.copy(0, seq).start()

    def cross(self, seq):
        rows = self.rows(seq)
        self.copy(0, seq).wait_recv()
        total = self.part[self.mine, rows].astype(jnp.float32) + self.got[rows].astype(
            jnp.float32
        )
        self.got[rows] = total.astype(jnp.bfloat16)
        self.copy(1, seq).start()

    def close(self, seq):
        rows = self.rows(seq)
        self.copy(1, seq).wait_recv()
        total = self.got[rows].astype(jnp.float32) + self.far[rows].astype(jnp.float32)
        self.full[self.mine, rows] = total.astype(jnp.bfloat16)
        self.copy(2, seq).start()

    def result(self, seq):
        rows = self.rows(seq)
        self.copy(2, seq, True).wait_recv()
        return jnp.concatenate([self.full[0, rows], self.full[1, rows]], axis=1).astype(
            jnp.float32
        )

    def finish(self, sequences):
        def sent(seq, carry):
            for hop in range(3):
                self.copy(hop, seq).wait_send()
            return carry

        lax.fori_loop(0, sequences, sent, 0)


def wt_sum_scratch(sequences, rows, width):
    half = width // 2
    return [
        pltpu.VMEM((2, rows, half), jnp.bfloat16),
        pltpu.VMEM((rows, half), jnp.bfloat16),
        pltpu.VMEM((rows, half), jnp.bfloat16),
        pltpu.VMEM((2, rows, half), jnp.bfloat16),
        pltpu.SemaphoreType.DMA((3, sequences)),
        pltpu.SemaphoreType.DMA((3, sequences)),
    ]


def ring_scratch(count, arrays, rows, width):
    return [
        pltpu.VMEM((arrays, count, rows, width), jnp.bfloat16),
        pltpu.SemaphoreType.DMA((arrays, count - 1, 2)),
        pltpu.SemaphoreType.DMA((arrays, count - 1, 2)),
    ]


class GainSum:
    def __init__(self, here, slots, beside, sends, recvs, pair_sends, pair_recvs):
        self.here, self.slots, self.beside = here, slots, beside
        self.sends, self.recvs = sends, recvs
        self.pair_sends, self.pair_recvs = pair_sends, pair_recvs

    def copy(self, shift, arriving=False):
        here = self.here
        target = lax.rem(here.ctx + shift, here.count)
        origin = lax.rem(here.ctx + here.count - shift, here.count)
        ref = self.slots.at[origin if arriving else here.ctx]
        return send_to(
            ref, ref, self.sends.at[shift - 1], self.recvs.at[shift - 1], (target, here.wt)
        )

    def pair_copy(self, hop):
        device = (self.here.core, self.here.chip)[hop]
        return send_to(
            self.beside.at[hop, 0],
            self.beside.at[hop, 1],
            self.pair_sends.at[hop],
            self.pair_recvs.at[hop],
            device,
        )

    def start(self):
        for shift in range(1, self.here.count):
            self.copy(shift).start()

    def total(self):
        for shift in range(1, self.here.count):
            self.copy(shift, True).wait_recv()
        total = self.slots[0]
        for index in range(1, self.here.count):
            total = total + self.slots[index]
        for hop in range(2):
            self.beside[hop, 0] = total
            self.pair_copy(hop).start()
            self.pair_copy(hop).wait_recv()
            total = total + self.beside[hop, 1]
        for shift in range(1, self.here.count):
            self.copy(shift).wait_send()
        for hop in range(2):
            self.pair_copy(hop).wait_send()
        return total


class Mover:
    def __init__(self, pairs, sems):
        self.copies = [
            pltpu.make_async_copy(source, target, sems.at[i])
            for i, (source, target) in enumerate(pairs)
        ]

    def start(self, *which):
        for i in which:
            self.copies[i].start()

    def wait(self, *which):
        for i in which:
            self.copies[i].wait()


def forward_kernel(count, names, *refs):
    ref = dict(zip(names, refs, strict=True))
    tokens, segments = ref["tokens"], ref["segments"]
    residual, mixed_t, query_t = ref["residual"], ref["mixed_t"], ref["query_t"]
    logs, starts, keys_values = ref["logs"], ref["starts"], ref["keys_values"]
    keys_t, query_raw, key_raw = ref["keys_t"], ref["query_raw"], ref["key_raw"]
    normed_t, grad_res, lefts = ref["normed_t"], ref["grad_res"], ref["lefts"]
    ffn_grads, ffn_gain_part = ref["ffn_grads"], ref["ffn_gain_part"]
    ring_state = ref["ring_state"]
    all_segs, all_out, all_heads = ref["all_segs"], ref["all_out"], ref["all_heads"]
    acc, row_sum = ref["acc"], ref["row_sum"]
    w_gate, w_up, w_down = ref["w_gate"], ref["w_up"], ref["w_down"]
    gate_t, up_t, grad_hidden = ref["gate_t"], ref["up_t"], ref["grad_hidden"]
    cotangent, table = ref["cotangent"], ref["table"]
    sequences, tile = segments.shape
    head_dim = ref["q_gain"].shape[0]
    pair = 2 * head_dim
    levels = count // 2
    here = Place(count)
    me = here.ctx
    loads = Mover(
        [
            (ref["table_in"].at[pl.ds(pl.multiple_of(me * tile, tile), tile)], table),
            (ref["cotangent_in"], cotangent),
            (ref["w_down_in"], w_down),
            (ref["w_gate_in"], w_gate),
            (ref["w_up_in"], w_up),
        ],
        ref["load_sems"],
    )
    loads.start(0, 1, 2, 3, 4)
    stores = Mover(
        [
            (all_heads.at[here.wt] if name == "heads" else ref[name], ref[name + "_out"])
            for name in STORED
        ],
        ref["store_sems"],
    )
    wt_sum = WtSum(here, tile, *(ref[f"wt_sum{i}"] for i in range(6)))
    ffn = Ring(count, *(ref[f"ring{i}"] for i in range(3)))
    here.signal_near()
    all_segs[me] = jnp.zeros_like(all_segs[me])
    all_segs[me, pl.ds(0, sequences)] = segments[...]
    all_out[here.wt] = ref["w_out"][...].T

    def out_copy(hop, arriving=False):
        sent = (here.wt, here.wt, here.chip_wt)
        landed = (here.chip_wt, here.core_wt, here.far_wt)
        part = all_out.at[(landed if arriving else sent)[hop]]
        device = here.chip if hop == 0 else here.core
        return send_to(part, part, ref["out_send"].at[hop], ref["out_recv"].at[hop], device)

    def rows_of(seq):
        return pl.ds(pl.multiple_of(seq * tile, tile), tile)

    def block_of(index, step):
        return lax.rem(index - 2 * step + 2 * count, count)

    def up_copy(step, seq, sems=None):
        rows = keys_values.at[block_of(me, step), rows_of(seq)]
        index = step if sems is None else sems
        return send_to(
            rows, rows, ref["up_send"].at[index, seq], ref["up_recv"].at[index, seq], here.above
        )

    def side_copy(step, seq, index=me):
        rows = keys_values.at[block_of(index, step), rows_of(seq)]
        return send_to(
            rows, rows, ref["side_send"].at[step, seq], ref["side_recv"].at[step, seq], here.beside
        )

    def seg_copy(step, way, index=me, sems=None):
        part = all_segs.at[block_of(index, step)]
        device = here.beside if way else here.above
        at = step if sems is None else sems
        return send_to(
            part, part, ref["seg_send"].at[at, way], ref["seg_recv"].at[at, way], device
        )

    def goes_up(step):
        return here.has_above & (me >= 2 * step)

    def goes_aside(step):
        block = me - 2 * step
        return (block >= 0) & (block < here.beside_ctx)

    def comes_aside(step):
        block = here.beside_ctx - 2 * step
        return (block >= 0) & (block < me)

    def pass_segs(step):
        @pl.when(goes_up(step))
        def _():
            seg_copy(step, 0).start()

        @pl.when(goes_aside(step))
        def _():
            seg_copy(step, 1).start()

    def pass_rows(step, seq):
        @pl.when(goes_up(step))
        def _():
            up_copy(step, seq).start()

        @pl.when(goes_aside(step))
        def _():
            side_copy(step, seq).start()

    gain = as_row(ref["attn_gain"])
    q_gain_pair = double(as_row(ref["q_gain"]))
    k_gain_pair = double(as_row(ref["k_gain"]))
    ffn_gain_row = as_row(ref["ffn_gain"])
    loads.wait(0)

    def turn(values):
        cosine = table[:, pl.ds(0, pair)]
        sine = table[:, pl.ds(pair, pair)]
        return values * cosine + swap_halves(values, head_dim) * sine

    def project(seq, carry):
        rows = rows_of(seq)
        inputs = tokens[rows, :].astype(jnp.float32)
        inverse = lax.rsqrt(jnp.mean(inputs * inputs, axis=-1, keepdims=True) + EPS)
        normed = (inputs * inverse * gain).astype(jnp.bfloat16)
        raw_k = dot_nn(normed, ref["w_key"][...])
        key_raw[rows, :] = raw_k
        unit, unused = pair_norm(raw_k, head_dim)
        keys_values[me, rows, pl.ds(0, pair)] = turn(unit * k_gain_pair).astype(jnp.bfloat16)
        keys_values[me, rows, pl.ds(pair, pair)] = dot_nn(normed, ref["w_value"][...]).astype(
            jnp.bfloat16
        )

        @pl.when(seq == 0)
        def _():
            here.await_near()
            pass_segs(0)

        @pl.when(seq < 2)
        def _():
            pass_rows(0, seq)

        @pl.when(seq == 0)
        def _():
            out_copy(0).start()
            out_copy(1).start()

        raw_q = dot_nn(normed, ref["w_query"][...])
        query_raw[rows, :] = raw_q
        query_t[seq] = jnp.zeros_like(query_t[seq])
        for group in range(2):
            unit, unused = pair_norm(raw_q[:, group * pair : (group + 1) * pair], head_dim)
            turned = turn(unit * q_gain_pair) * (head_dim**-0.5)
            flipped = turned.T.astype(jnp.bfloat16)
            for member in range(2):
                query_t[
                    seq,
                    pl.ds(group * head_dim, head_dim),
                    pl.ds((2 * group + member) * tile, tile),
                ] = flipped[member * head_dim : (member + 1) * head_dim]
        normed_t[:, rows] = normed.T
        acc[seq] = jnp.zeros_like(acc[seq])
        row_sum[seq] = jnp.zeros_like(row_sum[seq])
        starts[seq] = jnp.zeros_like(starts[seq])
        return carry

    lax.fori_loop(0, sequences, project, 0)
    loads.wait(1, 2)

    def back_down(seq, carry):
        rows = rows_of(seq)
        grads = cotangent[rows, :]
        lefts[0, :, rows] = grads.T
        grad_hidden[rows, :] = dot_nn(grads, w_down[...]).astype(jnp.bfloat16)
        return carry

    lax.fori_loop(0, sequences, back_down, 0)

    def route(seq):
        def level(step, carry):
            @pl.when(me >= 2 * step)
            def _():
                @pl.when(seq == 0)
                def _():
                    seg_copy(step, 0, me, step - 1).wait_recv()
                    pass_segs(step)

                up_copy(step, seq, step - 1).wait_recv()
                pass_rows(step, seq)

            return carry

        lax.fori_loop(1, levels, level, 0)

    route(0)
    loads.wait(3, 4)

    def flip(index, carry):
        rows = pl.ds(pl.multiple_of(index * 128, 128), 128)
        gate_t[:, rows] = w_gate[rows, :].T
        up_t[:, rows] = w_up[rows, :].T
        return carry

    lax.fori_loop(0, tokens.shape[1] // 128, flip, 0)
    key_rows = lax.broadcasted_iota(jnp.int32, (tile, 4 * tile), 0)
    query_cols = lax.rem(lax.broadcasted_iota(jnp.int32, (tile, 4 * tile), 1), tile)

    def attend(block, seq, own):
        rows = rows_of(seq)
        keys = keys_values[block, rows, pl.ds(0, pair)]
        values = keys_values[block, rows, pl.ds(pair, pair)]
        seg_query = all_segs[me, pl.ds(seq, 1)].astype(jnp.float32)
        seg_key = as_column(all_segs[block, pl.ds(seq, 1)].astype(jnp.float32))
        earlier = jnp.where(seg_key < seg_query, 1.0, 0.0)
        starts[seq] += jnp.sum(earlier, axis=0, keepdims=True)
        seg_wide = jnp.concatenate([seg_query] * 4, axis=1)
        if own:
            allowed = (seg_key == seg_wide) & (key_rows <= query_cols)
        else:
            allowed = seg_key >= seg_wide
        scores = dot_nn(keys, query_t[seq])
        weights = jnp.where(allowed, jnp.exp(scores), 0.0)
        row_sum[seq] += jnp.sum(weights, axis=0, keepdims=True)
        low = weights.astype(jnp.bfloat16)
        values_t = values.T
        for group in range(2):
            acc[seq, group] += dot_nn(
                values_t[group * head_dim : (group + 1) * head_dim],
                low[:, group * 2 * tile : (group + 1) * 2 * tile],
            )
        keys_t[block, seq] = keys.T

    def head_copy(hop, seq, arriving=False):
        sent = (here.wt, here.wt, here.chip_wt)
        landed = (here.chip_wt, here.core_wt, here.far_wt)
        part = all_heads.at[(landed if arriving else sent)[hop], rows_of(seq)]
        device = here.chip if hop == 0 else here.core
        return send_to(
            part, part, ref["head_send"].at[hop, seq], ref["head_recv"].at[hop, seq], device
        )

    def relay(seq):
        head_copy(0, seq, True).wait_recv()
        head_copy(2, seq).start()

    def mix(seq):
        rows = rows_of(seq)
        total = row_sum[seq]
        logs[seq] = jnp.log(total)
        for group in range(2):
            cols = slice(group * 2 * tile, (group + 1) * 2 * tile)
            part = acc[seq, group] / total[:, cols]
            mixed = jnp.concatenate([part[:, :tile], part[:, tile:]], axis=0)
            mixed_t[seq, group] = mixed
            all_heads[here.wt, rows, pl.ds(group * pair, pair)] = mixed.T.astype(jnp.bfloat16)
        head_copy(0, seq).start()
        head_copy(1, seq).start()

    def ffn_unit(rows):
        values = residual[rows, :]
        inverse = lax.rsqrt(jnp.mean(values * values, axis=-1, keepdims=True) + EPS)
        return values * inverse, inverse

    def feed(seq):
        rows = rows_of(seq)
        head_copy(1, seq, True).wait_recv()
        head_copy(2, seq, True).wait_recv()
        total = tokens[rows, :].astype(jnp.float32)
        for slot in range(4):
            total = total + dot_nn(all_heads[slot, rows], all_out[slot])
        residual[rows, :] = total
        unit, unused = ffn_unit(rows)
        normed = (unit * ffn_gain_row).astype(jnp.bfloat16)
        lefts[1, :, rows] = normed.T
        gate = dot_nn(normed, w_gate[...])
        up = dot_nn(normed, w_up[...])
        sigmoid = jax.nn.sigmoid(gate)
        silu = gate * sigmoid
        ffn_grads[0, rows] = (silu * up).astype(jnp.bfloat16)
        grads = grad_hidden[rows, :].astype(jnp.float32)
        grad_gate = (grads * up * sigmoid * (1.0 + gate * (1.0 - sigmoid))).astype(jnp.bfloat16)
        grad_up = (grads * silu).astype(jnp.bfloat16)
        ffn_grads[1, rows] = grad_gate
        ffn_grads[2, rows] = grad_up
        grad_normed = dot_nn(grad_gate, gate_t[...]) + dot_nn(grad_up, up_t[...])
        ffn_gain_part[...] += jnp.sum(grad_normed * unit, axis=0, keepdims=True)
        wt_sum.offer(seq, grad_normed)

    ffn_gain_part[...] = jnp.zeros_like(ffn_gain_part)

    def sequence_turn(turn_, carry):
        @pl.when(turn_ < sequences)
        def _():
            attend(me, turn_, True)

            @pl.when(turn_ + 2 < sequences)
            def _():
                pass_rows(0, turn_ + 2)

            @pl.when(comes_aside(0))
            def _():
                @pl.when(turn_ == 0)
                def _():
                    seg_copy(0, 1, here.beside_ctx).wait_recv()

                side_copy(0, turn_, here.beside_ctx).wait_recv()
                attend(here.beside_ctx, turn_, False)

        @pl.when(turn_ + 1 < sequences)
        def _():
            route(turn_ + 1)

        @pl.when(turn_ == 1)
        def _():
            out_copy(0, True).wait_recv()
            out_copy(2).start()

        @pl.when(turn_ > 0)
        def _():
            relay(turn_ - 1)

        @pl.when(turn_ < sequences)
        def _():
            def level(step, carry):
                @pl.when(me >= 2 * step)
                def _():
                    @pl.when(turn_ == 0)
                    def _():
                        seg_copy(step, 1, here.beside_ctx).wait_recv()

                    attend(block_of(me, step), turn_, False)
                    side_copy(step, turn_, here.beside_ctx).wait_recv()
                    attend(block_of(here.beside_ctx, step), turn_, False)

                return carry

            lax.fori_loop(1, levels, level, 0)
            mix(turn_)

        @pl.when(turn_ == 1)
        def _():
            out_copy(1, True).wait_recv()
            out_copy(2, True).wait_recv()

        @pl.when(turn_ > 1)
        def _():
            wt_sum.cross(turn_ - 2)

        @pl.when(turn_ > 0)
        def _():
            feed(turn_ - 1)

        @pl.when(turn_ > 2)
        def _():
            wt_sum.close(turn_ - 3)

        return carry

    lax.fori_loop(0, sequences + 1, sequence_turn, 0)
    for i in range(3):
        ffn.tick(i, 0, lefts.at[min(i, 1)], ffn_grads.at[i], first=True)
    stores.start(*range(len(STORED) - 2))
    wt_sum.cross(sequences - 1)
    wt_sum.close(sequences - 2)

    def back_norm(seq):
        rows = rows_of(seq)
        unit, inverse = ffn_unit(rows)
        scaled = wt_sum.result(seq) * ffn_gain_row
        grads = inverse * (scaled - unit * jnp.mean(scaled * unit, axis=-1, keepdims=True))
        grad_res[rows, :] = (cotangent[rows, :].astype(jnp.float32) + grads).astype(jnp.bfloat16)

    def back_turn(seq, carry):
        back_norm(seq)
        return carry

    lax.fori_loop(0, sequences - 1, back_turn, 0)
    wt_sum.close(sequences - 1)
    back_norm(sequences - 1)
    stores.start(len(STORED) - 2)
    for i in range(3):
        ffn.arrived(i, 1)
        ring_state[i] = ffn.slots[i, 1]
    stores.start(len(STORED) - 1)
    for i in range(3):
        ffn.finish(i, 1)
    wt_sum.finish(sequences)
    for hop in range(3):
        out_copy(hop).wait_send()

        def sent(seq, carry):
            head_copy(hop, seq).wait_send()
            return carry

        lax.fori_loop(0, sequences, sent, 0)

    def drain(step, carry):
        @pl.when(goes_up(step))
        def _():
            seg_copy(step, 0).wait_send()

            def sent(seq, carry):
                up_copy(step, seq).wait_send()
                return carry

            lax.fori_loop(0, sequences, sent, 0)

        @pl.when(goes_aside(step))
        def _():
            seg_copy(step, 1).wait_send()

            def sent(seq, carry):
                side_copy(step, seq).wait_send()
                return carry

            lax.fori_loop(0, sequences, sent, 0)

        return carry

    lax.fori_loop(0, levels, drain, 0)
    stores.wait(*range(len(STORED)))


STORED = (
    "heads",
    "residual",
    "mixed_t",
    "query_t",
    "logs",
    "starts",
    "keys_values",
    "keys_t",
    "query_raw",
    "key_raw",
    "normed_t",
    "lefts",
    "ffn_grads",
    "ffn_gain_part",
    "grad_res",
    "ring_state",
)


def forward(inputs):
    count = lax.axis_size("ctx")
    sequences, tile = inputs["segments"].shape
    rows, width = inputs["tokens"].shape
    head_dim = inputs["q_gain"].shape[0]
    hidden = inputs["w_gate_in"].shape[1]
    pair = 2 * head_dim
    levels = count // 2
    f32, bf16 = jnp.float32, jnp.bfloat16
    dma = pltpu.SemaphoreType.DMA
    stored = {
        "heads": ((rows, 2 * pair), bf16),
        "residual": ((rows, width), f32),
        "mixed_t": ((sequences, 2, pair, tile), f32),
        "query_t": ((sequences, pair, 4 * tile), bf16),
        "logs": ((sequences, 1, 4 * tile), f32),
        "starts": ((sequences, 1, tile), f32),
        "keys_values": ((count, rows, 2 * pair), bf16),
        "keys_t": ((count, sequences, pair, tile), bf16),
        "query_raw": ((rows, 2 * pair), f32),
        "key_raw": ((rows, pair), f32),
        "normed_t": ((width, rows), bf16),
        "lefts": ((2, width, rows), bf16),
        "ffn_grads": ((3, rows, hidden), bf16),
        "ffn_gain_part": ((1, width), f32),
        "grad_res": ((rows, width), bf16),
        "ring_state": ((3, width // count, hidden), bf16),
    }
    scratch = {name: pltpu.VMEM(*spec) for name, spec in stored.items() if name != "heads"}
    scratch |= {
        "all_segs": pltpu.VMEM((count, 8, tile), jnp.int32),
        "all_out": pltpu.VMEM((4, 2 * pair, width), bf16),
        "all_heads": pltpu.VMEM((4, rows, 2 * pair), bf16),
        "acc": pltpu.VMEM((sequences, 2, head_dim, 2 * tile), f32),
        "row_sum": pltpu.VMEM((sequences, 1, 4 * tile), f32),
        "table": pltpu.VMEM((tile, 2 * pair), f32),
        "cotangent": pltpu.VMEM((rows, width), bf16),
        "w_down": pltpu.VMEM((width, hidden), bf16),
        "w_gate": pltpu.VMEM((width, hidden), bf16),
        "w_up": pltpu.VMEM((width, hidden), bf16),
        "gate_t": pltpu.VMEM((hidden, width), bf16),
        "up_t": pltpu.VMEM((hidden, width), bf16),
        "grad_hidden": pltpu.VMEM((rows, hidden), bf16),
        "up_send": dma((levels, sequences)),
        "up_recv": dma((levels, sequences)),
        "side_send": dma((levels, sequences)),
        "side_recv": dma((levels, sequences)),
        "seg_send": dma((levels, 2)),
        "seg_recv": dma((levels, 2)),
        "out_send": dma((3,)),
        "out_recv": dma((3,)),
        "head_send": dma((3, sequences)),
        "head_recv": dma((3, sequences)),
        "load_sems": dma((5,)),
        "store_sems": dma((len(STORED),)),
    }
    for i, kind in enumerate(wt_sum_scratch(sequences, rows, width)):
        scratch[f"wt_sum{i}"] = kind
    for i, kind in enumerate(ring_scratch(2, 3, width // count, hidden)):
        scratch[f"ring{i}"] = kind
    vmem, anywhere = pl.BlockSpec(memory_space=pltpu.VMEM), pl.BlockSpec(memory_space=pl.ANY)
    names = (*inputs, *(name + "_out" for name in STORED), *scratch)
    results = pl.pallas_call(
        partial(forward_kernel, count, names),
        out_shape=[jax.ShapeDtypeStruct(*stored[name]) for name in STORED],
        in_specs=[anywhere if name.endswith("_in") else vmem for name in inputs],
        out_specs=[anywhere] * len(STORED),
        scratch_shapes=list(scratch.values()),
        compiler_params=pltpu.CompilerParams(
            collective_id=2, has_side_effects=True, vmem_limit_bytes=62 * MIB
        ),
    )(*inputs.values())
    return dict(zip(STORED, results, strict=True))


LOADED = (
    "ring_state",
    "lefts",
    "ffn_grads",
    "grad_res",
    "w_out",
    "mixed_t",
    "query_t",
    "logs",
    "starts",
    "keys_values",
    "keys_t",
    "w_down",
    "heads",
    "residual",
    "table",
    "query_raw",
    "key_raw",
    "w_query",
    "w_key",
    "w_value",
    "tokens",
    "normed_t",
)
RESULTS = (
    "output",
    "tokens_grad",
    "w_down_sum",
    "w_gate_sum",
    "w_up_sum",
    "w_out_sum",
    "w_query_sum",
    "w_key_sum",
    "w_value_sum",
    "attn_gain_sum",
    "ffn_gain_sum",
    "q_gain_sum",
    "k_gain_sum",
)


def backward_kernel(count, names, *refs):
    ref = dict(zip(names, refs, strict=True))
    residual, mixed_t, query_t = ref["residual"], ref["mixed_t"], ref["query_t"]
    logs, starts, keys_values = ref["logs"], ref["starts"], ref["keys_values"]
    keys_t, query_raw, key_raw = ref["keys_t"], ref["query_raw"], ref["key_raw"]
    normed_t, grad_res, lefts = ref["normed_t"], ref["grad_res"], ref["lefts"]
    ffn_grads, ring_state, heads = ref["ffn_grads"], ref["ring_state"], ref["heads"]
    tokens, table = ref["tokens"], ref["table"]
    grad_res_t, grad_heads_t = ref["grad_res_t"], ref["grad_heads_t"]
    deltas, grad_query_t = ref["deltas"], ref["grad_query_t"]
    own_grads, grad_qkv = ref["own_grads"], ref["grad_qkv"]
    side_in, side_out = ref["side_in"], ref["side_out"]
    line_in, line_out = ref["line_in"], ref["line_out"]
    ffn_sums, qkv_total = ref["ffn_sums"], ref["qkv_total"]
    sequences, tile = mixed_t.shape[0], mixed_t.shape[3]
    head_dim = ref["q_gain"].shape[0]
    pair = 2 * head_dim
    levels = count // 2
    last = count - 1
    here = Place(count)
    me = here.ctx
    loads = Mover(
        [
            (
                ref["table_in"].at[pl.ds(pl.multiple_of(me * tile, tile), tile)]
                if name == "table"
                else ref[name + "_in"],
                ref[name],
            )
            for name in LOADED
        ],
        ref["load_sems"],
    )
    loads.start(*range(len(LOADED)))
    sources = {
        "w_down_sum": ffn_sums.at[0],
        "w_gate_sum": ffn_sums.at[1],
        "w_up_sum": ffn_sums.at[2],
        "w_query_sum": qkv_total.at[:, pl.ds(0, 2 * pair)],
        "w_key_sum": qkv_total.at[:, pl.ds(2 * pair, pair)],
        "w_value_sum": qkv_total.at[:, pl.ds(3 * pair, pair)],
    }
    stores = Mover(
        [(sources[name] if name in sources else ref[name], ref[name + "_res"]) for name in RESULTS],
        ref["store_sems"],
    )
    wt_sum = WtSum(here, tile, *(ref[f"wt_sum{i}"] for i in range(6)))
    mlp_sum = WtSum(here, tile, *(ref[f"mlp_sum{i}"] for i in range(6)))
    gains = GainSum(here, *(ref[f"gains{i}"] for i in range(6)))
    gain_slots = ref["gains0"]
    ffn = Ring(count, *(ref[f"ffn{i}"] for i in range(3)), base=1)
    out = Ring(count, *(ref[f"out{i}"] for i in range(3)))
    qkv = Ring(count, *(ref[f"qkv{i}"] for i in range(3)))
    here.signal_all()
    loads.wait(0, 1, 2)
    here.await_all()
    for i in range(3):
        ffn.tick(i, 1, lefts.at[min(i, 1)], ffn_grads.at[i], given=ring_state.at[i])

    def ffn_tick(index):
        step, which = lax.div(index, 3), lax.rem(index, 3)
        ffn.tick(
            which,
            step,
            lefts.at[lax.min(which, 1)],
            ffn_grads.at[which],
            result=ffn_sums.at[which],
            final=step == last,
        )

    def rows_of(seq):
        return pl.ds(pl.multiple_of(seq * tile, tile), tile)

    def prepare(seq):
        rows = rows_of(seq)
        grads = grad_res[rows, :]
        grad_res_t[:, rows] = grads.T
        grad_heads_t[seq] = jnp.zeros_like(grad_heads_t[seq])
        low = dot_nn(grads, ref["w_out"][...]).astype(jnp.bfloat16)
        for group in range(2):
            flipped = low[:, group * pair : (group + 1) * pair].T
            product_t = flipped.astype(jnp.float32) * mixed_t[seq, group]
            for member in range(2):
                part = slice(member * head_dim, (member + 1) * head_dim)
                cols = pl.ds((2 * group + member) * tile, tile)
                grad_heads_t[seq, pl.ds(group * head_dim, head_dim), cols] = flipped[part]
                deltas[seq, :, cols] = jnp.sum(product_t[part], axis=0, keepdims=True)
        grad_query_t[seq] = jnp.zeros_like(grad_query_t[seq])

    key_rows = lax.broadcasted_iota(jnp.int32, (tile, 4 * tile), 0)
    query_cols = lax.rem(lax.broadcasted_iota(jnp.int32, (tile, 4 * tile), 1), tile)

    def grads_of(block, seq, own):
        rows = rows_of(seq)
        keys = keys_values[block, rows, pl.ds(0, pair)]
        values = keys_values[block, rows, pl.ds(pair, pair)]
        places = (key_rows + block * tile).astype(jnp.float32)
        start = starts[seq]
        allowed = places >= jnp.concatenate([start] * 4, axis=1)
        if own:
            allowed = allowed & (key_rows <= query_cols)
        queries = query_t[seq]
        grad_heads = grad_heads_t[seq]
        scores = dot_nn(keys, queries)
        probs = jnp.where(allowed, jnp.exp(scores - logs[seq]), 0.0)
        grad_probs = dot_nn(values, grad_heads)
        grad_scores = (probs * (grad_probs - deltas[seq])).astype(jnp.bfloat16)
        flipped = keys_t[block, seq]
        for group in range(2):
            cols = slice(group * 2 * tile, (group + 1) * 2 * tile)
            grad_query_t[seq, group] += dot_nn(
                flipped[group * head_dim : (group + 1) * head_dim], grad_scores[:, cols]
            )
        grad_keys = dot_nt(grad_scores, queries)
        grad_values = dot_nt(probs.astype(jnp.bfloat16), grad_heads)
        return jnp.concatenate([grad_keys, grad_values], axis=1)

    def side_copy(step, seq):
        return send_to(
            side_out.at[step, rows_of(seq)],
            side_in.at[step, rows_of(seq)],
            ref["side_send"].at[step, seq],
            ref["side_recv"].at[step, seq],
            here.beside,
        )

    def line_copy(step, seq):
        earlier = step - 1
        return send_to(
            line_out.at[earlier, rows_of(seq)],
            line_in.at[earlier, rows_of(seq)],
            ref["line_send"].at[earlier, seq],
            ref["line_recv"].at[earlier, seq],
            here.below,
        )

    def block_there(step):
        block = here.beside_ctx - 2 * step
        return (block >= 0) & (block < me)

    def send_aside(step, seq):
        @pl.when(block_there(step))
        def _():
            side_out[step, rows_of(seq)] = grads_of(
                here.beside_ctx - 2 * step, seq, False
            ).astype(jnp.bfloat16)
            side_copy(step, seq).start()

    def send_down(step, seq):
        @pl.when(me >= 2 * step)
        def _():
            rows = rows_of(seq)
            own_grads[rows, :] = grads_of(me - 2 * step, seq, False)
            side_copy(step, seq).wait_recv()
            own_grads[rows, :] += side_in[step, rows].astype(jnp.float32)

            @pl.when(here.has_above)
            def _():
                line_copy(step + 1, seq).wait_recv()
                own_grads[rows, :] += line_in[step, rows].astype(jnp.float32)

            line_out[step - 1, rows] = own_grads[rows, :].astype(jnp.bfloat16)
            line_copy(step, seq).start()

    gain = as_row(ref["attn_gain"])
    q_gain_pair = double(as_row(ref["q_gain"]))
    k_gain_pair = double(as_row(ref["k_gain"]))
    gain_slots[me] = jnp.zeros_like(gain_slots[me])
    gain_slots[me, pl.ds(1, 1)] = ref["ffn_gain_part"][...]

    def back_through(grads, raw, gain_pair, row):
        cosine = table[:, pl.ds(0, pair)]
        sine = table[:, pl.ds(pair, pair)]
        turned = grads * cosine - swap_halves(grads, head_dim) * sine
        unit, inverse = pair_norm(raw, head_dim)
        gain_slots[me, pl.ds(row, 1), pl.ds(0, pair)] += jnp.sum(
            turned * unit, axis=0, keepdims=True
        )
        scaled = turned * gain_pair
        return (inverse * (scaled - unit * pair_mean(scaled * unit, head_dim))).astype(
            jnp.bfloat16
        )

    def token_unit(rows):
        inputs = tokens[rows, :].astype(jnp.float32)
        inverse = lax.rsqrt(jnp.mean(inputs * inputs, axis=-1, keepdims=True) + EPS)
        return inputs * inverse, inverse

    def project_back(seq):
        rows = rows_of(seq)
        for group in range(2):
            grads = grad_query_t[seq, group] * (head_dim**-0.5)
            grads = jnp.concatenate([grads[:, :tile], grads[:, tile:]], axis=0).T
            cols = pl.ds(group * pair, pair)
            grad_qkv[rows, cols] = back_through(grads, query_raw[rows, cols], q_gain_pair, 2)

        @pl.when(me < here.beside_ctx)
        def _():
            side_copy(0, seq).wait_recv()
            own_grads[rows, :] += side_in[0, rows].astype(jnp.float32)

        @pl.when(here.has_above)
        def _():
            line_copy(1, seq).wait_recv()
            own_grads[rows, :] += line_in[0, rows].astype(jnp.float32)

        grad_qkv[rows, pl.ds(2 * pair, pair)] = back_through(
            own_grads[rows, pl.ds(0, pair)], key_raw[rows, :], k_gain_pair, 3
        )
        grad_qkv[rows, pl.ds(3 * pair, pair)] = own_grads[rows, pl.ds(pair, pair)].astype(
            jnp.bfloat16
        )
        grads = (
            dot_nt(grad_qkv[rows, pl.ds(0, 2 * pair)], ref["w_query"][...])
            + dot_nt(grad_qkv[rows, pl.ds(2 * pair, pair)], ref["w_key"][...])
            + dot_nt(grad_qkv[rows, pl.ds(3 * pair, pair)], ref["w_value"][...])
        )
        unit, unused = token_unit(rows)
        gain_slots[me, pl.ds(0, 1)] += jnp.sum(grads * unit, axis=0, keepdims=True)
        wt_sum.offer(seq, grads)

    def output_rows(seq):
        rows = rows_of(seq)
        ref["output"][rows, :] = (residual[rows, :] + mlp_sum.result(seq)).astype(jnp.bfloat16)

    def token_rows(seq):
        rows = rows_of(seq)
        unit, inverse = token_unit(rows)
        scaled = wt_sum.result(seq) * gain
        grads = inverse * (scaled - unit * jnp.mean(scaled * unit, axis=-1, keepdims=True))
        ref["tokens_grad"][rows, :] = (grad_res[rows, :].astype(jnp.float32) + grads).astype(
            jnp.bfloat16
        )

    loads.wait(*range(3, len(LOADED)))

    def sequence_turn(turn_, carry):
        @pl.when(turn_ + 1 < sequences)
        def _():
            prepare(turn_ + 1)

            def aside(index, carry):
                send_aside(levels - 1 - index, turn_ + 1)
                return carry

            lax.fori_loop(0, levels, aside, 0)

        @pl.when((turn_ >= 0) & (turn_ < sequences))
        def _():
            def down(index, carry):
                send_down(levels - 1 - index, turn_)
                return carry

            lax.fori_loop(0, levels - 1, down, 0)
            rows = rows_of(turn_)
            own_grads[rows, :] = grads_of(me, turn_, True)
            mlp_sum.offer(turn_, dot_nt(ffn_grads[0, rows], ref["w_down"][...]))

        ffn_tick(turn_ + 7)

        @pl.when((turn_ >= 1) & (turn_ <= sequences))
        def _():
            mlp_sum.cross(turn_ - 1)

        @pl.when(turn_ == sequences)
        def _():
            out.tick(0, 0, grad_res_t, heads, first=True)

        @pl.when(turn_ == sequences + 1)
        def _():
            out.tick(0, 1, grad_res_t, heads)

        @pl.when(turn_ >= 2)
        def _():
            project_back(turn_ - 2)
            mlp_sum.close(turn_ - 2)

        @pl.when(turn_ >= 3)
        def _():
            wt_sum.cross(turn_ - 3)
            output_rows(turn_ - 3)

        return carry

    turns = sequences + 3
    lax.fori_loop(-1, turns - 1, sequence_turn, 0)
    qkv.tick(0, 0, normed_t, grad_qkv, first=True)
    gains.start()
    wt_sum.cross(sequences - 1)
    output_rows(sequences - 1)
    stores.start(0)
    left_over = 3 * count - 6 - turns
    each = -(-left_over // (last - 1))

    def tail(step, carry):
        for i in range(each):
            index = 6 + turns + each * (step - 1) + i

            @pl.when(index < 3 * count)
            def _():
                ffn_tick(index)

        qkv.tick(0, step, normed_t, grad_qkv)

        @pl.when(step < last)
        def _():
            out.tick(
                0, step + 1, grad_res_t, heads, result=ref["w_out_sum"], final=step + 1 == last
            )

        @pl.when(step <= sequences)
        def _():
            wt_sum.close(step - 1)

        @pl.when((step >= 2) & (step <= sequences + 1))
        def _():
            token_rows(step - 2)

        return carry

    middle = min(4, last)
    lax.fori_loop(1, middle, tail, 0)
    total = gains.total()
    ref["attn_gain_sum"][...] = total[0:1]
    ref["ffn_gain_sum"][...] = total[1:2]
    folded = total[:, :pair]
    folded = folded + pltpu.roll(folded, head_dim, 1)
    ref["q_gain_sum"][...] = folded[2:3]
    ref["k_gain_sum"][...] = folded[3:4]
    stores.start(9, 10, 11, 12)
    lax.fori_loop(middle, last, tail, 0)
    stores.start(1, 2, 3, 4, 5)
    qkv.tick(0, last, normed_t, grad_qkv, result=qkv_total)
    stores.start(6, 7, 8)
    wt_sum.finish(sequences)
    mlp_sum.finish(sequences)
    for i in range(3):
        ffn.finish(i, last)
    out.finish(0, last)
    qkv.finish(0, last)

    def drain(step, carry):
        @pl.when(block_there(step))
        def _():
            def sent(seq, carry):
                side_copy(step, seq).wait_send()
                return carry

            lax.fori_loop(0, sequences, sent, 0)

        @pl.when((step > 0) & (me >= 2 * step))
        def _():
            def sent(seq, carry):
                line_copy(step, seq).wait_send()
                return carry

            lax.fori_loop(0, sequences, sent, 0)

        return carry

    lax.fori_loop(0, levels, drain, 0)
    stores.wait(*range(len(RESULTS)))


def backward(inputs):
    count = lax.axis_size("ctx")
    sequences, tile = inputs["mixed_t_in"].shape[0], inputs["mixed_t_in"].shape[3]
    rows, width = inputs["tokens_in"].shape
    head_dim = inputs["q_gain"].shape[0]
    hidden = inputs["ffn_grads_in"].shape[2]
    pair = 2 * head_dim
    levels = count // 2
    block = width // count
    f32, bf16 = jnp.float32, jnp.bfloat16
    dma = pltpu.SemaphoreType.DMA
    results = {
        "output": ((rows, width), bf16),
        "tokens_grad": ((rows, width), bf16),
        "w_down_sum": ((block, hidden), f32),
        "w_gate_sum": ((block, hidden), f32),
        "w_up_sum": ((block, hidden), f32),
        "w_out_sum": ((block, 2 * pair), f32),
        "w_query_sum": ((block, 2 * pair), f32),
        "w_key_sum": ((block, pair), f32),
        "w_value_sum": ((block, pair), f32),
        "attn_gain_sum": ((1, width), f32),
        "ffn_gain_sum": ((1, width), f32),
        "q_gain_sum": ((1, pair), f32),
        "k_gain_sum": ((1, pair), f32),
    }
    staged = ("output", "tokens_grad", "w_out_sum") + RESULTS[9:]
    scratch = {name: pltpu.VMEM(*results[name]) for name in staged}
    for name in LOADED:
        kind = inputs[name + "_in"]
        shape = (tile, kind.shape[1]) if name == "table" else kind.shape
        scratch[name] = pltpu.VMEM(shape, kind.dtype)
    scratch |= {
        "grad_res_t": pltpu.VMEM((width, rows), bf16),
        "grad_heads_t": pltpu.VMEM((sequences, pair, 4 * tile), bf16),
        "deltas": pltpu.VMEM((sequences, 1, 4 * tile), f32),
        "grad_query_t": pltpu.VMEM((sequences, 2, head_dim, 2 * tile), f32),
        "own_grads": pltpu.VMEM((rows, 2 * pair), f32),
        "grad_qkv": pltpu.VMEM((rows, 4 * pair), bf16),
        "side_in": pltpu.VMEM((levels, rows, 2 * pair), bf16),
        "side_out": pltpu.VMEM((levels, rows, 2 * pair), bf16),
        "line_in": pltpu.VMEM((levels - 1, rows, 2 * pair), bf16),
        "line_out": pltpu.VMEM((levels - 1, rows, 2 * pair), bf16),
        "ffn_sums": pltpu.VMEM((3, block, hidden), f32),
        "qkv_total": pltpu.VMEM((block, 4 * pair), f32),
        "side_send": dma((levels, sequences)),
        "side_recv": dma((levels, sequences)),
        "line_send": dma((levels - 1, sequences)),
        "line_recv": dma((levels - 1, sequences)),
        "load_sems": dma((len(LOADED),)),
        "store_sems": dma((len(RESULTS),)),
        "gains0": pltpu.VMEM((count, 8, width), f32),
        "gains1": pltpu.VMEM((2, 2, 8, width), f32),
        "gains2": dma((count - 1,)),
        "gains3": dma((count - 1,)),
        "gains4": dma((2,)),
        "gains5": dma((2,)),
    }
    for label, kinds in (
        ("wt_sum", wt_sum_scratch(sequences, rows, width)),
        ("mlp_sum", wt_sum_scratch(sequences, rows, width)),
        ("ffn", ring_scratch(count - 1, 3, block, hidden)),
        ("out", ring_scratch(count, 1, block, 2 * pair)),
        ("qkv", ring_scratch(count, 1, block, 4 * pair)),
    ):
        scratch |= {f"{label}{i}": kind for i, kind in enumerate(kinds)}
    vmem, anywhere = pl.BlockSpec(memory_space=pltpu.VMEM), pl.BlockSpec(memory_space=pl.ANY)
    names = (*inputs, *(name + "_res" for name in RESULTS), *scratch)
    arrays = pl.pallas_call(
        partial(backward_kernel, count, names),
        out_shape=[jax.ShapeDtypeStruct(*results[name]) for name in RESULTS],
        in_specs=[anywhere if name.endswith("_in") else vmem for name in inputs],
        out_specs=[anywhere] * len(RESULTS),
        scratch_shapes=list(scratch.values()),
        compiler_params=pltpu.CompilerParams(
            collective_id=3, has_side_effects=True, vmem_limit_bytes=62 * MIB
        ),
    )(*inputs.values())
    return dict(zip(RESULTS, arrays, strict=True))


def hand_over_kernel(count, *refs):
    for source, target in zip(refs[:count], refs[count:], strict=True):
        target[...] = source[...]


def hand_over(arrays):
    vmem = pl.BlockSpec(memory_space=pltpu.VMEM)
    return pl.pallas_call(
        partial(hand_over_kernel, len(arrays)),
        out_shape=[jax.ShapeDtypeStruct(array.shape, array.dtype) for array in arrays],
        in_specs=[vmem] * len(arrays),
        out_specs=[vmem] * len(arrays),
        compiler_params=pltpu.CompilerParams(vmem_limit_bytes=32 * MIB),
    )(*arrays)


def rotary_table(length, head_dim):
    half = head_dim // 2
    frequency = THETA ** (-2.0 * np.arange(half) / head_dim)
    angles = np.arange(length)[:, None] * frequency[None, :]
    cosine, sine = np.cos(angles), np.sin(angles)
    return np.concatenate([cosine] * 4 + [-sine, sine] * 2, axis=1).astype(np.float32)


def kernels_fit(tokens, w_query, key_matrix, q_gain):
    sequences, tile, width = tokens.shape
    count, head_dim = lax.axis_size("ctx"), q_gain.shape[0]
    return (
        lax.axis_size("wt") == 4
        and count % 2 == 0
        and count >= 4
        and tile == 128
        and sequences <= 8
        and sequences * count <= 40
        and head_dim == 64
        and w_query.shape[1] == 4 * head_dim
        and key_matrix.shape[1] == 2 * head_dim
        and width % (128 * count) == 0
    )


def on_device_plain(
    tokens,
    segments,
    attn_gain,
    w_query,
    key_matrix,
    value_matrix,
    q_gain,
    k_gain,
    w_out,
    ffn_gain,
    w_gate,
    w_up,
    w_down,
    cotangent,
):
    sequences, seq_rows, model_width = tokens.shape
    head_dim = q_gain.shape[0]
    q_local = w_query.shape[1] // head_dim
    kv_local = key_matrix.shape[1] // head_dim
    per_group = q_local // kv_local
    score_scale = 1.0 / math.sqrt(head_dim)
    all_rows = sequences * seq_rows
    places = lax.axis_index("ctx") * seq_rows + jnp.arange(seq_rows, dtype=jnp.int32)
    frequency = THETA ** (-jnp.arange(0, head_dim, 2, dtype=jnp.float32) / head_dim)
    angles = places.astype(jnp.float32)[None, :, None] * frequency
    cosine_table = jnp.cos(angles)[:, :, None, :]
    sine_table = jnp.sin(angles)[:, :, None, :]
    inputs = tokens.astype(jnp.float32).reshape(all_rows, model_width)
    normed, attn_unit, attn_inverse = norm_rows(inputs, attn_gain)
    normed_low = normed.astype(jnp.bfloat16)
    query_raw = product(normed_low, w_query).reshape(sequences, seq_rows, q_local, head_dim)
    key_raw = product(normed_low, key_matrix).reshape(sequences, seq_rows, kv_local, head_dim)
    value_low = (
        product(normed_low, value_matrix)
        .astype(jnp.bfloat16)
        .reshape(sequences, seq_rows, kv_local * head_dim)
    )
    query_normed, query_unit, query_inverse = norm_rows(query_raw, q_gain)
    key_normed, key_unit, key_inverse = norm_rows(key_raw, k_gain)
    query_low = rotate(query_normed, cosine_table, sine_table, 1.0).astype(jnp.bfloat16)
    key_low = rotate(key_normed, cosine_table, sine_table, 1.0).astype(jnp.bfloat16)
    key_flat = key_low.reshape(sequences, seq_rows, kv_local * head_dim)
    query_groups = query_low.reshape(sequences, seq_rows, kv_local, per_group, head_dim)
    attend = partial(
        attend_piece,
        queries=query_groups,
        query_places=places,
        query_segs=segments,
        score_scale=score_scale,
    )
    start_state = (
        jnp.full((sequences, kv_local, per_group, seq_rows), NEG, jnp.float32),
        jnp.zeros((sequences, kv_local, per_group, seq_rows), jnp.float32),
        jnp.zeros((sequences, seq_rows, kv_local, per_group, head_dim), jnp.float32),
    )
    keys_values = lax.all_gather(
        jnp.concatenate([key_flat, value_low], axis=-1), "ctx", axis=1, tiled=True
    )
    kv_width = kv_local * head_dim
    gathered = (
        keys_values[..., :kv_width],
        keys_values[..., kv_width:],
        lax.all_gather(segments, "ctx", axis=1, tiled=True),
    )
    row_max, row_sum, weighted = attend(
        start_state,
        gathered,
        jnp.int32(0),
    )
    mixed_heads = weighted / jnp.transpose(row_sum, (0, 3, 1, 2))[..., None]
    mixed_low = mixed_heads.astype(jnp.bfloat16).reshape(all_rows, q_local * head_dim)
    attn_term = by_transpose(mixed_low, w_out)
    residual = inputs + lax.psum(attn_term.astype(jnp.bfloat16), "wt").astype(jnp.float32)
    normed_ffn, ffn_unit, ffn_inverse = norm_rows(residual, ffn_gain)
    normed_ffn_low = normed_ffn.astype(jnp.bfloat16)
    gate_proj = product(normed_ffn_low, w_gate)
    up_proj = product(normed_ffn_low, w_up)
    gate_sigmoid = jax.nn.sigmoid(gate_proj)
    gate_silu = gate_proj * gate_sigmoid
    hidden_low = (gate_silu * up_proj).astype(jnp.bfloat16)
    mlp_term = by_transpose(hidden_low, w_down)
    output_rows = (
        residual + lax.psum(mlp_term.astype(jnp.bfloat16), "wt").astype(jnp.float32)
    ).astype(jnp.bfloat16)
    log_total = row_max + jnp.log(row_sum)
    grad_rows = cotangent.reshape(all_rows, model_width)
    grad_hidden = product(grad_rows, w_down)
    grad_gate = (
        grad_hidden * up_proj * gate_sigmoid * (1.0 + gate_proj * (1.0 - gate_sigmoid))
    ).astype(jnp.bfloat16)
    grad_up = (grad_hidden * gate_silu).astype(jnp.bfloat16)
    grad_normed_ffn = by_transpose(grad_gate, w_gate) + by_transpose(grad_up, w_up)
    ffn_gain_part = jnp.sum(grad_normed_ffn * ffn_unit, axis=0)
    grad_normed_ffn = lax.psum(grad_normed_ffn.astype(jnp.bfloat16), "wt").astype(jnp.float32)
    grad_residual = grad_rows.astype(jnp.float32) + norm_back(
        grad_normed_ffn, ffn_unit, ffn_inverse, ffn_gain
    )
    grad_residual_low = grad_residual.astype(jnp.bfloat16)
    grad_heads_low = product(grad_residual_low, w_out).astype(jnp.bfloat16)
    grad_groups = grad_heads_low.reshape(sequences, seq_rows, kv_local, per_group, head_dim)
    delta_rows = jnp.sum(grad_groups.astype(jnp.float32) * mixed_heads, axis=-1)
    delta_cols = jnp.transpose(delta_rows, (0, 2, 3, 1))
    query_grad_fn = partial(
        grad_piece,
        queries=query_groups,
        grad_heads=grad_groups,
        log_total=log_total,
        row_delta=delta_cols,
        query_places=places,
        query_segs=segments,
        score_scale=score_scale,
    )
    grad_query, grad_pairs = query_grad_fn(
        jnp.zeros((sequences, seq_rows, kv_local, per_group, head_dim), jnp.float32),
        gathered,
        jnp.int32(0),
    )
    grad_pairs = lax.psum_scatter(grad_pairs, "ctx", scatter_dimension=1, tiled=True).astype(
        jnp.float32
    )
    grad_key = grad_pairs[:, :, 0]
    grad_value = grad_pairs[:, :, 1]
    grad_query = rotate(
        grad_query.reshape(sequences, seq_rows, q_local, head_dim) * score_scale,
        cosine_table,
        sine_table,
        -1.0,
    )
    grad_key = rotate(grad_key * score_scale, cosine_table, sine_table, -1.0)
    q_gain_part = jnp.sum(grad_query * query_unit, axis=(0, 1, 2))
    k_gain_part = jnp.sum(grad_key * key_unit, axis=(0, 1, 2))
    grad_query_low = (
        norm_back(grad_query, query_unit, query_inverse, q_gain)
        .astype(jnp.bfloat16)
        .reshape(all_rows, q_local * head_dim)
    )
    grad_key_low = (
        norm_back(grad_key, key_unit, key_inverse, k_gain)
        .astype(jnp.bfloat16)
        .reshape(all_rows, kv_local * head_dim)
    )
    grad_value_low = grad_value.astype(jnp.bfloat16).reshape(all_rows, kv_local * head_dim)
    grad_normed = (
        by_transpose(grad_query_low, w_query)
        + by_transpose(grad_key_low, key_matrix)
        + by_transpose(grad_value_low, value_matrix)
    )
    attn_gain_part = jnp.sum(grad_normed * attn_unit, axis=0)
    grad_normed = lax.psum(grad_normed.astype(jnp.bfloat16), "wt").astype(jnp.float32)
    tokens_rows = (
        grad_residual + norm_back(grad_normed, attn_unit, attn_inverse, attn_gain)
    ).astype(jnp.bfloat16)
    output = output_rows.reshape(sequences, seq_rows, model_width)
    tokens_grad = tokens_rows.reshape(sequences, seq_rows, model_width)
    partial_sums = (
        transpose_by(grad_rows, hidden_low),
        transpose_by(normed_ffn_low, grad_gate),
        transpose_by(normed_ffn_low, grad_up),
        transpose_by(grad_residual_low, mixed_low),
        transpose_by(normed_low, grad_query_low),
        transpose_by(normed_low, grad_key_low),
        transpose_by(normed_low, grad_value_low),
    )
    summed = [
        lax.psum_scatter(part.astype(jnp.bfloat16), "ctx", scatter_dimension=0, tiled=True).astype(
            jnp.float32
        )
        for part in partial_sums
    ]
    w_down_grad, w_gate_grad, w_up_grad, w_out_grad = summed[:4]
    w_query_grad, w_key_grad, w_value_grad = summed[4:]
    attn_gain_grad, q_gain_grad, k_gain_grad, ffn_gain_grad = lax.psum(
        (attn_gain_part, q_gain_part, k_gain_part, ffn_gain_part), ("ctx", "wt")
    )
    return (
        output,
        tokens_grad,
        attn_gain_grad,
        w_query_grad,
        w_key_grad,
        w_value_grad,
        q_gain_grad,
        k_gain_grad,
        w_out_grad,
        ffn_gain_grad,
        w_gate_grad,
        w_up_grad,
        w_down_grad,
    )


def on_device(
    tokens,
    segments,
    attn_gain,
    w_query,
    key_matrix,
    value_matrix,
    q_gain,
    k_gain,
    w_out,
    ffn_gain,
    w_gate,
    w_up,
    w_down,
    cotangent,
):
    if not kernels_fit(tokens, w_query, key_matrix, q_gain):
        return on_device_plain(
            tokens,
            segments,
            attn_gain,
            w_query,
            key_matrix,
            value_matrix,
            q_gain,
            k_gain,
            w_out,
            ffn_gain,
            w_gate,
            w_up,
            w_down,
            cotangent,
        )
    sequences, seq_rows, model_width = tokens.shape
    count, head_dim = lax.axis_size("ctx"), q_gain.shape[0]
    token_rows = tokens.reshape(sequences * seq_rows, model_width)
    table = jnp.asarray(rotary_table(count * seq_rows, head_dim))
    gains = {"attn_gain": attn_gain, "q_gain": q_gain, "k_gain": k_gain}
    kept = forward(
        {
            "tokens": token_rows,
            "segments": segments,
            **gains,
            "ffn_gain": ffn_gain,
            "w_query": w_query,
            "w_key": key_matrix,
            "w_value": value_matrix,
            "w_out": w_out,
            "table_in": table,
            "cotangent_in": cotangent.reshape(token_rows.shape),
            "w_down_in": w_down,
            "w_gate_in": w_gate,
            "w_up_in": w_up,
        }
    )
    ffn_gain_part = kept.pop("ffn_gain_part")
    sums = backward(
        {
            **gains,
            "ffn_gain_part": ffn_gain_part,
            **{name + "_in": array for name, array in kept.items()},
            "tokens_in": token_rows,
            "table_in": table,
            "w_query_in": w_query,
            "w_key_in": key_matrix,
            "w_value_in": value_matrix,
            "w_out_in": w_out,
            "w_down_in": w_down,
        }
    )
    done = dict(zip(RESULTS, hand_over([sums[name] for name in RESULTS]), strict=True))
    return (
        done["output"].reshape(tokens.shape),
        done["tokens_grad"].reshape(tokens.shape),
        done["attn_gain_sum"][0],
        done["w_query_sum"],
        done["w_key_sum"],
        done["w_value_sum"],
        done["q_gain_sum"][0, :head_dim],
        done["k_gain_sum"][0, :head_dim],
        done["w_out_sum"],
        done["ffn_gain_sum"][0],
        done["w_gate_sum"],
        done["w_up_sum"],
        done["w_down_sum"],
    )


def solution(mesh):
    in_specs = (
        P(None, "ctx", None),
        P(None, "ctx"),
        P(),
        P(None, "wt"),
        P(None, "wt"),
        P(None, "wt"),
        P(),
        P(),
        P(None, "wt"),
        P(),
        P(None, "wt"),
        P(None, "wt"),
        P(None, "wt"),
        P(None, "ctx", None),
    )
    out_specs = (
        P(None, "ctx", None),
        P(None, "ctx", None),
        P(),
        P("ctx", "wt"),
        P("ctx", "wt"),
        P("ctx", "wt"),
        P(),
        P(),
        P("ctx", "wt"),
        P(),
        P("ctx", "wt"),
        P("ctx", "wt"),
        P("ctx", "wt"),
    )
    return jax.shard_map(
        on_device, mesh=mesh, in_specs=in_specs, out_specs=out_specs, check_vma=False
    )
```

```python
from functools import partial
import math

import jax
import jax.numpy as jnp
import numpy as np
from jax import lax
from jax.experimental import pallas as pl
from jax.experimental.pallas import tpu as pltpu
from jax.sharding import PartitionSpec as P

EPS = 1e-05
THETA = 1000000.0
NEG = -1e30


def product(left, right):
    return jnp.dot(left, right, preferred_element_type=jnp.float32)


def by_transpose(left, right):
    return lax.dot_general(
        left, right, (((1,), (1,)), ((), ())), preferred_element_type=jnp.float32
    )


def transpose_by(left, right):
    return lax.dot_general(
        left, right, (((0,), (0,)), ((), ())), preferred_element_type=jnp.float32
    )


def norm_rows(values, gain):
    inverse = lax.rsqrt(jnp.mean(values * values, axis=-1, keepdims=True) + EPS)
    unit_rows = values * inverse
    return (unit_rows * gain, unit_rows, inverse)


def norm_back(grads, unit_rows, inverse, gain):
    scaled = grads * gain
    return inverse * (scaled - unit_rows * jnp.mean(scaled * unit_rows, axis=-1, keepdims=True))


def rotate(values, cosine_table, sine_table, direction):
    half_dim = values.shape[-1] // 2
    first_half = values[..., :half_dim]
    second_half = values[..., half_dim:]
    return jnp.concatenate(
        [
            first_half * cosine_table - direction * second_half * sine_table,
            second_half * cosine_table + direction * first_half * sine_table,
        ],
        axis=-1,
    )


def split_blocks(array, block_len):
    shaped = array.reshape(
        (array.shape[0], array.shape[1] // block_len, block_len) + array.shape[2:]
    )
    return jnp.moveaxis(shaped, 1, 0)


def attend_piece(folded, pieces, first_row, queries, query_places, query_segs, score_scale):
    key_piece, value_piece, seg_piece = pieces
    sequences, piece_rows = seg_piece.shape
    kv_local = queries.shape[2]
    head_dim = queries.shape[4]
    block_len = math.gcd(piece_rows, 512)
    key_blocks = split_blocks(
        key_piece.reshape(sequences, piece_rows, kv_local, head_dim), block_len
    )
    value_tiles = split_blocks(
        value_piece.reshape(sequences, piece_rows, kv_local, head_dim), block_len
    )
    seg_blocks = split_blocks(seg_piece, block_len)
    offsets = block_len * jnp.arange(piece_rows // block_len, dtype=jnp.int32)

    def attend_block_step(running, block_item):
        row_max, row_sum, weighted = running
        key_block, value_block, seg_block, offset = block_item
        key_places = offset + jnp.arange(block_len, dtype=jnp.int32)
        allowed = (key_places[None, None, :] <= query_places[None, :, None]) & (
            query_segs[:, :, None] == seg_block[:, None, :]
        )
        allowed = allowed[:, None, None]
        scores = (
            jnp.einsum("sqgrd,skgd->sgrqk", queries, key_block, preferred_element_type=jnp.float32)
            * score_scale
        )
        scores = jnp.where(allowed, scores, NEG)
        new_max = jnp.maximum(row_max, jnp.max(scores, axis=-1))
        weights = jnp.where(allowed, jnp.exp(scores - new_max[..., None]), 0.0)
        fading = jnp.exp(row_max - new_max)
        row_sum = row_sum * fading + jnp.sum(weights, axis=-1)
        fade_rows = jnp.transpose(fading, (0, 3, 1, 2))[..., None]
        weighted = weighted * fade_rows + jnp.einsum(
            "sgrqk,skgd->sqgrd",
            weights.astype(jnp.bfloat16),
            value_block,
            preferred_element_type=jnp.float32,
        )
        return ((new_max, row_sum, weighted), None)

    folded, unused = lax.scan(
        attend_block_step, folded, (key_blocks, value_tiles, seg_blocks, offsets)
    )
    return folded


def grad_piece(
    folded,
    pieces,
    first_row,
    queries,
    grad_heads,
    log_total,
    row_delta,
    query_places,
    query_segs,
    score_scale,
):
    key_piece, value_piece, seg_piece = pieces
    sequences, piece_rows = seg_piece.shape
    kv_local = queries.shape[2]
    head_dim = queries.shape[4]
    block_len = math.gcd(piece_rows, 512)
    key_blocks = split_blocks(
        key_piece.reshape(sequences, piece_rows, kv_local, head_dim), block_len
    )
    value_tiles = split_blocks(
        value_piece.reshape(sequences, piece_rows, kv_local, head_dim), block_len
    )
    seg_blocks = split_blocks(seg_piece, block_len)
    offsets = block_len * jnp.arange(piece_rows // block_len, dtype=jnp.int32)

    def grad_block_step(running, block_item):
        key_block, value_block, seg_block, offset = block_item
        key_places = offset + jnp.arange(block_len, dtype=jnp.int32)
        allowed = (key_places[None, None, :] <= query_places[None, :, None]) & (
            query_segs[:, :, None] == seg_block[:, None, :]
        )
        allowed = allowed[:, None, None]
        scores = (
            jnp.einsum("sqgrd,skgd->sgrqk", queries, key_block, preferred_element_type=jnp.float32)
            * score_scale
        )
        probs = jnp.where(allowed, jnp.exp(scores - log_total[..., None]), 0.0)
        grad_probs = jnp.einsum(
            "sqgrd,skgd->sgrqk", grad_heads, value_block, preferred_element_type=jnp.float32
        )
        grad_scores = (probs * (grad_probs - row_delta[..., None])).astype(jnp.bfloat16)
        running = running + jnp.einsum(
            "sgrqk,skgd->sqgrd", grad_scores, key_block, preferred_element_type=jnp.float32
        )
        grad_keys = jnp.einsum(
            "sgrqk,sqgrd->skgd", grad_scores, queries, preferred_element_type=jnp.float32
        )
        grad_values = jnp.einsum(
            "sgrqk,sqgrd->skgd",
            probs.astype(jnp.bfloat16),
            grad_heads,
            preferred_element_type=jnp.float32,
        )
        grads = jnp.stack([grad_keys, grad_values], axis=2).astype(jnp.bfloat16)
        return (running, grads)

    folded, grads = lax.scan(
        grad_block_step, folded, (key_blocks, value_tiles, seg_blocks, offsets)
    )
    return folded, jnp.moveaxis(grads, 0, 1).reshape((sequences, piece_rows) + grads.shape[3:])


MESH = pl.DeviceIdType.MESH
MIB = 1 << 20


def ring_place(index, count):
    return lax.select(
        lax.rem(index, 2) == 0, lax.div(index, 2), count - 1 - lax.div(index, 2)
    )


def ring_index(place, count):
    place = lax.rem(place + 2 * count, count)
    return lax.select(
        place < lax.div(count, 2), 2 * place, 2 * (count - 1 - place) + 1
    )


class Ring:
    def __init__(self, count, slots, send_sems, recv_sems, base=0):
        self.count, self.slots, self.base = count, slots, base
        self.send_sems, self.recv_sems = send_sems, recv_sems
        self.other = lax.axis_index("wt")
        self.place = ring_place(lax.axis_index("ctx"), count)
        self.right = ring_index(self.place + 1, count)
        self.left = ring_index(self.place + count - 1, count)
        self.half = slots.shape[2] // 2

    def copy(self, which, step, way):
        rows = pl.ds(way * self.half, self.half)
        slot = step - self.base
        return pltpu.make_async_remote_copy(
            src_ref=self.slots.at[which, slot, rows],
            dst_ref=self.slots.at[which, slot + 1, rows],
            send_sem=self.send_sems.at[which, slot, way],
            recv_sem=self.recv_sems.at[which, slot, way],
            device_id=((self.right, self.left)[way], self.other),
            device_id_type=MESH,
        )

    def arrived(self, which, step):
        for way in range(2):
            self.copy(which, step - 1, way).wait_recv()

    def tick(
        self,
        which,
        step,
        left_ref,
        right_ref,
        first=False,
        given=None,
        result=None,
        final=True,
    ):
        half = self.half
        rows = [
            ring_index(target, self.count) * (2 * half) + way * half
            for way, target in enumerate(
                (self.place + self.count - 1 - step, self.place + 1 + step)
            )
        ]
        left = jnp.concatenate(
            [left_ref[pl.ds(pl.multiple_of(row, half), half), :] for row in rows], axis=0
        )
        total = jnp.dot(left, right_ref[...], preferred_element_type=jnp.float32)
        if given is not None:
            total = total + given[...].astype(jnp.float32)
        elif not first:
            self.arrived(which, step)
            total = total + self.slots[which, step - self.base].astype(jnp.float32)
        def pass_on():
            self.slots[which, step - self.base] = total.astype(jnp.bfloat16)
            for way in range(2):
                self.copy(which, step, way).start()

        def keep():
            result[...] = total

        if result is None:
            pass_on()
        elif final is True:
            keep()
        else:
            pl.when(final)(keep)
            pl.when(jnp.logical_not(final))(pass_on)

    def finish(self, which, end):
        for way in range(2):

            def wait(step, carry):
                self.copy(which, step, way).wait_send()
                return carry

            lax.fori_loop(self.base, end, wait, 0)


def pair_lanes(shape):
    return lax.broadcasted_iota(jnp.int32, shape, 1)


def swap_halves(values, head_dim):
    lanes = pair_lanes(values.shape)
    width = values.shape[1]
    quarter = head_dim // 2
    return jnp.where(
        lax.rem(lanes, head_dim) < quarter,
        pltpu.roll(values, width - quarter, 1),
        pltpu.roll(values, quarter, 1),
    )


def pair_mean(values, head_dim):
    low = pair_lanes(values.shape) < head_dim
    first = jnp.sum(jnp.where(low, values, 0.0), axis=-1, keepdims=True)
    second = jnp.sum(jnp.where(low, 0.0, values), axis=-1, keepdims=True)
    return jnp.where(low, first, second) * (1.0 / head_dim)


def pair_norm(values, head_dim):
    inverse = lax.rsqrt(pair_mean(values * values, head_dim) + EPS)
    return values * inverse, inverse


def as_row(ref):
    return ref[...].astype(jnp.float32).reshape(1, -1)


def double(row):
    return jnp.concatenate([row, row], axis=-1)


def dot_nn(left, right):
    return jnp.dot(left, right, preferred_element_type=jnp.float32)


def dot_nt(left, right):
    return lax.dot_general(
        left, right, (((1,), (1,)), ((), ())), preferred_element_type=jnp.float32
    )


def as_column(row):
    size = row.shape[1]
    rows = lax.broadcasted_iota(jnp.int32, (size, size), 0)
    lanes = lax.broadcasted_iota(jnp.int32, (size, size), 1)
    return jnp.sum(jnp.where(rows == lanes, row, 0.0), axis=1, keepdims=True)


class Place:
    def __init__(self, count):
        self.count = count
        self.ctx, self.wt = lax.axis_index("ctx"), lax.axis_index("wt")
        self.odd = lax.rem(self.ctx, 2)
        self.level = lax.div(self.ctx, 2)
        self.core_bit = lax.rem(self.wt, 2)
        self.beside_ctx = self.ctx + 1 - 2 * self.odd
        self.beside = (self.beside_ctx, self.wt)
        self.above = (lax.rem(self.ctx + 2, count), self.wt)
        self.below = (lax.rem(self.ctx + count - 2, count), self.wt)
        self.has_above = self.ctx + 2 < count
        self.has_below = self.ctx >= 2
        self.core_wt = self.wt + 1 - 2 * self.core_bit
        self.chip_wt = lax.rem(self.wt + 2, 4)
        self.far_wt = lax.rem(self.core_wt + 2, 4)
        self.core = (self.ctx, self.core_wt)
        self.chip = (self.ctx, self.chip_wt)

    def signal(self, peer):
        pl.semaphore_signal(
            pltpu.get_barrier_semaphore(), inc=1, device_id=peer, device_id_type=MESH
        )

    def signal_all(self):
        for shift in range(1, self.count):
            self.signal((lax.rem(self.ctx + shift, self.count), self.wt))
        self.signal(self.core)
        self.signal(self.chip)

    def await_all(self):
        pl.semaphore_wait(pltpu.get_barrier_semaphore(), self.count + 1)


def send_to(source, target, send_sem, recv_sem, device):
    return pltpu.make_async_remote_copy(
        src_ref=source,
        dst_ref=target,
        send_sem=send_sem,
        recv_sem=recv_sem,
        device_id=device,
        device_id_type=MESH,
    )


class WtSum:
    def __init__(self, here, tile, part, got, far, full, send_sems, recv_sems, before=None):
        self.here, self.tile, self.before = here, tile, before
        self.part, self.got, self.far, self.full = part, got, far, full
        self.send_sems, self.recv_sems = send_sems, recv_sems
        self.mine, self.theirs = here.core_bit, 1 - here.core_bit
        self.half = got.shape[1]

    def rows(self, seq):
        return pl.ds(pl.multiple_of(seq * self.tile, self.tile), self.tile)

    def cols(self, half):
        return pl.ds(pl.multiple_of(half * self.half, self.half), self.half)

    def copy(self, hop, seq, arriving=False):
        rows = self.rows(seq)
        half = self.theirs if arriving else self.mine
        source = (
            self.part.at[rows, self.cols(self.theirs)],
            self.got.at[rows],
            self.full.at[half, rows],
        )[hop]
        target = (self.got.at[rows], self.far.at[rows], self.full.at[half, rows])[hop]
        device = self.here.chip if hop == 1 else self.here.core
        return send_to(
            source, target, self.send_sems.at[hop, seq], self.recv_sems.at[hop, seq], device
        )

    def offer(self, seq, value):
        self.part[self.rows(seq), pl.ds(0, 2 * self.half)] = value.astype(jnp.bfloat16)
        self.copy(0, seq).start()

    def cross(self, seq):
        rows = self.rows(seq)
        self.copy(0, seq).wait_recv()
        total = self.part[rows, self.cols(self.mine)].astype(jnp.float32) + self.got[
            rows
        ].astype(jnp.float32)
        self.got[rows] = total.astype(jnp.bfloat16)
        self.copy(1, seq).start()

    def close(self, seq):
        rows = self.rows(seq)
        self.copy(1, seq).wait()
        total = self.got[rows].astype(jnp.float32) + self.far[rows].astype(jnp.float32)
        if self.before is not None:
            self.before.copy(2, seq).wait_send()
        self.full[self.mine, rows] = total.astype(jnp.bfloat16)
        self.copy(2, seq).start()

    def result(self, seq):
        rows = self.rows(seq)
        self.copy(2, seq, True).wait_recv()
        return jnp.concatenate([self.full[0, rows], self.full[1, rows]], axis=1).astype(
            jnp.float32
        )

    def finish(self, sequences, hops=(0, 2)):
        def sent(seq, carry):
            for hop in hops:
                self.copy(hop, seq).wait_send()
            return carry

        lax.fori_loop(0, sequences, sent, 0)


def ring_scratch(count, arrays, rows, width):
    return [
        pltpu.VMEM((arrays, count, rows, width), jnp.bfloat16),
        pltpu.SemaphoreType.DMA((arrays, count - 1, 2)),
        pltpu.SemaphoreType.DMA((arrays, count - 1, 2)),
    ]


class GainSum:
    def __init__(self, here, slots, beside, sends, recvs, pair_sends, pair_recvs):
        self.here, self.slots, self.beside = here, slots, beside
        self.sends, self.recvs = sends, recvs
        self.pair_sends, self.pair_recvs = pair_sends, pair_recvs

    def copy(self, shift, arriving=False):
        here = self.here
        target = lax.rem(here.ctx + shift, here.count)
        origin = lax.rem(here.ctx + here.count - shift, here.count)
        ref = self.slots.at[origin if arriving else here.ctx]
        return send_to(
            ref, ref, self.sends.at[shift - 1], self.recvs.at[shift - 1], (target, here.wt)
        )

    def pair_copy(self, hop):
        device = (self.here.core, self.here.chip)[hop]
        return send_to(
            self.beside.at[hop, 0],
            self.beside.at[hop, 1],
            self.pair_sends.at[hop],
            self.pair_recvs.at[hop],
            device,
        )

    def start(self):
        for shift in range(1, self.here.count):
            self.copy(shift).start()

    def total(self):
        for shift in range(1, self.here.count):
            self.copy(shift, True).wait_recv()
        total = self.slots[0]
        for index in range(1, self.here.count):
            total = total + self.slots[index]
        for hop in range(2):
            self.beside[hop, 0] = total
            self.pair_copy(hop).start()
            self.pair_copy(hop).wait_recv()
            total = total + self.beside[hop, 1]
        for shift in range(1, self.here.count):
            self.copy(shift).wait_send()
        for hop in range(2):
            self.pair_copy(hop).wait_send()
        return total


class Mover:
    def __init__(self, pairs, sems):
        self.copies = [
            pltpu.make_async_copy(source, target, sems.at[i])
            for i, (source, target) in enumerate(pairs)
        ]

    def start(self, *which):
        for i in which:
            self.copies[i].start()

    def wait(self, *which):
        for i in which:
            self.copies[i].wait()


TURN_TICKS = 1
VMEM_LIMIT = 63 * MIB
RESULTS = (
    "output",
    "tokens_grad",
    "w_down_sum",
    "w_gate_sum",
    "w_up_sum",
    "w_out_sum",
    "w_query_sum",
    "w_key_sum",
    "w_value_sum",
    "attn_gain_sum",
    "ffn_gain_sum",
    "q_gain_sum",
    "k_gain_sum",
)


def layer_kernel(count, names, *refs):
    ref = dict(zip(names, refs, strict=True))
    tokens, segments = ref["tokens"], ref["segments"]
    residual, mixed_t, query_t = ref["residual"], ref["mixed_t"], ref["query_t"]
    logs, starts, keys_values = ref["logs"], ref["starts"], ref["keys_values"]
    query_raw, key_raw = ref["query_raw"], ref["key_raw"]
    grad_res, lefts = ref["grad_res"], ref["lefts"]
    ffn_grads, ffn_gain_part = ref["ffn_grads"], ref["ffn_gain_part"]
    all_segs, all_out, all_heads = ref["all_segs"], ref["all_out"], ref["all_heads"]
    acc, row_sum = ref["acc"], ref["row_sum"]
    w_gate, w_up, w_down = ref["w_gate"], ref["w_up"], ref["w_down"]
    gate_t, up_t, grad_hidden = ref["gate_t"], ref["up_t"], ref["grad_hidden"]
    cotangent, table = ref["cotangent"], ref["table"]
    sequences, tile = segments.shape
    head_dim = ref["q_gain"].shape[0]
    pair = 2 * head_dim
    levels = count // 2
    here = Place(count)
    me = here.ctx
    loads = Mover(
        [
            (ref["table_in"].at[pl.ds(pl.multiple_of(me * tile, tile), tile)], table),
            (ref["cotangent_in"], cotangent),
            (ref["w_down_in"], w_down),
            (ref["w_gate_in"], w_gate),
            (ref["w_up_in"], w_up),
            (ref["tokens_in"], tokens),
        ],
        ref["load_sems"],
    )
    loads.start(5, 0, 1, 2, 3, 4)
    shared = [ref[name] for name in ("sum_got", "sum_far", "sum_full")]
    ffn_sum = WtSum(here, tile, ref["ffn_part"], *shared, ref["ffn_send"], ref["ffn_recv"])
    ffn = Ring(count, *(ref[f"ffn{i}"] for i in range(3)))
    here.signal_all()
    all_segs[me] = jnp.zeros_like(all_segs[me])
    all_segs[me, pl.ds(0, sequences)] = segments[...]
    all_out[here.wt] = ref["w_out"][...].T

    def out_copy(hop, arriving=False):
        sent = (here.wt, here.wt, here.chip_wt)
        landed = (here.chip_wt, here.core_wt, here.far_wt)
        part = all_out.at[(landed if arriving else sent)[hop]]
        device = here.chip if hop == 0 else here.core
        return send_to(part, part, ref["out_send"].at[hop], ref["out_recv"].at[hop], device)

    def rows_of(seq):
        return pl.ds(pl.multiple_of(seq * tile, tile), tile)

    def block_of(index, step):
        return lax.rem(index - 2 * step + 2 * count, count)

    def up_copy(step, seq, sems=None):
        rows = keys_values.at[block_of(me, step), rows_of(seq)]
        index = step if sems is None else sems
        return send_to(
            rows, rows, ref["up_send"].at[index, seq], ref["up_recv"].at[index, seq], here.above
        )

    def side_copy(step, seq, index=me):
        rows = keys_values.at[block_of(index, step), rows_of(seq)]
        return send_to(
            rows, rows, ref["side_send"].at[step, seq], ref["side_recv"].at[step, seq], here.beside
        )

    def seg_copy(step, way, index=me, sems=None):
        part = all_segs.at[block_of(index, step)]
        device = here.beside if way else here.above
        at = step if sems is None else sems
        return send_to(
            part, part, ref["seg_send"].at[at, way], ref["seg_recv"].at[at, way], device
        )

    def goes_up(step):
        return here.has_above & (me >= 2 * step)

    def goes_aside(step):
        block = me - 2 * step
        return (block >= 0) & (block < here.beside_ctx)

    def comes_aside(step):
        block = here.beside_ctx - 2 * step
        return (block >= 0) & (block < me)

    def pass_segs(step):
        @pl.when(goes_up(step))
        def _():
            seg_copy(step, 0).start()

        @pl.when(goes_aside(step))
        def _():
            seg_copy(step, 1).start()

    def pass_rows(step, seq):
        @pl.when(goes_up(step))
        def _():
            up_copy(step, seq).start()

        @pl.when(goes_aside(step))
        def _():
            side_copy(step, seq).start()

    gain = as_row(ref["attn_gain"])
    q_gain_pair = double(as_row(ref["q_gain"]))
    k_gain_pair = double(as_row(ref["k_gain"]))
    ffn_gain_row = as_row(ref["ffn_gain"])
    loads.wait(0, 5)

    def turn(values):
        cosine = table[:, pl.ds(0, pair)]
        sine = table[:, pl.ds(pair, pair)]
        return values * cosine + swap_halves(values, head_dim) * sine

    def project(seq, carry):
        rows = rows_of(seq)
        inputs = tokens[rows, :].astype(jnp.float32)
        inverse = lax.rsqrt(jnp.mean(inputs * inputs, axis=-1, keepdims=True) + EPS)
        normed = (inputs * inverse * gain).astype(jnp.bfloat16)
        raw_k = dot_nn(normed, ref["w_key"][...])
        key_raw[rows, :] = raw_k
        unit, unused = pair_norm(raw_k, head_dim)
        keys_values[me, rows, pl.ds(0, pair)] = turn(unit * k_gain_pair).astype(jnp.bfloat16)
        keys_values[me, rows, pl.ds(pair, pair)] = dot_nn(normed, ref["w_value"][...]).astype(
            jnp.bfloat16
        )

        @pl.when(seq == 0)
        def _():
            here.await_all()
            pass_segs(0)

        @pl.when(seq < 2)
        def _():
            pass_rows(0, seq)

        @pl.when(seq == 0)
        def _():
            out_copy(0).start()
            out_copy(1).start()

        raw_q = dot_nn(normed, ref["w_query"][...])
        query_raw[rows, :] = raw_q
        query_t[seq] = jnp.zeros_like(query_t[seq])
        for group in range(2):
            unit, unused = pair_norm(raw_q[:, group * pair : (group + 1) * pair], head_dim)
            turned = turn(unit * q_gain_pair) * (head_dim**-0.5)
            flipped = turned.T.astype(jnp.bfloat16)
            for member in range(2):
                query_t[
                    seq,
                    pl.ds(group * head_dim, head_dim),
                    pl.ds((2 * group + member) * tile, tile),
                ] = flipped[member * head_dim : (member + 1) * head_dim]
        acc[seq] = jnp.zeros_like(acc[seq])
        row_sum[seq] = jnp.zeros_like(row_sum[seq])
        starts[seq] = jnp.zeros_like(starts[seq])
        return carry

    lax.fori_loop(0, sequences, project, 0)
    loads.wait(1, 2)

    def back_down(seq, carry):
        rows = rows_of(seq)
        grads = cotangent[rows, :]
        lefts[0, :, rows] = grads.T
        grad_hidden[rows, :] = dot_nn(grads, w_down[...]).astype(jnp.bfloat16)
        return carry

    lax.fori_loop(0, sequences, back_down, 0)

    def route(seq):
        def level(step, carry):
            @pl.when(me >= 2 * step)
            def _():
                @pl.when(seq == 0)
                def _():
                    seg_copy(step, 0, me, step - 1).wait_recv()
                    pass_segs(step)

                up_copy(step, seq, step - 1).wait_recv()
                pass_rows(step, seq)

            return carry

        lax.fori_loop(1, levels, level, 0)

    route(0)
    loads.wait(3, 4)

    def flip(index, carry):
        rows = pl.ds(pl.multiple_of(index * 128, 128), 128)
        gate_t[:, rows] = w_gate[rows, :].T
        up_t[:, rows] = w_up[rows, :].T
        return carry

    lax.fori_loop(0, tokens.shape[1] // 128, flip, 0)
    key_rows = lax.broadcasted_iota(jnp.int32, (tile, tile), 0)
    query_cols = lax.broadcasted_iota(jnp.int32, (tile, tile), 1)

    def attend(blocks, seq):
        rows = rows_of(seq)
        seg_query = all_segs[me, pl.ds(seq, 1)].astype(jnp.float32)
        masks, values_t = [], []
        for block in blocks:
            seg_key = as_column(all_segs[block, pl.ds(seq, 1)].astype(jnp.float32))
            earlier = jnp.where(seg_key < seg_query, 1.0, 0.0)
            starts[seq] += jnp.sum(earlier, axis=0, keepdims=True)
            if block is me:
                same = (seg_key == seg_query) & (key_rows <= query_cols)
                masks.append(jnp.where(same, 1.0, 0.0))
            else:
                masks.append(1.0 - earlier)
            values_t.append(keys_values[block, rows, pl.ds(pair, pair)].T)
        keys = [keys_values[block, rows, pl.ds(0, pair)] for block in blocks]
        mask = jnp.concatenate(masks, axis=0)
        scores = dot_nn(jnp.concatenate(keys, axis=0), query_t[seq])
        weights = jnp.exp(scores) * jnp.concatenate([mask] * 4, axis=1)
        row_sum[seq] += jnp.sum(weights, axis=0, keepdims=True)
        low = weights.astype(jnp.bfloat16)
        value_rows = jnp.concatenate(values_t, axis=1)
        for group in range(2):
            acc[seq, group] += dot_nn(
                value_rows[group * head_dim : (group + 1) * head_dim],
                low[:, group * 2 * tile : (group + 1) * 2 * tile],
            )

    def head_copy(hop, seq, arriving=False):
        sent = (here.wt, here.wt, here.chip_wt)
        landed = (here.chip_wt, here.core_wt, here.far_wt)
        part = all_heads.at[(landed if arriving else sent)[hop], rows_of(seq)]
        device = here.chip if hop == 0 else here.core
        return send_to(
            part, part, ref["head_send"].at[hop, seq], ref["head_recv"].at[hop, seq], device
        )

    def relay(seq):
        head_copy(0, seq, True).wait_recv()
        head_copy(2, seq).start()

    def mix(seq):
        rows = rows_of(seq)
        total = row_sum[seq]
        logs[seq] = jnp.log(total)
        for group in range(2):
            cols = slice(group * 2 * tile, (group + 1) * 2 * tile)
            part = acc[seq, group] / total[:, cols]
            mixed = jnp.concatenate([part[:, :tile], part[:, tile:]], axis=0)
            mixed_t[seq, group] = mixed
            all_heads[here.wt, rows, pl.ds(group * pair, pair)] = mixed.T.astype(jnp.bfloat16)
        head_copy(0, seq).start()
        head_copy(1, seq).start()

    def ffn_unit(rows):
        values = residual[rows, :]
        inverse = lax.rsqrt(jnp.mean(values * values, axis=-1, keepdims=True) + EPS)
        return values * inverse, inverse

    def feed(seq):
        rows = rows_of(seq)
        head_copy(1, seq, True).wait_recv()
        head_copy(2, seq, True).wait_recv()
        total = tokens[rows, :].astype(jnp.float32)
        for slot in range(4):
            total = total + dot_nn(all_heads[slot, rows], all_out[slot])
        residual[rows, :] = total
        unit, unused = ffn_unit(rows)
        normed = (unit * ffn_gain_row).astype(jnp.bfloat16)
        lefts[1, :, rows] = normed.T
        gate = dot_nn(normed, w_gate[...])
        up = dot_nn(normed, w_up[...])
        sigmoid = 0.5 * jnp.tanh(0.5 * gate) + 0.5
        silu = gate * sigmoid
        ffn_grads[0, rows] = (silu * up).astype(jnp.bfloat16)
        grads = grad_hidden[rows, :].astype(jnp.float32)
        grad_gate = (grads * up * sigmoid * (1.0 + gate * (1.0 - sigmoid))).astype(jnp.bfloat16)
        grad_up = (grads * silu).astype(jnp.bfloat16)
        ffn_grads[1, rows] = grad_gate
        ffn_grads[2, rows] = grad_up
        grad_normed = dot_nn(grad_gate, gate_t[...]) + dot_nn(grad_up, up_t[...])
        ffn_gain_part[...] += jnp.sum(grad_normed * unit, axis=0, keepdims=True)
        ffn_sum.offer(seq, grad_normed)

    ffn_gain_part[...] = jnp.zeros_like(ffn_gain_part)

    def sequence_turn(turn_, carry):
        @pl.when(turn_ < sequences)
        def _():
            @pl.when(turn_ + 2 < sequences)
            def _():
                pass_rows(0, turn_ + 2)

            @pl.when(comes_aside(0))
            def _():
                @pl.when(turn_ == 0)
                def _():
                    seg_copy(0, 1, here.beside_ctx).wait_recv()

                side_copy(0, turn_, here.beside_ctx).wait_recv()
                attend([me, here.beside_ctx], turn_)

            @pl.when(jnp.logical_not(comes_aside(0)))
            def _():
                attend([me], turn_)

        @pl.when(turn_ + 1 < sequences)
        def _():
            route(turn_ + 1)

        @pl.when(turn_ == 1)
        def _():
            out_copy(0, True).wait_recv()
            out_copy(2).start()

        @pl.when(turn_ > 0)
        def _():
            relay(turn_ - 1)

        @pl.when(turn_ < sequences)
        def _():
            def level(step, carry):
                @pl.when(me >= 2 * step)
                def _():
                    @pl.when(turn_ == 0)
                    def _():
                        seg_copy(step, 1, here.beside_ctx).wait_recv()

                    side_copy(step, turn_, here.beside_ctx).wait_recv()
                    attend([block_of(me, step), block_of(here.beside_ctx, step)], turn_)

                return carry

            lax.fori_loop(1, levels, level, 0)
            mix(turn_)

        @pl.when(turn_ == 1)
        def _():
            out_copy(1, True).wait_recv()
            out_copy(2, True).wait_recv()

        @pl.when(turn_ > 1)
        def _():
            ffn_sum.cross(turn_ - 2)

        @pl.when(turn_ > 0)
        def _():
            feed(turn_ - 1)

        @pl.when(turn_ > 2)
        def _():
            ffn_sum.close(turn_ - 3)

        return carry

    lax.fori_loop(0, sequences + 1, sequence_turn, 0)
    for i in range(3):
        ffn.tick(i, 0, lefts.at[min(i, 1)], ffn_grads.at[i], first=True)
    rows_all, width = tokens.shape
    last = count - 1
    deltas, own_grads = ref["deltas"], ref["own_grads"]
    side_in, side_out = ref["side_in"], ref["side_out"]
    line_in, line_out = ref["line_in"], ref["line_out"]
    ffn_sums, qkv_total = ref["ffn_sums"], ref["qkv_total"]
    grad_query_t = acc
    grad_res_t = w_gate.at[:, pl.ds(0, rows_all)]
    grad_heads_t = w_gate
    query_n = gate_t.at[pl.ds(0, 4 * tile)]
    grad_heads_n = gate_t.at[pl.ds(4 * tile, 4 * tile)]
    grad_qkv = w_up.at[pl.ds(0, rows_all), pl.ds(0, 4 * pair)]
    normed_t = w_up.at[:, pl.ds(4 * pair, rows_all)]
    qkv_t = up_t.at[pl.ds(rows_all, 4 * pair)]
    heads = all_heads.at[here.wt]
    sources = {
        "output": cotangent,
        "tokens_grad": tokens,
        "w_down_sum": ffn_sums.at[0],
        "w_gate_sum": ffn_sums.at[1],
        "w_up_sum": ffn_sums.at[2],
        "w_query_sum": qkv_total.at[:, pl.ds(0, 2 * pair)],
        "w_key_sum": qkv_total.at[:, pl.ds(2 * pair, pair)],
        "w_value_sum": qkv_total.at[:, pl.ds(3 * pair, pair)],
    }
    stores = Mover(
        [(sources[name] if name in sources else ref[name], ref[name + "_res"]) for name in RESULTS],
        ref["store_sems"],
    )
    wt_sum = WtSum(here, tile, up_t, *shared, ref["wt_send"], ref["wt_recv"], ffn_sum)
    mlp_sum = WtSum(here, tile, grad_hidden, *(ref[f"mlp_sum{i}"] for i in range(5)))
    gains = GainSum(here, *(ref[f"gains{i}"] for i in range(6)))
    gain_slots = ref["gains0"]
    out = Ring(count, *(ref[f"out{i}"] for i in range(3)))
    qkv = Ring(count, *(ref[f"qkv{i}"] for i in range(3)))

    def heads_at(seq):
        start = pl.multiple_of(seq * pair, pair)
        return (pl.ds(start, pair), pl.ds(rows_all, 4 * tile))

    def seq_cols(seq):
        return (slice(None), pl.ds(pl.multiple_of(seq * tile, tile), tile))

    def ffn_tick(index):
        step, which = lax.div(index, 3), lax.rem(index, 3)
        ffn.tick(
            which,
            step,
            lefts.at[lax.min(which, 1)],
            ffn_grads.at[which],
            result=ffn_sums.at[which],
            final=step == last,
        )

    def token_unit(rows):
        inputs = tokens[rows, :].astype(jnp.float32)
        inverse = lax.rsqrt(jnp.mean(inputs * inputs, axis=-1, keepdims=True) + EPS)
        return inputs * inverse, inverse

    def prepare(seq):
        rows = rows_of(seq)
        unit, inverse = ffn_unit(rows)
        scaled = ffn_sum.result(seq) * ffn_gain_row
        back = inverse * (scaled - unit * jnp.mean(scaled * unit, axis=-1, keepdims=True))
        grads = (cotangent[rows, :].astype(jnp.float32) + back).astype(jnp.bfloat16)
        grad_res[rows, :] = grads
        grad_res_t[:, rows] = grads.T
        unit, unused = token_unit(rows)
        normed_t[:, rows] = (unit * gain).astype(jnp.bfloat16).T
        grad_heads_t[heads_at(seq)] = jnp.zeros((pair, 4 * tile), jnp.bfloat16)
        low = dot_nn(grads, ref["w_out"][...]).astype(jnp.bfloat16)
        for group in range(2):
            flipped = low[:, group * pair : (group + 1) * pair].T
            product_t = flipped.astype(jnp.float32) * mixed_t[seq, group]
            for member in range(2):
                part = slice(member * head_dim, (member + 1) * head_dim)
                cols = pl.ds((2 * group + member) * tile, tile)
                into = pl.ds(pl.multiple_of(seq * pair + group * head_dim, head_dim), head_dim)
                spot = pl.ds(rows_all + (2 * group + member) * tile, tile)
                grad_heads_t[into, spot] = flipped[part]
                deltas[seq, :, cols] = jnp.sum(product_t[part], axis=0, keepdims=True)
        grad_heads_n[seq_cols(seq)] = grad_heads_t[heads_at(seq)].T
        query_n[seq_cols(seq)] = query_t[seq].T
        grad_query_t[seq] = jnp.zeros_like(grad_query_t[seq])

    def grads_of(blocks, seq):
        rows = rows_of(seq)
        keys = [keys_values[block, rows, pl.ds(0, pair)] for block in blocks]
        values = [keys_values[block, rows, pl.ds(pair, pair)] for block in blocks]
        masks = []
        for block in blocks:
            allowed = key_rows.astype(jnp.float32) >= starts[seq] - (block * tile).astype(
                jnp.float32
            )
            if block is me:
                allowed = allowed & (key_rows <= query_cols)
            masks.append(jnp.where(allowed, 1.0, 0.0))
        mask = jnp.concatenate(masks, axis=0)
        grad_heads = grad_heads_t[heads_at(seq)]
        scores = dot_nn(jnp.concatenate(keys, axis=0), query_t[seq])
        probs = jnp.exp(scores - logs[seq]) * jnp.concatenate([mask] * 4, axis=1)
        grad_probs = dot_nn(jnp.concatenate(values, axis=0), grad_heads)
        grad_scores = (probs * (grad_probs - deltas[seq])).astype(jnp.bfloat16)
        flipped = jnp.concatenate([part.T for part in keys], axis=1)
        for group in range(2):
            cols = slice(group * 2 * tile, (group + 1) * 2 * tile)
            grad_query_t[seq, group] += dot_nn(
                flipped[group * head_dim : (group + 1) * head_dim], grad_scores[:, cols]
            )
        grad_keys = dot_nn(grad_scores, query_n[seq_cols(seq)])
        grad_values = dot_nn(probs.astype(jnp.bfloat16), grad_heads_n[seq_cols(seq)])
        both = jnp.concatenate([grad_keys, grad_values], axis=1)
        return [both[i * tile : (i + 1) * tile] for i in range(len(blocks))]

    def side_grad_copy(step, seq):
        return send_to(
            side_out.at[step, rows_of(seq)],
            side_in.at[step, rows_of(seq)],
            ref["side_grad_send"].at[step, seq],
            ref["side_grad_recv"].at[step, seq],
            here.beside,
        )

    def line_copy(step, seq):
        earlier = step - 1
        return send_to(
            line_out.at[earlier, rows_of(seq)],
            line_in.at[earlier, rows_of(seq)],
            ref["line_send"].at[earlier, seq],
            ref["line_recv"].at[earlier, seq],
            here.below,
        )

    def find_grads(seq):
        rows = rows_of(seq)

        def level(index, carry):
            step = levels - 1 - index

            @pl.when(me >= 2 * step)
            def _():
                line, side = grads_of(
                    [block_of(me, step), block_of(here.beside_ctx, step)], seq
                )
                side_out[step, rows] = side.astype(jnp.bfloat16)
                side_grad_copy(step, seq).start()
                line_out[step - 1, rows] = line.astype(jnp.bfloat16)

            return carry

        lax.fori_loop(0, levels - 1, level, 0)

        @pl.when(comes_aside(0))
        def _():
            own, side = grads_of([me, here.beside_ctx], seq)
            side_out[0, rows] = side.astype(jnp.bfloat16)
            side_grad_copy(0, seq).start()
            own_grads[rows, :] = own

        @pl.when(jnp.logical_not(comes_aside(0)))
        def _():
            own_grads[rows, :] = grads_of([me], seq)[0]

    def send_down(step, seq):
        @pl.when(me >= 2 * step)
        def _():
            rows = rows_of(seq)
            side_grad_copy(step, seq).wait_recv()
            total = line_out[step - 1, rows].astype(jnp.float32) + side_in[step, rows].astype(
                jnp.float32
            )

            @pl.when(here.has_above)
            def _():
                line_copy(step + 1, seq).wait_recv()
                line_out[step - 1, rows] = (
                    total + line_in[step, rows].astype(jnp.float32)
                ).astype(jnp.bfloat16)

            @pl.when(jnp.logical_not(here.has_above))
            def _():
                line_out[step - 1, rows] = total.astype(jnp.bfloat16)

            line_copy(step, seq).start()

    gain_slots[me] = jnp.zeros_like(gain_slots[me])
    gain_slots[me, pl.ds(1, 1)] = ffn_gain_part[...]

    def back_through(grads, raw, gain_pair, row):
        cosine = table[:, pl.ds(0, pair)]
        sine = table[:, pl.ds(pair, pair)]
        turned = grads * cosine - swap_halves(grads, head_dim) * sine
        unit, inverse = pair_norm(raw, head_dim)
        gain_slots[me, pl.ds(row, 1), pl.ds(0, pair)] += jnp.sum(
            turned * unit, axis=0, keepdims=True
        )
        scaled = turned * gain_pair
        return (inverse * (scaled - unit * pair_mean(scaled * unit, head_dim))).astype(
            jnp.bfloat16
        )

    def project_back(seq):
        rows = rows_of(seq)
        for group in range(2):
            grads = grad_query_t[seq, group] * (head_dim**-0.5)
            grads = jnp.concatenate([grads[:, :tile], grads[:, tile:]], axis=0).T
            cols = pl.ds(group * pair, pair)
            grad_qkv[rows, cols] = back_through(grads, query_raw[rows, cols], q_gain_pair, 2)

        @pl.when(me < here.beside_ctx)
        def _():
            side_grad_copy(0, seq).wait_recv()
            own_grads[rows, :] += side_in[0, rows].astype(jnp.float32)

        @pl.when(here.has_above)
        def _():
            line_copy(1, seq).wait_recv()
            own_grads[rows, :] += line_in[0, rows].astype(jnp.float32)

        grad_qkv[rows, pl.ds(2 * pair, pair)] = back_through(
            own_grads[rows, pl.ds(0, pair)], key_raw[rows, :], k_gain_pair, 3
        )
        grad_qkv[rows, pl.ds(3 * pair, pair)] = own_grads[rows, pl.ds(pair, pair)].astype(
            jnp.bfloat16
        )
        grads = dot_nn(grad_qkv[rows, :], qkv_t[...])
        unit, unused = token_unit(rows)
        gain_slots[me, pl.ds(0, 1)] += jnp.sum(grads * unit, axis=0, keepdims=True)
        wt_sum.offer(seq, grads)

    def output_rows(seq):
        rows = rows_of(seq)
        cotangent[rows, :] = (residual[rows, :] + mlp_sum.result(seq)).astype(jnp.bfloat16)

    def token_rows(seq):
        rows = rows_of(seq)
        unit, inverse = token_unit(rows)
        scaled = wt_sum.result(seq) * gain
        grads = inverse * (scaled - unit * jnp.mean(scaled * unit, axis=-1, keepdims=True))
        tokens[rows, :] = (grad_res[rows, :].astype(jnp.float32) + grads).astype(
            jnp.bfloat16
        )

    qkv_t[pl.ds(0, 2 * pair), :] = ref["w_query"][...].T
    qkv_t[pl.ds(2 * pair, pair), :] = ref["w_key"][...].T
    qkv_t[pl.ds(3 * pair, pair), :] = ref["w_value"][...].T
    ffn_sum.cross(sequences - 1)

    def grad_turn(turn_, carry):
        @pl.when(turn_ + 1 < sequences)
        def _():
            prepare(turn_ + 1)
            find_grads(turn_ + 1)

        @pl.when((turn_ == 0) | (turn_ == 1))
        def _():
            ffn_sum.close(sequences - 2 + turn_)

        @pl.when((turn_ >= 0) & (turn_ < sequences))
        def _():
            def down(index, carry):
                send_down(levels - 1 - index, turn_)
                return carry

            lax.fori_loop(0, levels - 1, down, 0)
            mlp_sum.offer(turn_, dot_nt(ffn_grads[0, rows_of(turn_)], w_down[...]))

        for i in range(TURN_TICKS):
            ffn_tick(3 + TURN_TICKS * (turn_ + 1) + i)

        @pl.when((turn_ >= 1) & (turn_ <= sequences))
        def _():
            mlp_sum.cross(turn_ - 1)

        @pl.when(turn_ == sequences)
        def _():
            out.tick(0, 0, grad_res_t, heads, first=True)

        @pl.when(turn_ == sequences + 1)
        def _():
            out.tick(0, 1, grad_res_t, heads)

        @pl.when(turn_ >= 2)
        def _():
            project_back(turn_ - 2)
            mlp_sum.close(turn_ - 2)

        @pl.when(turn_ >= 3)
        def _():
            wt_sum.cross(turn_ - 3)
            output_rows(turn_ - 3)

        return carry

    turns = sequences + 3
    lax.fori_loop(-1, turns - 1, grad_turn, 0)
    qkv.tick(0, 0, normed_t, grad_qkv, first=True)
    gains.start()
    wt_sum.cross(sequences - 1)
    output_rows(sequences - 1)
    stores.start(0)
    done = 3 + TURN_TICKS * turns
    left_over = 3 * count - done
    each = -(-left_over // (last - 1))

    def tail(step, carry):
        for i in range(each):
            index = done + each * (step - 1) + i

            @pl.when(index < 3 * count)
            def _():
                ffn_tick(index)

        qkv.tick(0, step, normed_t, grad_qkv)

        @pl.when(step < last)
        def _():
            out.tick(
                0, step + 1, grad_res_t, heads, result=ref["w_out_sum"], final=step + 1 == last
            )

        @pl.when(step <= sequences)
        def _():
            wt_sum.close(step - 1)

        @pl.when((step >= 2) & (step <= sequences + 1))
        def _():
            token_rows(step - 2)

        return carry

    middle = min(4, last)
    lax.fori_loop(1, middle, tail, 0)
    total = gains.total()
    ref["attn_gain_sum"][...] = total[0:1]
    ref["ffn_gain_sum"][...] = total[1:2]
    folded = total[:, :pair]
    folded = folded + pltpu.roll(folded, head_dim, 1)
    ref["q_gain_sum"][...] = folded[2:3]
    ref["k_gain_sum"][...] = folded[3:4]
    stores.start(9, 10, 11, 12)
    lax.fori_loop(middle, last, tail, 0)
    stores.start(1, 2, 3, 4, 5)
    qkv.tick(0, last, normed_t, grad_qkv, result=qkv_total)
    stores.start(6, 7, 8)
    ffn_sum.finish(sequences, (0,))
    wt_sum.finish(sequences)
    mlp_sum.finish(sequences)
    for i in range(3):
        ffn.finish(i, last)
    out.finish(0, last)
    qkv.finish(0, last)
    for hop in range(3):
        out_copy(hop).wait_send()

        def sent(seq, carry):
            head_copy(hop, seq).wait_send()
            return carry

        lax.fori_loop(0, sequences, sent, 0)

    def each_seq(step):
        def one(seq, carry):
            step(seq)
            return carry

        lax.fori_loop(0, sequences, one, 0)

    def drain(step, carry):
        @pl.when(goes_up(step))
        def _():
            seg_copy(step, 0).wait_send()
            each_seq(lambda seq: up_copy(step, seq).wait_send())

        @pl.when(goes_aside(step))
        def _():
            seg_copy(step, 1).wait_send()
            each_seq(lambda seq: side_copy(step, seq).wait_send())

        @pl.when(comes_aside(step))
        def _():
            each_seq(lambda seq: side_grad_copy(step, seq).wait_send())

        @pl.when((step > 0) & (me >= 2 * step))
        def _():
            each_seq(lambda seq: line_copy(step, seq).wait_send())

        return carry

    lax.fori_loop(0, levels, drain, 0)
    stores.wait(*range(len(RESULTS)))


def layer(inputs):
    count = lax.axis_size("ctx")
    sequences, tile = inputs["segments"].shape
    rows, width = inputs["tokens_in"].shape
    head_dim = inputs["q_gain"].shape[0]
    hidden = inputs["w_gate_in"].shape[1]
    pair = 2 * head_dim
    levels = count // 2
    block = width // count
    f32, bf16 = jnp.float32, jnp.bfloat16
    dma = pltpu.SemaphoreType.DMA
    results = {
        "output": ((rows, width), bf16),
        "tokens_grad": ((rows, width), bf16),
        "w_down_sum": ((block, hidden), f32),
        "w_gate_sum": ((block, hidden), f32),
        "w_up_sum": ((block, hidden), f32),
        "w_out_sum": ((block, 2 * pair), f32),
        "w_query_sum": ((block, 2 * pair), f32),
        "w_key_sum": ((block, pair), f32),
        "w_value_sum": ((block, pair), f32),
        "attn_gain_sum": ((1, width), f32),
        "ffn_gain_sum": ((1, width), f32),
        "q_gain_sum": ((1, pair), f32),
        "k_gain_sum": ((1, pair), f32),
    }
    staged = ("w_out_sum",) + RESULTS[9:]
    scratch = {name: pltpu.VMEM(*results[name]) for name in staged}
    buffers = {
        "tokens": ((rows, width), bf16),
        "residual": ((rows, width), f32),
        "mixed_t": ((sequences, 2, pair, tile), f32),
        "query_t": ((sequences, pair, 4 * tile), bf16),
        "logs": ((sequences, 1, 4 * tile), f32),
        "starts": ((sequences, 1, tile), f32),
        "keys_values": ((count, rows, 2 * pair), bf16),
        "query_raw": ((rows, 2 * pair), f32),
        "key_raw": ((rows, pair), f32),
        "lefts": ((2, width, rows), bf16),
        "ffn_grads": ((3, rows, hidden), bf16),
        "ffn_gain_part": ((1, width), f32),
        "grad_res": ((rows, width), bf16),
        "all_segs": ((count, 8, tile), jnp.int32),
        "all_out": ((4, 2 * pair, width), bf16),
        "all_heads": ((4, rows, 2 * pair), bf16),
        "acc": ((sequences, 2, head_dim, 2 * tile), f32),
        "row_sum": ((sequences, 1, 4 * tile), f32),
        "table": ((tile, 2 * pair), f32),
        "cotangent": ((rows, width), bf16),
        "w_down": ((width, hidden), bf16),
        "w_gate": ((width, hidden), bf16),
        "w_up": ((width, hidden), bf16),
        "gate_t": ((hidden, width), bf16),
        "up_t": ((hidden, width), bf16),
        "grad_hidden": ((rows, hidden), bf16),
        "ffn_part": ((rows, width), bf16),
        "sum_got": ((rows, width // 2), bf16),
        "sum_far": ((rows, width // 2), bf16),
        "sum_full": ((2, rows, width // 2), bf16),
        "mlp_sum0": ((rows, width // 2), bf16),
        "mlp_sum1": ((rows, width // 2), bf16),
        "mlp_sum2": ((2, rows, width // 2), bf16),
        "deltas": ((sequences, 1, 4 * tile), f32),
        "own_grads": ((rows, 2 * pair), f32),
        "side_in": ((levels, rows, 2 * pair), bf16),
        "side_out": ((levels, rows, 2 * pair), bf16),
        "line_in": ((levels - 1, rows, 2 * pair), bf16),
        "line_out": ((levels - 1, rows, 2 * pair), bf16),
        "ffn_sums": ((3, block, hidden), f32),
        "qkv_total": ((block, 4 * pair), f32),
        "gains0": ((count, 8, width), f32),
        "gains1": ((2, 2, 8, width), f32),
    }
    scratch |= {name: pltpu.VMEM(*spec) for name, spec in buffers.items()}
    semaphores = {
        "load_sems": (6,),
        "store_sems": (len(RESULTS),),
        "up_send": (levels, sequences),
        "up_recv": (levels, sequences),
        "side_send": (levels, sequences),
        "side_recv": (levels, sequences),
        "seg_send": (levels, 2),
        "seg_recv": (levels, 2),
        "out_send": (3,),
        "out_recv": (3,),
        "head_send": (3, sequences),
        "head_recv": (3, sequences),
        "ffn_send": (3, sequences),
        "ffn_recv": (3, sequences),
        "wt_send": (3, sequences),
        "wt_recv": (3, sequences),
        "mlp_sum3": (3, sequences),
        "mlp_sum4": (3, sequences),
        "side_grad_send": (levels, sequences),
        "side_grad_recv": (levels, sequences),
        "line_send": (levels - 1, sequences),
        "line_recv": (levels - 1, sequences),
        "gains2": (count - 1,),
        "gains3": (count - 1,),
        "gains4": (2,),
        "gains5": (2,),
    }
    scratch |= {name: dma(shape) for name, shape in semaphores.items()}
    for label, kinds in (
        ("ffn", ring_scratch(count, 3, block, hidden)),
        ("out", ring_scratch(count, 1, block, 2 * pair)),
        ("qkv", ring_scratch(count, 1, block, 4 * pair)),
    ):
        scratch |= {f"{label}{i}": kind for i, kind in enumerate(kinds)}
    vmem, anywhere = pl.BlockSpec(memory_space=pltpu.VMEM), pl.BlockSpec(memory_space=pl.ANY)
    names = (*inputs, *(name + "_res" for name in RESULTS), *scratch)
    arrays = pl.pallas_call(
        partial(layer_kernel, count, names),
        out_shape=[jax.ShapeDtypeStruct(*results[name]) for name in RESULTS],
        in_specs=[anywhere if name.endswith("_in") else vmem for name in inputs],
        out_specs=[anywhere] * len(RESULTS),
        scratch_shapes=list(scratch.values()),
        compiler_params=pltpu.CompilerParams(
            collective_id=2, has_side_effects=True, vmem_limit_bytes=VMEM_LIMIT
        ),
    )(*inputs.values())
    return dict(zip(RESULTS, arrays, strict=True))


def hand_over_kernel(count, *refs):
    sources, targets, staged = refs[:count], refs[count : 2 * count], refs[2 * count : 3 * count]
    loads = Mover(list(zip(sources, staged, strict=True)), refs[3 * count])
    stores = Mover(list(zip(staged, targets, strict=True)), refs[3 * count + 1])
    loads.start(*range(count))
    for i in range(count):
        loads.wait(i)
        stores.start(i)
    stores.wait(*range(count))


def hand_over(arrays):
    anywhere = pl.BlockSpec(memory_space=pl.ANY)
    dma = pltpu.SemaphoreType.DMA((len(arrays),))
    return pl.pallas_call(
        partial(hand_over_kernel, len(arrays)),
        out_shape=[jax.ShapeDtypeStruct(array.shape, array.dtype) for array in arrays],
        in_specs=[anywhere] * len(arrays),
        out_specs=[anywhere] * len(arrays),
        scratch_shapes=[pltpu.VMEM(array.shape, array.dtype) for array in arrays] + [dma, dma],
        compiler_params=pltpu.CompilerParams(vmem_limit_bytes=60 * MIB),
    )(*arrays)


def rotary_table(length, head_dim):
    half = head_dim // 2
    frequency = THETA ** (-2.0 * np.arange(half) / head_dim)
    angles = np.arange(length)[:, None] * frequency[None, :]
    cosine, sine = np.cos(angles), np.sin(angles)
    return np.concatenate([cosine] * 4 + [-sine, sine] * 2, axis=1).astype(np.float32)


def kernels_fit(tokens, w_query, key_matrix, q_gain, w_gate):
    sequences, tile, width = tokens.shape
    count, head_dim = lax.axis_size("ctx"), q_gain.shape[0]
    return (
        lax.axis_size("wt") == 4
        and count % 2 == 0
        and count >= 4
        and tile == 128
        and sequences <= 8
        and sequences * count <= 40
        and head_dim == 64
        and w_query.shape[1] == 4 * head_dim
        and key_matrix.shape[1] == 2 * head_dim
        and width % (128 * count) == 0
        and w_gate.shape[1] >= max(width, sequences * tile + 512)
        and w_gate.shape[1] <= 1152
        and width <= 1024
    )


def on_device_plain(
    tokens,
    segments,
    attn_gain,
    w_query,
    key_matrix,
    value_matrix,
    q_gain,
    k_gain,
    w_out,
    ffn_gain,
    w_gate,
    w_up,
    w_down,
    cotangent,
):
    sequences, seq_rows, model_width = tokens.shape
    head_dim = q_gain.shape[0]
    q_local = w_query.shape[1] // head_dim
    kv_local = key_matrix.shape[1] // head_dim
    per_group = q_local // kv_local
    score_scale = 1.0 / math.sqrt(head_dim)
    all_rows = sequences * seq_rows
    places = lax.axis_index("ctx") * seq_rows + jnp.arange(seq_rows, dtype=jnp.int32)
    frequency = THETA ** (-jnp.arange(0, head_dim, 2, dtype=jnp.float32) / head_dim)
    angles = places.astype(jnp.float32)[None, :, None] * frequency
    cosine_table = jnp.cos(angles)[:, :, None, :]
    sine_table = jnp.sin(angles)[:, :, None, :]
    inputs = tokens.astype(jnp.float32).reshape(all_rows, model_width)
    normed, attn_unit, attn_inverse = norm_rows(inputs, attn_gain)
    normed_low = normed.astype(jnp.bfloat16)
    query_raw = product(normed_low, w_query).reshape(sequences, seq_rows, q_local, head_dim)
    key_raw = product(normed_low, key_matrix).reshape(sequences, seq_rows, kv_local, head_dim)
    value_low = (
        product(normed_low, value_matrix)
        .astype(jnp.bfloat16)
        .reshape(sequences, seq_rows, kv_local * head_dim)
    )
    query_normed, query_unit, query_inverse = norm_rows(query_raw, q_gain)
    key_normed, key_unit, key_inverse = norm_rows(key_raw, k_gain)
    query_low = rotate(query_normed, cosine_table, sine_table, 1.0).astype(jnp.bfloat16)
    key_low = rotate(key_normed, cosine_table, sine_table, 1.0).astype(jnp.bfloat16)
    key_flat = key_low.reshape(sequences, seq_rows, kv_local * head_dim)
    query_groups = query_low.reshape(sequences, seq_rows, kv_local, per_group, head_dim)
    attend = partial(
        attend_piece,
        queries=query_groups,
        query_places=places,
        query_segs=segments,
        score_scale=score_scale,
    )
    start_state = (
        jnp.full((sequences, kv_local, per_group, seq_rows), NEG, jnp.float32),
        jnp.zeros((sequences, kv_local, per_group, seq_rows), jnp.float32),
        jnp.zeros((sequences, seq_rows, kv_local, per_group, head_dim), jnp.float32),
    )
    keys_values = lax.all_gather(
        jnp.concatenate([key_flat, value_low], axis=-1), "ctx", axis=1, tiled=True
    )
    kv_width = kv_local * head_dim
    gathered = (
        keys_values[..., :kv_width],
        keys_values[..., kv_width:],
        lax.all_gather(segments, "ctx", axis=1, tiled=True),
    )
    row_max, row_sum, weighted = attend(
        start_state,
        gathered,
        jnp.int32(0),
    )
    mixed_heads = weighted / jnp.transpose(row_sum, (0, 3, 1, 2))[..., None]
    mixed_low = mixed_heads.astype(jnp.bfloat16).reshape(all_rows, q_local * head_dim)
    attn_term = by_transpose(mixed_low, w_out)
    residual = inputs + lax.psum(attn_term.astype(jnp.bfloat16), "wt").astype(jnp.float32)
    normed_ffn, ffn_unit, ffn_inverse = norm_rows(residual, ffn_gain)
    normed_ffn_low = normed_ffn.astype(jnp.bfloat16)
    gate_proj = product(normed_ffn_low, w_gate)
    up_proj = product(normed_ffn_low, w_up)
    gate_sigmoid = jax.nn.sigmoid(gate_proj)
    gate_silu = gate_proj * gate_sigmoid
    hidden_low = (gate_silu * up_proj).astype(jnp.bfloat16)
    mlp_term = by_transpose(hidden_low, w_down)
    output_rows = (
        residual + lax.psum(mlp_term.astype(jnp.bfloat16), "wt").astype(jnp.float32)
    ).astype(jnp.bfloat16)
    log_total = row_max + jnp.log(row_sum)
    grad_rows = cotangent.reshape(all_rows, model_width)
    grad_hidden = product(grad_rows, w_down)
    grad_gate = (
        grad_hidden * up_proj * gate_sigmoid * (1.0 + gate_proj * (1.0 - gate_sigmoid))
    ).astype(jnp.bfloat16)
    grad_up = (grad_hidden * gate_silu).astype(jnp.bfloat16)
    grad_normed_ffn = by_transpose(grad_gate, w_gate) + by_transpose(grad_up, w_up)
    ffn_gain_part = jnp.sum(grad_normed_ffn * ffn_unit, axis=0)
    grad_normed_ffn = lax.psum(grad_normed_ffn.astype(jnp.bfloat16), "wt").astype(jnp.float32)
    grad_residual = grad_rows.astype(jnp.float32) + norm_back(
        grad_normed_ffn, ffn_unit, ffn_inverse, ffn_gain
    )
    grad_residual_low = grad_residual.astype(jnp.bfloat16)
    grad_heads_low = product(grad_residual_low, w_out).astype(jnp.bfloat16)
    grad_groups = grad_heads_low.reshape(sequences, seq_rows, kv_local, per_group, head_dim)
    delta_rows = jnp.sum(grad_groups.astype(jnp.float32) * mixed_heads, axis=-1)
    delta_cols = jnp.transpose(delta_rows, (0, 2, 3, 1))
    query_grad_fn = partial(
        grad_piece,
        queries=query_groups,
        grad_heads=grad_groups,
        log_total=log_total,
        row_delta=delta_cols,
        query_places=places,
        query_segs=segments,
        score_scale=score_scale,
    )
    grad_query, grad_pairs = query_grad_fn(
        jnp.zeros((sequences, seq_rows, kv_local, per_group, head_dim), jnp.float32),
        gathered,
        jnp.int32(0),
    )
    grad_pairs = lax.psum_scatter(grad_pairs, "ctx", scatter_dimension=1, tiled=True).astype(
        jnp.float32
    )
    grad_key = grad_pairs[:, :, 0]
    grad_value = grad_pairs[:, :, 1]
    grad_query = rotate(
        grad_query.reshape(sequences, seq_rows, q_local, head_dim) * score_scale,
        cosine_table,
        sine_table,
        -1.0,
    )
    grad_key = rotate(grad_key * score_scale, cosine_table, sine_table, -1.0)
    q_gain_part = jnp.sum(grad_query * query_unit, axis=(0, 1, 2))
    k_gain_part = jnp.sum(grad_key * key_unit, axis=(0, 1, 2))
    grad_query_low = (
        norm_back(grad_query, query_unit, query_inverse, q_gain)
        .astype(jnp.bfloat16)
        .reshape(all_rows, q_local * head_dim)
    )
    grad_key_low = (
        norm_back(grad_key, key_unit, key_inverse, k_gain)
        .astype(jnp.bfloat16)
        .reshape(all_rows, kv_local * head_dim)
    )
    grad_value_low = grad_value.astype(jnp.bfloat16).reshape(all_rows, kv_local * head_dim)
    grad_normed = (
        by_transpose(grad_query_low, w_query)
        + by_transpose(grad_key_low, key_matrix)
        + by_transpose(grad_value_low, value_matrix)
    )
    attn_gain_part = jnp.sum(grad_normed * attn_unit, axis=0)
    grad_normed = lax.psum(grad_normed.astype(jnp.bfloat16), "wt").astype(jnp.float32)
    tokens_rows = (
        grad_residual + norm_back(grad_normed, attn_unit, attn_inverse, attn_gain)
    ).astype(jnp.bfloat16)
    output = output_rows.reshape(sequences, seq_rows, model_width)
    tokens_grad = tokens_rows.reshape(sequences, seq_rows, model_width)
    partial_sums = (
        transpose_by(grad_rows, hidden_low),
        transpose_by(normed_ffn_low, grad_gate),
        transpose_by(normed_ffn_low, grad_up),
        transpose_by(grad_residual_low, mixed_low),
        transpose_by(normed_low, grad_query_low),
        transpose_by(normed_low, grad_key_low),
        transpose_by(normed_low, grad_value_low),
    )
    summed = [
        lax.psum_scatter(part.astype(jnp.bfloat16), "ctx", scatter_dimension=0, tiled=True).astype(
            jnp.float32
        )
        for part in partial_sums
    ]
    w_down_grad, w_gate_grad, w_up_grad, w_out_grad = summed[:4]
    w_query_grad, w_key_grad, w_value_grad = summed[4:]
    attn_gain_grad, q_gain_grad, k_gain_grad, ffn_gain_grad = lax.psum(
        (attn_gain_part, q_gain_part, k_gain_part, ffn_gain_part), ("ctx", "wt")
    )
    return (
        output,
        tokens_grad,
        attn_gain_grad,
        w_query_grad,
        w_key_grad,
        w_value_grad,
        q_gain_grad,
        k_gain_grad,
        w_out_grad,
        ffn_gain_grad,
        w_gate_grad,
        w_up_grad,
        w_down_grad,
    )


def on_device(
    tokens,
    segments,
    attn_gain,
    w_query,
    key_matrix,
    value_matrix,
    q_gain,
    k_gain,
    w_out,
    ffn_gain,
    w_gate,
    w_up,
    w_down,
    cotangent,
):
    if not kernels_fit(tokens, w_query, key_matrix, q_gain, w_gate):
        return on_device_plain(
            tokens,
            segments,
            attn_gain,
            w_query,
            key_matrix,
            value_matrix,
            q_gain,
            k_gain,
            w_out,
            ffn_gain,
            w_gate,
            w_up,
            w_down,
            cotangent,
        )
    sequences, seq_rows, model_width = tokens.shape
    count, head_dim = lax.axis_size("ctx"), q_gain.shape[0]
    token_rows = tokens.reshape(sequences * seq_rows, model_width)
    table = jnp.asarray(rotary_table(count * seq_rows, head_dim))
    gains = {"attn_gain": attn_gain, "q_gain": q_gain, "k_gain": k_gain}
    sums = layer(
        {
            "segments": segments,
            **gains,
            "ffn_gain": ffn_gain,
            "w_query": w_query,
            "w_key": key_matrix,
            "w_value": value_matrix,
            "w_out": w_out,
            "tokens_in": token_rows,
            "table_in": table,
            "cotangent_in": cotangent.reshape(token_rows.shape),
            "w_down_in": w_down,
            "w_gate_in": w_gate,
            "w_up_in": w_up,
        }
    )
    done = dict(zip(RESULTS, hand_over([sums[name] for name in RESULTS]), strict=True))
    return (
        done["output"].reshape(tokens.shape),
        done["tokens_grad"].reshape(tokens.shape),
        done["attn_gain_sum"][0],
        done["w_query_sum"],
        done["w_key_sum"],
        done["w_value_sum"],
        done["q_gain_sum"][0, :head_dim],
        done["k_gain_sum"][0, :head_dim],
        done["w_out_sum"],
        done["ffn_gain_sum"][0],
        done["w_gate_sum"],
        done["w_up_sum"],
        done["w_down_sum"],
    )


def solution(mesh):
    in_specs = (
        P(None, "ctx", None),
        P(None, "ctx"),
        P(),
        P(None, "wt"),
        P(None, "wt"),
        P(None, "wt"),
        P(),
        P(),
        P(None, "wt"),
        P(),
        P(None, "wt"),
        P(None, "wt"),
        P(None, "wt"),
        P(None, "ctx", None),
    )
    out_specs = (
        P(None, "ctx", None),
        P(None, "ctx", None),
        P(),
        P("ctx", "wt"),
        P("ctx", "wt"),
        P("ctx", "wt"),
        P(),
        P(),
        P("ctx", "wt"),
        P(),
        P("ctx", "wt"),
        P("ctx", "wt"),
        P("ctx", "wt"),
    )
    return jax.shard_map(
        on_device, mesh=mesh, in_specs=in_specs, out_specs=out_specs, check_vma=False
    )
```

```python
from functools import partial
import math

import jax
import jax.numpy as jnp
import numpy as np
from jax import lax
from jax.experimental import pallas as pl
from jax.experimental.pallas import tpu as pltpu
from jax.sharding import PartitionSpec as P

EPS = 1e-05
THETA = 1000000.0
NEG = -1e30


def product(left, right):
    return jnp.dot(left, right, preferred_element_type=jnp.float32)


def by_transpose(left, right):
    return lax.dot_general(
        left, right, (((1,), (1,)), ((), ())), preferred_element_type=jnp.float32
    )


def transpose_by(left, right):
    return lax.dot_general(
        left, right, (((0,), (0,)), ((), ())), preferred_element_type=jnp.float32
    )


def norm_rows(values, gain):
    inverse = lax.rsqrt(jnp.mean(values * values, axis=-1, keepdims=True) + EPS)
    unit_rows = values * inverse
    return (unit_rows * gain, unit_rows, inverse)


def norm_back(grads, unit_rows, inverse, gain):
    scaled = grads * gain
    return inverse * (scaled - unit_rows * jnp.mean(scaled * unit_rows, axis=-1, keepdims=True))


def rotate(values, cosine_table, sine_table, direction):
    half_dim = values.shape[-1] // 2
    first_half = values[..., :half_dim]
    second_half = values[..., half_dim:]
    return jnp.concatenate(
        [
            first_half * cosine_table - direction * second_half * sine_table,
            second_half * cosine_table + direction * first_half * sine_table,
        ],
        axis=-1,
    )


def split_blocks(array, block_len):
    shaped = array.reshape(
        (array.shape[0], array.shape[1] // block_len, block_len) + array.shape[2:]
    )
    return jnp.moveaxis(shaped, 1, 0)


def attend_piece(folded, pieces, first_row, queries, query_places, query_segs, score_scale):
    key_piece, value_piece, seg_piece = pieces
    sequences, piece_rows = seg_piece.shape
    kv_local = queries.shape[2]
    head_dim = queries.shape[4]
    block_len = math.gcd(piece_rows, 512)
    key_blocks = split_blocks(
        key_piece.reshape(sequences, piece_rows, kv_local, head_dim), block_len
    )
    value_tiles = split_blocks(
        value_piece.reshape(sequences, piece_rows, kv_local, head_dim), block_len
    )
    seg_blocks = split_blocks(seg_piece, block_len)
    offsets = block_len * jnp.arange(piece_rows // block_len, dtype=jnp.int32)

    def attend_block_step(running, block_item):
        row_max, row_sum, weighted = running
        key_block, value_block, seg_block, offset = block_item
        key_places = offset + jnp.arange(block_len, dtype=jnp.int32)
        allowed = (key_places[None, None, :] <= query_places[None, :, None]) & (
            query_segs[:, :, None] == seg_block[:, None, :]
        )
        allowed = allowed[:, None, None]
        scores = (
            jnp.einsum("sqgrd,skgd->sgrqk", queries, key_block, preferred_element_type=jnp.float32)
            * score_scale
        )
        scores = jnp.where(allowed, scores, NEG)
        new_max = jnp.maximum(row_max, jnp.max(scores, axis=-1))
        weights = jnp.where(allowed, jnp.exp(scores - new_max[..., None]), 0.0)
        fading = jnp.exp(row_max - new_max)
        row_sum = row_sum * fading + jnp.sum(weights, axis=-1)
        fade_rows = jnp.transpose(fading, (0, 3, 1, 2))[..., None]
        weighted = weighted * fade_rows + jnp.einsum(
            "sgrqk,skgd->sqgrd",
            weights.astype(jnp.bfloat16),
            value_block,
            preferred_element_type=jnp.float32,
        )
        return ((new_max, row_sum, weighted), None)

    folded, unused = lax.scan(
        attend_block_step, folded, (key_blocks, value_tiles, seg_blocks, offsets)
    )
    return folded


def grad_piece(
    folded,
    pieces,
    first_row,
    queries,
    grad_heads,
    log_total,
    row_delta,
    query_places,
    query_segs,
    score_scale,
):
    key_piece, value_piece, seg_piece = pieces
    sequences, piece_rows = seg_piece.shape
    kv_local = queries.shape[2]
    head_dim = queries.shape[4]
    block_len = math.gcd(piece_rows, 512)
    key_blocks = split_blocks(
        key_piece.reshape(sequences, piece_rows, kv_local, head_dim), block_len
    )
    value_tiles = split_blocks(
        value_piece.reshape(sequences, piece_rows, kv_local, head_dim), block_len
    )
    seg_blocks = split_blocks(seg_piece, block_len)
    offsets = block_len * jnp.arange(piece_rows // block_len, dtype=jnp.int32)

    def grad_block_step(running, block_item):
        key_block, value_block, seg_block, offset = block_item
        key_places = offset + jnp.arange(block_len, dtype=jnp.int32)
        allowed = (key_places[None, None, :] <= query_places[None, :, None]) & (
            query_segs[:, :, None] == seg_block[:, None, :]
        )
        allowed = allowed[:, None, None]
        scores = (
            jnp.einsum("sqgrd,skgd->sgrqk", queries, key_block, preferred_element_type=jnp.float32)
            * score_scale
        )
        probs = jnp.where(allowed, jnp.exp(scores - log_total[..., None]), 0.0)
        grad_probs = jnp.einsum(
            "sqgrd,skgd->sgrqk", grad_heads, value_block, preferred_element_type=jnp.float32
        )
        grad_scores = (probs * (grad_probs - row_delta[..., None])).astype(jnp.bfloat16)
        running = running + jnp.einsum(
            "sgrqk,skgd->sqgrd", grad_scores, key_block, preferred_element_type=jnp.float32
        )
        grad_keys = jnp.einsum(
            "sgrqk,sqgrd->skgd", grad_scores, queries, preferred_element_type=jnp.float32
        )
        grad_values = jnp.einsum(
            "sgrqk,sqgrd->skgd",
            probs.astype(jnp.bfloat16),
            grad_heads,
            preferred_element_type=jnp.float32,
        )
        grads = jnp.stack([grad_keys, grad_values], axis=2).astype(jnp.bfloat16)
        return (running, grads)

    folded, grads = lax.scan(
        grad_block_step, folded, (key_blocks, value_tiles, seg_blocks, offsets)
    )
    return folded, jnp.moveaxis(grads, 0, 1).reshape((sequences, piece_rows) + grads.shape[3:])


MESH = pl.DeviceIdType.MESH
MIB = 1 << 20


def ring_place(index, count):
    return lax.select(
        lax.rem(index, 2) == 0, lax.div(index, 2), count - 1 - lax.div(index, 2)
    )


def ring_index(place, count):
    place = lax.rem(place + 2 * count, count)
    return lax.select(
        place < lax.div(count, 2), 2 * place, 2 * (count - 1 - place) + 1
    )


class Ring:
    def __init__(self, count, slots, send_sems, recv_sems, base=0):
        self.count, self.slots, self.base = count, slots, base
        self.send_sems, self.recv_sems = send_sems, recv_sems
        self.other = lax.axis_index("wt")
        self.place = ring_place(lax.axis_index("ctx"), count)
        self.right = ring_index(self.place + 1, count)
        self.left = ring_index(self.place + count - 1, count)
        self.half = slots.shape[2] // 2

    def copy(self, which, step, way):
        rows = pl.ds(way * self.half, self.half)
        slot = step - self.base
        return pltpu.make_async_remote_copy(
            src_ref=self.slots.at[which, slot, rows],
            dst_ref=self.slots.at[which, slot + 1, rows],
            send_sem=self.send_sems.at[which, slot, way],
            recv_sem=self.recv_sems.at[which, slot, way],
            device_id=((self.right, self.left)[way], self.other),
            device_id_type=MESH,
        )

    def arrived(self, which, step):
        for way in range(2):
            self.copy(which, step - 1, way).wait_recv()

    def tick(
        self,
        which,
        step,
        left_ref,
        right_ref,
        first=False,
        given=None,
        result=None,
        final=True,
    ):
        half = self.half
        rows = [
            ring_index(target, self.count) * (2 * half) + way * half
            for way, target in enumerate(
                (self.place + self.count - 1 - step, self.place + 1 + step)
            )
        ]
        left = jnp.concatenate(
            [left_ref[pl.ds(pl.multiple_of(row, half), half), :] for row in rows], axis=0
        )
        total = jnp.dot(left, right_ref[...], preferred_element_type=jnp.float32)
        if given is not None:
            total = total + given[...].astype(jnp.float32)
        elif not first:
            self.arrived(which, step)
            total = total + self.slots[which, step - self.base].astype(jnp.float32)
        def pass_on():
            self.slots[which, step - self.base] = total.astype(jnp.bfloat16)
            for way in range(2):
                self.copy(which, step, way).start()

        def keep():
            result[...] = total

        if result is None:
            pass_on()
        elif final is True:
            keep()
        else:
            pl.when(final)(keep)
            pl.when(jnp.logical_not(final))(pass_on)

    def finish(self, which, end):
        for way in range(2):

            def wait(step, carry):
                self.copy(which, step, way).wait_send()
                return carry

            lax.fori_loop(self.base, end, wait, 0)


def pair_lanes(shape):
    return lax.broadcasted_iota(jnp.int32, shape, 1)


def swap_halves(values, head_dim):
    lanes = pair_lanes(values.shape)
    width = values.shape[1]
    quarter = head_dim // 2
    return jnp.where(
        lax.rem(lanes, head_dim) < quarter,
        pltpu.roll(values, width - quarter, 1),
        pltpu.roll(values, quarter, 1),
    )


def pair_mean(values, head_dim):
    low = pair_lanes(values.shape) < head_dim
    first = jnp.sum(jnp.where(low, values, 0.0), axis=-1, keepdims=True)
    second = jnp.sum(jnp.where(low, 0.0, values), axis=-1, keepdims=True)
    return jnp.where(low, first, second) * (1.0 / head_dim)


def pair_norm(values, head_dim):
    inverse = lax.rsqrt(pair_mean(values * values, head_dim) + EPS)
    return values * inverse, inverse


def as_row(ref):
    return ref[...].astype(jnp.float32).reshape(1, -1)


def double(row):
    return jnp.concatenate([row, row], axis=-1)


def dot_nn(left, right):
    return jnp.dot(left, right, preferred_element_type=jnp.float32)


def dot_nt(left, right):
    return lax.dot_general(
        left, right, (((1,), (1,)), ((), ())), preferred_element_type=jnp.float32
    )


def as_column(row):
    size = row.shape[1]
    rows = lax.broadcasted_iota(jnp.int32, (size, size), 0)
    lanes = lax.broadcasted_iota(jnp.int32, (size, size), 1)
    return jnp.sum(jnp.where(rows == lanes, row, 0.0), axis=1, keepdims=True)


class Place:
    def __init__(self, count):
        self.count = count
        self.ctx, self.wt = lax.axis_index("ctx"), lax.axis_index("wt")
        self.odd = lax.rem(self.ctx, 2)
        self.level = lax.div(self.ctx, 2)
        self.core_bit = lax.rem(self.wt, 2)
        self.beside_ctx = self.ctx + 1 - 2 * self.odd
        self.beside = (self.beside_ctx, self.wt)
        self.above = (lax.rem(self.ctx + 2, count), self.wt)
        self.below = (lax.rem(self.ctx + count - 2, count), self.wt)
        self.has_above = self.ctx + 2 < count
        self.has_below = self.ctx >= 2
        self.core_wt = self.wt + 1 - 2 * self.core_bit
        self.chip_wt = lax.rem(self.wt + 2, 4)
        self.far_wt = lax.rem(self.core_wt + 2, 4)
        self.core = (self.ctx, self.core_wt)
        self.chip = (self.ctx, self.chip_wt)
        self.far = (self.ctx, self.far_wt)

    def signal(self, peer):
        pl.semaphore_signal(
            pltpu.get_barrier_semaphore(), inc=1, device_id=peer, device_id_type=MESH
        )

    def signal_all(self):
        for shift in range(1, self.count):
            self.signal((lax.rem(self.ctx + shift, self.count), self.wt))
        self.signal(self.core)
        self.signal(self.chip)
        self.signal(self.far)

    def await_all(self):
        pl.semaphore_wait(pltpu.get_barrier_semaphore(), self.count + 2)


def send_to(source, target, send_sem, recv_sem, device):
    return pltpu.make_async_remote_copy(
        src_ref=source,
        dst_ref=target,
        send_sem=send_sem,
        recv_sem=recv_sem,
        device_id=device,
        device_id_type=MESH,
    )


class WtSum:
    def __init__(self, here, tile, part, got, far, full, send_sems, recv_sems, before=None):
        self.here, self.tile, self.before = here, tile, before
        self.part, self.got, self.far, self.full = part, got, far, full
        self.send_sems, self.recv_sems = send_sems, recv_sems
        self.mine, self.theirs = here.core_bit, 1 - here.core_bit
        self.half = got.shape[1]

    def rows(self, seq):
        return pl.ds(pl.multiple_of(seq * self.tile, self.tile), self.tile)

    def cols(self, half):
        return pl.ds(pl.multiple_of(half * self.half, self.half), self.half)

    def copy(self, hop, seq, arriving=False):
        rows = self.rows(seq)
        half = self.theirs if arriving else self.mine
        source = (
            self.part.at[rows, self.cols(self.theirs)],
            self.got.at[rows],
            self.full.at[half, rows],
        )[hop]
        target = (self.got.at[rows], self.far.at[rows], self.full.at[half, rows])[hop]
        device = self.here.chip if hop == 1 else self.here.core
        return send_to(
            source, target, self.send_sems.at[hop, seq], self.recv_sems.at[hop, seq], device
        )

    def offer(self, seq, value):
        self.part[self.rows(seq), pl.ds(0, 2 * self.half)] = value.astype(jnp.bfloat16)
        self.copy(0, seq).start()

    def cross(self, seq):
        rows = self.rows(seq)
        self.copy(0, seq).wait_recv()
        total = self.part[rows, self.cols(self.mine)].astype(jnp.float32) + self.got[
            rows
        ].astype(jnp.float32)
        self.got[rows] = total.astype(jnp.bfloat16)
        self.copy(1, seq).start()

    def close(self, seq):
        rows = self.rows(seq)
        self.copy(1, seq).wait()
        total = self.got[rows].astype(jnp.float32) + self.far[rows].astype(jnp.float32)
        if self.before is not None:
            self.before.copy(2, seq).wait_send()
        self.full[self.mine, rows] = total.astype(jnp.bfloat16)
        self.copy(2, seq).start()

    def result(self, seq):
        rows = self.rows(seq)
        self.copy(2, seq, True).wait_recv()
        return jnp.concatenate([self.full[0, rows], self.full[1, rows]], axis=1).astype(
            jnp.float32
        )

    def finish(self, sequences, hops=(0, 2)):
        def sent(seq, carry):
            for hop in hops:
                self.copy(hop, seq).wait_send()
            return carry

        lax.fori_loop(0, sequences, sent, 0)


def ring_scratch(count, arrays, rows, width):
    return [
        pltpu.VMEM((arrays, count, rows, width), jnp.bfloat16),
        pltpu.SemaphoreType.DMA((arrays, count - 1, 2)),
        pltpu.SemaphoreType.DMA((arrays, count - 1, 2)),
    ]


class GainSum:
    def __init__(self, here, slots, beside, sends, recvs, pair_sends, pair_recvs):
        self.here, self.slots, self.beside = here, slots, beside
        self.sends, self.recvs = sends, recvs
        self.pair_sends, self.pair_recvs = pair_sends, pair_recvs

    def copy(self, shift, arriving=False):
        here = self.here
        target = lax.rem(here.ctx + shift, here.count)
        origin = lax.rem(here.ctx + here.count - shift, here.count)
        ref = self.slots.at[origin if arriving else here.ctx]
        return send_to(
            ref, ref, self.sends.at[shift - 1], self.recvs.at[shift - 1], (target, here.wt)
        )

    def pair_copy(self, hop):
        device = (self.here.core, self.here.chip)[hop]
        return send_to(
            self.beside.at[hop, 0],
            self.beside.at[hop, 1],
            self.pair_sends.at[hop],
            self.pair_recvs.at[hop],
            device,
        )

    def start(self):
        for shift in range(1, self.here.count):
            self.copy(shift).start()

    def total(self):
        for shift in range(1, self.here.count):
            self.copy(shift, True).wait_recv()
        total = self.slots[0]
        for index in range(1, self.here.count):
            total = total + self.slots[index]
        for hop in range(2):
            self.beside[hop, 0] = total
            self.pair_copy(hop).start()
            self.pair_copy(hop).wait_recv()
            total = total + self.beside[hop, 1]
        for shift in range(1, self.here.count):
            self.copy(shift).wait_send()
        for hop in range(2):
            self.pair_copy(hop).wait_send()
        return total


class Mover:
    def __init__(self, pairs, sems):
        self.copies = [
            pltpu.make_async_copy(source, target, sems.at[i])
            for i, (source, target) in enumerate(pairs)
        ]

    def start(self, *which):
        for i in which:
            self.copies[i].start()

    def wait(self, *which):
        for i in which:
            self.copies[i].wait()


TICKS = (1, 1, 5)
REACH = 2
VMEM_LIMIT = 63 * MIB
RESULTS = (
    "output",
    "tokens_grad",
    "w_down_sum",
    "w_gate_sum",
    "w_up_sum",
    "w_out_sum",
    "w_query_sum",
    "w_key_sum",
    "w_value_sum",
    "attn_gain_sum",
    "ffn_gain_sum",
    "q_gain_sum",
    "k_gain_sum",
)


def layer_kernel(count, names, *refs):
    ref = dict(zip(names, refs, strict=True))
    tokens, segments = ref["tokens"], ref["segments"]
    residual, mixed_t, query_t = ref["residual"], ref["mixed_t"], ref["query_t"]
    logs, starts, keys_values = ref["logs"], ref["starts"], ref["keys_values"]
    query_raw, key_raw = ref["query_raw"], ref["key_raw"]
    grad_res, lefts = ref["grad_res"], ref["lefts"]
    ffn_grads, ffn_gain_part = ref["ffn_grads"], ref["ffn_gain_part"]
    all_segs, all_out, all_heads = ref["all_segs"], ref["all_out"], ref["all_heads"]
    acc, row_sum = ref["acc"], ref["row_sum"]
    w_gate, w_up, w_down = ref["w_gate"], ref["w_up"], ref["w_down"]
    gate_t, up_t, grad_hidden = ref["gate_t"], ref["up_t"], ref["grad_hidden"]
    cotangent, table = ref["cotangent"], ref["table"]
    sequences, tile = segments.shape
    head_dim = ref["q_gain"].shape[0]
    pair = 2 * head_dim
    levels = count // 2
    here = Place(count)
    me = here.ctx
    loads = Mover(
        [
            (ref["table_in"].at[pl.ds(pl.multiple_of(me * tile, tile), tile)], table),
            (ref["cotangent_in"], cotangent),
            (ref["w_down_in"], w_down),
            (ref["w_gate_in"], w_gate),
            (ref["w_up_in"], w_up),
            (ref["tokens_in"], tokens),
        ],
        ref["load_sems"],
    )
    loads.start(5, 0, 1, 2, 3, 4)
    shared = [ref[name] for name in ("sum_got", "sum_far", "sum_full")]
    ffn_sum = WtSum(here, tile, ref["ffn_part"], *shared, ref["ffn_send"], ref["ffn_recv"])
    ffn = Ring(count, *(ref[f"ffn{i}"] for i in range(3)))
    here.signal_all()
    all_segs[me] = jnp.zeros_like(all_segs[me])
    all_segs[me, pl.ds(0, sequences)] = segments[...]
    all_out[here.wt] = ref["w_out"][...].T

    def out_copy(hop, arriving=False):
        sent = (here.wt, here.wt, here.chip_wt)
        landed = (here.chip_wt, here.core_wt, here.far_wt)
        part = all_out.at[(landed if arriving else sent)[hop]]
        device = here.chip if hop == 0 else here.core
        return send_to(part, part, ref["out_send"].at[hop], ref["out_recv"].at[hop], device)

    def rows_of(seq):
        return pl.ds(pl.multiple_of(seq * tile, tile), tile)

    def block_of(index, step):
        return lax.rem(index - 2 * step + 2 * count, count)

    def up_copy(step, seq, arriving=False, forward=False):
        block = block_of(me, step) if arriving else block_of(me, step - 1) if forward else me
        rows = keys_values.at[block, rows_of(seq)]
        device = (lax.rem(me + (2 if forward else 2 * step), count), here.wt)
        return send_to(
            rows, rows, ref["up_send"].at[step, seq], ref["up_recv"].at[step, seq], device
        )

    def side_copy(step, seq, index=me):
        rows = keys_values.at[block_of(index, step), rows_of(seq)]
        return send_to(
            rows, rows, ref["side_send"].at[step, seq], ref["side_recv"].at[step, seq], here.beside
        )

    def seg_up_copy(step, arriving=False):
        part = all_segs.at[block_of(me, step) if arriving else me]
        device = (lax.rem(me + 2 * step, count), here.wt)
        return send_to(
            part, part, ref["seg_send"].at[step, 0], ref["seg_recv"].at[step, 0], device
        )

    def seg_side_copy(step, index=me):
        part = all_segs.at[block_of(index, step)]
        return send_to(
            part, part, ref["seg_send"].at[step, 1], ref["seg_recv"].at[step, 1], here.beside
        )

    def goes_up(step):
        return me + 2 * step < count

    def goes_aside(step):
        block = me - 2 * step
        return (block >= 0) & (block < here.beside_ctx)

    def comes_aside(step):
        block = here.beside_ctx - 2 * step
        return (block >= 0) & (block < me)

    def pass_segs():
        for step in range(1, levels):

            @pl.when(goes_up(step))
            def _():
                seg_up_copy(step).start()

        @pl.when(goes_aside(0))
        def _():
            seg_side_copy(0).start()

    def forwards(step):
        return (step > REACH) & (me >= 2 * (step - 1)) & here.has_above

    def pass_rows(seq):
        @pl.when(goes_aside(0))
        def _():
            side_copy(0, seq).start()

        for step in range(1, min(REACH + 1, levels)):

            @pl.when(goes_up(step))
            def _():
                up_copy(step, seq).start()

    gain = as_row(ref["attn_gain"])
    q_gain_pair = double(as_row(ref["q_gain"]))
    k_gain_pair = double(as_row(ref["k_gain"]))
    ffn_gain_row = as_row(ref["ffn_gain"])
    loads.wait(0, 5)

    def turn(values):
        cosine = table[:, pl.ds(0, pair)]
        sine = table[:, pl.ds(pair, pair)]
        return values * cosine + swap_halves(values, head_dim) * sine

    def project(seq, carry):
        rows = rows_of(seq)
        inputs = tokens[rows, :].astype(jnp.float32)
        inverse = lax.rsqrt(jnp.mean(inputs * inputs, axis=-1, keepdims=True) + EPS)
        normed = (inputs * inverse * gain).astype(jnp.bfloat16)
        raw_k = dot_nn(normed, ref["w_key"][...])
        key_raw[rows, :] = raw_k
        unit, unused = pair_norm(raw_k, head_dim)
        keys_values[me, rows, pl.ds(0, pair)] = turn(unit * k_gain_pair).astype(jnp.bfloat16)
        keys_values[me, rows, pl.ds(pair, pair)] = dot_nn(normed, ref["w_value"][...]).astype(
            jnp.bfloat16
        )

        @pl.when(seq == 0)
        def _():
            here.await_all()
            pass_segs()

        @pl.when(seq == 0)
        def _():
            pass_rows(seq)

        @pl.when(seq == 0)
        def _():
            out_copy(0).start()
            out_copy(1).start()

        raw_q = dot_nn(normed, ref["w_query"][...])
        query_raw[rows, :] = raw_q
        query_t[seq] = jnp.zeros_like(query_t[seq])
        for group in range(2):
            unit, unused = pair_norm(raw_q[:, group * pair : (group + 1) * pair], head_dim)
            turned = turn(unit * q_gain_pair) * (head_dim**-0.5)
            flipped = turned.T.astype(jnp.bfloat16)
            for member in range(2):
                query_t[
                    seq,
                    pl.ds(group * head_dim, head_dim),
                    pl.ds((2 * group + member) * tile, tile),
                ] = flipped[member * head_dim : (member + 1) * head_dim]
        acc[seq] = jnp.zeros_like(acc[seq])
        row_sum[seq] = jnp.zeros_like(row_sum[seq])
        starts[seq] = jnp.zeros_like(starts[seq])
        return carry

    def route_level(step, seq):
        @pl.when(me >= 2 * step)
        def _():
            @pl.when(seq == 0)
            def _():
                seg_up_copy(step, True).wait_recv()
                seg_side_copy(step).start()

            up_copy(step, seq, True).wait_recv()
            side_copy(step, seq).start()

            @pl.when(forwards(step + 1))
            def _():
                up_copy(step + 1, seq, forward=True).start()

    def route(seq):
        def level(step, carry):
            route_level(step, seq)
            return carry

        lax.fori_loop(1, levels, level, 0)

    lax.fori_loop(0, sequences, project, 0)
    pass_rows(1)
    for step in range(1, min(REACH + 1, levels)):
        route_level(step, 0)
    loads.wait(1, 2)

    def back_down(seq, carry):
        rows = rows_of(seq)
        grads = cotangent[rows, :]
        lefts[0, :, rows] = grads.T
        grad_hidden[rows, :] = dot_nn(grads, w_down[...]).astype(jnp.bfloat16)
        return carry

    lax.fori_loop(0, sequences, back_down, 0)
    for step in range(REACH + 1, levels):
        route_level(step, 0)

    loads.wait(3, 4)

    def flip(index, carry):
        rows = pl.ds(pl.multiple_of(index * 128, 128), 128)
        gate_t[:, rows] = w_gate[rows, :].T
        up_t[:, rows] = w_up[rows, :].T
        return carry

    lax.fori_loop(0, tokens.shape[1] // 128, flip, 0)
    key_rows = lax.broadcasted_iota(jnp.int32, (tile, tile), 0)
    query_cols = lax.broadcasted_iota(jnp.int32, (tile, tile), 1)

    def attend(blocks, seq):
        rows = rows_of(seq)
        seg_query = all_segs[me, pl.ds(seq, 1)].astype(jnp.float32)
        masks, values_t = [], []
        for block in blocks:
            seg_key = as_column(all_segs[block, pl.ds(seq, 1)].astype(jnp.float32))
            earlier = jnp.where(seg_key < seg_query, 1.0, 0.0)
            starts[seq] += jnp.sum(earlier, axis=0, keepdims=True)
            if block is me:
                same = (seg_key == seg_query) & (key_rows <= query_cols)
                masks.append(jnp.where(same, 1.0, 0.0))
            else:
                masks.append(1.0 - earlier)
            values_t.append(keys_values[block, rows, pl.ds(pair, pair)].T)
        keys = [keys_values[block, rows, pl.ds(0, pair)] for block in blocks]
        mask = jnp.concatenate(masks, axis=0)
        scores = dot_nn(jnp.concatenate(keys, axis=0), query_t[seq])
        weights = jnp.exp(scores) * jnp.concatenate([mask] * 4, axis=1)
        row_sum[seq] += jnp.sum(weights, axis=0, keepdims=True)
        low = weights.astype(jnp.bfloat16)
        value_rows = jnp.concatenate(values_t, axis=1)
        for group in range(2):
            acc[seq, group] += dot_nn(
                value_rows[group * head_dim : (group + 1) * head_dim],
                low[:, group * 2 * tile : (group + 1) * 2 * tile],
            )

    def attend_own(seq, carry):
        attend([me], seq)
        return carry

    lax.fori_loop(0, sequences, attend_own, 0)

    def head_copy(hop, seq, arriving=False):
        sent = (here.wt, here.wt, here.chip_wt)
        landed = (here.chip_wt, here.core_wt, here.far_wt)
        part = all_heads.at[(landed if arriving else sent)[hop], rows_of(seq)]
        device = here.chip if hop == 0 else here.core
        return send_to(
            part, part, ref["head_send"].at[hop, seq], ref["head_recv"].at[hop, seq], device
        )

    def far_copy(seq):
        part = all_heads.at[here.wt, rows_of(seq)]
        return send_to(
            part, part, ref["head_send"].at[2, seq], ref["head_recv"].at[2, seq], here.far
        )

    def relay(seq):
        head_copy(0, seq, True).wait_recv()

        @pl.when(seq < sequences - 1)
        def _():
            head_copy(2, seq).start()

    def mix(seq):
        rows = rows_of(seq)
        total = row_sum[seq]
        logs[seq] = jnp.log(total)
        for group in range(2):
            cols = slice(group * 2 * tile, (group + 1) * 2 * tile)
            part = acc[seq, group] / total[:, cols]
            mixed = jnp.concatenate([part[:, :tile], part[:, tile:]], axis=0)
            mixed_t[seq, group] = mixed
            all_heads[here.wt, rows, pl.ds(group * pair, pair)] = mixed.T.astype(jnp.bfloat16)
        head_copy(0, seq).start()
        head_copy(1, seq).start()

        @pl.when(seq == sequences - 1)
        def _():
            far_copy(seq).start()

    def ffn_unit(rows):
        values = residual[rows, :]
        inverse = lax.rsqrt(jnp.mean(values * values, axis=-1, keepdims=True) + EPS)
        return values * inverse, inverse

    def feed(seq):
        rows = rows_of(seq)
        head_copy(1, seq, True).wait_recv()
        head_copy(2, seq, True).wait_recv()
        total = tokens[rows, :].astype(jnp.float32)
        for slot in range(4):
            total = total + dot_nn(all_heads[slot, rows], all_out[slot])
        residual[rows, :] = total
        unit, unused = ffn_unit(rows)
        normed = (unit * ffn_gain_row).astype(jnp.bfloat16)
        lefts[1, :, rows] = normed.T
        gate = dot_nn(normed, w_gate[...])
        up = dot_nn(normed, w_up[...])
        sigmoid = 0.5 * jnp.tanh(0.5 * gate) + 0.5
        silu = gate * sigmoid
        ffn_grads[0, rows] = (silu * up).astype(jnp.bfloat16)
        grads = grad_hidden[rows, :].astype(jnp.float32)
        grad_gate = (grads * up * sigmoid * (1.0 + gate * (1.0 - sigmoid))).astype(jnp.bfloat16)
        grad_up = (grads * silu).astype(jnp.bfloat16)
        ffn_grads[1, rows] = grad_gate
        ffn_grads[2, rows] = grad_up
        grad_normed = dot_nn(grad_gate, gate_t[...]) + dot_nn(grad_up, up_t[...])
        ffn_gain_part[...] += jnp.sum(grad_normed * unit, axis=0, keepdims=True)
        ffn_sum.offer(seq, grad_normed)

    ffn_gain_part[...] = jnp.zeros_like(ffn_gain_part)

    def sequence_turn(turn_, carry):
        @pl.when(turn_ < sequences)
        def _():
            @pl.when(turn_ + 2 < sequences)
            def _():
                pass_rows(turn_ + 2)

            @pl.when(comes_aside(0))
            def _():
                @pl.when(turn_ == 0)
                def _():
                    seg_side_copy(0, here.beside_ctx).wait_recv()

                side_copy(0, turn_, here.beside_ctx).wait_recv()
                attend([here.beside_ctx], turn_)

        @pl.when(turn_ + 1 < sequences)
        def _():
            for step in range(1, min(REACH + 1, levels)):
                route_level(step, turn_ + 1)

        @pl.when(turn_ == 1)
        def _():
            out_copy(0, True).wait_recv()
            out_copy(2).start()

        @pl.when((turn_ > 0) & (turn_ <= sequences))
        def _():
            relay(turn_ - 1)

        @pl.when(turn_ < sequences)
        def _():
            def level(step, carry):
                @pl.when(me >= 2 * step)
                def _():
                    @pl.when(turn_ == 0)
                    def _():
                        seg_side_copy(step, here.beside_ctx).wait_recv()

                    side_copy(step, turn_, here.beside_ctx).wait_recv()
                    attend([block_of(me, step), block_of(here.beside_ctx, step)], turn_)

                return carry

            lax.fori_loop(1, levels, level, 0)
            mix(turn_)

        @pl.when(turn_ + 1 < sequences)
        def _():
            for step in range(REACH + 1, levels):
                route_level(step, turn_ + 1)

        @pl.when(turn_ == 1)
        def _():
            out_copy(1, True).wait_recv()
            out_copy(2, True).wait_recv()

        @pl.when(turn_ > 1)
        def _():
            ffn_sum.cross(turn_ - 2)

        @pl.when(turn_ > 0)
        def _():
            feed(turn_ - 1)

        @pl.when(turn_ > 2)
        def _():
            ffn_sum.close(turn_ - 3)

        return carry

    lax.fori_loop(0, sequences + 1, sequence_turn, 0)
    for i in range(3):
        ffn.tick(i, 0, lefts.at[min(i, 1)], ffn_grads.at[i], first=True)
    rows_all, width = tokens.shape
    last = count - 1
    deltas, own_grads = ref["deltas"], ref["own_grads"]
    side_in, side_out = ref["side_in"], ref["side_out"]
    line_in, line_out = ref["line_in"], ref["line_out"]
    ffn_sums, qkv_total = ref["ffn_sums"], ref["qkv_total"]
    grad_query_t = acc
    grad_res_t = w_gate.at[:, pl.ds(0, rows_all)]
    grad_heads_t = w_gate
    query_n = gate_t.at[pl.ds(0, 4 * tile)]
    grad_heads_n = gate_t.at[pl.ds(4 * tile, 4 * tile)]
    grad_qkv = w_up.at[pl.ds(0, rows_all), pl.ds(0, 4 * pair)]
    normed_t = w_up.at[:, pl.ds(4 * pair, rows_all)]
    qkv_t = up_t.at[pl.ds(rows_all, 4 * pair)]
    heads = all_heads.at[here.wt]
    sources = {
        "output": cotangent,
        "tokens_grad": tokens,
        "w_down_sum": ffn_sums.at[0],
        "w_gate_sum": ffn_sums.at[1],
        "w_up_sum": ffn_sums.at[2],
        "w_query_sum": qkv_total.at[:, pl.ds(0, 2 * pair)],
        "w_key_sum": qkv_total.at[:, pl.ds(2 * pair, pair)],
        "w_value_sum": qkv_total.at[:, pl.ds(3 * pair, pair)],
    }
    stores = Mover(
        [(sources[name] if name in sources else ref[name], ref[name + "_res"]) for name in RESULTS],
        ref["store_sems"],
    )
    wt_sum = WtSum(here, tile, up_t, *shared, ref["wt_send"], ref["wt_recv"], ffn_sum)
    mlp_sum = WtSum(here, tile, grad_hidden, *(ref[f"mlp_sum{i}"] for i in range(5)))
    gains = GainSum(here, *(ref[f"gains{i}"] for i in range(6)))
    gain_slots = ref["gains0"]
    out = Ring(count, *(ref[f"out{i}"] for i in range(3)))
    qkv = Ring(count, *(ref[f"qkv{i}"] for i in range(3)))

    def heads_at(seq):
        start = pl.multiple_of(seq * pair, pair)
        return (pl.ds(start, pair), pl.ds(rows_all, 4 * tile))

    def seq_cols(seq):
        return (slice(None), pl.ds(pl.multiple_of(seq * tile, tile), tile))

    def ffn_tick(index):
        step, which = lax.div(index, 3), lax.rem(index, 3)
        ffn.tick(
            which,
            step,
            lefts.at[lax.min(which, 1)],
            ffn_grads.at[which],
            result=ffn_sums.at[which],
            final=step == last,
        )

    def token_unit(rows):
        inputs = tokens[rows, :].astype(jnp.float32)
        inverse = lax.rsqrt(jnp.mean(inputs * inputs, axis=-1, keepdims=True) + EPS)
        return inputs * inverse, inverse

    def prepare(seq):
        rows = rows_of(seq)
        unit, inverse = ffn_unit(rows)
        scaled = ffn_sum.result(seq) * ffn_gain_row
        back = inverse * (scaled - unit * jnp.mean(scaled * unit, axis=-1, keepdims=True))
        grads = (cotangent[rows, :].astype(jnp.float32) + back).astype(jnp.bfloat16)
        grad_res[rows, :] = grads
        grad_res_t[:, rows] = grads.T
        unit, unused = token_unit(rows)
        normed_t[:, rows] = (unit * gain).astype(jnp.bfloat16).T
        grad_heads_t[heads_at(seq)] = jnp.zeros((pair, 4 * tile), jnp.bfloat16)
        low = dot_nn(grads, ref["w_out"][...]).astype(jnp.bfloat16)
        for group in range(2):
            flipped = low[:, group * pair : (group + 1) * pair].T
            product_t = flipped.astype(jnp.float32) * mixed_t[seq, group]
            for member in range(2):
                part = slice(member * head_dim, (member + 1) * head_dim)
                cols = pl.ds((2 * group + member) * tile, tile)
                into = pl.ds(pl.multiple_of(seq * pair + group * head_dim, head_dim), head_dim)
                spot = pl.ds(rows_all + (2 * group + member) * tile, tile)
                grad_heads_t[into, spot] = flipped[part]
                deltas[seq, :, cols] = jnp.sum(product_t[part], axis=0, keepdims=True)
        grad_heads_n[seq_cols(seq)] = grad_heads_t[heads_at(seq)].T
        query_n[seq_cols(seq)] = query_t[seq].T
        grad_query_t[seq] = jnp.zeros_like(grad_query_t[seq])

    def grads_of(blocks, seq):
        rows = rows_of(seq)
        keys = [keys_values[block, rows, pl.ds(0, pair)] for block in blocks]
        values = [keys_values[block, rows, pl.ds(pair, pair)] for block in blocks]
        masks = []
        for block in blocks:
            allowed = key_rows.astype(jnp.float32) >= starts[seq] - (block * tile).astype(
                jnp.float32
            )
            if block is me:
                allowed = allowed & (key_rows <= query_cols)
            masks.append(jnp.where(allowed, 1.0, 0.0))
        mask = jnp.concatenate(masks, axis=0)
        grad_heads = grad_heads_t[heads_at(seq)]
        scores = dot_nn(jnp.concatenate(keys, axis=0), query_t[seq])
        probs = jnp.exp(scores - logs[seq]) * jnp.concatenate([mask] * 4, axis=1)
        grad_probs = dot_nn(jnp.concatenate(values, axis=0), grad_heads)
        grad_scores = (probs * (grad_probs - deltas[seq])).astype(jnp.bfloat16)
        flipped = jnp.concatenate([part.T for part in keys], axis=1)
        for group in range(2):
            cols = slice(group * 2 * tile, (group + 1) * 2 * tile)
            grad_query_t[seq, group] += dot_nn(
                flipped[group * head_dim : (group + 1) * head_dim], grad_scores[:, cols]
            )
        grad_keys = dot_nn(grad_scores, query_n[seq_cols(seq)])
        grad_values = dot_nn(probs.astype(jnp.bfloat16), grad_heads_n[seq_cols(seq)])
        both = jnp.concatenate([grad_keys, grad_values], axis=1)
        return [both[i * tile : (i + 1) * tile] for i in range(len(blocks))]

    def side_grad_copy(step, seq):
        return send_to(
            side_out.at[step, rows_of(seq)],
            side_in.at[step, rows_of(seq)],
            ref["side_grad_send"].at[step, seq],
            ref["side_grad_recv"].at[step, seq],
            here.beside,
        )

    def line_copy(step, seq):
        earlier = step - 1
        return send_to(
            line_out.at[earlier, rows_of(seq)],
            line_in.at[earlier, rows_of(seq)],
            ref["line_send"].at[earlier, seq],
            ref["line_recv"].at[earlier, seq],
            here.below,
        )

    def find_grads(seq):
        rows = rows_of(seq)

        def level(index, carry):
            step = levels - 1 - index

            @pl.when(me >= 2 * step)
            def _():
                line, side = grads_of(
                    [block_of(me, step), block_of(here.beside_ctx, step)], seq
                )
                side_out[step, rows] = side.astype(jnp.bfloat16)
                side_grad_copy(step, seq).start()
                line_out[step - 1, rows] = line.astype(jnp.bfloat16)

            return carry

        lax.fori_loop(0, levels - 1, level, 0)

        @pl.when(comes_aside(0))
        def _():
            own, side = grads_of([me, here.beside_ctx], seq)
            side_out[0, rows] = side.astype(jnp.bfloat16)
            side_grad_copy(0, seq).start()
            own_grads[rows, :] = own

        @pl.when(jnp.logical_not(comes_aside(0)))
        def _():
            own_grads[rows, :] = grads_of([me], seq)[0]

    def send_down(step, seq):
        @pl.when(me >= 2 * step)
        def _():
            rows = rows_of(seq)
            side_grad_copy(step, seq).wait_recv()
            total = line_out[step - 1, rows].astype(jnp.float32) + side_in[step, rows].astype(
                jnp.float32
            )

            @pl.when(here.has_above)
            def _():
                line_copy(step + 1, seq).wait_recv()
                line_out[step - 1, rows] = (
                    total + line_in[step, rows].astype(jnp.float32)
                ).astype(jnp.bfloat16)

            @pl.when(jnp.logical_not(here.has_above))
            def _():
                line_out[step - 1, rows] = total.astype(jnp.bfloat16)

            line_copy(step, seq).start()

    gain_slots[me] = jnp.zeros_like(gain_slots[me])
    gain_slots[me, pl.ds(1, 1)] = ffn_gain_part[...]

    def back_through(grads, raw, gain_pair, row):
        cosine = table[:, pl.ds(0, pair)]
        sine = table[:, pl.ds(pair, pair)]
        turned = grads * cosine - swap_halves(grads, head_dim) * sine
        unit, inverse = pair_norm(raw, head_dim)
        gain_slots[me, pl.ds(row, 1), pl.ds(0, pair)] += jnp.sum(
            turned * unit, axis=0, keepdims=True
        )
        scaled = turned * gain_pair
        return (inverse * (scaled - unit * pair_mean(scaled * unit, head_dim))).astype(
            jnp.bfloat16
        )

    def project_back(seq):
        rows = rows_of(seq)
        for group in range(2):
            grads = grad_query_t[seq, group] * (head_dim**-0.5)
            grads = jnp.concatenate([grads[:, :tile], grads[:, tile:]], axis=0).T
            cols = pl.ds(group * pair, pair)
            grad_qkv[rows, cols] = back_through(grads, query_raw[rows, cols], q_gain_pair, 2)

        @pl.when(me < here.beside_ctx)
        def _():
            side_grad_copy(0, seq).wait_recv()
            own_grads[rows, :] += side_in[0, rows].astype(jnp.float32)

        @pl.when(here.has_above)
        def _():
            line_copy(1, seq).wait_recv()
            own_grads[rows, :] += line_in[0, rows].astype(jnp.float32)

        grad_qkv[rows, pl.ds(2 * pair, pair)] = back_through(
            own_grads[rows, pl.ds(0, pair)], key_raw[rows, :], k_gain_pair, 3
        )
        grad_qkv[rows, pl.ds(3 * pair, pair)] = own_grads[rows, pl.ds(pair, pair)].astype(
            jnp.bfloat16
        )
        grads = dot_nn(grad_qkv[rows, :], qkv_t[...])
        unit, unused = token_unit(rows)
        gain_slots[me, pl.ds(0, 1)] += jnp.sum(grads * unit, axis=0, keepdims=True)
        wt_sum.offer(seq, grads)

    def output_rows(seq):
        rows = rows_of(seq)
        cotangent[rows, :] = (residual[rows, :] + mlp_sum.result(seq)).astype(jnp.bfloat16)

    def token_rows(seq):
        rows = rows_of(seq)
        unit, inverse = token_unit(rows)
        scaled = wt_sum.result(seq) * gain
        grads = inverse * (scaled - unit * jnp.mean(scaled * unit, axis=-1, keepdims=True))
        tokens[rows, :] = (grad_res[rows, :].astype(jnp.float32) + grads).astype(
            jnp.bfloat16
        )

    qkv_t[pl.ds(0, 2 * pair), :] = ref["w_query"][...].T
    qkv_t[pl.ds(2 * pair, pair), :] = ref["w_key"][...].T
    qkv_t[pl.ds(3 * pair, pair), :] = ref["w_value"][...].T
    ffn_sum.cross(sequences - 1)

    few, more, early = TICKS

    def ticks_before(turn_):
        return 3 + few * lax.min(turn_, early) + more * lax.max(turn_ - early, 0)

    def grad_turn(turn_, carry):
        @pl.when(turn_ < sequences)
        def _():
            prepare(turn_)
            find_grads(turn_)

        @pl.when((turn_ == 1) | (turn_ == 2))
        def _():
            ffn_sum.close(sequences - 3 + turn_)

        @pl.when((turn_ >= 2) & (turn_ < sequences + 2))
        def _():
            def down(index, carry):
                send_down(levels - 1 - index, turn_ - 2)
                return carry

            lax.fori_loop(0, levels - 1, down, 0)

        for i in range(max(few, more)):

            @pl.when(ticks_before(turn_) + i < ticks_before(turn_ + 1))
            def _():
                ffn_tick(ticks_before(turn_) + i)

        @pl.when((turn_ >= 1) & (turn_ <= sequences))
        def _():
            seq = turn_ - 1
            mlp_sum.offer(seq, dot_nt(ffn_grads[0, rows_of(seq)], w_down[...]))

        @pl.when((turn_ >= 2) & (turn_ <= sequences + 1))
        def _():
            mlp_sum.cross(turn_ - 2)

        @pl.when((turn_ >= 3) & (turn_ <= sequences + 2))
        def _():
            mlp_sum.close(turn_ - 3)

        @pl.when(turn_ >= 4)
        def _():
            output_rows(turn_ - 4)
            project_back(turn_ - 4)

        @pl.when(turn_ >= 5)
        def _():
            wt_sum.cross(turn_ - 5)

        for i in range(4):

            @pl.when(turn_ == sequences + i)
            def _():
                out.tick(0, i, grad_res_t, heads, first=i == 0)

        return carry

    turns = sequences + 4
    lax.fori_loop(0, turns, grad_turn, 0)
    qkv.tick(0, 0, normed_t, grad_qkv, first=True)
    gains.start()
    wt_sum.cross(sequences - 1)
    stores.start(0)
    done = 3 + few * early + more * (turns - early)
    left_over = 3 * count - done
    each = -(-left_over // last)

    def tail(step, carry):
        for i in range(each):
            index = done + each * (step - 1) + i

            @pl.when(index < 3 * count)
            def _():
                ffn_tick(index)

        qkv.tick(0, step, normed_t, grad_qkv, result=qkv_total, final=step == last)

        @pl.when(step + 3 <= last)
        def _():
            out.tick(
                0, step + 3, grad_res_t, heads, result=ref["w_out_sum"], final=step + 3 == last
            )

        @pl.when(step <= sequences)
        def _():
            wt_sum.close(step - 1)

        @pl.when((step >= 2) & (step <= sequences + 1))
        def _():
            token_rows(step - 2)

        return carry

    middle = min(4, last)
    lax.fori_loop(1, middle, tail, 0)
    total = gains.total()
    ref["attn_gain_sum"][...] = total[0:1]
    ref["ffn_gain_sum"][...] = total[1:2]
    folded = total[:, :pair]
    folded = folded + pltpu.roll(folded, head_dim, 1)
    ref["q_gain_sum"][...] = folded[2:3]
    ref["k_gain_sum"][...] = folded[3:4]
    stores.start(9, 10, 11, 12)
    lax.fori_loop(middle, last + 1, tail, 0)
    stores.start(1, 2, 3, 4, 5, 6, 7, 8)
    ffn_sum.finish(sequences, (0,))
    wt_sum.finish(sequences)
    mlp_sum.finish(sequences)
    for i in range(3):
        ffn.finish(i, last)
    out.finish(0, last)
    qkv.finish(0, last)
    for hop in range(3):
        out_copy(hop).wait_send()

        def sent(seq, carry):
            head_copy(hop, seq).wait_send()
            return carry

        lax.fori_loop(0, sequences, sent, 0)

    def each_seq(step):
        def one(seq, carry):
            step(seq)
            return carry

        lax.fori_loop(0, sequences, one, 0)

    def drain(step, carry):
        @pl.when((step > 0) & goes_up(step))
        def _():
            seg_up_copy(step).wait_send()

        @pl.when(((step > 0) & (step <= REACH) & goes_up(step)) | forwards(step))
        def _():
            each_seq(lambda seq: up_copy(step, seq).wait_send())

        @pl.when(goes_aside(step))
        def _():
            seg_side_copy(step).wait_send()
            each_seq(lambda seq: side_copy(step, seq).wait_send())

        @pl.when(comes_aside(step))
        def _():
            each_seq(lambda seq: side_grad_copy(step, seq).wait_send())

        @pl.when((step > 0) & (me >= 2 * step))
        def _():
            each_seq(lambda seq: line_copy(step, seq).wait_send())

        return carry

    lax.fori_loop(0, levels, drain, 0)
    stores.wait(*range(len(RESULTS)))


def layer(inputs):
    count = lax.axis_size("ctx")
    sequences, tile = inputs["segments"].shape
    rows, width = inputs["tokens_in"].shape
    head_dim = inputs["q_gain"].shape[0]
    hidden = inputs["w_gate_in"].shape[1]
    pair = 2 * head_dim
    levels = count // 2
    block = width // count
    f32, bf16 = jnp.float32, jnp.bfloat16
    dma = pltpu.SemaphoreType.DMA
    results = {
        "output": ((rows, width), bf16),
        "tokens_grad": ((rows, width), bf16),
        "w_down_sum": ((block, hidden), f32),
        "w_gate_sum": ((block, hidden), f32),
        "w_up_sum": ((block, hidden), f32),
        "w_out_sum": ((block, 2 * pair), f32),
        "w_query_sum": ((block, 2 * pair), f32),
        "w_key_sum": ((block, pair), f32),
        "w_value_sum": ((block, pair), f32),
        "attn_gain_sum": ((1, width), f32),
        "ffn_gain_sum": ((1, width), f32),
        "q_gain_sum": ((1, pair), f32),
        "k_gain_sum": ((1, pair), f32),
    }
    staged = ("w_out_sum",) + RESULTS[9:]
    scratch = {name: pltpu.VMEM(*results[name]) for name in staged}
    buffers = {
        "tokens": ((rows, width), bf16),
        "residual": ((rows, width), f32),
        "mixed_t": ((sequences, 2, pair, tile), f32),
        "query_t": ((sequences, pair, 4 * tile), bf16),
        "logs": ((sequences, 1, 4 * tile), f32),
        "starts": ((sequences, 1, tile), f32),
        "keys_values": ((count, rows, 2 * pair), bf16),
        "query_raw": ((rows, 2 * pair), f32),
        "key_raw": ((rows, pair), f32),
        "lefts": ((2, width, rows), bf16),
        "ffn_grads": ((3, rows, hidden), bf16),
        "ffn_gain_part": ((1, width), f32),
        "grad_res": ((rows, width), bf16),
        "all_segs": ((count, 8, tile), jnp.int32),
        "all_out": ((4, 2 * pair, width), bf16),
        "all_heads": ((4, rows, 2 * pair), bf16),
        "acc": ((sequences, 2, head_dim, 2 * tile), f32),
        "row_sum": ((sequences, 1, 4 * tile), f32),
        "table": ((tile, 2 * pair), f32),
        "cotangent": ((rows, width), bf16),
        "w_down": ((width, hidden), bf16),
        "w_gate": ((width, hidden), bf16),
        "w_up": ((width, hidden), bf16),
        "gate_t": ((hidden, width), bf16),
        "up_t": ((hidden, width), bf16),
        "grad_hidden": ((rows, hidden), bf16),
        "ffn_part": ((rows, width), bf16),
        "sum_got": ((rows, width // 2), bf16),
        "sum_far": ((rows, width // 2), bf16),
        "sum_full": ((2, rows, width // 2), bf16),
        "mlp_sum0": ((rows, width // 2), bf16),
        "mlp_sum1": ((rows, width // 2), bf16),
        "mlp_sum2": ((2, rows, width // 2), bf16),
        "deltas": ((sequences, 1, 4 * tile), f32),
        "own_grads": ((rows, 2 * pair), f32),
        "side_in": ((levels, rows, 2 * pair), bf16),
        "side_out": ((levels, rows, 2 * pair), bf16),
        "line_in": ((levels - 1, rows, 2 * pair), bf16),
        "line_out": ((levels - 1, rows, 2 * pair), bf16),
        "ffn_sums": ((3, block, hidden), f32),
        "qkv_total": ((block, 4 * pair), f32),
        "gains0": ((count, 8, width), f32),
        "gains1": ((2, 2, 8, width), f32),
    }
    scratch |= {name: pltpu.VMEM(*spec) for name, spec in buffers.items()}
    semaphores = {
        "load_sems": (6,),
        "store_sems": (len(RESULTS),),
        "up_send": (levels, sequences),
        "up_recv": (levels, sequences),
        "side_send": (levels, sequences),
        "side_recv": (levels, sequences),
        "seg_send": (levels, 2),
        "seg_recv": (levels, 2),
        "out_send": (3,),
        "out_recv": (3,),
        "head_send": (3, sequences),
        "head_recv": (3, sequences),
        "ffn_send": (3, sequences),
        "ffn_recv": (3, sequences),
        "wt_send": (3, sequences),
        "wt_recv": (3, sequences),
        "mlp_sum3": (3, sequences),
        "mlp_sum4": (3, sequences),
        "side_grad_send": (levels, sequences),
        "side_grad_recv": (levels, sequences),
        "line_send": (levels - 1, sequences),
        "line_recv": (levels - 1, sequences),
        "gains2": (count - 1,),
        "gains3": (count - 1,),
        "gains4": (2,),
        "gains5": (2,),
    }
    scratch |= {name: dma(shape) for name, shape in semaphores.items()}
    for label, kinds in (
        ("ffn", ring_scratch(count, 3, block, hidden)),
        ("out", ring_scratch(count, 1, block, 2 * pair)),
        ("qkv", ring_scratch(count, 1, block, 4 * pair)),
    ):
        scratch |= {f"{label}{i}": kind for i, kind in enumerate(kinds)}
    vmem, anywhere = pl.BlockSpec(memory_space=pltpu.VMEM), pl.BlockSpec(memory_space=pl.ANY)
    names = (*inputs, *(name + "_res" for name in RESULTS), *scratch)
    arrays = pl.pallas_call(
        partial(layer_kernel, count, names),
        out_shape=[jax.ShapeDtypeStruct(*results[name]) for name in RESULTS],
        in_specs=[anywhere if name.endswith("_in") else vmem for name in inputs],
        out_specs=[anywhere] * len(RESULTS),
        scratch_shapes=list(scratch.values()),
        compiler_params=pltpu.CompilerParams(
            collective_id=2, has_side_effects=True, vmem_limit_bytes=VMEM_LIMIT
        ),
    )(*inputs.values())
    return dict(zip(RESULTS, arrays, strict=True))


def hand_over_kernel(count, *refs):
    sources, targets, staged = refs[:count], refs[count : 2 * count], refs[2 * count : 3 * count]
    loads = Mover(list(zip(sources, staged, strict=True)), refs[3 * count])
    stores = Mover(list(zip(staged, targets, strict=True)), refs[3 * count + 1])
    loads.start(*range(count))
    for i in range(count):
        loads.wait(i)
        stores.start(i)
    stores.wait(*range(count))


def hand_over(arrays):
    anywhere = pl.BlockSpec(memory_space=pl.ANY)
    dma = pltpu.SemaphoreType.DMA((len(arrays),))
    return pl.pallas_call(
        partial(hand_over_kernel, len(arrays)),
        out_shape=[jax.ShapeDtypeStruct(array.shape, array.dtype) for array in arrays],
        in_specs=[anywhere] * len(arrays),
        out_specs=[anywhere] * len(arrays),
        scratch_shapes=[pltpu.VMEM(array.shape, array.dtype) for array in arrays] + [dma, dma],
        compiler_params=pltpu.CompilerParams(vmem_limit_bytes=60 * MIB),
    )(*arrays)


def rotary_table(length, head_dim):
    half = head_dim // 2
    frequency = THETA ** (-2.0 * np.arange(half) / head_dim)
    angles = np.arange(length)[:, None] * frequency[None, :]
    cosine, sine = np.cos(angles), np.sin(angles)
    return np.concatenate([cosine] * 4 + [-sine, sine] * 2, axis=1).astype(np.float32)


def kernels_fit(tokens, w_query, key_matrix, q_gain, w_gate):
    sequences, tile, width = tokens.shape
    count, head_dim = lax.axis_size("ctx"), q_gain.shape[0]
    return (
        lax.axis_size("wt") == 4
        and count % 2 == 0
        and count >= 4
        and tile == 128
        and sequences <= 8
        and sequences * count <= 40
        and head_dim == 64
        and w_query.shape[1] == 4 * head_dim
        and key_matrix.shape[1] == 2 * head_dim
        and width % (128 * count) == 0
        and w_gate.shape[1] >= max(width, sequences * tile + 512)
        and w_gate.shape[1] <= 1152
        and width <= 1024
    )


def on_device_plain(
    tokens,
    segments,
    attn_gain,
    w_query,
    key_matrix,
    value_matrix,
    q_gain,
    k_gain,
    w_out,
    ffn_gain,
    w_gate,
    w_up,
    w_down,
    cotangent,
):
    sequences, seq_rows, model_width = tokens.shape
    head_dim = q_gain.shape[0]
    q_local = w_query.shape[1] // head_dim
    kv_local = key_matrix.shape[1] // head_dim
    per_group = q_local // kv_local
    score_scale = 1.0 / math.sqrt(head_dim)
    all_rows = sequences * seq_rows
    places = lax.axis_index("ctx") * seq_rows + jnp.arange(seq_rows, dtype=jnp.int32)
    frequency = THETA ** (-jnp.arange(0, head_dim, 2, dtype=jnp.float32) / head_dim)
    angles = places.astype(jnp.float32)[None, :, None] * frequency
    cosine_table = jnp.cos(angles)[:, :, None, :]
    sine_table = jnp.sin(angles)[:, :, None, :]
    inputs = tokens.astype(jnp.float32).reshape(all_rows, model_width)
    normed, attn_unit, attn_inverse = norm_rows(inputs, attn_gain)
    normed_low = normed.astype(jnp.bfloat16)
    query_raw = product(normed_low, w_query).reshape(sequences, seq_rows, q_local, head_dim)
    key_raw = product(normed_low, key_matrix).reshape(sequences, seq_rows, kv_local, head_dim)
    value_low = (
        product(normed_low, value_matrix)
        .astype(jnp.bfloat16)
        .reshape(sequences, seq_rows, kv_local * head_dim)
    )
    query_normed, query_unit, query_inverse = norm_rows(query_raw, q_gain)
    key_normed, key_unit, key_inverse = norm_rows(key_raw, k_gain)
    query_low = rotate(query_normed, cosine_table, sine_table, 1.0).astype(jnp.bfloat16)
    key_low = rotate(key_normed, cosine_table, sine_table, 1.0).astype(jnp.bfloat16)
    key_flat = key_low.reshape(sequences, seq_rows, kv_local * head_dim)
    query_groups = query_low.reshape(sequences, seq_rows, kv_local, per_group, head_dim)
    attend = partial(
        attend_piece,
        queries=query_groups,
        query_places=places,
        query_segs=segments,
        score_scale=score_scale,
    )
    start_state = (
        jnp.full((sequences, kv_local, per_group, seq_rows), NEG, jnp.float32),
        jnp.zeros((sequences, kv_local, per_group, seq_rows), jnp.float32),
        jnp.zeros((sequences, seq_rows, kv_local, per_group, head_dim), jnp.float32),
    )
    keys_values = lax.all_gather(
        jnp.concatenate([key_flat, value_low], axis=-1), "ctx", axis=1, tiled=True
    )
    kv_width = kv_local * head_dim
    gathered = (
        keys_values[..., :kv_width],
        keys_values[..., kv_width:],
        lax.all_gather(segments, "ctx", axis=1, tiled=True),
    )
    row_max, row_sum, weighted = attend(
        start_state,
        gathered,
        jnp.int32(0),
    )
    mixed_heads = weighted / jnp.transpose(row_sum, (0, 3, 1, 2))[..., None]
    mixed_low = mixed_heads.astype(jnp.bfloat16).reshape(all_rows, q_local * head_dim)
    attn_term = by_transpose(mixed_low, w_out)
    residual = inputs + lax.psum(attn_term.astype(jnp.bfloat16), "wt").astype(jnp.float32)
    normed_ffn, ffn_unit, ffn_inverse = norm_rows(residual, ffn_gain)
    normed_ffn_low = normed_ffn.astype(jnp.bfloat16)
    gate_proj = product(normed_ffn_low, w_gate)
    up_proj = product(normed_ffn_low, w_up)
    gate_sigmoid = jax.nn.sigmoid(gate_proj)
    gate_silu = gate_proj * gate_sigmoid
    hidden_low = (gate_silu * up_proj).astype(jnp.bfloat16)
    mlp_term = by_transpose(hidden_low, w_down)
    output_rows = (
        residual + lax.psum(mlp_term.astype(jnp.bfloat16), "wt").astype(jnp.float32)
    ).astype(jnp.bfloat16)
    log_total = row_max + jnp.log(row_sum)
    grad_rows = cotangent.reshape(all_rows, model_width)
    grad_hidden = product(grad_rows, w_down)
    grad_gate = (
        grad_hidden * up_proj * gate_sigmoid * (1.0 + gate_proj * (1.0 - gate_sigmoid))
    ).astype(jnp.bfloat16)
    grad_up = (grad_hidden * gate_silu).astype(jnp.bfloat16)
    grad_normed_ffn = by_transpose(grad_gate, w_gate) + by_transpose(grad_up, w_up)
    ffn_gain_part = jnp.sum(grad_normed_ffn * ffn_unit, axis=0)
    grad_normed_ffn = lax.psum(grad_normed_ffn.astype(jnp.bfloat16), "wt").astype(jnp.float32)
    grad_residual = grad_rows.astype(jnp.float32) + norm_back(
        grad_normed_ffn, ffn_unit, ffn_inverse, ffn_gain
    )
    grad_residual_low = grad_residual.astype(jnp.bfloat16)
    grad_heads_low = product(grad_residual_low, w_out).astype(jnp.bfloat16)
    grad_groups = grad_heads_low.reshape(sequences, seq_rows, kv_local, per_group, head_dim)
    delta_rows = jnp.sum(grad_groups.astype(jnp.float32) * mixed_heads, axis=-1)
    delta_cols = jnp.transpose(delta_rows, (0, 2, 3, 1))
    query_grad_fn = partial(
        grad_piece,
        queries=query_groups,
        grad_heads=grad_groups,
        log_total=log_total,
        row_delta=delta_cols,
        query_places=places,
        query_segs=segments,
        score_scale=score_scale,
    )
    grad_query, grad_pairs = query_grad_fn(
        jnp.zeros((sequences, seq_rows, kv_local, per_group, head_dim), jnp.float32),
        gathered,
        jnp.int32(0),
    )
    grad_pairs = lax.psum_scatter(grad_pairs, "ctx", scatter_dimension=1, tiled=True).astype(
        jnp.float32
    )
    grad_key = grad_pairs[:, :, 0]
    grad_value = grad_pairs[:, :, 1]
    grad_query = rotate(
        grad_query.reshape(sequences, seq_rows, q_local, head_dim) * score_scale,
        cosine_table,
        sine_table,
        -1.0,
    )
    grad_key = rotate(grad_key * score_scale, cosine_table, sine_table, -1.0)
    q_gain_part = jnp.sum(grad_query * query_unit, axis=(0, 1, 2))
    k_gain_part = jnp.sum(grad_key * key_unit, axis=(0, 1, 2))
    grad_query_low = (
        norm_back(grad_query, query_unit, query_inverse, q_gain)
        .astype(jnp.bfloat16)
        .reshape(all_rows, q_local * head_dim)
    )
    grad_key_low = (
        norm_back(grad_key, key_unit, key_inverse, k_gain)
        .astype(jnp.bfloat16)
        .reshape(all_rows, kv_local * head_dim)
    )
    grad_value_low = grad_value.astype(jnp.bfloat16).reshape(all_rows, kv_local * head_dim)
    grad_normed = (
        by_transpose(grad_query_low, w_query)
        + by_transpose(grad_key_low, key_matrix)
        + by_transpose(grad_value_low, value_matrix)
    )
    attn_gain_part = jnp.sum(grad_normed * attn_unit, axis=0)
    grad_normed = lax.psum(grad_normed.astype(jnp.bfloat16), "wt").astype(jnp.float32)
    tokens_rows = (
        grad_residual + norm_back(grad_normed, attn_unit, attn_inverse, attn_gain)
    ).astype(jnp.bfloat16)
    output = output_rows.reshape(sequences, seq_rows, model_width)
    tokens_grad = tokens_rows.reshape(sequences, seq_rows, model_width)
    partial_sums = (
        transpose_by(grad_rows, hidden_low),
        transpose_by(normed_ffn_low, grad_gate),
        transpose_by(normed_ffn_low, grad_up),
        transpose_by(grad_residual_low, mixed_low),
        transpose_by(normed_low, grad_query_low),
        transpose_by(normed_low, grad_key_low),
        transpose_by(normed_low, grad_value_low),
    )
    summed = [
        lax.psum_scatter(part.astype(jnp.bfloat16), "ctx", scatter_dimension=0, tiled=True).astype(
            jnp.float32
        )
        for part in partial_sums
    ]
    w_down_grad, w_gate_grad, w_up_grad, w_out_grad = summed[:4]
    w_query_grad, w_key_grad, w_value_grad = summed[4:]
    attn_gain_grad, q_gain_grad, k_gain_grad, ffn_gain_grad = lax.psum(
        (attn_gain_part, q_gain_part, k_gain_part, ffn_gain_part), ("ctx", "wt")
    )
    return (
        output,
        tokens_grad,
        attn_gain_grad,
        w_query_grad,
        w_key_grad,
        w_value_grad,
        q_gain_grad,
        k_gain_grad,
        w_out_grad,
        ffn_gain_grad,
        w_gate_grad,
        w_up_grad,
        w_down_grad,
    )


def on_device(
    tokens,
    segments,
    attn_gain,
    w_query,
    key_matrix,
    value_matrix,
    q_gain,
    k_gain,
    w_out,
    ffn_gain,
    w_gate,
    w_up,
    w_down,
    cotangent,
):
    if not kernels_fit(tokens, w_query, key_matrix, q_gain, w_gate):
        return on_device_plain(
            tokens,
            segments,
            attn_gain,
            w_query,
            key_matrix,
            value_matrix,
            q_gain,
            k_gain,
            w_out,
            ffn_gain,
            w_gate,
            w_up,
            w_down,
            cotangent,
        )
    sequences, seq_rows, model_width = tokens.shape
    count, head_dim = lax.axis_size("ctx"), q_gain.shape[0]
    token_rows = tokens.reshape(sequences * seq_rows, model_width)
    table = jnp.asarray(rotary_table(count * seq_rows, head_dim))
    gains = {"attn_gain": attn_gain, "q_gain": q_gain, "k_gain": k_gain}
    sums = layer(
        {
            "segments": segments,
            **gains,
            "ffn_gain": ffn_gain,
            "w_query": w_query,
            "w_key": key_matrix,
            "w_value": value_matrix,
            "w_out": w_out,
            "tokens_in": token_rows,
            "table_in": table,
            "cotangent_in": cotangent.reshape(token_rows.shape),
            "w_down_in": w_down,
            "w_gate_in": w_gate,
            "w_up_in": w_up,
        }
    )
    done = dict(zip(RESULTS, hand_over([sums[name] for name in RESULTS]), strict=True))
    return (
        done["output"].reshape(tokens.shape),
        done["tokens_grad"].reshape(tokens.shape),
        done["attn_gain_sum"][0],
        done["w_query_sum"],
        done["w_key_sum"],
        done["w_value_sum"],
        done["q_gain_sum"][0, :head_dim],
        done["k_gain_sum"][0, :head_dim],
        done["w_out_sum"],
        done["ffn_gain_sum"][0],
        done["w_gate_sum"],
        done["w_up_sum"],
        done["w_down_sum"],
    )


def solution(mesh):
    in_specs = (
        P(None, "ctx", None),
        P(None, "ctx"),
        P(),
        P(None, "wt"),
        P(None, "wt"),
        P(None, "wt"),
        P(),
        P(),
        P(None, "wt"),
        P(),
        P(None, "wt"),
        P(None, "wt"),
        P(None, "wt"),
        P(None, "ctx", None),
    )
    out_specs = (
        P(None, "ctx", None),
        P(None, "ctx", None),
        P(),
        P("ctx", "wt"),
        P("ctx", "wt"),
        P("ctx", "wt"),
        P(),
        P(),
        P("ctx", "wt"),
        P(),
        P("ctx", "wt"),
        P("ctx", "wt"),
        P("ctx", "wt"),
    )
    return jax.shard_map(
        on_device, mesh=mesh, in_specs=in_specs, out_specs=out_specs, check_vma=False
    )
```

```python
from functools import partial
import math

import jax
import jax.numpy as jnp
import numpy as np
from jax import lax
from jax.experimental import pallas as pl
from jax.experimental.pallas import tpu as pltpu
from jax.sharding import PartitionSpec as P

EPS = 1e-05
THETA = 1000000.0
NEG = -1e30


def product(left, right):
    return jnp.dot(left, right, preferred_element_type=jnp.float32)


def by_transpose(left, right):
    return lax.dot_general(
        left, right, (((1,), (1,)), ((), ())), preferred_element_type=jnp.float32
    )


def transpose_by(left, right):
    return lax.dot_general(
        left, right, (((0,), (0,)), ((), ())), preferred_element_type=jnp.float32
    )


def norm_rows(values, gain):
    inverse = lax.rsqrt(jnp.mean(values * values, axis=-1, keepdims=True) + EPS)
    unit_rows = values * inverse
    return (unit_rows * gain, unit_rows, inverse)


def norm_back(grads, unit_rows, inverse, gain):
    scaled = grads * gain
    return inverse * (scaled - unit_rows * jnp.mean(scaled * unit_rows, axis=-1, keepdims=True))


def rotate(values, cosine_table, sine_table, direction):
    half_dim = values.shape[-1] // 2
    first_half = values[..., :half_dim]
    second_half = values[..., half_dim:]
    return jnp.concatenate(
        [
            first_half * cosine_table - direction * second_half * sine_table,
            second_half * cosine_table + direction * first_half * sine_table,
        ],
        axis=-1,
    )


def split_blocks(array, block_len):
    shaped = array.reshape(
        (array.shape[0], array.shape[1] // block_len, block_len) + array.shape[2:]
    )
    return jnp.moveaxis(shaped, 1, 0)


def attend_piece(folded, pieces, first_row, queries, query_places, query_segs, score_scale):
    key_piece, value_piece, seg_piece = pieces
    sequences, piece_rows = seg_piece.shape
    kv_local = queries.shape[2]
    head_dim = queries.shape[4]
    block_len = math.gcd(piece_rows, 512)
    key_blocks = split_blocks(
        key_piece.reshape(sequences, piece_rows, kv_local, head_dim), block_len
    )
    value_tiles = split_blocks(
        value_piece.reshape(sequences, piece_rows, kv_local, head_dim), block_len
    )
    seg_blocks = split_blocks(seg_piece, block_len)
    offsets = block_len * jnp.arange(piece_rows // block_len, dtype=jnp.int32)

    def attend_block_step(running, block_item):
        row_max, row_sum, weighted = running
        key_block, value_block, seg_block, offset = block_item
        key_places = offset + jnp.arange(block_len, dtype=jnp.int32)
        allowed = (key_places[None, None, :] <= query_places[None, :, None]) & (
            query_segs[:, :, None] == seg_block[:, None, :]
        )
        allowed = allowed[:, None, None]
        scores = (
            jnp.einsum("sqgrd,skgd->sgrqk", queries, key_block, preferred_element_type=jnp.float32)
            * score_scale
        )
        scores = jnp.where(allowed, scores, NEG)
        new_max = jnp.maximum(row_max, jnp.max(scores, axis=-1))
        weights = jnp.where(allowed, jnp.exp(scores - new_max[..., None]), 0.0)
        fading = jnp.exp(row_max - new_max)
        row_sum = row_sum * fading + jnp.sum(weights, axis=-1)
        fade_rows = jnp.transpose(fading, (0, 3, 1, 2))[..., None]
        weighted = weighted * fade_rows + jnp.einsum(
            "sgrqk,skgd->sqgrd",
            weights.astype(jnp.bfloat16),
            value_block,
            preferred_element_type=jnp.float32,
        )
        return ((new_max, row_sum, weighted), None)

    folded, unused = lax.scan(
        attend_block_step, folded, (key_blocks, value_tiles, seg_blocks, offsets)
    )
    return folded


def grad_piece(
    folded,
    pieces,
    first_row,
    queries,
    grad_heads,
    log_total,
    row_delta,
    query_places,
    query_segs,
    score_scale,
):
    key_piece, value_piece, seg_piece = pieces
    sequences, piece_rows = seg_piece.shape
    kv_local = queries.shape[2]
    head_dim = queries.shape[4]
    block_len = math.gcd(piece_rows, 512)
    key_blocks = split_blocks(
        key_piece.reshape(sequences, piece_rows, kv_local, head_dim), block_len
    )
    value_tiles = split_blocks(
        value_piece.reshape(sequences, piece_rows, kv_local, head_dim), block_len
    )
    seg_blocks = split_blocks(seg_piece, block_len)
    offsets = block_len * jnp.arange(piece_rows // block_len, dtype=jnp.int32)

    def grad_block_step(running, block_item):
        key_block, value_block, seg_block, offset = block_item
        key_places = offset + jnp.arange(block_len, dtype=jnp.int32)
        allowed = (key_places[None, None, :] <= query_places[None, :, None]) & (
            query_segs[:, :, None] == seg_block[:, None, :]
        )
        allowed = allowed[:, None, None]
        scores = (
            jnp.einsum("sqgrd,skgd->sgrqk", queries, key_block, preferred_element_type=jnp.float32)
            * score_scale
        )
        probs = jnp.where(allowed, jnp.exp(scores - log_total[..., None]), 0.0)
        grad_probs = jnp.einsum(
            "sqgrd,skgd->sgrqk", grad_heads, value_block, preferred_element_type=jnp.float32
        )
        grad_scores = (probs * (grad_probs - row_delta[..., None])).astype(jnp.bfloat16)
        running = running + jnp.einsum(
            "sgrqk,skgd->sqgrd", grad_scores, key_block, preferred_element_type=jnp.float32
        )
        grad_keys = jnp.einsum(
            "sgrqk,sqgrd->skgd", grad_scores, queries, preferred_element_type=jnp.float32
        )
        grad_values = jnp.einsum(
            "sgrqk,sqgrd->skgd",
            probs.astype(jnp.bfloat16),
            grad_heads,
            preferred_element_type=jnp.float32,
        )
        grads = jnp.stack([grad_keys, grad_values], axis=2).astype(jnp.bfloat16)
        return (running, grads)

    folded, grads = lax.scan(
        grad_block_step, folded, (key_blocks, value_tiles, seg_blocks, offsets)
    )
    return folded, jnp.moveaxis(grads, 0, 1).reshape((sequences, piece_rows) + grads.shape[3:])


MESH = pl.DeviceIdType.MESH
MIB = 1 << 20


def ring_place(index, count):
    return lax.select(
        lax.rem(index, 2) == 0, lax.div(index, 2), count - 1 - lax.div(index, 2)
    )


def ring_index(place, count):
    place = lax.rem(place + 2 * count, count)
    return lax.select(
        place < lax.div(count, 2), 2 * place, 2 * (count - 1 - place) + 1
    )


class Ring:
    def __init__(self, count, slots, send_sems, recv_sems, base=0):
        self.count, self.slots, self.base = count, slots, base
        self.send_sems, self.recv_sems = send_sems, recv_sems
        self.other = lax.axis_index("wt")
        self.place = ring_place(lax.axis_index("ctx"), count)
        self.right = ring_index(self.place + 1, count)
        self.left = ring_index(self.place + count - 1, count)
        self.half = slots.shape[2] // 2

    def copy(self, which, step, way):
        rows = pl.ds(way * self.half, self.half)
        slot = step - self.base
        return pltpu.make_async_remote_copy(
            src_ref=self.slots.at[which, slot, rows],
            dst_ref=self.slots.at[which, slot + 1, rows],
            send_sem=self.send_sems.at[which, slot, way],
            recv_sem=self.recv_sems.at[which, slot, way],
            device_id=((self.right, self.left)[way], self.other),
            device_id_type=MESH,
        )

    def arrived(self, which, step):
        for way in range(2):
            self.copy(which, step - 1, way).wait_recv()

    def tick(
        self,
        which,
        step,
        left_ref,
        right_ref,
        first=False,
        given=None,
        result=None,
        final=True,
    ):
        half = self.half
        rows = [
            ring_index(target, self.count) * (2 * half) + way * half
            for way, target in enumerate(
                (self.place + self.count - 1 - step, self.place + 1 + step)
            )
        ]
        left = jnp.concatenate(
            [left_ref[pl.ds(pl.multiple_of(row, half), half), :] for row in rows], axis=0
        )
        total = jnp.dot(left, right_ref[...], preferred_element_type=jnp.float32)
        if given is not None:
            total = total + given[...].astype(jnp.float32)
        elif not first:
            self.arrived(which, step)
            total = total + self.slots[which, step - self.base].astype(jnp.float32)
        def pass_on():
            self.slots[which, step - self.base] = total.astype(jnp.bfloat16)
            for way in range(2):
                self.copy(which, step, way).start()

        def keep():
            result[...] = total

        if result is None:
            pass_on()
        elif final is True:
            keep()
        else:
            pl.when(final)(keep)
            pl.when(jnp.logical_not(final))(pass_on)

    def finish(self, which, end):
        for way in range(2):

            def wait(step, carry):
                self.copy(which, step, way).wait_send()
                return carry

            lax.fori_loop(self.base, end, wait, 0)


def pair_lanes(shape):
    return lax.broadcasted_iota(jnp.int32, shape, 1)


def swap_halves(values, head_dim):
    lanes = pair_lanes(values.shape)
    width = values.shape[1]
    quarter = head_dim // 2
    return jnp.where(
        lax.rem(lanes, head_dim) < quarter,
        pltpu.roll(values, width - quarter, 1),
        pltpu.roll(values, quarter, 1),
    )


def pair_mean(values, head_dim):
    low = pair_lanes(values.shape) < head_dim
    first = jnp.sum(jnp.where(low, values, 0.0), axis=-1, keepdims=True)
    second = jnp.sum(jnp.where(low, 0.0, values), axis=-1, keepdims=True)
    return jnp.where(low, first, second) * (1.0 / head_dim)


def pair_norm(values, head_dim):
    inverse = lax.rsqrt(pair_mean(values * values, head_dim) + EPS)
    return values * inverse, inverse


def as_row(ref):
    return ref[...].astype(jnp.float32).reshape(1, -1)


def double(row):
    return jnp.concatenate([row, row], axis=-1)


def dot_nn(left, right):
    return jnp.dot(left, right, preferred_element_type=jnp.float32)


def dot_nt(left, right):
    return lax.dot_general(
        left, right, (((1,), (1,)), ((), ())), preferred_element_type=jnp.float32
    )


def as_column(row):
    size = row.shape[1]
    rows = lax.broadcasted_iota(jnp.int32, (size, size), 0)
    lanes = lax.broadcasted_iota(jnp.int32, (size, size), 1)
    return jnp.sum(jnp.where(rows == lanes, row, 0.0), axis=1, keepdims=True)


class Place:
    def __init__(self, count):
        self.count = count
        self.ctx, self.wt = lax.axis_index("ctx"), lax.axis_index("wt")
        self.odd = lax.rem(self.ctx, 2)
        self.level = lax.div(self.ctx, 2)
        self.core_bit = lax.rem(self.wt, 2)
        self.beside_ctx = self.ctx + 1 - 2 * self.odd
        self.beside = (self.beside_ctx, self.wt)
        self.above = (lax.rem(self.ctx + 2, count), self.wt)
        self.below = (lax.rem(self.ctx + count - 2, count), self.wt)
        self.has_above = self.ctx + 2 < count
        self.top = self.ctx >= count - 2
        self.serves = (self.ctx >= count - 4) & (self.ctx < count - 2)
        self.has_below = self.ctx >= 2
        self.core_wt = self.wt + 1 - 2 * self.core_bit
        self.chip_wt = lax.rem(self.wt + 2, 4)
        self.far_wt = lax.rem(self.core_wt + 2, 4)
        self.core = (self.ctx, self.core_wt)
        self.chip = (self.ctx, self.chip_wt)
        self.far = (self.ctx, self.far_wt)

    def signal(self, peer):
        pl.semaphore_signal(
            pltpu.get_barrier_semaphore(), inc=1, device_id=peer, device_id_type=MESH
        )

    def signal_all(self):
        for shift in range(1, self.count):
            self.signal((lax.rem(self.ctx + shift, self.count), self.wt))
        self.signal(self.core)
        self.signal(self.chip)
        self.signal(self.far)

    def await_all(self):
        pl.semaphore_wait(pltpu.get_barrier_semaphore(), self.count + 2)


def send_to(source, target, send_sem, recv_sem, device):
    return pltpu.make_async_remote_copy(
        src_ref=source,
        dst_ref=target,
        send_sem=send_sem,
        recv_sem=recv_sem,
        device_id=device,
        device_id_type=MESH,
    )


class WtSum:
    def __init__(self, here, tile, part, got, far, full, send_sems, recv_sems, before=None):
        self.here, self.tile, self.before = here, tile, before
        self.part, self.got, self.far, self.full = part, got, far, full
        self.send_sems, self.recv_sems = send_sems, recv_sems
        self.mine, self.theirs = here.core_bit, 1 - here.core_bit
        self.half = got.shape[1]

    def rows(self, seq):
        return pl.ds(pl.multiple_of(seq * self.tile, self.tile), self.tile)

    def cols(self, half):
        return pl.ds(pl.multiple_of(half * self.half, self.half), self.half)

    def copy(self, hop, seq, arriving=False):
        rows = self.rows(seq)
        half = self.theirs if arriving else self.mine
        source = (
            self.part.at[rows, self.cols(self.theirs)],
            self.got.at[rows],
            self.full.at[half, rows],
        )[hop]
        target = (self.got.at[rows], self.far.at[rows], self.full.at[half, rows])[hop]
        device = self.here.chip if hop == 1 else self.here.core
        return send_to(
            source, target, self.send_sems.at[hop, seq], self.recv_sems.at[hop, seq], device
        )

    def offer(self, seq, value):
        self.part[self.rows(seq), pl.ds(0, 2 * self.half)] = value.astype(jnp.bfloat16)
        self.copy(0, seq).start()

    def cross(self, seq):
        rows = self.rows(seq)
        self.copy(0, seq).wait_recv()
        total = self.part[rows, self.cols(self.mine)].astype(jnp.float32) + self.got[
            rows
        ].astype(jnp.float32)
        self.got[rows] = total.astype(jnp.bfloat16)
        self.copy(1, seq).start()

    def close(self, seq):
        rows = self.rows(seq)
        self.copy(1, seq).wait()
        total = self.got[rows].astype(jnp.float32) + self.far[rows].astype(jnp.float32)
        if self.before is not None:
            self.before.copy(2, seq).wait_send()
        self.full[self.mine, rows] = total.astype(jnp.bfloat16)
        self.copy(2, seq).start()

    def result(self, seq):
        rows = self.rows(seq)
        self.copy(2, seq, True).wait_recv()
        return jnp.concatenate([self.full[0, rows], self.full[1, rows]], axis=1).astype(
            jnp.float32
        )

    def finish(self, sequences, hops=(0, 2)):
        def sent(seq, carry):
            for hop in hops:
                self.copy(hop, seq).wait_send()
            return carry

        lax.fori_loop(0, sequences, sent, 0)


def ring_scratch(count, arrays, rows, width):
    return [
        pltpu.VMEM((arrays, count, rows, width), jnp.bfloat16),
        pltpu.SemaphoreType.DMA((arrays, count - 1, 2)),
        pltpu.SemaphoreType.DMA((arrays, count - 1, 2)),
    ]


class GainSum:
    def __init__(self, here, slots, beside, sends, recvs, pair_sends, pair_recvs):
        self.here, self.slots, self.beside = here, slots, beside
        self.sends, self.recvs = sends, recvs
        self.pair_sends, self.pair_recvs = pair_sends, pair_recvs

    def copy(self, shift, arriving=False):
        here = self.here
        target = lax.rem(here.ctx + shift, here.count)
        origin = lax.rem(here.ctx + here.count - shift, here.count)
        ref = self.slots.at[origin if arriving else here.ctx]
        return send_to(
            ref, ref, self.sends.at[shift - 1], self.recvs.at[shift - 1], (target, here.wt)
        )

    def pair_copy(self, hop):
        device = (self.here.core, self.here.chip)[hop]
        return send_to(
            self.beside.at[hop, 0],
            self.beside.at[hop, 1],
            self.pair_sends.at[hop],
            self.pair_recvs.at[hop],
            device,
        )

    def start(self):
        for shift in range(1, self.here.count):
            self.copy(shift).start()

    def sum_ctx(self):
        for shift in range(1, self.here.count):
            self.copy(shift, True).wait_recv()
        total = self.slots[0]
        for index in range(1, self.here.count):
            total = total + self.slots[index]
        self.beside[0, 0] = total
        self.pair_copy(0).start()

    def sum_cores(self):
        self.pair_copy(0).wait_recv()
        self.beside[1, 0] = self.beside[0, 0] + self.beside[0, 1]
        self.pair_copy(1).start()

    def sum_chips(self):
        self.pair_copy(1).wait_recv()
        return self.beside[1, 0] + self.beside[1, 1]

    def finish(self):
        for shift in range(1, self.here.count):
            self.copy(shift).wait_send()
        for hop in range(2):
            self.pair_copy(hop).wait_send()


class Mover:
    def __init__(self, pairs, sems):
        self.copies = [
            pltpu.make_async_copy(source, target, sems.at[i])
            for i, (source, target) in enumerate(pairs)
        ]

    def start(self, *which):
        for i in which:
            self.copies[i].start()

    def wait(self, *which):
        for i in which:
            self.copies[i].wait()


TICKS = (1, 1, 5)
REACH = 2
VMEM_LIMIT = 63 * MIB
RESULTS = (
    "output",
    "tokens_grad",
    "w_down_sum",
    "w_gate_sum",
    "w_up_sum",
    "w_out_sum",
    "w_query_sum",
    "w_key_sum",
    "w_value_sum",
    "attn_gain_sum",
    "ffn_gain_sum",
    "q_gain_sum",
    "k_gain_sum",
)


def layer_kernel(count, names, *refs):
    ref = dict(zip(names, refs, strict=True))
    tokens, segments = ref["tokens"], ref["segments"]
    residual, mixed_t, query_t = ref["residual"], ref["mixed_t"], ref["query_t"]
    logs, starts, keys_values = ref["logs"], ref["starts"], ref["keys_values"]
    query_raw, key_raw = ref["query_raw"], ref["key_raw"]
    grad_res, lefts = ref["grad_res"], ref["lefts"]
    ffn_grads, ffn_gain_part = ref["ffn_grads"], ref["ffn_gain_part"]
    all_segs, all_out, all_heads = ref["all_segs"], ref["all_out"], ref["all_heads"]
    acc, row_sum = ref["acc"], ref["row_sum"]
    w_gate, w_up, w_down = ref["w_gate"], ref["w_up"], ref["w_down"]
    gate_t, up_t, grad_hidden = ref["gate_t"], ref["up_t"], ref["grad_hidden"]
    cotangent, table = ref["cotangent"], ref["table"]
    sequences, tile = segments.shape
    head_dim = ref["q_gain"].shape[0]
    pair = 2 * head_dim
    levels = count // 2
    here = Place(count)
    me = here.ctx
    loads = Mover(
        [
            (ref["table_in"].at[pl.ds(pl.multiple_of(me * tile, tile), tile)], table),
            (ref["cotangent_in"], cotangent),
            (ref["w_down_in"], w_down),
            (ref["w_gate_in"], w_gate),
            (ref["w_up_in"], w_up),
            (ref["tokens_in"], tokens),
        ],
        ref["load_sems"],
    )
    loads.start(5, 0, 1, 2, 3, 4)
    shared = [ref[name] for name in ("sum_got", "sum_far", "sum_full")]
    ffn_sum = WtSum(here, tile, ref["ffn_part"], *shared, ref["ffn_send"], ref["ffn_recv"])
    ffn = Ring(count, *(ref[f"ffn{i}"] for i in range(3)))
    here.signal_all()
    all_segs[me] = jnp.zeros_like(all_segs[me])
    all_segs[me, pl.ds(0, sequences)] = segments[...]
    all_out[here.wt] = ref["w_out"][...].T

    rows_all, width = tokens.shape
    grad_heads_t = w_gate

    heads_small = gate_t.at[pl.ds(4 * tile, 2 * pair), pl.ds(2 * pair, sequences * tile)]

    def heads_at(seq):
        start = pl.multiple_of(seq * pair, pair)
        return (pl.ds(start, pair), pl.ds(rows_all, 4 * tile))

    def out_copy(hop, arriving=False):
        sent = (here.wt, here.wt, here.chip_wt)
        landed = (here.chip_wt, here.core_wt, here.far_wt)
        part = all_out.at[(landed if arriving else sent)[hop]]
        device = here.chip if hop == 0 else here.core
        return send_to(part, part, ref["out_send"].at[hop], ref["out_recv"].at[hop], device)

    def rows_of(seq):
        return pl.ds(pl.multiple_of(seq * tile, tile), tile)

    def block_of(index, step):
        return lax.rem(index - 2 * step + 2 * count, count)

    def up_copy(step, seq, arriving=False, forward=False):
        block = block_of(me, step) if arriving else block_of(me, step - 1) if forward else me
        rows = keys_values.at[block, rows_of(seq)]
        device = (lax.rem(me + (2 if forward else 2 * step), count), here.wt)
        return send_to(
            rows, rows, ref["up_send"].at[step, seq], ref["up_recv"].at[step, seq], device
        )

    def side_copy(step, seq, index=me):
        rows = keys_values.at[block_of(index, step), rows_of(seq)]
        return send_to(
            rows, rows, ref["side_send"].at[step, seq], ref["side_recv"].at[step, seq], here.beside
        )

    def seg_up_copy(step, arriving=False):
        part = all_segs.at[block_of(me, step) if arriving else me]
        device = (lax.rem(me + 2 * step, count), here.wt)
        return send_to(
            part, part, ref["seg_send"].at[step, 0], ref["seg_recv"].at[step, 0], device
        )

    def seg_side_copy(step, index=me):
        part = all_segs.at[block_of(index, step)]
        return send_to(
            part, part, ref["seg_send"].at[step, 1], ref["seg_recv"].at[step, 1], here.beside
        )

    def goes_up(step):
        return me + 2 * step < count

    def goes_aside(step):
        block = me - 2 * step
        return (block >= 0) & (block < here.beside_ctx)

    def comes_aside(step):
        block = here.beside_ctx - 2 * step
        return (block >= 0) & (block < me)

    def pass_segs():
        for step in range(1, levels):

            @pl.when(goes_up(step))
            def _():
                seg_up_copy(step).start()

        @pl.when(goes_aside(0))
        def _():
            seg_side_copy(0).start()

    def forwards(step):
        return (step > REACH) & (me >= 2 * (step - 1)) & here.has_above

    def pass_rows(seq):
        @pl.when(goes_aside(0))
        def _():
            side_copy(0, seq).start()

        for step in range(1, min(REACH + 1, levels)):

            @pl.when(goes_up(step))
            def _():
                up_copy(step, seq).start()

    gain = as_row(ref["attn_gain"])
    q_gain_pair = double(as_row(ref["q_gain"]))
    k_gain_pair = double(as_row(ref["k_gain"]))
    ffn_gain_row = as_row(ref["ffn_gain"])
    loads.wait(0, 5)

    def share_copy(what, seq):
        source = (
            query_t.at[seq],
            ref["stats_out"].at[seq],
            heads_small.at[:, pl.ds(pl.multiple_of(seq * tile, tile), tile)],
            ref["deltas"].at[seq],
        )[what]
        target = (
            ref["upper_query_t"],
            ref["stats_in"],
            ref["upper_heads"],
            ref["upper_deltas"],
        )[what].at[seq]
        sems = ref["share_send"].at[what, seq], ref["share_recv"].at[what, seq]
        return send_to(source, target, *sems, here.below)

    def turn(values):
        cosine = table[:, pl.ds(0, pair)]
        sine = table[:, pl.ds(pair, pair)]
        return values * cosine + swap_halves(values, head_dim) * sine

    def project(seq, carry):
        rows = rows_of(seq)
        inputs = tokens[rows, :].astype(jnp.float32)
        inverse = lax.rsqrt(jnp.mean(inputs * inputs, axis=-1, keepdims=True) + EPS)
        normed = (inputs * inverse * gain).astype(jnp.bfloat16)
        raw_k = dot_nn(normed, ref["w_key"][...])
        key_raw[rows, :] = raw_k
        unit, unused = pair_norm(raw_k, head_dim)
        keys_values[me, rows, pl.ds(0, pair)] = turn(unit * k_gain_pair).astype(jnp.bfloat16)
        keys_values[me, rows, pl.ds(pair, pair)] = dot_nn(normed, ref["w_value"][...]).astype(
            jnp.bfloat16
        )

        @pl.when(seq == 0)
        def _():
            here.await_all()
            pass_segs()

        @pl.when(seq == 0)
        def _():
            pass_rows(seq)

        @pl.when(seq == 0)
        def _():
            out_copy(0).start()
            out_copy(1).start()

        raw_q = dot_nn(normed, ref["w_query"][...])
        query_raw[rows, :] = raw_q
        query_t[seq] = jnp.zeros_like(query_t[seq])
        for group in range(2):
            unit, unused = pair_norm(raw_q[:, group * pair : (group + 1) * pair], head_dim)
            turned = turn(unit * q_gain_pair) * (head_dim**-0.5)
            flipped = turned.T.astype(jnp.bfloat16)
            for member in range(2):
                query_t[
                    seq,
                    pl.ds(group * head_dim, head_dim),
                    pl.ds((2 * group + member) * tile, tile),
                ] = flipped[member * head_dim : (member + 1) * head_dim]

        @pl.when(here.top)
        def _():
            share_copy(0, seq).start()

        acc[seq] = jnp.zeros_like(acc[seq])
        row_sum[seq] = jnp.zeros_like(row_sum[seq])
        starts[seq] = jnp.zeros_like(starts[seq])
        return carry

    def route_level(step, seq):
        @pl.when(me >= 2 * step)
        def _():
            @pl.when(seq == 0)
            def _():
                seg_up_copy(step, True).wait_recv()
                seg_side_copy(step).start()

            up_copy(step, seq, True).wait_recv()
            side_copy(step, seq).start()

            @pl.when(forwards(step + 1))
            def _():
                up_copy(step + 1, seq, forward=True).start()

    def route(seq):
        def level(step, carry):
            route_level(step, seq)
            return carry

        lax.fori_loop(1, levels, level, 0)

    lax.fori_loop(0, sequences, project, 0)
    pass_rows(1)
    for step in range(1, min(REACH + 1, levels)):
        route_level(step, 0)
    loads.wait(1, 2)

    def back_down(seq, carry):
        rows = rows_of(seq)
        grads = cotangent[rows, :]
        lefts[0, :, rows] = grads.T
        grad_hidden[rows, :] = dot_nn(grads, w_down[...]).astype(jnp.bfloat16)
        return carry

    lax.fori_loop(0, sequences, back_down, 0)
    for step in range(REACH + 1, levels):
        route_level(step, 0)

    loads.wait(3, 4)

    def flip(index, carry):
        rows = pl.ds(pl.multiple_of(index * 128, 128), 128)
        gate_t[:, rows] = w_gate[rows, :].T
        up_t[:, rows] = w_up[rows, :].T
        return carry

    lax.fori_loop(0, tokens.shape[1] // 128, flip, 0)
    key_rows = lax.broadcasted_iota(jnp.int32, (tile, tile), 0)
    query_cols = lax.broadcasted_iota(jnp.int32, (tile, tile), 1)

    def attend(blocks, seq):
        rows = rows_of(seq)
        seg_query = all_segs[me, pl.ds(seq, 1)].astype(jnp.float32)
        masks, values_t = [], []
        for block in blocks:
            seg_key = as_column(all_segs[block, pl.ds(seq, 1)].astype(jnp.float32))
            earlier = jnp.where(seg_key < seg_query, 1.0, 0.0)
            starts[seq] += jnp.sum(earlier, axis=0, keepdims=True)
            if block is me:
                same = (seg_key == seg_query) & (key_rows <= query_cols)
                masks.append(jnp.where(same, 1.0, 0.0))
            else:
                masks.append(1.0 - earlier)
            values_t.append(keys_values[block, rows, pl.ds(pair, pair)].T)
        keys = [keys_values[block, rows, pl.ds(0, pair)] for block in blocks]
        mask = jnp.concatenate(masks, axis=0)
        scores = dot_nn(jnp.concatenate(keys, axis=0), query_t[seq])
        weights = jnp.exp(scores) * jnp.concatenate([mask] * 4, axis=1)
        row_sum[seq] += jnp.sum(weights, axis=0, keepdims=True)
        low = weights.astype(jnp.bfloat16)
        value_rows = jnp.concatenate(values_t, axis=1)
        for group in range(2):
            acc[seq, group] += dot_nn(
                value_rows[group * head_dim : (group + 1) * head_dim],
                low[:, group * 2 * tile : (group + 1) * 2 * tile],
            )

    def attend_own(seq, carry):
        attend([me], seq)
        return carry

    lax.fori_loop(0, sequences, attend_own, 0)

    def head_copy(hop, seq, arriving=False):
        sent = (here.wt, here.wt, here.chip_wt)
        landed = (here.chip_wt, here.core_wt, here.far_wt)
        part = all_heads.at[(landed if arriving else sent)[hop], rows_of(seq)]
        device = here.chip if hop == 0 else here.core
        return send_to(
            part, part, ref["head_send"].at[hop, seq], ref["head_recv"].at[hop, seq], device
        )

    def far_copy(seq):
        part = all_heads.at[here.wt, rows_of(seq)]
        return send_to(
            part, part, ref["head_send"].at[2, seq], ref["head_recv"].at[2, seq], here.far
        )

    def relay(seq):
        head_copy(0, seq, True).wait_recv()

        @pl.when(seq < sequences - 1)
        def _():
            head_copy(2, seq).start()

    def mix(seq):
        rows = rows_of(seq)
        total = row_sum[seq]
        logs[seq] = jnp.log(total)
        for group in range(2):
            cols = slice(group * 2 * tile, (group + 1) * 2 * tile)
            part = acc[seq, group] / total[:, cols]
            mixed = jnp.concatenate([part[:, :tile], part[:, tile:]], axis=0)
            mixed_t[seq, group] = mixed
            all_heads[here.wt, rows, pl.ds(group * pair, pair)] = mixed.T.astype(jnp.bfloat16)
        head_copy(0, seq).start()
        head_copy(1, seq).start()

        @pl.when(here.top)
        def _():
            stats_out = ref["stats_out"]
            stats_out[seq] = jnp.zeros_like(stats_out[seq])
            stats_out[seq, pl.ds(0, 1)] = logs[seq]
            stats_out[seq, pl.ds(1, 1), pl.ds(0, tile)] = starts[seq]
            share_copy(1, seq).start()

        @pl.when(seq == sequences - 1)
        def _():
            far_copy(seq).start()

    def ffn_unit(rows):
        values = residual[rows, :]
        inverse = lax.rsqrt(jnp.mean(values * values, axis=-1, keepdims=True) + EPS)
        return values * inverse, inverse

    def feed(seq):
        rows = rows_of(seq)
        head_copy(1, seq, True).wait_recv()
        head_copy(2, seq, True).wait_recv()
        total = tokens[rows, :].astype(jnp.float32)
        for slot in range(4):
            total = total + dot_nn(all_heads[slot, rows], all_out[slot])
        residual[rows, :] = total
        unit, unused = ffn_unit(rows)
        normed = (unit * ffn_gain_row).astype(jnp.bfloat16)
        lefts[1, :, rows] = normed.T
        gate = dot_nn(normed, w_gate[...])
        up = dot_nn(normed, w_up[...])
        sigmoid = 0.5 * jnp.tanh(0.5 * gate) + 0.5
        silu = gate * sigmoid
        ffn_grads[0, rows] = (silu * up).astype(jnp.bfloat16)
        grads = grad_hidden[rows, :].astype(jnp.float32)
        grad_gate = (grads * up * sigmoid * (1.0 + gate * (1.0 - sigmoid))).astype(jnp.bfloat16)
        grad_up = (grads * silu).astype(jnp.bfloat16)
        ffn_grads[1, rows] = grad_gate
        ffn_grads[2, rows] = grad_up
        grad_normed = dot_nn(grad_gate, gate_t[...]) + dot_nn(grad_up, up_t[...])
        ffn_gain_part[...] += jnp.sum(grad_normed * unit, axis=0, keepdims=True)
        ffn_sum.offer(seq, grad_normed)

    ffn_gain_part[...] = jnp.zeros_like(ffn_gain_part)

    def sequence_turn(turn_, carry):
        @pl.when(turn_ < sequences)
        def _():
            @pl.when(turn_ + 2 < sequences)
            def _():
                pass_rows(turn_ + 2)

            @pl.when(comes_aside(0))
            def _():
                @pl.when(turn_ == 0)
                def _():
                    seg_side_copy(0, here.beside_ctx).wait_recv()

                side_copy(0, turn_, here.beside_ctx).wait_recv()
                attend([here.beside_ctx], turn_)

        @pl.when(turn_ + 1 < sequences)
        def _():
            for step in range(1, min(REACH + 1, levels)):
                route_level(step, turn_ + 1)

        @pl.when(turn_ == 1)
        def _():
            out_copy(0, True).wait_recv()
            out_copy(2).start()

        @pl.when((turn_ > 0) & (turn_ <= sequences))
        def _():
            relay(turn_ - 1)

        @pl.when(turn_ < sequences)
        def _():
            def level(step, carry):
                @pl.when(me >= 2 * step)
                def _():
                    @pl.when(turn_ == 0)
                    def _():
                        seg_side_copy(step, here.beside_ctx).wait_recv()

                    side_copy(step, turn_, here.beside_ctx).wait_recv()
                    attend([block_of(me, step), block_of(here.beside_ctx, step)], turn_)

                return carry

            lax.fori_loop(1, levels, level, 0)
            mix(turn_)

        @pl.when(turn_ + 1 < sequences)
        def _():
            for step in range(REACH + 1, levels):
                route_level(step, turn_ + 1)

        @pl.when(turn_ == 1)
        def _():
            out_copy(1, True).wait_recv()
            out_copy(2, True).wait_recv()

        @pl.when(turn_ > 1)
        def _():
            ffn_sum.cross(turn_ - 2)

        @pl.when(turn_ > 0)
        def _():
            feed(turn_ - 1)

        @pl.when(turn_ > 2)
        def _():
            ffn_sum.close(turn_ - 3)

        return carry

    lax.fori_loop(0, sequences + 1, sequence_turn, 0)
    for i in range(3):
        ffn.tick(i, 0, lefts.at[min(i, 1)], ffn_grads.at[i], first=True)
    last = count - 1
    deltas, own_grads = ref["deltas"], ref["own_grads"]
    side_in, side_out = ref["side_in"], ref["side_out"]
    line_in, line_out = ref["line_in"], ref["line_out"]
    ffn_sums, qkv_total = ref["ffn_sums"], ref["qkv_total"]
    grad_query_t = acc
    grad_res_t = w_gate.at[:, pl.ds(0, rows_all)]
    query_n = gate_t.at[pl.ds(0, 4 * tile), pl.ds(0, pair)]
    grad_heads_n = gate_t.at[pl.ds(4 * tile, 4 * tile), pl.ds(0, pair)]
    upper_query_n = gate_t.at[pl.ds(0, 4 * tile), pl.ds(pair, pair)]
    upper_heads_t = gate_t.at[pl.ds(0, pair), pl.ds(2 * pair, 4 * tile)]
    upper_heads_n = gate_t.at[pl.ds(4 * tile, 4 * tile), pl.ds(pair, pair)]
    grad_qkv = w_up.at[pl.ds(0, rows_all), pl.ds(0, 4 * pair)]
    normed_t = w_up.at[:, pl.ds(4 * pair, rows_all)]
    qkv_t = up_t.at[pl.ds(rows_all, 4 * pair)]
    heads = all_heads.at[here.wt]
    sources = {
        "output": cotangent,
        "tokens_grad": tokens,
        "w_down_sum": ffn_sums.at[0],
        "w_gate_sum": ffn_sums.at[1],
        "w_up_sum": ffn_sums.at[2],
        "w_query_sum": qkv_total.at[:, pl.ds(0, 2 * pair)],
        "w_key_sum": qkv_total.at[:, pl.ds(2 * pair, pair)],
        "w_value_sum": qkv_total.at[:, pl.ds(3 * pair, pair)],
    }
    stores = Mover(
        [(sources[name] if name in sources else ref[name], ref[name + "_res"]) for name in RESULTS],
        ref["store_sems"],
    )
    wt_sum = WtSum(here, tile, up_t, *shared, ref["wt_send"], ref["wt_recv"], ffn_sum)
    mlp_sum = WtSum(here, tile, grad_hidden, *(ref[f"mlp_sum{i}"] for i in range(5)))
    gains = GainSum(here, *(ref[f"gains{i}"] for i in range(6)))
    gain_slots = ref["gains0"]
    out = Ring(count, *(ref[f"out{i}"] for i in range(3)))
    qkv = Ring(count, *(ref[f"qkv{i}"] for i in range(3)))

    def ffn_tick(index):
        step, which = lax.div(index, 3), lax.rem(index, 3)
        ffn.tick(
            which,
            step,
            lefts.at[lax.min(which, 1)],
            ffn_grads.at[which],
            result=ffn_sums.at[which],
            final=step == last,
        )

    def token_unit(rows):
        inputs = tokens[rows, :].astype(jnp.float32)
        inverse = lax.rsqrt(jnp.mean(inputs * inputs, axis=-1, keepdims=True) + EPS)
        return inputs * inverse, inverse

    def prepare(seq):
        rows = rows_of(seq)
        unit, inverse = ffn_unit(rows)
        scaled = ffn_sum.result(seq) * ffn_gain_row
        back = inverse * (scaled - unit * jnp.mean(scaled * unit, axis=-1, keepdims=True))
        grads = (cotangent[rows, :].astype(jnp.float32) + back).astype(jnp.bfloat16)
        grad_res[rows, :] = grads
        grad_res_t[:, rows] = grads.T
        unit, unused = token_unit(rows)
        normed_t[:, rows] = (unit * gain).astype(jnp.bfloat16).T
        grad_heads_t[heads_at(seq)] = jnp.zeros((pair, 4 * tile), jnp.bfloat16)
        low = dot_nn(grads, ref["w_out"][...]).astype(jnp.bfloat16)
        for group in range(2):
            flipped = low[:, group * pair : (group + 1) * pair].T
            small = pl.ds(pl.multiple_of(seq * tile, tile), tile)
            heads_small[pl.ds(group * pair, pair), small] = flipped
            product_t = flipped.astype(jnp.float32) * mixed_t[seq, group]
            for member in range(2):
                part = slice(member * head_dim, (member + 1) * head_dim)
                cols = pl.ds((2 * group + member) * tile, tile)
                into = pl.ds(pl.multiple_of(seq * pair + group * head_dim, head_dim), head_dim)
                spot = pl.ds(rows_all + (2 * group + member) * tile, tile)
                grad_heads_t[into, spot] = flipped[part]
                deltas[seq, :, cols] = jnp.sum(product_t[part], axis=0, keepdims=True)
        grad_query_t[seq] = jnp.zeros_like(grad_query_t[seq])

        @pl.when(here.top)
        def _():
            share_copy(2, seq).start()
            share_copy(3, seq).start()

    def grads_of(blocks, seq, upper=False):
        rows = rows_of(seq)
        keys = [keys_values[block, rows, pl.ds(0, pair)] for block in blocks]
        values = [keys_values[block, rows, pl.ds(pair, pair)] for block in blocks]
        if upper:
            stats = ref["stats_in"]
            log, start = stats[seq, pl.ds(0, 1)], stats[seq, pl.ds(1, 1), pl.ds(0, tile)]
            delta = ref["upper_deltas"][seq]
            queries, grad_heads = ref["upper_query_t"][seq], upper_heads_t[...]
            query_rows, grad_rows = upper_query_n, upper_heads_n
        else:
            log, start, delta = logs[seq], starts[seq], deltas[seq]
            queries, grad_heads = query_t[seq], grad_heads_t[heads_at(seq)]
            query_rows, grad_rows = query_n, grad_heads_n
        masks = []
        for block in blocks:
            allowed = key_rows.astype(jnp.float32) >= start - (block * tile).astype(jnp.float32)
            if block is me and not upper:
                allowed = allowed & (key_rows <= query_cols)
            masks.append(jnp.where(allowed, 1.0, 0.0))
        mask = jnp.concatenate(masks, axis=0)
        scores = dot_nn(jnp.concatenate(keys, axis=0), queries)
        probs = jnp.exp(scores - log) * jnp.concatenate([mask] * 4, axis=1)
        grad_probs = dot_nn(jnp.concatenate(values, axis=0), grad_heads)
        grad_scores = (probs * (grad_probs - delta)).astype(jnp.bfloat16)
        flipped = jnp.concatenate([part.T for part in keys], axis=1)
        for group in range(2):
            cols = slice(group * 2 * tile, (group + 1) * 2 * tile)
            grads = dot_nn(
                flipped[group * head_dim : (group + 1) * head_dim], grad_scores[:, cols]
            )
            if upper:
                ref["upper_grad"][group] += grads
            else:
                grad_query_t[seq, group] += grads
        grad_keys = dot_nn(grad_scores, query_rows[...])
        grad_values = dot_nn(probs.astype(jnp.bfloat16), grad_rows[...])
        return jnp.concatenate([grad_keys, grad_values], axis=1)

    def side_grad_copy(step, seq):
        return send_to(
            side_out.at[step, rows_of(seq)],
            side_in.at[step, rows_of(seq)],
            ref["side_grad_send"].at[step, seq],
            ref["side_grad_recv"].at[step, seq],
            here.beside,
        )

    def line_copy(step, seq):
        earlier = step - 1
        return send_to(
            line_out.at[earlier, rows_of(seq)],
            line_in.at[earlier, rows_of(seq)],
            ref["line_send"].at[earlier, seq],
            ref["line_recv"].at[earlier, seq],
            here.below,
        )

    two = ref["two_grads"]

    def hands_down(step):
        return (me >= 2 * step) & (here.has_above | (step == 1))

    def upper_grad_copy(seq):
        return send_to(
            ref["upper_grad_out"].at[seq],
            ref["upper_grad_in"].at[seq],
            ref["upper_send"].at[seq],
            ref["upper_recv"].at[seq],
            here.above,
        )

    def send_side(step, seq):
        side_out[step, rows_of(seq)] = two[pl.ds(tile, tile)].astype(jnp.bfloat16)
        side_grad_copy(step, seq).start()

    def find_grads(seq):
        rows = rows_of(seq)
        query_n[...] = query_t[seq].T
        grad_heads_n[...] = grad_heads_t[heads_at(seq)].T

        @pl.when(here.serves)
        def _():
            for what in range(4):
                share_copy(what, seq).wait_recv()
            upper_heads_t[...] = jnp.zeros_like(upper_heads_t)
            for group in range(2):
                for member in range(2):
                    part = ref["upper_heads"][
                        seq, pl.ds(group * pair + member * head_dim, head_dim)
                    ]
                    cols = pl.ds((2 * group + member) * tile, tile)
                    upper_heads_t[pl.ds(group * head_dim, head_dim), cols] = part
            upper_query_n[...] = ref["upper_query_t"][seq].T
            upper_heads_n[...] = upper_heads_t[...].T
            ref["upper_grad"][...] = jnp.zeros_like(ref["upper_grad"])

        def level(index, carry):
            step = levels - 2 - index

            @pl.when(hands_down(step))
            def _():
                blocks = [block_of(me, step), block_of(here.beside_ctx, step)]
                two[...] = grads_of(blocks, seq)

                @pl.when(here.serves)
                def _():
                    two[...] += grads_of(blocks, seq, True)

                send_side(step, seq)
                line_out[step - 1, rows] = two[pl.ds(0, tile)].astype(jnp.bfloat16)

            return carry

        lax.fori_loop(0, levels - 2, level, 0)

        @pl.when(comes_aside(0))
        def _():
            two[...] = grads_of([me, here.beside_ctx], seq)

        @pl.when(jnp.logical_not(comes_aside(0)))
        def _():
            two[pl.ds(0, tile)] = grads_of([me], seq)

        @pl.when(here.serves)
        def _():
            ref["upper_grad_out"][seq] = ref["upper_grad"][...].astype(jnp.bfloat16)
            upper_grad_copy(seq).start()

        @pl.when(comes_aside(0))
        def _():
            send_side(0, seq)

        own_grads[rows, :] = two[pl.ds(0, tile)]

    gets_line = me < count - 4

    def send_down(step, seq):
        @pl.when(hands_down(step))
        def _():
            rows = rows_of(seq)
            side_grad_copy(step, seq).wait_recv()
            total = line_out[step - 1, rows].astype(jnp.float32) + side_in[step, rows].astype(
                jnp.float32
            )

            @pl.when(gets_line)
            def _():
                line_copy(step + 1, seq).wait_recv()
                line_out[step - 1, rows] = (
                    total + line_in[step, rows].astype(jnp.float32)
                ).astype(jnp.bfloat16)

            @pl.when(jnp.logical_not(gets_line))
            def _():
                line_out[step - 1, rows] = total.astype(jnp.bfloat16)

            line_copy(step, seq).start()

    gain_slots[me] = jnp.zeros_like(gain_slots[me])
    gain_slots[me, pl.ds(1, 1)] = ffn_gain_part[...]

    def back_through(grads, raw, gain_pair, row):
        cosine = table[:, pl.ds(0, pair)]
        sine = table[:, pl.ds(pair, pair)]
        turned = grads * cosine - swap_halves(grads, head_dim) * sine
        unit, inverse = pair_norm(raw, head_dim)
        gain_slots[me, pl.ds(row, 1), pl.ds(0, pair)] += jnp.sum(
            turned * unit, axis=0, keepdims=True
        )
        scaled = turned * gain_pair
        return (inverse * (scaled - unit * pair_mean(scaled * unit, head_dim))).astype(
            jnp.bfloat16
        )

    def project_back(seq):
        rows = rows_of(seq)

        @pl.when(here.top)
        def _():
            upper_grad_copy(seq).wait_recv()
            grad_query_t[seq] += ref["upper_grad_in"][seq].astype(jnp.float32)

        for group in range(2):
            grads = grad_query_t[seq, group] * (head_dim**-0.5)
            grads = jnp.concatenate([grads[:, :tile], grads[:, tile:]], axis=0).T
            cols = pl.ds(group * pair, pair)
            grad_qkv[rows, cols] = back_through(grads, query_raw[rows, cols], q_gain_pair, 2)

        @pl.when(me < here.beside_ctx)
        def _():
            side_grad_copy(0, seq).wait_recv()
            own_grads[rows, :] += side_in[0, rows].astype(jnp.float32)

        @pl.when(here.has_above)
        def _():
            line_copy(1, seq).wait_recv()
            own_grads[rows, :] += line_in[0, rows].astype(jnp.float32)

        grad_qkv[rows, pl.ds(2 * pair, pair)] = back_through(
            own_grads[rows, pl.ds(0, pair)], key_raw[rows, :], k_gain_pair, 3
        )
        grad_qkv[rows, pl.ds(3 * pair, pair)] = own_grads[rows, pl.ds(pair, pair)].astype(
            jnp.bfloat16
        )
        grads = dot_nn(grad_qkv[rows, :], qkv_t[...])
        unit, unused = token_unit(rows)
        gain_slots[me, pl.ds(0, 1)] += jnp.sum(grads * unit, axis=0, keepdims=True)
        wt_sum.offer(seq, grads)

    def output_rows(seq):
        rows = rows_of(seq)
        cotangent[rows, :] = (residual[rows, :] + mlp_sum.result(seq)).astype(jnp.bfloat16)

    def token_rows(seq):
        rows = rows_of(seq)
        unit, inverse = token_unit(rows)
        scaled = wt_sum.result(seq) * gain
        grads = inverse * (scaled - unit * jnp.mean(scaled * unit, axis=-1, keepdims=True))
        tokens[rows, :] = (grad_res[rows, :].astype(jnp.float32) + grads).astype(
            jnp.bfloat16
        )

    few, more, early = TICKS

    def ticks_before(turn_):
        return 3 + few * lax.min(turn_, early) + more * lax.max(turn_ - early, 0)

    def grad_turn(turn_, carry):
        @pl.when(turn_ < sequences)
        def _():
            prepare(turn_)

        @pl.when((turn_ >= 1) & (turn_ <= sequences))
        def _():
            find_grads(turn_ - 1)

        @pl.when(turn_ == 0)
        def _():
            ffn_sum.cross(sequences - 1)
            qkv_t[pl.ds(0, 2 * pair), :] = ref["w_query"][...].T
            qkv_t[pl.ds(2 * pair, pair), :] = ref["w_key"][...].T
            qkv_t[pl.ds(3 * pair, pair), :] = ref["w_value"][...].T

        @pl.when((turn_ == 1) | (turn_ == 2))
        def _():
            ffn_sum.close(sequences - 3 + turn_)

        @pl.when((turn_ >= 3) & (turn_ < sequences + 3))
        def _():
            def down(index, carry):
                send_down(levels - 2 - index, turn_ - 3)
                return carry

            lax.fori_loop(0, levels - 2, down, 0)

        for i in range(max(few, more)):

            @pl.when(ticks_before(turn_) + i < ticks_before(turn_ + 1))
            def _():
                ffn_tick(ticks_before(turn_) + i)

        @pl.when((turn_ >= 1) & (turn_ <= sequences))
        def _():
            seq = turn_ - 1
            mlp_sum.offer(seq, dot_nt(ffn_grads[0, rows_of(seq)], w_down[...]))

        @pl.when((turn_ >= 2) & (turn_ <= sequences + 1))
        def _():
            mlp_sum.cross(turn_ - 2)

        @pl.when((turn_ >= 3) & (turn_ <= sequences + 2))
        def _():
            mlp_sum.close(turn_ - 3)

        @pl.when(turn_ >= 5)
        def _():
            output_rows(turn_ - 5)
            project_back(turn_ - 5)

        @pl.when(turn_ >= 6)
        def _():
            wt_sum.cross(turn_ - 6)

        for i in range(4):

            @pl.when(turn_ == sequences + i)
            def _():
                out.tick(0, i, grad_res_t, heads, first=i == 0)

        return carry

    turns = sequences + 5
    lax.fori_loop(0, turns, grad_turn, 0)
    qkv.tick(0, 0, normed_t, grad_qkv, first=True)
    gains.start()
    wt_sum.cross(sequences - 1)
    stores.start(0)
    done = 3 + few * early + more * (turns - early)
    left_over = 3 * count - done
    each = -(-left_over // (last - 1))

    def tail(step, carry):
        @pl.when(step == 2)
        def _():
            gains.sum_ctx()

        @pl.when(step == 3)
        def _():
            gains.sum_cores()

        @pl.when(step == 4)
        def _():
            total = gains.sum_chips()
            ref["attn_gain_sum"][...] = total[0:1]
            ref["ffn_gain_sum"][...] = total[1:2]
            folded = total[:, :pair]
            folded = folded + pltpu.roll(folded, head_dim, 1)
            ref["q_gain_sum"][...] = folded[2:3]
            ref["k_gain_sum"][...] = folded[3:4]

        @pl.when(step == last)
        def _():
            stores.start(1, 2, 3, 4, 5, 9, 10, 11, 12)

        for i in range(each):
            index = done + each * (step - 1) + i

            @pl.when(index < 3 * count)
            def _():
                ffn_tick(index)

        qkv.tick(0, step, normed_t, grad_qkv, result=qkv_total, final=step == last)

        @pl.when(step + 3 <= last)
        def _():
            out.tick(
                0, step + 3, grad_res_t, heads, result=ref["w_out_sum"], final=step + 3 == last
            )

        @pl.when(step <= sequences)
        def _():
            wt_sum.close(step - 1)

        @pl.when((step >= 2) & (step <= sequences + 1))
        def _():
            token_rows(step - 2)

        return carry

    lax.fori_loop(1, count, tail, 0)
    stores.start(6, 7, 8)
    gains.finish()
    ffn_sum.finish(sequences, (0,))
    wt_sum.finish(sequences)
    mlp_sum.finish(sequences)
    for i in range(3):
        ffn.finish(i, last)
    out.finish(0, last)
    qkv.finish(0, last)
    for hop in range(3):
        out_copy(hop).wait_send()

        def sent(seq, carry):
            head_copy(hop, seq).wait_send()
            return carry

        lax.fori_loop(0, sequences, sent, 0)

    def each_seq(step):
        def one(seq, carry):
            step(seq)
            return carry

        lax.fori_loop(0, sequences, one, 0)

    def drain(step, carry):
        @pl.when((step > 0) & goes_up(step))
        def _():
            seg_up_copy(step).wait_send()

        @pl.when(((step > 0) & (step <= REACH) & goes_up(step)) | forwards(step))
        def _():
            each_seq(lambda seq: up_copy(step, seq).wait_send())

        @pl.when(goes_aside(step))
        def _():
            seg_side_copy(step).wait_send()

        @pl.when(goes_aside(step))
        def _():
            each_seq(lambda seq: side_copy(step, seq).wait_send())

        @pl.when((step > 0) & (step < levels - 1) & hands_down(step))
        def _():
            each_seq(lambda seq: side_grad_copy(step, seq).wait_send())
            each_seq(lambda seq: line_copy(step, seq).wait_send())

        return carry

    lax.fori_loop(0, levels, drain, 0)

    @pl.when(comes_aside(0))
    def _():
        each_seq(lambda seq: side_grad_copy(0, seq).wait_send())

    @pl.when(here.top)
    def _():
        for what in range(4):
            each_seq(lambda seq: share_copy(what, seq).wait_send())

    @pl.when(here.serves)
    def _():
        each_seq(lambda seq: upper_grad_copy(seq).wait_send())

    stores.wait(*range(len(RESULTS)))


def layer(inputs):
    count = lax.axis_size("ctx")
    sequences, tile = inputs["segments"].shape
    rows, width = inputs["tokens_in"].shape
    head_dim = inputs["q_gain"].shape[0]
    hidden = inputs["w_gate_in"].shape[1]
    pair = 2 * head_dim
    levels = count // 2
    block = width // count
    f32, bf16 = jnp.float32, jnp.bfloat16
    dma = pltpu.SemaphoreType.DMA
    results = {
        "output": ((rows, width), bf16),
        "tokens_grad": ((rows, width), bf16),
        "w_down_sum": ((block, hidden), f32),
        "w_gate_sum": ((block, hidden), f32),
        "w_up_sum": ((block, hidden), f32),
        "w_out_sum": ((block, 2 * pair), f32),
        "w_query_sum": ((block, 2 * pair), f32),
        "w_key_sum": ((block, pair), f32),
        "w_value_sum": ((block, pair), f32),
        "attn_gain_sum": ((1, width), f32),
        "ffn_gain_sum": ((1, width), f32),
        "q_gain_sum": ((1, pair), f32),
        "k_gain_sum": ((1, pair), f32),
    }
    staged = ("w_out_sum",) + RESULTS[9:]
    scratch = {name: pltpu.VMEM(*results[name]) for name in staged}
    buffers = {
        "tokens": ((rows, width), bf16),
        "residual": ((rows, width), f32),
        "mixed_t": ((sequences, 2, pair, tile), f32),
        "query_t": ((sequences, pair, 4 * tile), bf16),
        "logs": ((sequences, 1, 4 * tile), f32),
        "starts": ((sequences, 1, tile), f32),
        "keys_values": ((count, rows, 2 * pair), bf16),
        "query_raw": ((rows, 2 * pair), f32),
        "key_raw": ((rows, pair), f32),
        "lefts": ((2, width, rows), bf16),
        "ffn_grads": ((3, rows, hidden), bf16),
        "ffn_gain_part": ((1, width), f32),
        "grad_res": ((rows, width), bf16),
        "all_segs": ((count, 8, tile), jnp.int32),
        "all_out": ((4, 2 * pair, width), bf16),
        "all_heads": ((4, rows, 2 * pair), bf16),
        "acc": ((sequences, 2, head_dim, 2 * tile), f32),
        "row_sum": ((sequences, 1, 4 * tile), f32),
        "table": ((tile, 2 * pair), f32),
        "cotangent": ((rows, width), bf16),
        "w_down": ((width, hidden), bf16),
        "w_gate": ((width, hidden), bf16),
        "w_up": ((width, hidden), bf16),
        "gate_t": ((hidden, width), bf16),
        "up_t": ((hidden, width), bf16),
        "grad_hidden": ((rows, hidden), bf16),
        "ffn_part": ((rows, width), bf16),
        "sum_got": ((rows, width // 2), bf16),
        "sum_far": ((rows, width // 2), bf16),
        "sum_full": ((2, rows, width // 2), bf16),
        "mlp_sum0": ((rows, width // 2), bf16),
        "mlp_sum1": ((rows, width // 2), bf16),
        "mlp_sum2": ((2, rows, width // 2), bf16),
        "deltas": ((sequences, 1, 4 * tile), f32),
        "own_grads": ((rows, 2 * pair), f32),
        "side_in": ((levels - 1, rows, 2 * pair), bf16),
        "side_out": ((levels - 1, rows, 2 * pair), bf16),
        "line_in": ((levels - 2, rows, 2 * pair), bf16),
        "line_out": ((levels - 2, rows, 2 * pair), bf16),
        "two_grads": ((2 * tile, 2 * pair), f32),
        "upper_query_t": ((sequences, pair, 4 * tile), bf16),
        "upper_heads": ((sequences, 2 * pair, tile), bf16),
        "upper_deltas": ((sequences, 1, 4 * tile), f32),
        "stats_out": ((sequences, 8, 4 * tile), f32),
        "stats_in": ((sequences, 8, 4 * tile), f32),
        "upper_grad": ((2, head_dim, 2 * tile), f32),
        "upper_grad_out": ((sequences, 2, head_dim, 2 * tile), bf16),
        "upper_grad_in": ((sequences, 2, head_dim, 2 * tile), bf16),
        "ffn_sums": ((3, block, hidden), f32),
        "qkv_total": ((block, 4 * pair), f32),
        "gains0": ((count, 8, width), f32),
        "gains1": ((2, 2, 8, width), f32),
    }
    scratch |= {name: pltpu.VMEM(*spec) for name, spec in buffers.items()}
    semaphores = {
        "load_sems": (6,),
        "store_sems": (len(RESULTS),),
        "up_send": (levels, sequences),
        "up_recv": (levels, sequences),
        "side_send": (levels, sequences),
        "side_recv": (levels, sequences),
        "seg_send": (levels, 2),
        "seg_recv": (levels, 2),
        "out_send": (3,),
        "out_recv": (3,),
        "head_send": (3, sequences),
        "head_recv": (3, sequences),
        "ffn_send": (3, sequences),
        "ffn_recv": (3, sequences),
        "wt_send": (3, sequences),
        "wt_recv": (3, sequences),
        "mlp_sum3": (3, sequences),
        "mlp_sum4": (3, sequences),
        "side_grad_send": (levels - 1, sequences),
        "side_grad_recv": (levels - 1, sequences),
        "share_send": (4, sequences),
        "share_recv": (4, sequences),
        "upper_send": (sequences,),
        "upper_recv": (sequences,),
        "line_send": (levels - 2, sequences),
        "line_recv": (levels - 2, sequences),
        "gains2": (count - 1,),
        "gains3": (count - 1,),
        "gains4": (2,),
        "gains5": (2,),
    }
    scratch |= {name: dma(shape) for name, shape in semaphores.items()}
    for label, kinds in (
        ("ffn", ring_scratch(count, 3, block, hidden)),
        ("out", ring_scratch(count, 1, block, 2 * pair)),
        ("qkv", ring_scratch(count, 1, block, 4 * pair)),
    ):
        scratch |= {f"{label}{i}": kind for i, kind in enumerate(kinds)}
    vmem, anywhere = pl.BlockSpec(memory_space=pltpu.VMEM), pl.BlockSpec(memory_space=pl.ANY)
    names = (*inputs, *(name + "_res" for name in RESULTS), *scratch)
    arrays = pl.pallas_call(
        partial(layer_kernel, count, names),
        out_shape=[jax.ShapeDtypeStruct(*results[name]) for name in RESULTS],
        in_specs=[anywhere if name.endswith("_in") else vmem for name in inputs],
        out_specs=[anywhere] * len(RESULTS),
        scratch_shapes=list(scratch.values()),
        compiler_params=pltpu.CompilerParams(
            collective_id=2, has_side_effects=True, vmem_limit_bytes=VMEM_LIMIT
        ),
    )(*inputs.values())
    return dict(zip(RESULTS, arrays, strict=True))


def hand_over_kernel(count, *refs):
    sources, targets, staged = refs[:count], refs[count : 2 * count], refs[2 * count : 3 * count]
    loads = Mover(list(zip(sources, staged, strict=True)), refs[3 * count])
    stores = Mover(list(zip(staged, targets, strict=True)), refs[3 * count + 1])
    loads.start(*range(count))
    for i in range(count):
        loads.wait(i)
        stores.start(i)
    stores.wait(*range(count))


def hand_over(arrays):
    anywhere = pl.BlockSpec(memory_space=pl.ANY)
    dma = pltpu.SemaphoreType.DMA((len(arrays),))
    return pl.pallas_call(
        partial(hand_over_kernel, len(arrays)),
        out_shape=[jax.ShapeDtypeStruct(array.shape, array.dtype) for array in arrays],
        in_specs=[anywhere] * len(arrays),
        out_specs=[anywhere] * len(arrays),
        scratch_shapes=[pltpu.VMEM(array.shape, array.dtype) for array in arrays] + [dma, dma],
        compiler_params=pltpu.CompilerParams(vmem_limit_bytes=60 * MIB),
    )(*arrays)


def rotary_table(length, head_dim):
    half = head_dim // 2
    frequency = THETA ** (-2.0 * np.arange(half) / head_dim)
    angles = np.arange(length)[:, None] * frequency[None, :]
    cosine, sine = np.cos(angles), np.sin(angles)
    return np.concatenate([cosine] * 4 + [-sine, sine] * 2, axis=1).astype(np.float32)


def kernels_fit(tokens, w_query, key_matrix, q_gain, w_gate):
    sequences, tile, width = tokens.shape
    count, head_dim = lax.axis_size("ctx"), q_gain.shape[0]
    return (
        lax.axis_size("wt") == 4
        and count % 2 == 0
        and count >= 6
        and tile == 128
        and sequences <= 5
        and sequences * count <= 40
        and head_dim == 64
        and w_query.shape[1] == 4 * head_dim
        and key_matrix.shape[1] == 2 * head_dim
        and width % (128 * count) == 0
        and w_gate.shape[1] >= max(width, sequences * tile + 512)
        and w_gate.shape[1] <= 1152
        and width <= 1024
    )


def on_device_plain(
    tokens,
    segments,
    attn_gain,
    w_query,
    key_matrix,
    value_matrix,
    q_gain,
    k_gain,
    w_out,
    ffn_gain,
    w_gate,
    w_up,
    w_down,
    cotangent,
):
    sequences, seq_rows, model_width = tokens.shape
    head_dim = q_gain.shape[0]
    q_local = w_query.shape[1] // head_dim
    kv_local = key_matrix.shape[1] // head_dim
    per_group = q_local // kv_local
    score_scale = 1.0 / math.sqrt(head_dim)
    all_rows = sequences * seq_rows
    places = lax.axis_index("ctx") * seq_rows + jnp.arange(seq_rows, dtype=jnp.int32)
    frequency = THETA ** (-jnp.arange(0, head_dim, 2, dtype=jnp.float32) / head_dim)
    angles = places.astype(jnp.float32)[None, :, None] * frequency
    cosine_table = jnp.cos(angles)[:, :, None, :]
    sine_table = jnp.sin(angles)[:, :, None, :]
    inputs = tokens.astype(jnp.float32).reshape(all_rows, model_width)
    normed, attn_unit, attn_inverse = norm_rows(inputs, attn_gain)
    normed_low = normed.astype(jnp.bfloat16)
    query_raw = product(normed_low, w_query).reshape(sequences, seq_rows, q_local, head_dim)
    key_raw = product(normed_low, key_matrix).reshape(sequences, seq_rows, kv_local, head_dim)
    value_low = (
        product(normed_low, value_matrix)
        .astype(jnp.bfloat16)
        .reshape(sequences, seq_rows, kv_local * head_dim)
    )
    query_normed, query_unit, query_inverse = norm_rows(query_raw, q_gain)
    key_normed, key_unit, key_inverse = norm_rows(key_raw, k_gain)
    query_low = rotate(query_normed, cosine_table, sine_table, 1.0).astype(jnp.bfloat16)
    key_low = rotate(key_normed, cosine_table, sine_table, 1.0).astype(jnp.bfloat16)
    key_flat = key_low.reshape(sequences, seq_rows, kv_local * head_dim)
    query_groups = query_low.reshape(sequences, seq_rows, kv_local, per_group, head_dim)
    attend = partial(
        attend_piece,
        queries=query_groups,
        query_places=places,
        query_segs=segments,
        score_scale=score_scale,
    )
    start_state = (
        jnp.full((sequences, kv_local, per_group, seq_rows), NEG, jnp.float32),
        jnp.zeros((sequences, kv_local, per_group, seq_rows), jnp.float32),
        jnp.zeros((sequences, seq_rows, kv_local, per_group, head_dim), jnp.float32),
    )
    keys_values = lax.all_gather(
        jnp.concatenate([key_flat, value_low], axis=-1), "ctx", axis=1, tiled=True
    )
    kv_width = kv_local * head_dim
    gathered = (
        keys_values[..., :kv_width],
        keys_values[..., kv_width:],
        lax.all_gather(segments, "ctx", axis=1, tiled=True),
    )
    row_max, row_sum, weighted = attend(
        start_state,
        gathered,
        jnp.int32(0),
    )
    mixed_heads = weighted / jnp.transpose(row_sum, (0, 3, 1, 2))[..., None]
    mixed_low = mixed_heads.astype(jnp.bfloat16).reshape(all_rows, q_local * head_dim)
    attn_term = by_transpose(mixed_low, w_out)
    residual = inputs + lax.psum(attn_term.astype(jnp.bfloat16), "wt").astype(jnp.float32)
    normed_ffn, ffn_unit, ffn_inverse = norm_rows(residual, ffn_gain)
    normed_ffn_low = normed_ffn.astype(jnp.bfloat16)
    gate_proj = product(normed_ffn_low, w_gate)
    up_proj = product(normed_ffn_low, w_up)
    gate_sigmoid = jax.nn.sigmoid(gate_proj)
    gate_silu = gate_proj * gate_sigmoid
    hidden_low = (gate_silu * up_proj).astype(jnp.bfloat16)
    mlp_term = by_transpose(hidden_low, w_down)
    output_rows = (
        residual + lax.psum(mlp_term.astype(jnp.bfloat16), "wt").astype(jnp.float32)
    ).astype(jnp.bfloat16)
    log_total = row_max + jnp.log(row_sum)
    grad_rows = cotangent.reshape(all_rows, model_width)
    grad_hidden = product(grad_rows, w_down)
    grad_gate = (
        grad_hidden * up_proj * gate_sigmoid * (1.0 + gate_proj * (1.0 - gate_sigmoid))
    ).astype(jnp.bfloat16)
    grad_up = (grad_hidden * gate_silu).astype(jnp.bfloat16)
    grad_normed_ffn = by_transpose(grad_gate, w_gate) + by_transpose(grad_up, w_up)
    ffn_gain_part = jnp.sum(grad_normed_ffn * ffn_unit, axis=0)
    grad_normed_ffn = lax.psum(grad_normed_ffn.astype(jnp.bfloat16), "wt").astype(jnp.float32)
    grad_residual = grad_rows.astype(jnp.float32) + norm_back(
        grad_normed_ffn, ffn_unit, ffn_inverse, ffn_gain
    )
    grad_residual_low = grad_residual.astype(jnp.bfloat16)
    grad_heads_low = product(grad_residual_low, w_out).astype(jnp.bfloat16)
    grad_groups = grad_heads_low.reshape(sequences, seq_rows, kv_local, per_group, head_dim)
    delta_rows = jnp.sum(grad_groups.astype(jnp.float32) * mixed_heads, axis=-1)
    delta_cols = jnp.transpose(delta_rows, (0, 2, 3, 1))
    query_grad_fn = partial(
        grad_piece,
        queries=query_groups,
        grad_heads=grad_groups,
        log_total=log_total,
        row_delta=delta_cols,
        query_places=places,
        query_segs=segments,
        score_scale=score_scale,
    )
    grad_query, grad_pairs = query_grad_fn(
        jnp.zeros((sequences, seq_rows, kv_local, per_group, head_dim), jnp.float32),
        gathered,
        jnp.int32(0),
    )
    grad_pairs = lax.psum_scatter(grad_pairs, "ctx", scatter_dimension=1, tiled=True).astype(
        jnp.float32
    )
    grad_key = grad_pairs[:, :, 0]
    grad_value = grad_pairs[:, :, 1]
    grad_query = rotate(
        grad_query.reshape(sequences, seq_rows, q_local, head_dim) * score_scale,
        cosine_table,
        sine_table,
        -1.0,
    )
    grad_key = rotate(grad_key * score_scale, cosine_table, sine_table, -1.0)
    q_gain_part = jnp.sum(grad_query * query_unit, axis=(0, 1, 2))
    k_gain_part = jnp.sum(grad_key * key_unit, axis=(0, 1, 2))
    grad_query_low = (
        norm_back(grad_query, query_unit, query_inverse, q_gain)
        .astype(jnp.bfloat16)
        .reshape(all_rows, q_local * head_dim)
    )
    grad_key_low = (
        norm_back(grad_key, key_unit, key_inverse, k_gain)
        .astype(jnp.bfloat16)
        .reshape(all_rows, kv_local * head_dim)
    )
    grad_value_low = grad_value.astype(jnp.bfloat16).reshape(all_rows, kv_local * head_dim)
    grad_normed = (
        by_transpose(grad_query_low, w_query)
        + by_transpose(grad_key_low, key_matrix)
        + by_transpose(grad_value_low, value_matrix)
    )
    attn_gain_part = jnp.sum(grad_normed * attn_unit, axis=0)
    grad_normed = lax.psum(grad_normed.astype(jnp.bfloat16), "wt").astype(jnp.float32)
    tokens_rows = (
        grad_residual + norm_back(grad_normed, attn_unit, attn_inverse, attn_gain)
    ).astype(jnp.bfloat16)
    output = output_rows.reshape(sequences, seq_rows, model_width)
    tokens_grad = tokens_rows.reshape(sequences, seq_rows, model_width)
    partial_sums = (
        transpose_by(grad_rows, hidden_low),
        transpose_by(normed_ffn_low, grad_gate),
        transpose_by(normed_ffn_low, grad_up),
        transpose_by(grad_residual_low, mixed_low),
        transpose_by(normed_low, grad_query_low),
        transpose_by(normed_low, grad_key_low),
        transpose_by(normed_low, grad_value_low),
    )
    summed = [
        lax.psum_scatter(part.astype(jnp.bfloat16), "ctx", scatter_dimension=0, tiled=True).astype(
            jnp.float32
        )
        for part in partial_sums
    ]
    w_down_grad, w_gate_grad, w_up_grad, w_out_grad = summed[:4]
    w_query_grad, w_key_grad, w_value_grad = summed[4:]
    attn_gain_grad, q_gain_grad, k_gain_grad, ffn_gain_grad = lax.psum(
        (attn_gain_part, q_gain_part, k_gain_part, ffn_gain_part), ("ctx", "wt")
    )
    return (
        output,
        tokens_grad,
        attn_gain_grad,
        w_query_grad,
        w_key_grad,
        w_value_grad,
        q_gain_grad,
        k_gain_grad,
        w_out_grad,
        ffn_gain_grad,
        w_gate_grad,
        w_up_grad,
        w_down_grad,
    )


def on_device(
    tokens,
    segments,
    attn_gain,
    w_query,
    key_matrix,
    value_matrix,
    q_gain,
    k_gain,
    w_out,
    ffn_gain,
    w_gate,
    w_up,
    w_down,
    cotangent,
):
    if not kernels_fit(tokens, w_query, key_matrix, q_gain, w_gate):
        return on_device_plain(
            tokens,
            segments,
            attn_gain,
            w_query,
            key_matrix,
            value_matrix,
            q_gain,
            k_gain,
            w_out,
            ffn_gain,
            w_gate,
            w_up,
            w_down,
            cotangent,
        )
    sequences, seq_rows, model_width = tokens.shape
    count, head_dim = lax.axis_size("ctx"), q_gain.shape[0]
    token_rows = tokens.reshape(sequences * seq_rows, model_width)
    table = jnp.asarray(rotary_table(count * seq_rows, head_dim))
    gains = {"attn_gain": attn_gain, "q_gain": q_gain, "k_gain": k_gain}
    sums = layer(
        {
            "segments": segments,
            **gains,
            "ffn_gain": ffn_gain,
            "w_query": w_query,
            "w_key": key_matrix,
            "w_value": value_matrix,
            "w_out": w_out,
            "tokens_in": token_rows,
            "table_in": table,
            "cotangent_in": cotangent.reshape(token_rows.shape),
            "w_down_in": w_down,
            "w_gate_in": w_gate,
            "w_up_in": w_up,
        }
    )
    done = dict(zip(RESULTS, hand_over([sums[name] for name in RESULTS]), strict=True))
    return (
        done["output"].reshape(tokens.shape),
        done["tokens_grad"].reshape(tokens.shape),
        done["attn_gain_sum"][0],
        done["w_query_sum"],
        done["w_key_sum"],
        done["w_value_sum"],
        done["q_gain_sum"][0, :head_dim],
        done["k_gain_sum"][0, :head_dim],
        done["w_out_sum"],
        done["ffn_gain_sum"][0],
        done["w_gate_sum"],
        done["w_up_sum"],
        done["w_down_sum"],
    )


def solution(mesh):
    in_specs = (
        P(None, "ctx", None),
        P(None, "ctx"),
        P(),
        P(None, "wt"),
        P(None, "wt"),
        P(None, "wt"),
        P(),
        P(),
        P(None, "wt"),
        P(),
        P(None, "wt"),
        P(None, "wt"),
        P(None, "wt"),
        P(None, "ctx", None),
    )
    out_specs = (
        P(None, "ctx", None),
        P(None, "ctx", None),
        P(),
        P("ctx", "wt"),
        P("ctx", "wt"),
        P("ctx", "wt"),
        P(),
        P(),
        P("ctx", "wt"),
        P(),
        P("ctx", "wt"),
        P("ctx", "wt"),
        P("ctx", "wt"),
    )
    return jax.shard_map(
        on_device, mesh=mesh, in_specs=in_specs, out_specs=out_specs, check_vma=False
    )
```

```python
from functools import partial
import math

import jax
import jax.numpy as jnp
import numpy as np
from jax import lax
from jax.experimental import pallas as pl
from jax.experimental.pallas import tpu as pltpu
from jax.sharding import PartitionSpec as P

EPS = 1e-05
THETA = 1000000.0
NEG = -1e30


def product(left, right):
    return jnp.dot(left, right, preferred_element_type=jnp.float32)


def by_transpose(left, right):
    return lax.dot_general(
        left, right, (((1,), (1,)), ((), ())), preferred_element_type=jnp.float32
    )


def transpose_by(left, right):
    return lax.dot_general(
        left, right, (((0,), (0,)), ((), ())), preferred_element_type=jnp.float32
    )


def norm_rows(values, gain):
    inverse = lax.rsqrt(jnp.mean(values * values, axis=-1, keepdims=True) + EPS)
    unit_rows = values * inverse
    return (unit_rows * gain, unit_rows, inverse)


def norm_back(grads, unit_rows, inverse, gain):
    scaled = grads * gain
    return inverse * (scaled - unit_rows * jnp.mean(scaled * unit_rows, axis=-1, keepdims=True))


def rotate(values, cosine_table, sine_table, direction):
    half_dim = values.shape[-1] // 2
    first_half = values[..., :half_dim]
    second_half = values[..., half_dim:]
    return jnp.concatenate(
        [
            first_half * cosine_table - direction * second_half * sine_table,
            second_half * cosine_table + direction * first_half * sine_table,
        ],
        axis=-1,
    )


def split_blocks(array, block_len):
    shaped = array.reshape(
        (array.shape[0], array.shape[1] // block_len, block_len) + array.shape[2:]
    )
    return jnp.moveaxis(shaped, 1, 0)


def attend_piece(folded, pieces, first_row, queries, query_places, query_segs, score_scale):
    key_piece, value_piece, seg_piece = pieces
    sequences, piece_rows = seg_piece.shape
    kv_local = queries.shape[2]
    head_dim = queries.shape[4]
    block_len = math.gcd(piece_rows, 512)
    key_blocks = split_blocks(
        key_piece.reshape(sequences, piece_rows, kv_local, head_dim), block_len
    )
    value_tiles = split_blocks(
        value_piece.reshape(sequences, piece_rows, kv_local, head_dim), block_len
    )
    seg_blocks = split_blocks(seg_piece, block_len)
    offsets = block_len * jnp.arange(piece_rows // block_len, dtype=jnp.int32)

    def attend_block_step(running, block_item):
        row_max, row_sum, weighted = running
        key_block, value_block, seg_block, offset = block_item
        key_places = offset + jnp.arange(block_len, dtype=jnp.int32)
        allowed = (key_places[None, None, :] <= query_places[None, :, None]) & (
            query_segs[:, :, None] == seg_block[:, None, :]
        )
        allowed = allowed[:, None, None]
        scores = (
            jnp.einsum("sqgrd,skgd->sgrqk", queries, key_block, preferred_element_type=jnp.float32)
            * score_scale
        )
        scores = jnp.where(allowed, scores, NEG)
        new_max = jnp.maximum(row_max, jnp.max(scores, axis=-1))
        weights = jnp.where(allowed, jnp.exp(scores - new_max[..., None]), 0.0)
        fading = jnp.exp(row_max - new_max)
        row_sum = row_sum * fading + jnp.sum(weights, axis=-1)
        fade_rows = jnp.transpose(fading, (0, 3, 1, 2))[..., None]
        weighted = weighted * fade_rows + jnp.einsum(
            "sgrqk,skgd->sqgrd",
            weights.astype(jnp.bfloat16),
            value_block,
            preferred_element_type=jnp.float32,
        )
        return ((new_max, row_sum, weighted), None)

    folded, unused = lax.scan(
        attend_block_step, folded, (key_blocks, value_tiles, seg_blocks, offsets)
    )
    return folded


def grad_piece(
    folded,
    pieces,
    first_row,
    queries,
    grad_heads,
    log_total,
    row_delta,
    query_places,
    query_segs,
    score_scale,
):
    key_piece, value_piece, seg_piece = pieces
    sequences, piece_rows = seg_piece.shape
    kv_local = queries.shape[2]
    head_dim = queries.shape[4]
    block_len = math.gcd(piece_rows, 512)
    key_blocks = split_blocks(
        key_piece.reshape(sequences, piece_rows, kv_local, head_dim), block_len
    )
    value_tiles = split_blocks(
        value_piece.reshape(sequences, piece_rows, kv_local, head_dim), block_len
    )
    seg_blocks = split_blocks(seg_piece, block_len)
    offsets = block_len * jnp.arange(piece_rows // block_len, dtype=jnp.int32)

    def grad_block_step(running, block_item):
        key_block, value_block, seg_block, offset = block_item
        key_places = offset + jnp.arange(block_len, dtype=jnp.int32)
        allowed = (key_places[None, None, :] <= query_places[None, :, None]) & (
            query_segs[:, :, None] == seg_block[:, None, :]
        )
        allowed = allowed[:, None, None]
        scores = (
            jnp.einsum("sqgrd,skgd->sgrqk", queries, key_block, preferred_element_type=jnp.float32)
            * score_scale
        )
        probs = jnp.where(allowed, jnp.exp(scores - log_total[..., None]), 0.0)
        grad_probs = jnp.einsum(
            "sqgrd,skgd->sgrqk", grad_heads, value_block, preferred_element_type=jnp.float32
        )
        grad_scores = (probs * (grad_probs - row_delta[..., None])).astype(jnp.bfloat16)
        running = running + jnp.einsum(
            "sgrqk,skgd->sqgrd", grad_scores, key_block, preferred_element_type=jnp.float32
        )
        grad_keys = jnp.einsum(
            "sgrqk,sqgrd->skgd", grad_scores, queries, preferred_element_type=jnp.float32
        )
        grad_values = jnp.einsum(
            "sgrqk,sqgrd->skgd",
            probs.astype(jnp.bfloat16),
            grad_heads,
            preferred_element_type=jnp.float32,
        )
        grads = jnp.stack([grad_keys, grad_values], axis=2).astype(jnp.bfloat16)
        return (running, grads)

    folded, grads = lax.scan(
        grad_block_step, folded, (key_blocks, value_tiles, seg_blocks, offsets)
    )
    return folded, jnp.moveaxis(grads, 0, 1).reshape((sequences, piece_rows) + grads.shape[3:])


MESH = pl.DeviceIdType.MESH
MIB = 1 << 20


def ring_place(index, count):
    return lax.select(
        lax.rem(index, 2) == 0, lax.div(index, 2), count - 1 - lax.div(index, 2)
    )


def ring_index(place, count):
    place = lax.rem(place + 2 * count, count)
    return lax.select(
        place < lax.div(count, 2), 2 * place, 2 * (count - 1 - place) + 1
    )


class Ring:
    def __init__(self, count, slots, send_sems, recv_sems, base=0):
        self.count, self.slots, self.base = count, slots, base
        self.send_sems, self.recv_sems = send_sems, recv_sems
        self.other = lax.axis_index("wt")
        self.place = ring_place(lax.axis_index("ctx"), count)
        self.right = ring_index(self.place + 1, count)
        self.left = ring_index(self.place + count - 1, count)
        self.half = slots.shape[2] // 2

    def copy(self, which, step, way):
        rows = pl.ds(way * self.half, self.half)
        slot = step - self.base
        return pltpu.make_async_remote_copy(
            src_ref=self.slots.at[which, slot, rows],
            dst_ref=self.slots.at[which, slot + 1, rows],
            send_sem=self.send_sems.at[which, slot, way],
            recv_sem=self.recv_sems.at[which, slot, way],
            device_id=((self.right, self.left)[way], self.other),
            device_id_type=MESH,
        )

    def arrived(self, which, step):
        for way in range(2):
            self.copy(which, step - 1, way).wait_recv()

    def tick(
        self,
        which,
        step,
        left_ref,
        right_ref,
        first=False,
        given=None,
        result=None,
        final=True,
    ):
        half = self.half
        rows = [
            ring_index(target, self.count) * (2 * half) + way * half
            for way, target in enumerate(
                (self.place + self.count - 1 - step, self.place + 1 + step)
            )
        ]
        left = jnp.concatenate(
            [left_ref[pl.ds(pl.multiple_of(row, half), half), :] for row in rows], axis=0
        )
        total = jnp.dot(left, right_ref[...], preferred_element_type=jnp.float32)
        if given is not None:
            total = total + given[...].astype(jnp.float32)
        elif not first:
            self.arrived(which, step)
            total = total + self.slots[which, step - self.base].astype(jnp.float32)
        def pass_on():
            self.slots[which, step - self.base] = total.astype(jnp.bfloat16)
            for way in range(2):
                self.copy(which, step, way).start()

        def keep():
            result[...] = total

        if result is None:
            pass_on()
        elif final is True:
            keep()
        else:
            pl.when(final)(keep)
            pl.when(jnp.logical_not(final))(pass_on)

    def finish(self, which, end):
        for way in range(2):

            def wait(step, carry):
                self.copy(which, step, way).wait_send()
                return carry

            lax.fori_loop(self.base, end, wait, 0)


def pair_lanes(shape):
    return lax.broadcasted_iota(jnp.int32, shape, 1)


def swap_halves(values, head_dim):
    lanes = pair_lanes(values.shape)
    width = values.shape[1]
    quarter = head_dim // 2
    return jnp.where(
        lax.rem(lanes, head_dim) < quarter,
        pltpu.roll(values, width - quarter, 1),
        pltpu.roll(values, quarter, 1),
    )


def pair_mean(values, head_dim):
    low = pair_lanes(values.shape) < head_dim
    first = jnp.sum(jnp.where(low, values, 0.0), axis=-1, keepdims=True)
    second = jnp.sum(jnp.where(low, 0.0, values), axis=-1, keepdims=True)
    return jnp.where(low, first, second) * (1.0 / head_dim)


def pair_norm(values, head_dim):
    inverse = lax.rsqrt(pair_mean(values * values, head_dim) + EPS)
    return values * inverse, inverse


def as_row(ref):
    return ref[...].astype(jnp.float32).reshape(1, -1)


def double(row):
    return jnp.concatenate([row, row], axis=-1)


def dot_nn(left, right):
    return jnp.dot(left, right, preferred_element_type=jnp.float32)


def dot_nt(left, right):
    return lax.dot_general(
        left, right, (((1,), (1,)), ((), ())), preferred_element_type=jnp.float32
    )


def as_column(row):
    size = row.shape[1]
    rows = lax.broadcasted_iota(jnp.int32, (size, size), 0)
    lanes = lax.broadcasted_iota(jnp.int32, (size, size), 1)
    return jnp.sum(jnp.where(rows == lanes, row, 0.0), axis=1, keepdims=True)


class Place:
    def __init__(self, count):
        self.count = count
        self.ctx, self.wt = lax.axis_index("ctx"), lax.axis_index("wt")
        self.odd = lax.rem(self.ctx, 2)
        self.level = lax.div(self.ctx, 2)
        self.core_bit = lax.rem(self.wt, 2)
        self.beside_ctx = self.ctx + 1 - 2 * self.odd
        self.beside = (self.beside_ctx, self.wt)
        self.above = (lax.rem(self.ctx + 2, count), self.wt)
        self.below = (lax.rem(self.ctx + count - 2, count), self.wt)
        self.has_above = self.ctx + 2 < count
        self.top = self.ctx >= count - 2
        self.serves = (self.ctx >= count - 4) & (self.ctx < count - 2)
        self.has_below = self.ctx >= 2
        self.core_wt = self.wt + 1 - 2 * self.core_bit
        self.chip_wt = lax.rem(self.wt + 2, 4)
        self.far_wt = lax.rem(self.core_wt + 2, 4)
        self.core = (self.ctx, self.core_wt)
        self.chip = (self.ctx, self.chip_wt)
        self.far = (self.ctx, self.far_wt)

    def signal(self, peer):
        pl.semaphore_signal(
            pltpu.get_barrier_semaphore(), inc=1, device_id=peer, device_id_type=MESH
        )

    def signal_all(self):
        for shift in range(1, self.count):
            self.signal((lax.rem(self.ctx + shift, self.count), self.wt))
        self.signal(self.core)
        self.signal(self.chip)
        self.signal(self.far)

    def await_all(self):
        pl.semaphore_wait(pltpu.get_barrier_semaphore(), self.count + 2)


def send_to(source, target, send_sem, recv_sem, device):
    return pltpu.make_async_remote_copy(
        src_ref=source,
        dst_ref=target,
        send_sem=send_sem,
        recv_sem=recv_sem,
        device_id=device,
        device_id_type=MESH,
    )


class WtSum:
    def __init__(self, here, tile, part, got, far, full, send_sems, recv_sems, before=None):
        self.here, self.tile, self.before = here, tile, before
        self.part, self.got, self.far, self.full = part, got, far, full
        self.send_sems, self.recv_sems = send_sems, recv_sems
        self.mine, self.theirs = here.core_bit, 1 - here.core_bit
        self.half = got.shape[1]

    def rows(self, seq):
        return pl.ds(pl.multiple_of(seq * self.tile, self.tile), self.tile)

    def cols(self, half):
        return pl.ds(pl.multiple_of(half * self.half, self.half), self.half)

    def copy(self, hop, seq, arriving=False):
        rows = self.rows(seq)
        half = self.theirs if arriving else self.mine
        source = (
            self.part.at[rows, self.cols(self.theirs)],
            self.got.at[rows],
            self.full.at[half, rows],
        )[hop]
        target = (self.got.at[rows], self.far.at[rows], self.full.at[half, rows])[hop]
        device = self.here.chip if hop == 1 else self.here.core
        return send_to(
            source, target, self.send_sems.at[hop, seq], self.recv_sems.at[hop, seq], device
        )

    def offer(self, seq, value):
        self.part[self.rows(seq), pl.ds(0, 2 * self.half)] = value.astype(jnp.bfloat16)
        self.copy(0, seq).start()

    def cross(self, seq):
        rows = self.rows(seq)
        self.copy(0, seq).wait_recv()
        total = self.part[rows, self.cols(self.mine)].astype(jnp.float32) + self.got[
            rows
        ].astype(jnp.float32)
        self.got[rows] = total.astype(jnp.bfloat16)
        self.copy(1, seq).start()

    def close(self, seq):
        rows = self.rows(seq)
        self.copy(1, seq).wait()
        total = self.got[rows].astype(jnp.float32) + self.far[rows].astype(jnp.float32)
        if self.before is not None:
            self.before.copy(2, seq).wait_send()
        self.full[self.mine, rows] = total.astype(jnp.bfloat16)
        self.copy(2, seq).start()

    def result(self, seq):
        rows = self.rows(seq)
        self.copy(2, seq, True).wait_recv()
        return jnp.concatenate([self.full[0, rows], self.full[1, rows]], axis=1).astype(
            jnp.float32
        )

    def finish(self, sequences, hops=(0, 2)):
        def sent(seq, carry):
            for hop in hops:
                self.copy(hop, seq).wait_send()
            return carry

        lax.fori_loop(0, sequences, sent, 0)


def ring_scratch(count, arrays, rows, width):
    return [
        pltpu.VMEM((arrays, count, rows, width), jnp.bfloat16),
        pltpu.SemaphoreType.DMA((arrays, count - 1, 2)),
        pltpu.SemaphoreType.DMA((arrays, count - 1, 2)),
    ]


class GainSum:
    def __init__(self, here, slots, beside, sends, recvs, pair_sends, pair_recvs):
        self.here, self.slots, self.beside = here, slots, beside
        self.sends, self.recvs = sends, recvs
        self.pair_sends, self.pair_recvs = pair_sends, pair_recvs

    def copy(self, shift, arriving=False):
        here = self.here
        target = lax.rem(here.ctx + shift, here.count)
        origin = lax.rem(here.ctx + here.count - shift, here.count)
        ref = self.slots.at[origin if arriving else here.ctx]
        return send_to(
            ref, ref, self.sends.at[shift - 1], self.recvs.at[shift - 1], (target, here.wt)
        )

    def pair_copy(self, hop):
        device = (self.here.core, self.here.chip)[hop]
        return send_to(
            self.beside.at[hop, 0],
            self.beside.at[hop, 1],
            self.pair_sends.at[hop],
            self.pair_recvs.at[hop],
            device,
        )

    def start(self):
        for shift in range(1, self.here.count):
            self.copy(shift).start()

    def sum_ctx(self):
        for shift in range(1, self.here.count):
            self.copy(shift, True).wait_recv()
        total = self.slots[0]
        for index in range(1, self.here.count):
            total = total + self.slots[index]
        self.beside[0, 0] = total
        self.pair_copy(0).start()

    def sum_cores(self):
        self.pair_copy(0).wait_recv()
        self.beside[1, 0] = self.beside[0, 0] + self.beside[0, 1]
        self.pair_copy(1).start()

    def sum_chips(self):
        self.pair_copy(1).wait_recv()
        return self.beside[1, 0] + self.beside[1, 1]

    def finish(self):
        for shift in range(1, self.here.count):
            self.copy(shift).wait_send()
        for hop in range(2):
            self.pair_copy(hop).wait_send()


class Mover:
    def __init__(self, pairs, sems):
        self.copies = [
            pltpu.make_async_copy(source, target, sems.at[i])
            for i, (source, target) in enumerate(pairs)
        ]

    def start(self, *which):
        for i in which:
            self.copies[i].start()

    def wait(self, *which):
        for i in which:
            self.copies[i].wait()


TICKS = (1, 1, 5)
REACH = 2
VMEM_LIMIT = 63 * MIB
RESULTS = (
    "output",
    "tokens_grad",
    "w_down_sum",
    "w_gate_sum",
    "w_up_sum",
    "w_out_sum",
    "w_query_sum",
    "w_key_sum",
    "w_value_sum",
    "attn_gain_sum",
    "ffn_gain_sum",
    "q_gain_sum",
    "k_gain_sum",
)


def layer_kernel(count, names, *refs):
    ref = dict(zip(names, refs, strict=True))
    tokens, segments = ref["tokens"], ref["segments"]
    residual, mixed_t, query_t = ref["residual"], ref["mixed_t"], ref["query_t"]
    logs, starts, keys_values = ref["logs"], ref["starts"], ref["keys_values"]
    query_raw, key_raw = ref["query_raw"], ref["key_raw"]
    grad_res, lefts = ref["grad_res"], ref["lefts"]
    ffn_grads, ffn_gain_part = ref["ffn_grads"], ref["ffn_gain_part"]
    all_segs, all_out, all_heads = ref["all_segs"], ref["all_out"], ref["all_heads"]
    acc, row_sum = ref["acc"], ref["row_sum"]
    w_gate, w_up, w_down = ref["w_gate"], ref["w_up"], ref["w_down"]
    gate_t, up_t, grad_hidden = ref["gate_t"], ref["up_t"], ref["grad_hidden"]
    cotangent, table = ref["cotangent"], ref["table"]
    sequences, tile = segments.shape
    head_dim = ref["q_gain"].shape[0]
    pair = 2 * head_dim
    levels = count // 2
    here = Place(count)
    me = here.ctx
    loads = Mover(
        [
            (ref["table_in"].at[pl.ds(pl.multiple_of(me * tile, tile), tile)], table),
            (ref["cotangent_in"], cotangent),
            (ref["w_down_in"], w_down),
            (ref["w_gate_in"], w_gate),
            (ref["w_up_in"], w_up),
            (ref["tokens_in"], tokens),
        ],
        ref["load_sems"],
    )
    loads.start(5, 0, 1, 2, 3, 4)
    shared = [ref[name] for name in ("sum_got", "sum_far", "sum_full")]
    ffn_sum = WtSum(here, tile, ref["ffn_part"], *shared, ref["ffn_send"], ref["ffn_recv"])
    ffn = Ring(count, *(ref[f"ffn{i}"] for i in range(3)))
    here.signal_all()
    all_segs[me] = jnp.zeros_like(all_segs[me])
    all_segs[me, pl.ds(0, sequences)] = segments[...]
    all_out[here.wt] = ref["w_out"][...].T

    rows_all, width = tokens.shape
    grad_heads_t = w_gate

    heads_small = gate_t.at[pl.ds(4 * tile, 2 * pair), pl.ds(2 * pair, sequences * tile)]

    def heads_at(seq):
        start = pl.multiple_of(seq * pair, pair)
        return (pl.ds(start, pair), pl.ds(rows_all, 4 * tile))

    def out_copy(hop, arriving=False):
        sent = (here.wt, here.wt, here.chip_wt)
        landed = (here.chip_wt, here.core_wt, here.far_wt)
        part = all_out.at[(landed if arriving else sent)[hop]]
        device = here.chip if hop == 0 else here.core
        return send_to(part, part, ref["out_send"].at[hop], ref["out_recv"].at[hop], device)

    def rows_of(seq):
        return pl.ds(pl.multiple_of(seq * tile, tile), tile)

    def block_of(index, step):
        return lax.rem(index - 2 * step + 2 * count, count)

    def up_copy(step, seq, arriving=False, forward=False):
        block = block_of(me, step) if arriving else block_of(me, step - 1) if forward else me
        rows = keys_values.at[block, rows_of(seq)]
        device = (lax.rem(me + (2 if forward else 2 * step), count), here.wt)
        return send_to(
            rows, rows, ref["up_send"].at[step, seq], ref["up_recv"].at[step, seq], device
        )

    def side_copy(step, seq, index=me):
        rows = keys_values.at[block_of(index, step), rows_of(seq)]
        return send_to(
            rows, rows, ref["side_send"].at[step, seq], ref["side_recv"].at[step, seq], here.beside
        )

    def seg_up_copy(step, arriving=False):
        part = all_segs.at[block_of(me, step) if arriving else me]
        device = (lax.rem(me + 2 * step, count), here.wt)
        return send_to(
            part, part, ref["seg_send"].at[step, 0], ref["seg_recv"].at[step, 0], device
        )

    def seg_side_copy(step, index=me):
        part = all_segs.at[block_of(index, step)]
        return send_to(
            part, part, ref["seg_send"].at[step, 1], ref["seg_recv"].at[step, 1], here.beside
        )

    def goes_up(step):
        return me + 2 * step < count

    def goes_aside(step):
        block = me - 2 * step
        return (block >= 0) & (block < here.beside_ctx)

    def comes_aside(step):
        block = here.beside_ctx - 2 * step
        return (block >= 0) & (block < me)

    def pass_segs():
        for step in range(1, levels):

            @pl.when(goes_up(step))
            def _():
                seg_up_copy(step).start()

        @pl.when(goes_aside(0))
        def _():
            seg_side_copy(0).start()

    def forwards(step):
        return (step > REACH) & (me >= 2 * (step - 1)) & here.has_above

    def pass_rows(seq):
        @pl.when(goes_aside(0))
        def _():
            side_copy(0, seq).start()

        for step in range(1, min(REACH + 1, levels)):

            @pl.when(goes_up(step))
            def _():
                up_copy(step, seq).start()

    gain = as_row(ref["attn_gain"])
    q_gain_pair = double(as_row(ref["q_gain"]))
    k_gain_pair = double(as_row(ref["k_gain"]))
    ffn_gain_row = as_row(ref["ffn_gain"])
    loads.wait(0, 5)

    def share_copy(what, seq):
        source = (
            query_t.at[seq],
            ref["stats_out"].at[seq],
            heads_small.at[:, pl.ds(pl.multiple_of(seq * tile, tile), tile)],
            ref["deltas"].at[seq],
        )[what]
        target = (
            ref["upper_query_t"],
            ref["stats_in"],
            ref["upper_heads"],
            ref["upper_deltas"],
        )[what].at[seq]
        sems = ref["share_send"].at[what, seq], ref["share_recv"].at[what, seq]
        return send_to(source, target, *sems, here.below)

    def turn(values):
        cosine = table[:, pl.ds(0, pair)]
        sine = table[:, pl.ds(pair, pair)]
        return values * cosine + swap_halves(values, head_dim) * sine

    def project(seq, carry):
        rows = rows_of(seq)
        inputs = tokens[rows, :].astype(jnp.float32)
        inverse = lax.rsqrt(jnp.mean(inputs * inputs, axis=-1, keepdims=True) + EPS)
        normed = (inputs * inverse * gain).astype(jnp.bfloat16)
        raw_k = dot_nn(normed, ref["w_key"][...])
        key_raw[rows, :] = raw_k
        unit, unused = pair_norm(raw_k, head_dim)
        keys_values[me, rows, pl.ds(0, pair)] = turn(unit * k_gain_pair).astype(jnp.bfloat16)
        keys_values[me, rows, pl.ds(pair, pair)] = dot_nn(normed, ref["w_value"][...]).astype(
            jnp.bfloat16
        )

        @pl.when(seq == 0)
        def _():
            here.await_all()
            pass_segs()

        @pl.when(seq == 0)
        def _():
            pass_rows(seq)

        @pl.when(seq == 0)
        def _():
            out_copy(0).start()
            out_copy(1).start()

        raw_q = dot_nn(normed, ref["w_query"][...])
        query_raw[rows, :] = raw_q
        query_t[seq] = jnp.zeros_like(query_t[seq])
        for group in range(2):
            unit, unused = pair_norm(raw_q[:, group * pair : (group + 1) * pair], head_dim)
            turned = turn(unit * q_gain_pair) * (head_dim**-0.5)
            flipped = turned.T.astype(jnp.bfloat16)
            for member in range(2):
                query_t[
                    seq,
                    pl.ds(group * head_dim, head_dim),
                    pl.ds((2 * group + member) * tile, tile),
                ] = flipped[member * head_dim : (member + 1) * head_dim]

        @pl.when(here.top)
        def _():
            share_copy(0, seq).start()

        acc[seq] = jnp.zeros_like(acc[seq])
        row_sum[seq] = jnp.zeros_like(row_sum[seq])
        starts[seq] = jnp.zeros_like(starts[seq])
        return carry

    def route_level(step, seq):
        @pl.when(me >= 2 * step)
        def _():
            @pl.when(seq == 0)
            def _():
                seg_up_copy(step, True).wait_recv()
                seg_side_copy(step).start()

            up_copy(step, seq, True).wait_recv()
            side_copy(step, seq).start()

            @pl.when(forwards(step + 1))
            def _():
                up_copy(step + 1, seq, forward=True).start()

    def route(seq):
        def level(step, carry):
            route_level(step, seq)
            return carry

        lax.fori_loop(1, levels, level, 0)

    lax.fori_loop(0, sequences, project, 0)
    pass_rows(1)
    for step in range(1, min(REACH + 1, levels)):
        route_level(step, 0)
    loads.wait(1, 2)

    def back_down(seq, carry):
        rows = rows_of(seq)
        grads = cotangent[rows, :]
        lefts[0, :, rows] = grads.T
        grad_hidden[rows, :] = dot_nn(grads, w_down[...]).astype(jnp.bfloat16)
        return carry

    lax.fori_loop(0, sequences, back_down, 0)
    for step in range(REACH + 1, levels):
        route_level(step, 0)

    loads.wait(3, 4)

    def flip(index, carry):
        rows = pl.ds(pl.multiple_of(index * 128, 128), 128)
        gate_t[:, rows] = w_gate[rows, :].T
        up_t[:, rows] = w_up[rows, :].T
        return carry

    lax.fori_loop(0, tokens.shape[1] // 128, flip, 0)
    key_rows = lax.broadcasted_iota(jnp.int32, (tile, tile), 0)
    query_cols = lax.broadcasted_iota(jnp.int32, (tile, tile), 1)

    def attend(blocks, seq):
        rows = rows_of(seq)
        seg_query = all_segs[me, pl.ds(seq, 1)].astype(jnp.float32)
        masks, values_t = [], []
        for block in blocks:
            seg_key = as_column(all_segs[block, pl.ds(seq, 1)].astype(jnp.float32))
            earlier = jnp.where(seg_key < seg_query, 1.0, 0.0)
            starts[seq] += jnp.sum(earlier, axis=0, keepdims=True)
            if block is me:
                same = (seg_key == seg_query) & (key_rows <= query_cols)
                masks.append(jnp.where(same, 1.0, 0.0))
            else:
                masks.append(1.0 - earlier)
            values_t.append(keys_values[block, rows, pl.ds(pair, pair)].T)
        keys = [keys_values[block, rows, pl.ds(0, pair)] for block in blocks]
        mask = jnp.concatenate(masks, axis=0)
        scores = dot_nn(jnp.concatenate(keys, axis=0), query_t[seq])
        weights = jnp.exp(scores) * jnp.concatenate([mask] * 4, axis=1)
        row_sum[seq] += jnp.sum(weights, axis=0, keepdims=True)
        low = weights.astype(jnp.bfloat16)
        value_rows = jnp.concatenate(values_t, axis=1)
        for group in range(2):
            acc[seq, group] += dot_nn(
                value_rows[group * head_dim : (group + 1) * head_dim],
                low[:, group * 2 * tile : (group + 1) * 2 * tile],
            )

    def attend_own(seq, carry):
        attend([me], seq)
        return carry

    lax.fori_loop(0, sequences, attend_own, 0)

    def head_copy(hop, seq, arriving=False):
        sent = (here.wt, here.wt, here.chip_wt)
        landed = (here.chip_wt, here.core_wt, here.far_wt)
        part = all_heads.at[(landed if arriving else sent)[hop], rows_of(seq)]
        device = here.chip if hop == 0 else here.core
        return send_to(
            part, part, ref["head_send"].at[hop, seq], ref["head_recv"].at[hop, seq], device
        )

    def far_copy(seq):
        part = all_heads.at[here.wt, rows_of(seq)]
        return send_to(
            part, part, ref["head_send"].at[2, seq], ref["head_recv"].at[2, seq], here.far
        )

    def relay(seq):
        head_copy(0, seq, True).wait_recv()

        @pl.when(seq < sequences - 1)
        def _():
            head_copy(2, seq).start()

    def mix(seq):
        rows = rows_of(seq)
        total = row_sum[seq]
        logs[seq] = jnp.log(total)
        for group in range(2):
            cols = slice(group * 2 * tile, (group + 1) * 2 * tile)
            part = acc[seq, group] / total[:, cols]
            mixed = jnp.concatenate([part[:, :tile], part[:, tile:]], axis=0)
            mixed_t[seq, group] = mixed
            all_heads[here.wt, rows, pl.ds(group * pair, pair)] = mixed.T.astype(jnp.bfloat16)
        head_copy(0, seq).start()
        head_copy(1, seq).start()

        @pl.when(here.top)
        def _():
            stats_out = ref["stats_out"]
            stats_out[seq] = jnp.zeros_like(stats_out[seq])
            stats_out[seq, pl.ds(0, 1)] = logs[seq]
            stats_out[seq, pl.ds(1, 1), pl.ds(0, tile)] = starts[seq]
            share_copy(1, seq).start()

        @pl.when(seq == sequences - 1)
        def _():
            far_copy(seq).start()

    def ffn_unit(rows):
        values = residual[rows, :]
        inverse = lax.rsqrt(jnp.mean(values * values, axis=-1, keepdims=True) + EPS)
        return values * inverse, inverse

    def feed(seq):
        rows = rows_of(seq)
        head_copy(1, seq, True).wait_recv()
        head_copy(2, seq, True).wait_recv()
        total = tokens[rows, :].astype(jnp.float32)
        for slot in range(4):
            total = total + dot_nn(all_heads[slot, rows], all_out[slot])
        residual[rows, :] = total
        unit, unused = ffn_unit(rows)
        normed = (unit * ffn_gain_row).astype(jnp.bfloat16)
        lefts[1, :, rows] = normed.T
        gate = dot_nn(normed, w_gate[...])
        up = dot_nn(normed, w_up[...])
        sigmoid = 0.5 * jnp.tanh(0.5 * gate) + 0.5
        silu = gate * sigmoid
        ffn_grads[0, rows] = (silu * up).astype(jnp.bfloat16)
        grads = grad_hidden[rows, :].astype(jnp.float32)
        grad_gate = (grads * up * sigmoid * (1.0 + gate * (1.0 - sigmoid))).astype(jnp.bfloat16)
        grad_up = (grads * silu).astype(jnp.bfloat16)
        ffn_grads[1, rows] = grad_gate
        ffn_grads[2, rows] = grad_up
        grad_normed = dot_nn(grad_gate, gate_t[...]) + dot_nn(grad_up, up_t[...])
        ffn_gain_part[...] += jnp.sum(grad_normed * unit, axis=0, keepdims=True)
        ffn_sum.offer(seq, grad_normed)

    ffn_gain_part[...] = jnp.zeros_like(ffn_gain_part)

    def sequence_turn(turn_, carry):
        @pl.when(turn_ < sequences)
        def _():
            @pl.when(turn_ + 2 < sequences)
            def _():
                pass_rows(turn_ + 2)

            @pl.when(comes_aside(0))
            def _():
                @pl.when(turn_ == 0)
                def _():
                    seg_side_copy(0, here.beside_ctx).wait_recv()

                side_copy(0, turn_, here.beside_ctx).wait_recv()
                attend([here.beside_ctx], turn_)

        @pl.when(turn_ + 1 < sequences)
        def _():
            for step in range(1, min(REACH + 1, levels)):
                route_level(step, turn_ + 1)

        @pl.when(turn_ == 1)
        def _():
            out_copy(0, True).wait_recv()
            out_copy(2).start()

        @pl.when((turn_ > 0) & (turn_ <= sequences))
        def _():
            relay(turn_ - 1)

        @pl.when(turn_ < sequences)
        def _():
            def level(step, carry):
                @pl.when(me >= 2 * step)
                def _():
                    @pl.when(turn_ == 0)
                    def _():
                        seg_side_copy(step, here.beside_ctx).wait_recv()

                    side_copy(step, turn_, here.beside_ctx).wait_recv()
                    attend([block_of(me, step), block_of(here.beside_ctx, step)], turn_)

                return carry

            lax.fori_loop(1, levels, level, 0)
            mix(turn_)

        @pl.when(turn_ + 1 < sequences)
        def _():
            for step in range(REACH + 1, levels):
                route_level(step, turn_ + 1)

        @pl.when(turn_ == 1)
        def _():
            out_copy(1, True).wait_recv()
            out_copy(2, True).wait_recv()

        @pl.when(turn_ > 1)
        def _():
            ffn_sum.cross(turn_ - 2)

        @pl.when(turn_ > 0)
        def _():
            feed(turn_ - 1)

        @pl.when(turn_ > 2)
        def _():
            ffn_sum.close(turn_ - 3)

        return carry

    lax.fori_loop(0, sequences + 1, sequence_turn, 0)
    for i in range(3):
        ffn.tick(i, 0, lefts.at[min(i, 1)], ffn_grads.at[i], first=True)
    last = count - 1
    deltas, own_grads = ref["deltas"], ref["own_grads"]
    side_in, side_out = ref["side_in"], ref["side_out"]
    line_in, line_out = ref["line_in"], ref["line_out"]
    ffn_sums, qkv_total = ref["ffn_sums"], ref["qkv_total"]
    grad_query_t = acc
    grad_res_t = w_gate.at[:, pl.ds(0, rows_all)]
    query_n = gate_t.at[pl.ds(0, 4 * tile), pl.ds(0, pair)]
    grad_heads_n = gate_t.at[pl.ds(4 * tile, 4 * tile), pl.ds(0, pair)]
    upper_query_n = gate_t.at[pl.ds(0, 4 * tile), pl.ds(pair, pair)]
    upper_heads_t = gate_t.at[pl.ds(0, pair), pl.ds(2 * pair, 4 * tile)]
    upper_heads_n = gate_t.at[pl.ds(4 * tile, 4 * tile), pl.ds(pair, pair)]
    grad_qkv = w_up.at[pl.ds(0, rows_all), pl.ds(0, 4 * pair)]
    normed_t = w_up.at[:, pl.ds(4 * pair, rows_all)]
    qkv_t = up_t.at[pl.ds(rows_all, 4 * pair)]
    heads = all_heads.at[here.wt]
    sources = {
        "output": cotangent,
        "tokens_grad": tokens,
        "w_down_sum": ffn_sums.at[0],
        "w_gate_sum": ffn_sums.at[1],
        "w_up_sum": ffn_sums.at[2],
        "w_query_sum": qkv_total.at[:, pl.ds(0, 2 * pair)],
        "w_key_sum": qkv_total.at[:, pl.ds(2 * pair, pair)],
        "w_value_sum": qkv_total.at[:, pl.ds(3 * pair, pair)],
    }
    stores = Mover(
        [(sources[name] if name in sources else ref[name], ref[name + "_res"]) for name in RESULTS],
        ref["store_sems"],
    )
    wt_sum = WtSum(here, tile, up_t, *shared, ref["wt_send"], ref["wt_recv"], ffn_sum)
    mlp_sum = WtSum(here, tile, grad_hidden, *(ref[f"mlp_sum{i}"] for i in range(5)))
    gains = GainSum(here, *(ref[f"gains{i}"] for i in range(6)))
    gain_slots = ref["gains0"]
    out = Ring(count, *(ref[f"out{i}"] for i in range(3)))
    qkv = Ring(count, *(ref[f"qkv{i}"] for i in range(3)))

    def ffn_tick(index):
        step, which = lax.div(index, 3), lax.rem(index, 3)
        ffn.tick(
            which,
            step,
            lefts.at[lax.min(which, 1)],
            ffn_grads.at[which],
            result=ffn_sums.at[which],
            final=step == last,
        )

    def token_unit(rows):
        inputs = tokens[rows, :].astype(jnp.float32)
        inverse = lax.rsqrt(jnp.mean(inputs * inputs, axis=-1, keepdims=True) + EPS)
        return inputs * inverse, inverse

    def prepare(seq):
        rows = rows_of(seq)
        unit, inverse = ffn_unit(rows)
        scaled = ffn_sum.result(seq) * ffn_gain_row
        back = inverse * (scaled - unit * jnp.mean(scaled * unit, axis=-1, keepdims=True))
        grads = (cotangent[rows, :].astype(jnp.float32) + back).astype(jnp.bfloat16)
        grad_res[rows, :] = grads
        grad_res_t[:, rows] = grads.T
        unit, unused = token_unit(rows)
        normed_t[:, rows] = (unit * gain).astype(jnp.bfloat16).T
        grad_heads_t[heads_at(seq)] = jnp.zeros((pair, 4 * tile), jnp.bfloat16)
        low = dot_nn(grads, ref["w_out"][...]).astype(jnp.bfloat16)
        for group in range(2):
            flipped = low[:, group * pair : (group + 1) * pair].T
            small = pl.ds(pl.multiple_of(seq * tile, tile), tile)
            heads_small[pl.ds(group * pair, pair), small] = flipped
            product_t = flipped.astype(jnp.float32) * mixed_t[seq, group]
            for member in range(2):
                part = slice(member * head_dim, (member + 1) * head_dim)
                cols = pl.ds((2 * group + member) * tile, tile)
                into = pl.ds(pl.multiple_of(seq * pair + group * head_dim, head_dim), head_dim)
                spot = pl.ds(rows_all + (2 * group + member) * tile, tile)
                grad_heads_t[into, spot] = flipped[part]
                deltas[seq, :, cols] = jnp.sum(product_t[part], axis=0, keepdims=True)
        grad_query_t[seq] = jnp.zeros_like(grad_query_t[seq])

        @pl.when(here.top)
        def _():
            share_copy(2, seq).start()
            share_copy(3, seq).start()

    def grads_of(blocks, seq, upper=False):
        rows = rows_of(seq)
        keys = [keys_values[block, rows, pl.ds(0, pair)] for block in blocks]
        values = [keys_values[block, rows, pl.ds(pair, pair)] for block in blocks]
        if upper:
            stats = ref["stats_in"]
            log, start = stats[seq, pl.ds(0, 1)], stats[seq, pl.ds(1, 1), pl.ds(0, tile)]
            delta = ref["upper_deltas"][seq]
            queries, grad_heads = ref["upper_query_t"][seq], upper_heads_t[...]
            query_rows, grad_rows = upper_query_n, upper_heads_n
        else:
            log, start, delta = logs[seq], starts[seq], deltas[seq]
            queries, grad_heads = query_t[seq], grad_heads_t[heads_at(seq)]
            query_rows, grad_rows = query_n, grad_heads_n
        masks = []
        for block in blocks:
            allowed = key_rows.astype(jnp.float32) >= start - (block * tile).astype(jnp.float32)
            if block is me and not upper:
                allowed = allowed & (key_rows <= query_cols)
            masks.append(jnp.where(allowed, 1.0, 0.0))
        mask = jnp.concatenate(masks, axis=0)
        scores = dot_nn(jnp.concatenate(keys, axis=0), queries)
        probs = jnp.exp(scores - log) * jnp.concatenate([mask] * 4, axis=1)
        grad_probs = dot_nn(jnp.concatenate(values, axis=0), grad_heads)
        grad_scores = (probs * (grad_probs - delta)).astype(jnp.bfloat16)
        flipped = jnp.concatenate([part.T for part in keys], axis=1)
        for group in range(2):
            cols = slice(group * 2 * tile, (group + 1) * 2 * tile)
            grads = dot_nn(
                flipped[group * head_dim : (group + 1) * head_dim], grad_scores[:, cols]
            )
            if upper:
                ref["upper_grad"][group] += grads
            else:
                grad_query_t[seq, group] += grads
        grad_keys = dot_nn(grad_scores, query_rows[...])
        grad_values = dot_nn(probs.astype(jnp.bfloat16), grad_rows[...])
        return jnp.concatenate([grad_keys, grad_values], axis=1)

    def side_grad_copy(step, seq):
        return send_to(
            side_out.at[step, rows_of(seq)],
            side_in.at[step, rows_of(seq)],
            ref["side_grad_send"].at[step, seq],
            ref["side_grad_recv"].at[step, seq],
            here.beside,
        )

    def line_copy(step, seq):
        earlier = step - 1
        return send_to(
            line_out.at[earlier, rows_of(seq)],
            line_in.at[earlier, rows_of(seq)],
            ref["line_send"].at[earlier, seq],
            ref["line_recv"].at[earlier, seq],
            here.below,
        )

    two = ref["two_grads"]

    def hands_down(step):
        return (me >= 2 * step) & (here.has_above | (step == 1))

    def upper_grad_copy(seq):
        return send_to(
            ref["upper_grad_out"].at[seq],
            ref["upper_grad_in"].at[seq],
            ref["upper_send"].at[seq],
            ref["upper_recv"].at[seq],
            here.above,
        )

    def send_side(step, seq):
        side_out[step, rows_of(seq)] = two[pl.ds(tile, tile)].astype(jnp.bfloat16)
        side_grad_copy(step, seq).start()

    def find_grads(seq):
        rows = rows_of(seq)
        query_n[...] = query_t[seq].T
        grad_heads_n[...] = grad_heads_t[heads_at(seq)].T

        @pl.when(here.serves)
        def _():
            for what in range(4):
                share_copy(what, seq).wait_recv()
            upper_heads_t[...] = jnp.zeros_like(upper_heads_t)
            for group in range(2):
                for member in range(2):
                    part = ref["upper_heads"][
                        seq, pl.ds(group * pair + member * head_dim, head_dim)
                    ]
                    cols = pl.ds((2 * group + member) * tile, tile)
                    upper_heads_t[pl.ds(group * head_dim, head_dim), cols] = part
            upper_query_n[...] = ref["upper_query_t"][seq].T
            upper_heads_n[...] = upper_heads_t[...].T
            ref["upper_grad"][...] = jnp.zeros_like(ref["upper_grad"])

        def level(index, carry):
            step = levels - 2 - index

            @pl.when(hands_down(step))
            def _():
                blocks = [block_of(me, step), block_of(here.beside_ctx, step)]
                two[...] = grads_of(blocks, seq)

                @pl.when(here.serves)
                def _():
                    two[...] += grads_of(blocks, seq, True)

                send_side(step, seq)
                line_out[step - 1, rows] = two[pl.ds(0, tile)].astype(jnp.bfloat16)

            return carry

        lax.fori_loop(0, levels - 2, level, 0)

        @pl.when(comes_aside(0))
        def _():
            two[...] = grads_of([me, here.beside_ctx], seq)

        @pl.when(jnp.logical_not(comes_aside(0)))
        def _():
            two[pl.ds(0, tile)] = grads_of([me], seq)

        @pl.when(here.serves)
        def _():
            ref["upper_grad_out"][seq] = ref["upper_grad"][...].astype(jnp.bfloat16)
            upper_grad_copy(seq).start()

        @pl.when(comes_aside(0))
        def _():
            send_side(0, seq)

        own_grads[rows, :] = two[pl.ds(0, tile)]

    gets_line = me < count - 4

    def send_down(step, seq):
        @pl.when(hands_down(step))
        def _():
            rows = rows_of(seq)
            side_grad_copy(step, seq).wait_recv()
            total = line_out[step - 1, rows].astype(jnp.float32) + side_in[step, rows].astype(
                jnp.float32
            )

            @pl.when(gets_line)
            def _():
                line_copy(step + 1, seq).wait_recv()
                line_out[step - 1, rows] = (
                    total + line_in[step, rows].astype(jnp.float32)
                ).astype(jnp.bfloat16)

            @pl.when(jnp.logical_not(gets_line))
            def _():
                line_out[step - 1, rows] = total.astype(jnp.bfloat16)

            line_copy(step, seq).start()

    gain_slots[me] = jnp.zeros_like(gain_slots[me])
    gain_slots[me, pl.ds(1, 1)] = ffn_gain_part[...]

    def back_through(grads, raw, gain_pair, row):
        cosine = table[:, pl.ds(0, pair)]
        sine = table[:, pl.ds(pair, pair)]
        turned = grads * cosine - swap_halves(grads, head_dim) * sine
        unit, inverse = pair_norm(raw, head_dim)
        gain_slots[me, pl.ds(row, 1), pl.ds(0, pair)] += jnp.sum(
            turned * unit, axis=0, keepdims=True
        )
        scaled = turned * gain_pair
        return (inverse * (scaled - unit * pair_mean(scaled * unit, head_dim))).astype(
            jnp.bfloat16
        )

    def project_back(seq):
        rows = rows_of(seq)

        @pl.when(here.top)
        def _():
            upper_grad_copy(seq).wait_recv()
            grad_query_t[seq] += ref["upper_grad_in"][seq].astype(jnp.float32)

        for group in range(2):
            grads = grad_query_t[seq, group] * (head_dim**-0.5)
            grads = jnp.concatenate([grads[:, :tile], grads[:, tile:]], axis=0).T
            cols = pl.ds(group * pair, pair)
            grad_qkv[rows, cols] = back_through(grads, query_raw[rows, cols], q_gain_pair, 2)

        @pl.when(me < here.beside_ctx)
        def _():
            side_grad_copy(0, seq).wait_recv()
            own_grads[rows, :] += side_in[0, rows].astype(jnp.float32)

        @pl.when(here.has_above)
        def _():
            line_copy(1, seq).wait_recv()
            own_grads[rows, :] += line_in[0, rows].astype(jnp.float32)

        grad_qkv[rows, pl.ds(2 * pair, pair)] = back_through(
            own_grads[rows, pl.ds(0, pair)], key_raw[rows, :], k_gain_pair, 3
        )
        grad_qkv[rows, pl.ds(3 * pair, pair)] = own_grads[rows, pl.ds(pair, pair)].astype(
            jnp.bfloat16
        )
        grads = dot_nn(grad_qkv[rows, :], qkv_t[...])
        unit, unused = token_unit(rows)
        gain_slots[me, pl.ds(0, 1)] += jnp.sum(grads * unit, axis=0, keepdims=True)
        wt_sum.offer(seq, grads)

    def output_rows(seq):
        rows = rows_of(seq)
        cotangent[rows, :] = (residual[rows, :] + mlp_sum.result(seq)).astype(jnp.bfloat16)

    def token_rows(seq):
        rows = rows_of(seq)
        unit, inverse = token_unit(rows)
        scaled = wt_sum.result(seq) * gain
        grads = inverse * (scaled - unit * jnp.mean(scaled * unit, axis=-1, keepdims=True))
        tokens[rows, :] = (grad_res[rows, :].astype(jnp.float32) + grads).astype(
            jnp.bfloat16
        )

    few, more, early = TICKS

    def ticks_before(turn_):
        return 3 + few * lax.min(turn_, early) + more * lax.max(turn_ - early, 0)

    def grad_turn(turn_, carry):
        @pl.when(turn_ < sequences)
        def _():
            prepare(turn_)

        @pl.when((turn_ >= 1) & (turn_ <= sequences))
        def _():
            find_grads(turn_ - 1)

        @pl.when(turn_ == 0)
        def _():
            ffn_sum.cross(sequences - 1)
            qkv_t[pl.ds(0, 2 * pair), :] = ref["w_query"][...].T
            qkv_t[pl.ds(2 * pair, pair), :] = ref["w_key"][...].T
            qkv_t[pl.ds(3 * pair, pair), :] = ref["w_value"][...].T

        @pl.when((turn_ == 1) | (turn_ == 2))
        def _():
            ffn_sum.close(sequences - 3 + turn_)

        @pl.when((turn_ >= 3) & (turn_ < sequences + 3))
        def _():
            def down(index, carry):
                send_down(levels - 2 - index, turn_ - 3)
                return carry

            lax.fori_loop(0, levels - 2, down, 0)

        for i in range(max(few, more)):

            @pl.when(ticks_before(turn_) + i < ticks_before(turn_ + 1))
            def _():
                ffn_tick(ticks_before(turn_) + i)

        @pl.when((turn_ >= 1) & (turn_ <= sequences))
        def _():
            seq = turn_ - 1
            mlp_sum.offer(seq, dot_nt(ffn_grads[0, rows_of(seq)], w_down[...]))

        @pl.when((turn_ >= 2) & (turn_ <= sequences + 1))
        def _():
            mlp_sum.cross(turn_ - 2)

        @pl.when((turn_ >= 3) & (turn_ <= sequences + 2))
        def _():
            mlp_sum.close(turn_ - 3)

        @pl.when(turn_ >= 5)
        def _():
            output_rows(turn_ - 5)
            project_back(turn_ - 5)

        @pl.when(turn_ >= 6)
        def _():
            wt_sum.cross(turn_ - 6)

        for i in range(4):

            @pl.when(turn_ == sequences + i)
            def _():
                out.tick(0, i, grad_res_t, heads, first=i == 0)

        return carry

    turns = sequences + 5
    lax.fori_loop(0, turns, grad_turn, 0)
    qkv.tick(0, 0, normed_t, grad_qkv, first=True)
    gains.start()
    wt_sum.cross(sequences - 1)
    stores.start(0)
    done = 3 + few * early + more * (turns - early)
    left_over = 3 * count - done
    each = -(-left_over // (last - 1))

    def tail(step, carry):
        @pl.when(step == 2)
        def _():
            gains.sum_ctx()

        @pl.when(step == 3)
        def _():
            gains.sum_cores()

        @pl.when(step == 4)
        def _():
            total = gains.sum_chips()
            ref["attn_gain_sum"][...] = total[0:1]
            ref["ffn_gain_sum"][...] = total[1:2]
            folded = total[:, :pair]
            folded = folded + pltpu.roll(folded, head_dim, 1)
            ref["q_gain_sum"][...] = folded[2:3]
            ref["k_gain_sum"][...] = folded[3:4]

        @pl.when(step == last)
        def _():
            stores.start(1, 2, 3, 4, 5, 9, 10, 11, 12)

        for i in range(each):
            index = done + each * (step - 1) + i

            @pl.when(index < 3 * count)
            def _():
                ffn_tick(index)

        qkv.tick(0, step, normed_t, grad_qkv, result=qkv_total, final=step == last)

        @pl.when(step + 3 <= last)
        def _():
            out.tick(
                0, step + 3, grad_res_t, heads, result=ref["w_out_sum"], final=step + 3 == last
            )

        @pl.when(step <= sequences)
        def _():
            wt_sum.close(step - 1)

        @pl.when((step >= 2) & (step <= sequences + 1))
        def _():
            token_rows(step - 2)

        return carry

    lax.fori_loop(1, count, tail, 0)
    stores.start(6, 7, 8)
    gains.finish()
    ffn_sum.finish(sequences, (0,))
    wt_sum.finish(sequences)
    mlp_sum.finish(sequences)
    for i in range(3):
        ffn.finish(i, last)
    out.finish(0, last)
    qkv.finish(0, last)
    for hop in range(3):
        out_copy(hop).wait_send()

        def sent(seq, carry):
            head_copy(hop, seq).wait_send()
            return carry

        lax.fori_loop(0, sequences, sent, 0)

    def each_seq(step):
        def one(seq, carry):
            step(seq)
            return carry

        lax.fori_loop(0, sequences, one, 0)

    def drain(step, carry):
        @pl.when((step > 0) & goes_up(step))
        def _():
            seg_up_copy(step).wait_send()

        @pl.when(((step > 0) & (step <= REACH) & goes_up(step)) | forwards(step))
        def _():
            each_seq(lambda seq: up_copy(step, seq).wait_send())

        @pl.when(goes_aside(step))
        def _():
            seg_side_copy(step).wait_send()

        @pl.when(goes_aside(step))
        def _():
            each_seq(lambda seq: side_copy(step, seq).wait_send())

        @pl.when((step > 0) & (step < levels - 1) & hands_down(step))
        def _():
            each_seq(lambda seq: side_grad_copy(step, seq).wait_send())
            each_seq(lambda seq: line_copy(step, seq).wait_send())

        return carry

    lax.fori_loop(0, levels, drain, 0)

    @pl.when(comes_aside(0))
    def _():
        each_seq(lambda seq: side_grad_copy(0, seq).wait_send())

    @pl.when(here.top)
    def _():
        for what in range(4):
            each_seq(lambda seq: share_copy(what, seq).wait_send())

    @pl.when(here.serves)
    def _():
        each_seq(lambda seq: upper_grad_copy(seq).wait_send())

    stores.wait(*range(len(RESULTS)))


def layer(inputs):
    count = lax.axis_size("ctx")
    sequences, tile = inputs["segments"].shape
    rows, width = inputs["tokens_in"].shape
    head_dim = inputs["q_gain"].shape[0]
    hidden = inputs["w_gate_in"].shape[1]
    pair = 2 * head_dim
    levels = count // 2
    block = width // count
    f32, bf16 = jnp.float32, jnp.bfloat16
    dma = pltpu.SemaphoreType.DMA
    results = {
        "output": ((rows, width), bf16),
        "tokens_grad": ((rows, width), bf16),
        "w_down_sum": ((block, hidden), f32),
        "w_gate_sum": ((block, hidden), f32),
        "w_up_sum": ((block, hidden), f32),
        "w_out_sum": ((block, 2 * pair), f32),
        "w_query_sum": ((block, 2 * pair), f32),
        "w_key_sum": ((block, pair), f32),
        "w_value_sum": ((block, pair), f32),
        "attn_gain_sum": ((1, width), f32),
        "ffn_gain_sum": ((1, width), f32),
        "q_gain_sum": ((1, pair), f32),
        "k_gain_sum": ((1, pair), f32),
    }
    staged = ("w_out_sum",) + RESULTS[9:]
    scratch = {name: pltpu.VMEM(*results[name]) for name in staged}
    buffers = {
        "tokens": ((rows, width), bf16),
        "residual": ((rows, width), f32),
        "mixed_t": ((sequences, 2, pair, tile), f32),
        "query_t": ((sequences, pair, 4 * tile), bf16),
        "logs": ((sequences, 1, 4 * tile), f32),
        "starts": ((sequences, 1, tile), f32),
        "keys_values": ((count, rows, 2 * pair), bf16),
        "query_raw": ((rows, 2 * pair), f32),
        "key_raw": ((rows, pair), f32),
        "lefts": ((2, width, rows), bf16),
        "ffn_grads": ((3, rows, hidden), bf16),
        "ffn_gain_part": ((1, width), f32),
        "grad_res": ((rows, width), bf16),
        "all_segs": ((count, 8, tile), jnp.int32),
        "all_out": ((4, 2 * pair, width), bf16),
        "all_heads": ((4, rows, 2 * pair), bf16),
        "acc": ((sequences, 2, head_dim, 2 * tile), f32),
        "row_sum": ((sequences, 1, 4 * tile), f32),
        "table": ((tile, 2 * pair), f32),
        "cotangent": ((rows, width), bf16),
        "w_down": ((width, hidden), bf16),
        "w_gate": ((width, hidden), bf16),
        "w_up": ((width, hidden), bf16),
        "gate_t": ((hidden, width), bf16),
        "up_t": ((hidden, width), bf16),
        "grad_hidden": ((rows, hidden), bf16),
        "ffn_part": ((rows, width), bf16),
        "sum_got": ((rows, width // 2), bf16),
        "sum_far": ((rows, width // 2), bf16),
        "sum_full": ((2, rows, width // 2), bf16),
        "mlp_sum0": ((rows, width // 2), bf16),
        "mlp_sum1": ((rows, width // 2), bf16),
        "mlp_sum2": ((2, rows, width // 2), bf16),
        "deltas": ((sequences, 1, 4 * tile), f32),
        "own_grads": ((rows, 2 * pair), f32),
        "side_in": ((levels - 1, rows, 2 * pair), bf16),
        "side_out": ((levels - 1, rows, 2 * pair), bf16),
        "line_in": ((levels - 2, rows, 2 * pair), bf16),
        "line_out": ((levels - 2, rows, 2 * pair), bf16),
        "two_grads": ((2 * tile, 2 * pair), f32),
        "upper_query_t": ((sequences, pair, 4 * tile), bf16),
        "upper_heads": ((sequences, 2 * pair, tile), bf16),
        "upper_deltas": ((sequences, 1, 4 * tile), f32),
        "stats_out": ((sequences, 8, 4 * tile), f32),
        "stats_in": ((sequences, 8, 4 * tile), f32),
        "upper_grad": ((2, head_dim, 2 * tile), f32),
        "upper_grad_out": ((sequences, 2, head_dim, 2 * tile), bf16),
        "upper_grad_in": ((sequences, 2, head_dim, 2 * tile), bf16),
        "ffn_sums": ((3, block, hidden), f32),
        "qkv_total": ((block, 4 * pair), f32),
        "gains0": ((count, 8, width), f32),
        "gains1": ((2, 2, 8, width), f32),
    }
    scratch |= {name: pltpu.VMEM(*spec) for name, spec in buffers.items()}
    semaphores = {
        "load_sems": (6,),
        "store_sems": (len(RESULTS),),
        "up_send": (levels, sequences),
        "up_recv": (levels, sequences),
        "side_send": (levels, sequences),
        "side_recv": (levels, sequences),
        "seg_send": (levels, 2),
        "seg_recv": (levels, 2),
        "out_send": (3,),
        "out_recv": (3,),
        "head_send": (3, sequences),
        "head_recv": (3, sequences),
        "ffn_send": (3, sequences),
        "ffn_recv": (3, sequences),
        "wt_send": (3, sequences),
        "wt_recv": (3, sequences),
        "mlp_sum3": (3, sequences),
        "mlp_sum4": (3, sequences),
        "side_grad_send": (levels - 1, sequences),
        "side_grad_recv": (levels - 1, sequences),
        "share_send": (4, sequences),
        "share_recv": (4, sequences),
        "upper_send": (sequences,),
        "upper_recv": (sequences,),
        "line_send": (levels - 2, sequences),
        "line_recv": (levels - 2, sequences),
        "gains2": (count - 1,),
        "gains3": (count - 1,),
        "gains4": (2,),
        "gains5": (2,),
    }
    scratch |= {name: dma(shape) for name, shape in semaphores.items()}
    for label, kinds in (
        ("ffn", ring_scratch(count, 3, block, hidden)),
        ("out", ring_scratch(count, 1, block, 2 * pair)),
        ("qkv", ring_scratch(count, 1, block, 4 * pair)),
    ):
        scratch |= {f"{label}{i}": kind for i, kind in enumerate(kinds)}
    vmem, anywhere = pl.BlockSpec(memory_space=pltpu.VMEM), pl.BlockSpec(memory_space=pl.ANY)
    names = (*inputs, *(name + "_res" for name in RESULTS), *scratch)
    arrays = pl.pallas_call(
        partial(layer_kernel, count, names),
        out_shape=[jax.ShapeDtypeStruct(*results[name]) for name in RESULTS],
        in_specs=[anywhere if name.endswith("_in") else vmem for name in inputs],
        out_specs=[anywhere] * len(RESULTS),
        scratch_shapes=list(scratch.values()),
        compiler_params=pltpu.CompilerParams(
            collective_id=2, has_side_effects=True, vmem_limit_bytes=VMEM_LIMIT
        ),
    )(*inputs.values())
    return dict(zip(RESULTS, arrays, strict=True))


def pieces_of(shape):
    return max(shape[0] // 128, 1) if shape[0] % 128 == 0 else 1


def hand_over_kernel(count, *refs):
    sources, targets, staged = refs[:count], refs[count : 2 * count], refs[2 * count : 3 * count]
    ways_in, ways_out = [], []
    for source, target, stage in zip(sources, targets, staged, strict=True):
        parts = pieces_of(source.shape)
        size = source.shape[0] // parts
        for part in range(parts):
            rows = pl.ds(part * size, size)
            ways_in.append((source.at[rows], stage.at[rows]))
            ways_out.append((stage.at[rows], target.at[rows]))
    loads, stores = Mover(ways_in, refs[3 * count]), Mover(ways_out, refs[3 * count + 1])
    every = range(len(ways_in))
    loads.start(*every)
    for i in every:
        loads.wait(i)
        stores.start(i)
    stores.wait(*every)


def hand_over(arrays):
    anywhere = pl.BlockSpec(memory_space=pl.ANY)
    dma = pltpu.SemaphoreType.DMA((sum(pieces_of(array.shape) for array in arrays),))
    return pl.pallas_call(
        partial(hand_over_kernel, len(arrays)),
        out_shape=[jax.ShapeDtypeStruct(array.shape, array.dtype) for array in arrays],
        in_specs=[anywhere] * len(arrays),
        out_specs=[anywhere] * len(arrays),
        scratch_shapes=[pltpu.VMEM(array.shape, array.dtype) for array in arrays] + [dma, dma],
        compiler_params=pltpu.CompilerParams(vmem_limit_bytes=60 * MIB),
    )(*arrays)


def rotary_table(length, head_dim):
    half = head_dim // 2
    frequency = THETA ** (-2.0 * np.arange(half) / head_dim)
    angles = np.arange(length)[:, None] * frequency[None, :]
    cosine, sine = np.cos(angles), np.sin(angles)
    return np.concatenate([cosine] * 4 + [-sine, sine] * 2, axis=1).astype(np.float32)


def kernels_fit(tokens, w_query, key_matrix, q_gain, w_gate):
    sequences, tile, width = tokens.shape
    count, head_dim = lax.axis_size("ctx"), q_gain.shape[0]
    return (
        lax.axis_size("wt") == 4
        and count % 2 == 0
        and count >= 6
        and tile == 128
        and sequences <= 5
        and sequences * count <= 40
        and head_dim == 64
        and w_query.shape[1] == 4 * head_dim
        and key_matrix.shape[1] == 2 * head_dim
        and width % (128 * count) == 0
        and w_gate.shape[1] >= max(width, sequences * tile + 512)
        and w_gate.shape[1] <= 1152
        and width <= 1024
    )


def on_device_plain(
    tokens,
    segments,
    attn_gain,
    w_query,
    key_matrix,
    value_matrix,
    q_gain,
    k_gain,
    w_out,
    ffn_gain,
    w_gate,
    w_up,
    w_down,
    cotangent,
):
    sequences, seq_rows, model_width = tokens.shape
    head_dim = q_gain.shape[0]
    q_local = w_query.shape[1] // head_dim
    kv_local = key_matrix.shape[1] // head_dim
    per_group = q_local // kv_local
    score_scale = 1.0 / math.sqrt(head_dim)
    all_rows = sequences * seq_rows
    places = lax.axis_index("ctx") * seq_rows + jnp.arange(seq_rows, dtype=jnp.int32)
    frequency = THETA ** (-jnp.arange(0, head_dim, 2, dtype=jnp.float32) / head_dim)
    angles = places.astype(jnp.float32)[None, :, None] * frequency
    cosine_table = jnp.cos(angles)[:, :, None, :]
    sine_table = jnp.sin(angles)[:, :, None, :]
    inputs = tokens.astype(jnp.float32).reshape(all_rows, model_width)
    normed, attn_unit, attn_inverse = norm_rows(inputs, attn_gain)
    normed_low = normed.astype(jnp.bfloat16)
    query_raw = product(normed_low, w_query).reshape(sequences, seq_rows, q_local, head_dim)
    key_raw = product(normed_low, key_matrix).reshape(sequences, seq_rows, kv_local, head_dim)
    value_low = (
        product(normed_low, value_matrix)
        .astype(jnp.bfloat16)
        .reshape(sequences, seq_rows, kv_local * head_dim)
    )
    query_normed, query_unit, query_inverse = norm_rows(query_raw, q_gain)
    key_normed, key_unit, key_inverse = norm_rows(key_raw, k_gain)
    query_low = rotate(query_normed, cosine_table, sine_table, 1.0).astype(jnp.bfloat16)
    key_low = rotate(key_normed, cosine_table, sine_table, 1.0).astype(jnp.bfloat16)
    key_flat = key_low.reshape(sequences, seq_rows, kv_local * head_dim)
    query_groups = query_low.reshape(sequences, seq_rows, kv_local, per_group, head_dim)
    attend = partial(
        attend_piece,
        queries=query_groups,
        query_places=places,
        query_segs=segments,
        score_scale=score_scale,
    )
    start_state = (
        jnp.full((sequences, kv_local, per_group, seq_rows), NEG, jnp.float32),
        jnp.zeros((sequences, kv_local, per_group, seq_rows), jnp.float32),
        jnp.zeros((sequences, seq_rows, kv_local, per_group, head_dim), jnp.float32),
    )
    keys_values = lax.all_gather(
        jnp.concatenate([key_flat, value_low], axis=-1), "ctx", axis=1, tiled=True
    )
    kv_width = kv_local * head_dim
    gathered = (
        keys_values[..., :kv_width],
        keys_values[..., kv_width:],
        lax.all_gather(segments, "ctx", axis=1, tiled=True),
    )
    row_max, row_sum, weighted = attend(
        start_state,
        gathered,
        jnp.int32(0),
    )
    mixed_heads = weighted / jnp.transpose(row_sum, (0, 3, 1, 2))[..., None]
    mixed_low = mixed_heads.astype(jnp.bfloat16).reshape(all_rows, q_local * head_dim)
    attn_term = by_transpose(mixed_low, w_out)
    residual = inputs + lax.psum(attn_term.astype(jnp.bfloat16), "wt").astype(jnp.float32)
    normed_ffn, ffn_unit, ffn_inverse = norm_rows(residual, ffn_gain)
    normed_ffn_low = normed_ffn.astype(jnp.bfloat16)
    gate_proj = product(normed_ffn_low, w_gate)
    up_proj = product(normed_ffn_low, w_up)
    gate_sigmoid = jax.nn.sigmoid(gate_proj)
    gate_silu = gate_proj * gate_sigmoid
    hidden_low = (gate_silu * up_proj).astype(jnp.bfloat16)
    mlp_term = by_transpose(hidden_low, w_down)
    output_rows = (
        residual + lax.psum(mlp_term.astype(jnp.bfloat16), "wt").astype(jnp.float32)
    ).astype(jnp.bfloat16)
    log_total = row_max + jnp.log(row_sum)
    grad_rows = cotangent.reshape(all_rows, model_width)
    grad_hidden = product(grad_rows, w_down)
    grad_gate = (
        grad_hidden * up_proj * gate_sigmoid * (1.0 + gate_proj * (1.0 - gate_sigmoid))
    ).astype(jnp.bfloat16)
    grad_up = (grad_hidden * gate_silu).astype(jnp.bfloat16)
    grad_normed_ffn = by_transpose(grad_gate, w_gate) + by_transpose(grad_up, w_up)
    ffn_gain_part = jnp.sum(grad_normed_ffn * ffn_unit, axis=0)
    grad_normed_ffn = lax.psum(grad_normed_ffn.astype(jnp.bfloat16), "wt").astype(jnp.float32)
    grad_residual = grad_rows.astype(jnp.float32) + norm_back(
        grad_normed_ffn, ffn_unit, ffn_inverse, ffn_gain
    )
    grad_residual_low = grad_residual.astype(jnp.bfloat16)
    grad_heads_low = product(grad_residual_low, w_out).astype(jnp.bfloat16)
    grad_groups = grad_heads_low.reshape(sequences, seq_rows, kv_local, per_group, head_dim)
    delta_rows = jnp.sum(grad_groups.astype(jnp.float32) * mixed_heads, axis=-1)
    delta_cols = jnp.transpose(delta_rows, (0, 2, 3, 1))
    query_grad_fn = partial(
        grad_piece,
        queries=query_groups,
        grad_heads=grad_groups,
        log_total=log_total,
        row_delta=delta_cols,
        query_places=places,
        query_segs=segments,
        score_scale=score_scale,
    )
    grad_query, grad_pairs = query_grad_fn(
        jnp.zeros((sequences, seq_rows, kv_local, per_group, head_dim), jnp.float32),
        gathered,
        jnp.int32(0),
    )
    grad_pairs = lax.psum_scatter(grad_pairs, "ctx", scatter_dimension=1, tiled=True).astype(
        jnp.float32
    )
    grad_key = grad_pairs[:, :, 0]
    grad_value = grad_pairs[:, :, 1]
    grad_query = rotate(
        grad_query.reshape(sequences, seq_rows, q_local, head_dim) * score_scale,
        cosine_table,
        sine_table,
        -1.0,
    )
    grad_key = rotate(grad_key * score_scale, cosine_table, sine_table, -1.0)
    q_gain_part = jnp.sum(grad_query * query_unit, axis=(0, 1, 2))
    k_gain_part = jnp.sum(grad_key * key_unit, axis=(0, 1, 2))
    grad_query_low = (
        norm_back(grad_query, query_unit, query_inverse, q_gain)
        .astype(jnp.bfloat16)
        .reshape(all_rows, q_local * head_dim)
    )
    grad_key_low = (
        norm_back(grad_key, key_unit, key_inverse, k_gain)
        .astype(jnp.bfloat16)
        .reshape(all_rows, kv_local * head_dim)
    )
    grad_value_low = grad_value.astype(jnp.bfloat16).reshape(all_rows, kv_local * head_dim)
    grad_normed = (
        by_transpose(grad_query_low, w_query)
        + by_transpose(grad_key_low, key_matrix)
        + by_transpose(grad_value_low, value_matrix)
    )
    attn_gain_part = jnp.sum(grad_normed * attn_unit, axis=0)
    grad_normed = lax.psum(grad_normed.astype(jnp.bfloat16), "wt").astype(jnp.float32)
    tokens_rows = (
        grad_residual + norm_back(grad_normed, attn_unit, attn_inverse, attn_gain)
    ).astype(jnp.bfloat16)
    output = output_rows.reshape(sequences, seq_rows, model_width)
    tokens_grad = tokens_rows.reshape(sequences, seq_rows, model_width)
    partial_sums = (
        transpose_by(grad_rows, hidden_low),
        transpose_by(normed_ffn_low, grad_gate),
        transpose_by(normed_ffn_low, grad_up),
        transpose_by(grad_residual_low, mixed_low),
        transpose_by(normed_low, grad_query_low),
        transpose_by(normed_low, grad_key_low),
        transpose_by(normed_low, grad_value_low),
    )
    summed = [
        lax.psum_scatter(part.astype(jnp.bfloat16), "ctx", scatter_dimension=0, tiled=True).astype(
            jnp.float32
        )
        for part in partial_sums
    ]
    w_down_grad, w_gate_grad, w_up_grad, w_out_grad = summed[:4]
    w_query_grad, w_key_grad, w_value_grad = summed[4:]
    attn_gain_grad, q_gain_grad, k_gain_grad, ffn_gain_grad = lax.psum(
        (attn_gain_part, q_gain_part, k_gain_part, ffn_gain_part), ("ctx", "wt")
    )
    return (
        output,
        tokens_grad,
        attn_gain_grad,
        w_query_grad,
        w_key_grad,
        w_value_grad,
        q_gain_grad,
        k_gain_grad,
        w_out_grad,
        ffn_gain_grad,
        w_gate_grad,
        w_up_grad,
        w_down_grad,
    )


def on_device(
    tokens,
    segments,
    attn_gain,
    w_query,
    key_matrix,
    value_matrix,
    q_gain,
    k_gain,
    w_out,
    ffn_gain,
    w_gate,
    w_up,
    w_down,
    cotangent,
):
    if not kernels_fit(tokens, w_query, key_matrix, q_gain, w_gate):
        return on_device_plain(
            tokens,
            segments,
            attn_gain,
            w_query,
            key_matrix,
            value_matrix,
            q_gain,
            k_gain,
            w_out,
            ffn_gain,
            w_gate,
            w_up,
            w_down,
            cotangent,
        )
    sequences, seq_rows, model_width = tokens.shape
    count, head_dim = lax.axis_size("ctx"), q_gain.shape[0]
    token_rows = tokens.reshape(sequences * seq_rows, model_width)
    table = jnp.asarray(rotary_table(count * seq_rows, head_dim))
    gains = {"attn_gain": attn_gain, "q_gain": q_gain, "k_gain": k_gain}
    sums = layer(
        {
            "segments": segments,
            **gains,
            "ffn_gain": ffn_gain,
            "w_query": w_query,
            "w_key": key_matrix,
            "w_value": value_matrix,
            "w_out": w_out,
            "tokens_in": token_rows,
            "table_in": table,
            "cotangent_in": cotangent.reshape(token_rows.shape),
            "w_down_in": w_down,
            "w_gate_in": w_gate,
            "w_up_in": w_up,
        }
    )
    done = dict(zip(RESULTS, hand_over([sums[name] for name in RESULTS]), strict=True))
    return (
        done["output"].reshape(tokens.shape),
        done["tokens_grad"].reshape(tokens.shape),
        done["attn_gain_sum"][0],
        done["w_query_sum"],
        done["w_key_sum"],
        done["w_value_sum"],
        done["q_gain_sum"][0, :head_dim],
        done["k_gain_sum"][0, :head_dim],
        done["w_out_sum"],
        done["ffn_gain_sum"][0],
        done["w_gate_sum"],
        done["w_up_sum"],
        done["w_down_sum"],
    )


def solution(mesh):
    in_specs = (
        P(None, "ctx", None),
        P(None, "ctx"),
        P(),
        P(None, "wt"),
        P(None, "wt"),
        P(None, "wt"),
        P(),
        P(),
        P(None, "wt"),
        P(),
        P(None, "wt"),
        P(None, "wt"),
        P(None, "wt"),
        P(None, "ctx", None),
    )
    out_specs = (
        P(None, "ctx", None),
        P(None, "ctx", None),
        P(),
        P("ctx", "wt"),
        P("ctx", "wt"),
        P("ctx", "wt"),
        P(),
        P(),
        P("ctx", "wt"),
        P(),
        P("ctx", "wt"),
        P("ctx", "wt"),
        P("ctx", "wt"),
    )
    return jax.shard_map(
        on_device, mesh=mesh, in_specs=in_specs, out_specs=out_specs, check_vma=False
    )
```
